32 devices in a mesh: dp: 4 (over y, x), fsdp: 8 (over z, core).
Axes of the slice: x: 2, y: 2, z: 4, core: 2. Of those that a mesh axis runs over, the one named last changes fastest.
Arguments:
- tokens: bfloat16 [49152, 768], P(('dp', 'fsdp')), may hold values from -6 to 6
- doc_lengths: int32 [96, 16], P(('dp', 'fsdp')), may hold values from 0 to 512, as said below
- params: bfloat16 [4464640], P(('dp', 'fsdp')), as said below
- cotangent: bfloat16 [49152, 768], P(('dp', 'fsdp')), may hold values from -6 to 6
Outputs:
- output: bfloat16 [49152, 768], P(('dp', 'fsdp'))
- grad_tokens: bfloat16 [49152, 768], P(('dp', 'fsdp'))
- grad_params: float32 [4464640], P(('dp', 'fsdp'))
The draws below stay inside these ranges and needn't reach their ends.
Inputs may be any that keep to these rules, and one draw needn't show every extreme that they name: Row r holds its documents in order from its first position, doc_lengths[r, j] tokens in slot j (0 for an unused slot); a row's lengths sum to at most 512 and the rest of the row is padding; some row holds one document of 512 tokens. params holds, flattened row-major and in this order: proj_four [4, 768, 384] (query, key, value and convolution-value projections), point_w [768, 384], dense_w [768, 768], ffn_in [2, 384, 1536], ffn_out [2, 1536, 384], depth_w [9, 768], kernel_w [384, 54], query_bias, value_bias, conv_bias, point_bias (each 384), kernel_bias (54), dense_bias, norm1_gain, norm1_shift (each 768), ffn_in_bias (3072), ffn_out_bias, norm2_gain, norm2_shift (each 768); entries after 4460598 are unused.
All inputs are finite; a program needn't handle non-finite values.
Results may differ from the reference program's by a relative error of at most 0.02.
Values may be sent and summed in bfloat16 or wider, within the bound.
A program may use at most 320 MiB of HBM per device.

```python
import math
import jax
import jax.numpy as jnp
from jax import lax

D = 768
HEADS = 6
HEAD_DIM = 64
FF = 3072
GROUPS = 2
KS = 9
ROW_LEN = 512
SLOTS = 16
ROWS = 96
TOKENS = 49152
PARAMS = 4464640


def draw_doc_lengths(key, part):
    key = jax.random.fold_in(key, 5)
    key_list = jax.random.split(key, 4)
    levels = jax.random.randint(key_list[0], (ROWS, SLOTS), 0, 6)
    upper = ROW_LEN // jnp.power(2, levels)
    lower = jnp.maximum(upper // 2, 1)
    raw_lengths = jax.random.randint(key_list[1], (ROWS, SLOTS), lower, upper + 1)
    pad_sizes = jax.random.randint(key_list[2], (ROWS, 1), 0, ROW_LEN // 8 + 1)
    chosen = jax.random.randint(key_list[3], (), 0, ROWS)
    row_index = jnp.arange(ROWS, dtype=jnp.int32)[:, None]
    first_slot = (jnp.arange(SLOTS, dtype=jnp.int32) == 0)[None, :]
    whole_row = jnp.where(first_slot, ROW_LEN, 0)
    raw_lengths = jnp.where(row_index == chosen, whole_row, raw_lengths)
    pad_sizes = jnp.where(row_index == chosen, 0, pad_sizes)
    ends = jnp.minimum(jnp.cumsum(raw_lengths, axis=1), ROW_LEN - pad_sizes)
    starts = jnp.concatenate([jnp.zeros((ROWS, 1), jnp.int32), ends[:, :-1].astype(jnp.int32)], axis=1)
    return (ends - starts).astype(jnp.int32)


def draw_params(key, part):
    key = jax.random.fold_in(key, 11)
    noise = jax.random.normal(key, (PARAMS,), jnp.float32)
    att_width = HEADS * HEAD_DIM
    plan_list = [(4 * D * att_width, D ** (-0.5), 0.0), (D * att_width, D ** (-0.5), 0.0), (D * D, 3.0 * D ** (-0.5), 0.0), (D * FF // GROUPS, (D // GROUPS) ** (-0.5), 0.0), (FF * D // GROUPS, 1.5 * (FF // GROUPS) ** (-0.5), 0.0), (KS * D, KS ** (-0.5), 0.0), (att_width * HEADS * KS, att_width ** (-0.5), 0.0), (4 * att_width, 0.2, 0.0), (HEADS * KS, 0.5, 0.0), (D, 0.2, 0.0), (D, 0.1, 1.0), (D, 0.2, 0.0), (FF, 0.2, 0.0), (D, 0.2, 0.0), (D, 0.1, 1.0), (D, 0.2, 0.0)]
    used_size = sum((entry[0] for entry in plan_list))
    scales = jnp.concatenate([jnp.full((entry[0],), entry[1], jnp.float32) for entry in plan_list] + [jnp.zeros((PARAMS - used_size,), jnp.float32)])
    centres = jnp.concatenate([jnp.full((entry[0],), entry[2], jnp.float32) for entry in plan_list] + [jnp.zeros((PARAMS - used_size,), jnp.float32)])
    return (noise * scales + centres).astype(jnp.bfloat16)


def steps_of(own_key, shape, shards, smallest, high):
    loudness = 1.0
    for position, parts in shards:
        heights = jax.random.uniform(jax.random.fold_in(jax.random.fold_in(own_key, 6), position), (parts,), jnp.float32, smallest / len(shards), high / len(shards))
        loudness = loudness * jnp.repeat(jnp.exp(heights), shape[position] // parts).reshape((-1,) + (1,) * (len(shape) - 1 - position))
    return loudness


def gaussian(rng, dims, deviation, bound, cuts=(), held_as=jnp.bfloat16):
    entries = deviation * jax.random.normal(rng, dims, jnp.float32)
    if cuts:
        entries = entries * steps_of(rng, dims, cuts, -0.22, 0.18)
    return jnp.clip(entries, -bound, bound).astype(held_as)


def setup_inputs(seed: int = 0) -> dict:
    splits = jax.random.split(jax.random.key(seed), 5)
    return {
        "tokens": gaussian(splits[0], (TOKENS, D), 1.0, 6.0, ((0, 32),)),
        "doc_lengths": draw_doc_lengths(jax.random.fold_in(splits[4], 71), 0),
        "params": draw_params(jax.random.fold_in(splits[4], 71), 0),
        "cotangent": gaussian(splits[3], (TOKENS, D), 1.0, 6.0, ((0, 32),)),
    }


EPS = 1e-12

@jax.custom_vjp
def low(v):
    return lax.optimization_barrier(v.astype(jnp.bfloat16)).astype(jnp.float32)

@jax.custom_vjp
def low_back(v):
    return v

def low_keep(v):
    return (low(v), None)

def low_pass(kept, grad):
    return (grad,)

def back_keep(v):
    return (v, None)

def back_low(kept, grad):
    return (low(grad),)
low.defvjp(low_keep, low_pass)
low_back.defvjp(back_keep, back_low)

def layout_table():
    att_width = HEADS * HEAD_DIM
    return [('proj_four', (4, D, att_width)), ('point_w', (D, att_width)), ('dense_w', (D, D)), ('ffn_in', (GROUPS, D // GROUPS, FF // GROUPS)), ('ffn_out', (GROUPS, FF // GROUPS, D // GROUPS)), ('depth_w', (KS, D)), ('kernel_w', (att_width, HEADS * KS)), ('query_bias', (att_width,)), ('value_bias', (att_width,)), ('conv_bias', (att_width,)), ('point_bias', (att_width,)), ('kernel_bias', (HEADS * KS,)), ('dense_bias', (D,)), ('norm1_gain', (D,)), ('norm1_shift', (D,)), ('ffn_in_bias', (FF,)), ('ffn_out_bias', (D,)), ('norm2_gain', (D,)), ('norm2_shift', (D,))]

def unpack(flat_values):
    result = {}
    offset = 0
    for piece_name, piece_shape in layout_table():
        piece_size = math.prod(piece_shape)
        result[piece_name] = flat_values[offset:offset + piece_size].reshape(piece_shape)
        offset += piece_size
    return result

def layer_norm(values, gain, shift):
    centre = lax.optimization_barrier(jnp.mean(values, axis=-1, keepdims=True))
    centred = values - centre
    variance = lax.optimization_barrier(jnp.mean(centred * centred, axis=-1, keepdims=True))
    return centred * lax.rsqrt(variance + EPS) * gain + shift

def shift_rows(values, offset):
    length = values.shape[0]
    padded = jnp.pad(values, ((KS, KS), (0, 0)))
    return lax.slice_in_dim(padded, KS + offset, KS + offset + length, axis=0)

def shift_ids(doc_ids, offset):
    length = doc_ids.shape[0]
    padded = jnp.pad(doc_ids, ((KS, KS),), constant_values=-1)
    return lax.slice_in_dim(padded, KS + offset, KS + offset + length, axis=0)

def doc_numbers(doc_lengths):
    ends = jnp.cumsum(doc_lengths, axis=1).astype(jnp.int32)
    positions = jnp.arange(ROW_LEN, dtype=jnp.int32)
    doc_ids = lax.optimization_barrier(jnp.sum((positions[None, :, None] >= ends[:, None, :]).astype(jnp.int32), axis=-1)).astype(jnp.int32)
    valid_mask = (positions[None, :] < ends[:, -1:]).astype(jnp.float32)
    return (doc_ids, valid_mask)

def row_layer(weights, hidden, doc_ids, valid_mask):
    att_width = HEADS * HEAD_DIM
    half_taps = KS // 2
    high = lax.Precision.HIGHEST
    length = hidden.shape[0]
    projected = jnp.einsum('td,mda->tma', hidden, weights['proj_four'], precision=high)
    queries = low(low_back(projected[:, 0]) + weights['query_bias'])
    keys_low = low(low_back(projected[:, 1]))
    values = low(low_back(projected[:, 2]) + weights['value_bias'])
    conv_vals = low(low_back(projected[:, 3]) + weights['conv_bias'])
    tap_masks = [(shift_ids(doc_ids, tap_index - half_taps) == doc_ids).astype(jnp.float32)[:, None] for tap_index in range(KS)]
    depth_conv = sum((weights['depth_w'][tap_index] * shift_rows(hidden, tap_index - half_taps) * tap_masks[tap_index] for tap_index in range(KS)))
    keyconv = low_back(jnp.dot(low(depth_conv), weights['point_w'], precision=high)) + weights['point_bias']
    conv_attn = low(keyconv * queries)
    logits = low_back(jnp.dot(conv_attn, weights['kernel_w'], precision=high)) + weights['kernel_bias']
    tap_weights = jax.nn.softmax(logits.reshape(length, HEADS, KS), axis=-1)
    conv_out = sum((tap_weights[:, :, tap_index:tap_index + 1] * (shift_rows(conv_vals, tap_index - half_taps) * tap_masks[tap_index]).reshape(length, HEADS, HEAD_DIM) for tap_index in range(KS)))
    query_heads = queries.reshape(length, HEADS, HEAD_DIM)
    key_heads = keys_low.reshape(length, HEADS, HEAD_DIM)
    value_heads = values.reshape(length, HEADS, HEAD_DIM)
    scores = low_back(jnp.einsum('qhd,khd->hqk', query_heads, key_heads, precision=high) * HEAD_DIM ** (-0.5))
    allowed = doc_ids[:, None] == doc_ids[None, :]
    scores = jnp.where(allowed[None], scores, -1e+30)
    probs = low(jax.nn.softmax(scores, axis=-1))
    context = low_back(jnp.einsum('hqk,khd->qhd', probs, value_heads, precision=high).reshape(length, att_width))
    joined = low(jnp.concatenate([context, conv_out.reshape(length, att_width)], axis=-1))
    first_sum = low_back(jnp.dot(joined, weights['dense_w'], precision=high)) + weights['dense_bias'] + hidden
    normed = layer_norm(first_sum, weights['norm1_gain'], weights['norm1_shift'])
    grouped = low(normed).reshape(length, GROUPS, D // GROUPS)
    inner_sum = low_back(jnp.einsum('tgi,gio->tgo', grouped, weights['ffn_in'], precision=high)).reshape(length, FF) + weights['ffn_in_bias']
    active = low(jax.nn.gelu(inner_sum, approximate=False)).reshape(length, GROUPS, FF // GROUPS)
    second = low_back(jnp.einsum('tgi,gio->tgo', active, weights['ffn_out'], precision=high)).reshape(length, D) + weights['ffn_out_bias'] + normed
    return layer_norm(second, weights['norm2_gain'], weights['norm2_shift']) * valid_mask[:, None]

def reference(tokens, doc_lengths, params, cotangent):
    row_count = tokens.shape[0] // ROW_LEN
    group_rows = math.gcd(row_count, 8)
    doc_ids, valid_mask = doc_numbers(doc_lengths)
    doc_ids = doc_ids.reshape(row_count // group_rows, group_rows, ROW_LEN)
    valid_mask = valid_mask.reshape(row_count // group_rows, group_rows, ROW_LEN)
    step_fn = jax.checkpoint(jax.vmap(row_layer, in_axes=(None, 0, 0, 0)))

    def forward(flat_values, hidden):
        weights = unpack(flat_values)
        blocks = hidden.reshape(row_count // group_rows, group_rows, ROW_LEN, D)
        outputs = lax.map(lambda row_parts: step_fn(weights, row_parts[0], row_parts[1], row_parts[2]), (blocks, doc_ids, valid_mask))
        return outputs.reshape(row_count * ROW_LEN, D)
    output, pullback = jax.vjp(forward, params.astype(jnp.float32), tokens.astype(jnp.float32))
    grad_flat, grad_hidden = pullback(cotangent.astype(jnp.float32))
    return (output.astype(jnp.bfloat16), grad_hidden.astype(jnp.bfloat16), grad_flat)
```

```python
import math

import jax
import jax.numpy as jnp
from jax import lax
from jax.experimental import pallas as pl
from jax.experimental.pallas import tpu as pltpu
from jax.sharding import PartitionSpec as P

D = 768
HEADS = 6
HEAD_DIM = 64
ATT = HEADS * HEAD_DIM
FF = 3072
GROUPS = 2
KS = 9
HALF = KS // 2
SLOTS = 16
EPS = 1e-12
LANES = 128
NEG = -1e30
BIG = 3e38
SCALE = HEAD_DIM ** (-0.5)

f32 = jnp.float32
bf16 = jnp.bfloat16
i32 = jnp.int32

PIECES = [
    ("proj", 4 * D, ATT),
    ("point", D, ATT),
    ("dense", D, D),
    ("ffn_in", D, FF // GROUPS),
    ("ffn_out", FF, D // GROUPS),
]
START = {}
_at = 0
for _name, _r, _c in PIECES:
    START[_name] = _at
    _at += _r * _c // LANES
START["depth"] = _at
START["kernel"] = _at + KS * D // LANES
START["bias4"] = START["kernel"] + ATT * HEADS * KS // LANES
START["tail"] = START["bias4"] + 4 * ATT // LANES
USED = START["tail"] + 61
KB = HEADS * KS

QB, VB, CB, PB, KBR, DB, N1G, N1S, FIB, FOB, N2G, N2S, DW = range(13)
VROWS = 24
TAIL = [(DB, 6), (N1G, 6), (N1S, 6), (FIB, 24), (FOB, 6), (N2G, 6), (N2S, 6)]

VM = pltpu.VMEM
VMEM_LIMIT = 62 * 1024 * 1024


def nn(a, b):
    return lax.dot_general(a, b, (((1,), (0,)), ((), ())), preferred_element_type=f32)


def nt(a, b):
    return lax.dot_general(a, b, (((1,), (1,)), ((), ())), preferred_element_type=f32)


def tn(a, b):
    return lax.dot_general(a, b, (((0,), (0,)), ((), ())), preferred_element_type=f32)


def iota(shape, axis):
    return lax.broadcasted_iota(i32, shape, axis)


def loop(count, body, unroll=1):
    def step(i, carry):
        body(i)
        return carry

    lax.fori_loop(0, count, step, 0, unroll=unroll)


def tap_perm():
    k, n = iota((LANES, LANES), 0), iota((LANES, LANES), 1)
    head, tap = n & 7, n >> 3
    return jnp.where((k == head * KS + tap) & (head < HEADS) & (tap < KS), 1.0, 0.0).astype(bf16)


def used_taps(shape):
    n = iota(shape, len(shape) - 1)
    return ((n & 7) < HEADS) & ((n >> 3) < KS)


def padded(rows):
    return -(-rows // 16) * 16


def unpack_kernel(count, rows, g_ref, wp_ref, pw_ref, dw_ref, fi_ref, fo_ref, kw_ref, vec_ref, flat, kwt):
    pad = padded(rows)

    def spread(i):
        flat[pl.ds(i * rows, pad), :] = g_ref[i].astype(f32)

    for i in range(count):
        spread(i)

    def piece(name, out, height, width, row0, col0, skip):
        per = width // LANES
        base = START[name] + skip
        for c in range(per):
            for r in range(0, height, 256):
                part = min(256, height - r)
                out[row0 + r : row0 + r + part, col0 + c * LANES : col0 + (c + 1) * LANES] = flat[
                    pl.ds(base + r * per + c, part, stride=per), :
                ].astype(bf16)

    for m in range(4):
        piece("proj", wp_ref, D, ATT, 0, m * ATT, m * D * ATT // LANES)
    piece("point", pw_ref, D, ATT, 0, 0, 0)
    piece("dense", dw_ref, D, D, 0, 0, 0)
    piece("ffn_in", fi_ref, D, FF // GROUPS, 0, 0, 0)
    piece("ffn_out", fo_ref, FF, D // GROUPS, 0, 0, 0)

    vec_ref[...] = jnp.zeros_like(vec_ref)
    for row in range(4):
        for c in range(3):
            at = START["bias4"] + row * 3 + c
            vec_ref[row : row + 1, c * LANES : (c + 1) * LANES] = flat[at : at + 1, :]
    for j in range(KS):
        for c in range(6):
            at = START["depth"] + j * 6 + c
            vec_ref[DW + j : DW + j + 1, c * LANES : (c + 1) * LANES] = flat[at : at + 1, :]
    at = START["tail"]
    lane = iota((64, LANES), 1)
    first = pltpu.roll(flat[at : at + 64, :], LANES - KB, 1)
    second = pltpu.roll(flat[at + 1 : at + 65, :], LANES - KB, 1)
    kwt[0:64, :] = jnp.where(lane < LANES - KB, first, second)
    at = 0
    for row, many in TAIL:
        for c in range(many):
            vec_ref[row : row + 1, c * LANES : (c + 1) * LANES] = kwt[at + c : at + c + 1, :]
        at += many
    perm = tap_perm()
    lane8 = iota((16, LANES), 1)
    kb = jnp.broadcast_to(flat[START["tail"] : START["tail"] + 1, :], (16, LANES))
    kb = nn(jnp.where(lane8 < KB, kb, 0.0).astype(bf16), perm)
    kb = jnp.where(used_taps((16, LANES)), kb, NEG)
    vec_ref[KBR : KBR + 1, 0:LANES] = kb[0:1]

    lane = iota((8, LANES), 1)
    for a in range(64):
        c0, ln = divmod(a * KB, LANES)
        at = START["kernel"] + c0
        x = pltpu.roll(flat[pl.ds(at, 8, stride=27), :], (LANES - ln) % LANES, 1)
        if ln + KB > LANES:
            y = pltpu.roll(flat[pl.ds(at + 1, 8, stride=27), :], (LANES - ln) % LANES, 1)
            x = jnp.where(lane < LANES - ln, x, y)
        kwt[pl.ds(a, 8, stride=64), :] = jnp.where(lane < KB, x, 0.0)
    kw_ref[...] = nn(kwt[0:ATT, :].astype(bf16), perm).astype(bf16)


def flat_rows(count, rows):
    return -(-(max((count - 1) * rows + padded(rows), USED + 240)) // 8) * 8


def run_unpack(gathered, rows):
    count = gathered.shape[0]
    shapes = [(D, 4 * ATT), (D, ATT), (D, D), (D, FF // GROUPS), (FF, D // GROUPS), (ATT, LANES)]
    out = [jax.ShapeDtypeStruct(s, bf16) for s in shapes] + [jax.ShapeDtypeStruct((VROWS, FF), f32)]

    def body(*refs):
        unpack_kernel(count, rows, *refs)

    return pl.pallas_call(
        body,
        out_shape=out,
        in_specs=[pl.BlockSpec(memory_space=VM)],
        out_specs=[pl.BlockSpec(memory_space=VM)] * len(out),
        scratch_shapes=[VM((flat_rows(count, rows), LANES), f32), VM((512, LANES), f32)],
        compiler_params=pltpu.CompilerParams(vmem_limit_bytes=VMEM_LIMIT),
        name="unpack",
    )(gathered)


def pack_kernel(count, rows, gp_ref, gpw_ref, gdw_ref, gfi_ref, gfo_ref, gkw_ref, va_ref, vb_ref, send_ref, flat, kwt, vec):
    total = flat.shape[0]
    used8 = START["depth"] // 8 * 8
    flat[used8:total, :] = jnp.zeros((total - used8, LANES), f32)
    vec[...] = va_ref[...] + vb_ref[...]

    def piece(name, src, height, width, row0, col0, skip):
        per = width // LANES
        base = START[name] + skip
        for c in range(per):
            for r in range(0, height, 256):
                part = min(256, height - r)
                flat[pl.ds(base + r * per + c, part, stride=per), :] = src[
                    row0 + r : row0 + r + part, col0 + c * LANES : col0 + (c + 1) * LANES
                ]

    for m in range(4):
        piece("proj", gp_ref, D, ATT, 0, m * ATT, m * D * ATT // LANES)
    piece("point", gpw_ref, D, ATT, 0, 0, 0)
    piece("dense", gdw_ref, D, D, 0, 0, 0)
    piece("ffn_in", gfi_ref, D, FF // GROUPS, 0, 0, 0)
    piece("ffn_out", gfo_ref, FF, D // GROUPS, 0, 0, 0)

    perm = tap_perm()
    kwt[...] = jnp.zeros_like(kwt)
    kwt[0:ATT, :] = nt(gkw_ref[...].astype(bf16), perm)
    lane = iota((8, LANES), 1)
    for a in range(64):
        c0, ln = divmod(a * KB, LANES)
        at = START["kernel"] + c0
        x = pltpu.roll(kwt[pl.ds(a, 8, stride=64), :], ln, 1)
        if ln + KB > LANES:
            flat[pl.ds(at, 8, stride=27), :] += jnp.where(lane >= ln, x, 0.0)
            flat[pl.ds(at + 1, 8, stride=27), :] += jnp.where(lane < ln, x, 0.0)
        else:
            flat[pl.ds(at, 8, stride=27), :] += x
    for row in range(4):
        for c in range(3):
            at = START["bias4"] + row * 3 + c
            flat[at : at + 1, :] = vec[row : row + 1, c * LANES : (c + 1) * LANES]
    for j in range(KS):
        for c in range(6):
            at = START["depth"] + j * 6 + c
            flat[at : at + 1, :] = vec[DW + j : DW + j + 1, c * LANES : (c + 1) * LANES]
    kwt[...] = jnp.zeros_like(kwt)
    at = 8
    for row, many in TAIL:
        for c in range(many):
            kwt[at + c : at + c + 1, :] = vec[row : row + 1, c * LANES : (c + 1) * LANES]
        at += many
    lane = iota((72, LANES), 1)
    before = pltpu.roll(kwt[7:79, :], KB, 1)
    here = pltpu.roll(kwt[8:80, :], KB, 1)
    at = START["tail"]
    flat[at : at + 72, :] = jnp.where(lane < KB, before, here)
    kb = jnp.broadcast_to(vec[KBR : KBR + 1, 0:LANES], (16, LANES))
    kb = nt(jnp.where(used_taps((16, LANES)), kb, 0.0).astype(bf16), perm)
    lane = iota((1, LANES), 1)
    flat[at : at + 1, :] = jnp.where(lane < KB, kb[0:1], flat[at : at + 1, :])

    pad = padded(rows)
    for i in range(count):
        send_ref[i] = flat[i * rows : i * rows + pad, :].astype(bf16)


def run_pack(count, rows, gp, gpw, gdw, gfi, gfo, gkw, va, vb):
    def body(*refs):
        pack_kernel(count, rows, *refs)

    return pl.pallas_call(
        body,
        out_shape=jax.ShapeDtypeStruct((count, padded(rows), LANES), bf16),
        in_specs=[pl.BlockSpec(memory_space=VM)] * 8,
        out_specs=pl.BlockSpec(memory_space=VM),
        scratch_shapes=[
            VM((flat_rows(count, rows), LANES), f32),
            VM((512, LANES), f32),
            VM((VROWS, FF), f32),
        ],
        compiler_params=pltpu.CompilerParams(vmem_limit_bytes=VMEM_LIMIT),
        name="pack",
    )(gp, gpw, gdw, gfi, gfo, gkw, va, vb)


def doc_marks(r, length, len_ref, dcol, tm, mb):
    t = iota((length, LANES), 0)
    u = iota((8, length), 1)
    ends = jnp.int32(0)
    d = jnp.zeros((length, LANES), i32)
    e = jnp.zeros((8, length), i32)
    for j in range(SLOTS):
        ends = ends + len_ref[r, j]
        d = d + (t >= ends).astype(i32)
        e = e + (u >= ends).astype(i32)
    dcol[0:8, :] = jnp.full((8, LANES), -1, i32)
    dcol[8 : 8 + length, :] = d
    dcol[8 + length : 16 + length, :] = jnp.full((8, LANES), -1, i32)
    for j in range(KS):
        at = 8 + j - HALF
        tm[j] = (dcol[at : at + length, :] == d).astype(f32)
    for c in range(length // LANES):
        mb[:, c * LANES : (c + 1) * LANES] = jnp.where(d == e[0:1, c * LANES : (c + 1) * LANES], BIG, NEG)


def tap_lanes(tm, length):
    tap = iota((length, LANES), 1) >> 3
    out = jnp.zeros((length, LANES), f32)
    for j in range(KS):
        out = jnp.where(tap == j, tm[j], out)
    return jnp.where(used_taps((length, LANES)), out, 0.0)


def over_taps(x, op):
    for s in (8, 16, 32, 64):
        x = op(x, pltpu.roll(x, s, 1))
    return x


def fill_emat(emat):
    k, c = iota((2 * LANES, ATT), 0) & (LANES - 1), iota((2 * LANES, ATT), 1)
    for j in range(KS):
        emat[:, j * ATT : (j + 1) * ATT] = jnp.where(k == j * 8 + (c >> 6), 1.0, 0.0).astype(bf16)


def two_parts(x):
    high = x.astype(bf16)
    return jnp.concatenate([high, (x - high.astype(f32)).astype(bf16)], axis=1)


def zero_pads(ref, length):
    for c in range(ref.shape[0]):
        ref[c, 0:8, :] = jnp.zeros((8, LANES), f32)
        ref[c, 8 + length : 16 + length, :] = jnp.zeros((8, LANES), f32)


def fwd_kernel(length, len_ref, tok_ref, wp_ref, pw_ref, kw_ref, vec_ref,
               qkvc_ref, kc_ref, dep_ref, ca_ref, tap_ref, join_ref, lse_ref,
               xs, cs, dcol, tm, mb, emat, acc):
    row = pl.program_id(0)

    @pl.when(row == 0)
    def _():
        fill_emat(emat)

    doc_marks(row, length, len_ref, dcol, tm, mb)
    tok = tok_ref[...]
    zero_pads(xs, length)
    zero_pads(cs, length)
    for c in range(6):
        xs[c, 8 : 8 + length, :] = tok[:, c * LANES : (c + 1) * LANES].astype(f32)
    for m, bias in ((0, QB), (1, None), (2, VB), (3, CB)):
        x = nn(tok, wp_ref[:, m * ATT : (m + 1) * ATT])
        if bias is not None:
            x = x + vec_ref[bias : bias + 1, 0:ATT]
        x = x.astype(bf16)
        qkvc_ref[:, m * ATT : (m + 1) * ATT] = x
        if m == 3:
            for c in range(3):
                cs[c, 8 : 8 + length, :] = x[:, c * LANES : (c + 1) * LANES].astype(f32)

    step = 64

    for c in range(6):
        w = [vec_ref[DW + j : DW + j + 1, c * LANES : (c + 1) * LANES] for j in range(KS)]
        for r in range(0, length, step):
            total = w[HALF] * xs[c, 8 + r : 8 + r + step, :]
            for j in range(KS):
                if j != HALF:
                    at = 8 + r + j - HALF
                    total = total + w[j] * (xs[c, at : at + step, :] * tm[j, r : r + step, :])
            dep_ref[r : r + step, c * LANES : (c + 1) * LANES] = total.astype(bf16)

    keyconv = nn(dep_ref[...], pw_ref[...]) + vec_ref[PB : PB + 1, 0:ATT]
    kc_ref[...] = keyconv.astype(bf16)
    ca = (keyconv * qkvc_ref[:, 0:ATT].astype(f32)).astype(bf16)
    ca_ref[...] = ca
    logits = nn(ca, kw_ref[...]) + vec_ref[KBR : KBR + 1, 0:LANES]
    e = jnp.exp(logits - over_taps(logits, jnp.maximum))
    taps = e / over_taps(e, jnp.add)
    tap_ref[...] = taps
    spread = two_parts(taps * tap_lanes(tm, length))
    for j in range(KS):
        t = nn(spread, emat[:, j * ATT : (j + 1) * ATT])
        for c in range(3):
            at = 8 + j - HALF
            part = t[:, c * LANES : (c + 1) * LANES] * cs[c, at : at + length, :]
            if j:
                part = part + acc[:, c * LANES : (c + 1) * LANES]
            if j < KS - 1:
                acc[:, c * LANES : (c + 1) * LANES] = part
            else:
                join_ref[:, ATT + c * LANES : ATT + (c + 1) * LANES] = part.astype(bf16)

    for p in range(3):
        cols = slice(p * LANES, (p + 1) * LANES)
        q, k, v = (qkvc_ref[:, m * ATT + p * LANES : m * ATT + (p + 1) * LANES] for m in range(3))
        qs = q.astype(f32) * SCALE
        vt = v.astype(f32).T
        lane, sub = iota((length, LANES), 1), iota((LANES, length), 0)
        halves = []
        for h in range(2):
            qh = jnp.where((lane >= HEAD_DIM) == bool(h), qs, 0.0).astype(bf16)
            vh = jnp.where((sub >= HEAD_DIM) == bool(h), vt, 1.0).astype(bf16)
            z = jnp.minimum(nt(k, qh), mb[...])
            top = jnp.max(z, axis=0, keepdims=True)
            o = nn(vh, jnp.exp(z - top).astype(bf16))
            s = o[(1 - h) * HEAD_DIM : (1 - h) * HEAD_DIM + 1, :]
            lse_ref[0, 2 * p + h : 2 * p + h + 1, :] = top + jnp.log(s)
            halves.append(o[h * HEAD_DIM : (h + 1) * HEAD_DIM, :] / s)
        join_ref[:, cols] = jnp.concatenate(halves, axis=0).T.astype(bf16)


def blocked(rows, cols):
    return pl.BlockSpec((rows, cols), lambda r: (r, 0))


def row_scratch(length):
    return [
        VM((6, length + 16, LANES), f32),
        VM((3, length + 16, LANES), f32),
        VM((length + 16, LANES), i32),
        VM((KS, length, LANES), f32),
        VM((length, length), f32),
        VM((2 * LANES, KS * ATT), bf16),
    ]


def run_fwd(tokens, lengths, wp, pw, kw, vec):
    rows, count = lengths.shape[0], tokens.shape[0]
    length = count // rows

    def body(*refs):
        fwd_kernel(length, *refs)

    full = pl.BlockSpec(memory_space=VM)
    return pl.pallas_call(
        body,
        grid=(rows,),
        out_shape=[
            jax.ShapeDtypeStruct((count, 4 * ATT), bf16),
            jax.ShapeDtypeStruct((count, ATT), bf16),
            jax.ShapeDtypeStruct((count, D), bf16),
            jax.ShapeDtypeStruct((count, ATT), bf16),
            jax.ShapeDtypeStruct((count, LANES), f32),
            jax.ShapeDtypeStruct((count, D), bf16),
            jax.ShapeDtypeStruct((rows, 8, length), f32),
        ],
        in_specs=[pl.BlockSpec(memory_space=pltpu.SMEM), blocked(length, D), full, full, full, full],
        out_specs=[
            blocked(length, 4 * ATT),
            blocked(length, ATT),
            blocked(length, D),
            blocked(length, ATT),
            blocked(length, LANES),
            blocked(length, D),
            pl.BlockSpec((1, 8, length), lambda r: (r, 0, 0)),
        ],
        scratch_shapes=row_scratch(length) + [VM((length, ATT), f32)],
        compiler_params=pltpu.CompilerParams(vmem_limit_bytes=VMEM_LIMIT),
        name="row_forward",
    )(lengths, tokens, wp, pw, kw, vec)


def mid_kernel(length, len_ref, tok_ref, join_ref, cot_ref, dw_ref, fi_ref, fo_ref, vec_ref,
               out_ref, gf_ref, gj_ref, gdw_ref, gfi_ref, gfo_ref, gv_ref,
               xh1, rs1, nl, act, slope, gsec, gsl):
    row = pl.program_id(0)
    fg, dg = FF // GROUPS, D // GROUPS

    @pl.when(row == 0)
    def _():
        for ref in (gdw_ref, gfi_ref, gfo_ref, gv_ref):
            ref[...] = jnp.zeros_like(ref)

    used = jnp.int32(0)
    for j in range(SLOTS):
        used = used + len_ref[row, j]

    def vec(r, n=D):
        return vec_ref[r : r + 1, 0:n]

    step = 64
    gsec[...] = nn(join_ref[...], dw_ref[...])

    def norm1(i):
        at = pl.ds(pl.multiple_of(i * step, step), step)
        z = gsec[at, :] + vec(DB) + tok_ref[at, :].astype(f32)
        z = z - jnp.mean(z, axis=1, keepdims=True)
        r = lax.rsqrt(jnp.mean(z * z, axis=1, keepdims=True) + EPS)
        x = z * r
        xh1[at, :] = x
        rs1[at, :] = jnp.broadcast_to(r, (step, LANES))
        nl[at, :] = (x * vec(N1G) + vec(N1S)).astype(bf16)

    loop(length // step, norm1)

    tile = 512
    per = fg // tile

    for g in range(GROUPS):
        def widen(i, g=g):
            col = pl.ds(pl.multiple_of(i * tile, tile), tile)
            col2 = pl.ds(pl.multiple_of(g * fg + i * tile, tile), tile)
            x = nn(nl[:, g * dg : (g + 1) * dg], fi_ref[g * dg : (g + 1) * dg, col]) + vec_ref[FIB : FIB + 1, col2]
            e = jnp.exp(x * x * -0.5)
            t = pl.reciprocal(1.0 + 0.2316419 * jnp.abs(x), approx=True)
            poly = t * 0.53070271450 - 0.72657601350
            poly = poly * t + 0.71070687050
            poly = poly * t - 0.14224836800
            poly = poly * t + 0.12741479600
            q = poly * t * e
            phi = jnp.where(x >= 0, 1.0 - q, q)
            act[:, col2] = (x * phi).astype(bf16)
            slope[:, col2] = (phi + x * 0.3989422804014327 * e).astype(bf16)

        loop(per, widen)

    for g in range(GROUPS):
        gsec[:, g * dg : (g + 1) * dg] = nn(act[:, g * fg : (g + 1) * fg], fo_ref[g * fg : (g + 1) * fg, :])

    def rows8(x):
        total = x[0:8]
        for k in range(8, x.shape[0], 8):
            total = total + x[k : k + 8]
        return total

    def norm2(i, carry):
        at = pl.ds(pl.multiple_of(i * step, step), step)
        norm = xh1[at, :] * vec(N1G) + vec(N1S)
        z = gsec[at, :] + vec(FOB) + norm
        z = z - jnp.mean(z, axis=1, keepdims=True)
        r = lax.rsqrt(jnp.mean(z * z, axis=1, keepdims=True) + EPS)
        x = z * r
        keep = ((iota((step, 1), 0) + i * step) < used).astype(f32)
        out_ref[at, :] = ((x * vec(N2G) + vec(N2S)) * keep).astype(bf16)
        gf = cot_ref[at, :].astype(f32) * keep
        gx = gf * x
        e = gf * vec(N2G)
        gz = r * (e - jnp.mean(e, axis=1, keepdims=True) - x * jnp.mean(e * x, axis=1, keepdims=True))
        gsec[at, :] = gz
        gsl[at, :] = gz.astype(bf16)
        return (carry[0] + rows8(gx), carry[1] + rows8(gf), carry[2] + rows8(gz))

    none = jnp.zeros((8, D), f32)
    sums = lax.fori_loop(0, length // step, norm2, (none, none, none))

    def add(r, value):
        gv_ref[r : r + 1, 0 : value.shape[1]] += jnp.sum(value, axis=0, keepdims=True)

    for r, value in zip((N2G, N2S, FOB), sums):
        add(r, value)

    for g in range(GROUPS):
        def narrow(i, g=g):
            r0 = pl.ds(pl.multiple_of(g * fg + i * tile, tile), tile)
            x = nt(gsl[:, g * dg : (g + 1) * dg], fo_ref[r0, :]) * slope[:, r0].astype(f32)
            gv_ref[FIB : FIB + 1, r0] += jnp.sum(x, axis=0, keepdims=True)
            slope[:, r0] = x.astype(bf16)
            gfo_ref[r0, :] += tn(act[:, r0], gsl[:, g * dg : (g + 1) * dg])
            col = pl.ds(pl.multiple_of(i * tile, tile), tile)
            gfi_ref[g * dg : (g + 1) * dg, col] += tn(nl[:, g * dg : (g + 1) * dg], slope[:, r0])

        loop(per, narrow)
    for g in range(GROUPS):
        gsec[:, g * dg : (g + 1) * dg] += nt(slope[:, g * fg : (g + 1) * fg], fi_ref[g * dg : (g + 1) * dg, :])

    def norm1_back(i, carry):
        at = pl.ds(pl.multiple_of(i * step, step), step)
        gn = gsec[at, :]
        x = xh1[at, :]
        e = gn * vec(N1G)
        r = rs1[at, :]
        r = jnp.concatenate([r] * (D // LANES), axis=1)
        gz = r * (e - jnp.mean(e, axis=1, keepdims=True) - x * jnp.mean(e * x, axis=1, keepdims=True))
        gf_ref[at, :] = gz.astype(bf16)
        return (carry[0] + rows8(gn * x), carry[1] + rows8(gn), carry[2] + rows8(gz))

    sums = lax.fori_loop(0, length // step, norm1_back, (none, none, none))
    for r, value in zip((N1G, N1S, DB), sums):
        add(r, value)
    low = gf_ref[...]
    gj_ref[...] = nt(low, dw_ref[...]).astype(bf16)
    gdw_ref[...] += tn(join_ref[...], low)


def run_mid(tokens, lengths, joined, cotangent, dw, fi, fo, vec):
    rows, count = lengths.shape[0], tokens.shape[0]
    length = count // rows

    def body(*refs):
        mid_kernel(length, *refs)

    full = pl.BlockSpec(memory_space=VM)
    return pl.pallas_call(
        body,
        grid=(rows,),
        out_shape=[
            jax.ShapeDtypeStruct((count, D), bf16),
            jax.ShapeDtypeStruct((count, D), bf16),
            jax.ShapeDtypeStruct((count, D), bf16),
            jax.ShapeDtypeStruct((D, D), f32),
            jax.ShapeDtypeStruct((D, FF // GROUPS), f32),
            jax.ShapeDtypeStruct((FF, D // GROUPS), f32),
            jax.ShapeDtypeStruct((VROWS, FF), f32),
        ],
        in_specs=[pl.BlockSpec(memory_space=pltpu.SMEM)] + [blocked(length, D)] * 3 + [full] * 4,
        out_specs=[blocked(length, D)] * 3 + [full] * 4,
        scratch_shapes=[
            VM((length, D), f32),
            VM((length, LANES), f32),
            VM((length, D), bf16),
            VM((length, FF), bf16),
            VM((length, FF), bf16),
            VM((length, D), f32),
            VM((length, D), bf16),
        ],
        compiler_params=pltpu.CompilerParams(vmem_limit_bytes=VMEM_LIMIT),
        name="mid",
    )(lengths, tokens, joined, cotangent, dw, fi, fo, vec)


def bwd_kernel(length, len_ref, tok_ref, qkvc_ref, kc_ref, dep_ref, ca_ref, tap_ref, join_ref, lse_ref, gf_ref, gj_ref,
               wp_ref, pw_ref, kw_ref, vec_ref,
               gt_ref, gp_ref, gpw_ref, gkw_ref, gv_ref,
               ds, cs, dcol, tm, mb, emat, gs, tp, prod, gq, gfour, acc):
    row = pl.program_id(0)

    @pl.when(row == 0)
    def _():
        fill_emat(emat)
        for ref in (gp_ref, gpw_ref, gkw_ref, gv_ref):
            ref[...] = jnp.zeros_like(ref)

    doc_marks(row, length, len_ref, dcol, tm, mb)
    for ref in (ds, cs, gs, tp):
        zero_pads(ref, length)

    def add(r, value):
        gv_ref[r : r + 1, 0 : value.shape[1]] += jnp.sum(value, axis=0, keepdims=True)

    for p in range(3):
        cols = slice(p * LANES, (p + 1) * LANES)
        q, k, v = (qkvc_ref[:, m * ATT + p * LANES : m * ATT + (p + 1) * LANES] for m in range(3))
        g = gj_ref[:, cols]
        lane, sub = iota((length, LANES), 1), iota((16, LANES), 1)
        which = iota((16, LANES), 0)
        marks = jnp.where((sub >= HEAD_DIM) == (which >= 8), 1.0, 0.0).astype(bf16)
        dots = g.astype(f32) * join_ref[:, cols].astype(f32)
        high = dots.astype(bf16)
        dots = nt(marks, high) + nt(marks, (dots - high.astype(f32)).astype(bf16))
        qs = q.astype(f32) * SCALE
        kt = k.astype(f32).T.astype(bf16)
        gk, gv, gqt = None, None, []
        for h in range(2):
            own = (lane >= HEAD_DIM) == bool(h)
            qh = jnp.where(own, qs, 0.0).astype(bf16)
            gh = jnp.where(own, g.astype(f32), 0.0).astype(bf16)
            prob = jnp.exp(jnp.minimum(nt(k, qh), mb[...]) - lse_ref[0, 2 * p + h : 2 * p + h + 1, :])
            dsc = (prob * (nt(v, gh) - dots[8 * h : 8 * h + 1, :])).astype(bf16)
            a, b = nn(prob.astype(bf16), gh), nn(dsc, qh)
            gv, gk = (a, b) if h == 0 else (gv + a, gk + b)
            gqt.append(nn(kt, dsc)[h * HEAD_DIM : (h + 1) * HEAD_DIM, :])
        gq[:, cols] = jnp.concatenate(gqt, axis=0).T * SCALE
        gfour[:, ATT + p * LANES : ATT + (p + 1) * LANES] = gk.astype(bf16)
        gfour[:, 2 * ATT + p * LANES : 2 * ATT + (p + 1) * LANES] = gv.astype(bf16)
        gv_ref[VB : VB + 1, cols] += jnp.sum(gv, axis=0, keepdims=True)

    for c in range(3):
        cs[c, 8 : 8 + length, :] = qkvc_ref[:, 3 * ATT + c * LANES : 3 * ATT + (c + 1) * LANES].astype(f32)
        gs[c, 8 : 8 + length, :] = gj_ref[:, ATT + c * LANES : ATT + (c + 1) * LANES].astype(f32)
    for j in range(KS):
        for c in range(3):
            at = 8 + j - HALF
            prod[:, j * ATT + c * LANES : j * ATT + (c + 1) * LANES] = (
                gs[c, 8 : 8 + length, :] * cs[c, at : at + length, :]
            ).astype(bf16)
    marks = tap_lanes(tm, length)
    gtaps = nt(prod[...], emat[0:LANES, :]) * marks
    taps = jnp.where(used_taps((length, LANES)), tap_ref[...], 0.0)
    glog = taps * (gtaps - over_taps(taps * gtaps, jnp.add))
    add(KBR, glog)
    glog = glog.astype(bf16)
    gkw_ref[...] += tn(ca_ref[...], glog)
    gca = nt(glog, kw_ref[...])

    tp[0, 8 : 8 + length, :] = taps * marks
    tap = iota((length, LANES), 1) >> 3
    moved = jnp.zeros((length, LANES), f32)
    for j in range(KS):
        at = 8 + HALF - j
        moved = jnp.where(tap == j, tp[0, at : at + length, :], moved)
    spread = two_parts(moved)
    for j in range(KS):
        t = nn(spread, emat[:, j * ATT : (j + 1) * ATT])
        for c in range(3):
            at = 8 + HALF - j
            part = t[:, c * LANES : (c + 1) * LANES] * gs[c, at : at + length, :]
            if j:
                part = part + acc[:, c * LANES : (c + 1) * LANES]
            if j < KS - 1:
                acc[:, c * LANES : (c + 1) * LANES] = part
            else:
                gfour[:, 3 * ATT + c * LANES : 3 * ATT + (c + 1) * LANES] = part.astype(bf16)
                gv_ref[CB : CB + 1, c * LANES : (c + 1) * LANES] += jnp.sum(part, axis=0, keepdims=True)

    gkc = gca * qkvc_ref[:, 0:ATT].astype(f32)
    gquery = gq[...] + gca * kc_ref[...].astype(f32)
    add(QB, gquery)
    gfour[:, 0:ATT] = gquery.astype(bf16)
    add(PB, gkc)
    gkc = gkc.astype(bf16)
    gpw_ref[...] += tn(dep_ref[...], gkc)
    for c in range(3):
        x = nt(gkc, pw_ref[c * 256 : (c + 1) * 256, :])
        ds[2 * c, 8 : 8 + length, :] = x[:, 0:LANES]
        ds[2 * c + 1, 8 : 8 + length, :] = x[:, LANES:]
    for m in range(4):
        gp_ref[:, m * ATT : (m + 1) * ATT] += tn(tok_ref[...], gfour[:, m * ATT : (m + 1) * ATT])

    step = 64
    for c in range(6):
        cols = slice(c * LANES, (c + 1) * LANES)
        w = [vec_ref[DW + j : DW + j + 1, cols] for j in range(KS)]
        sums = [None] * KS
        if c % 2 == 0:
            direct = nt(gfour[...], wp_ref[c * LANES : (c + 2) * LANES, :])
        for r in range(0, length, step):
            tok = tok_ref[r : r + step, cols].astype(f32)
            total = gf_ref[r : r + step, cols].astype(f32) + direct[r : r + step, (c % 2) * LANES : (c % 2 + 1) * LANES]
            for j in range(KS):
                at = 8 + r + j - HALF
                u = ds[c, at : at + step, :]
                if j != HALF:
                    u = u * tm[j, r : r + step, :]
                total = total + w[KS - 1 - j] * u
                u = tok * u
                part = u[0:8]
                for s in range(8, step, 8):
                    part = part + u[s : s + 8]
                sums[j] = part if r == 0 else sums[j] + part
            gt_ref[r : r + step, cols] = total.astype(bf16)
        for j in range(KS):
            gv_ref[DW + KS - 1 - j : DW + KS - j, cols] += jnp.sum(sums[j], axis=0, keepdims=True)


def run_bwd(tokens, lengths, saved, gf, gj, wp, pw, kw, vec):
    qkvc, kc, dep, ca, taps, joined, lse = saved
    rows, count = lengths.shape[0], tokens.shape[0]
    length = count // rows

    def body(*refs):
        bwd_kernel(length, *refs)

    full = pl.BlockSpec(memory_space=VM)
    return pl.pallas_call(
        body,
        grid=(rows,),
        out_shape=[
            jax.ShapeDtypeStruct((count, D), bf16),
            jax.ShapeDtypeStruct((D, 4 * ATT), f32),
            jax.ShapeDtypeStruct((D, ATT), f32),
            jax.ShapeDtypeStruct((ATT, LANES), f32),
            jax.ShapeDtypeStruct((VROWS, FF), f32),
        ],
        in_specs=[
            pl.BlockSpec(memory_space=pltpu.SMEM),
            blocked(length, D),
            blocked(length, 4 * ATT),
            blocked(length, ATT),
            blocked(length, D),
            blocked(length, ATT),
            blocked(length, LANES),
            blocked(length, D),
            pl.BlockSpec((1, 8, length), lambda r: (r, 0, 0)),
            blocked(length, D),
            blocked(length, D),
            full,
            full,
            full,
            full,
        ],
        out_specs=[blocked(length, D)] + [full] * 4,
        scratch_shapes=row_scratch(length)
        + [
            VM((3, length + 16, LANES), f32),
            VM((1, length + 16, LANES), f32),
            VM((length, KS * ATT), bf16),
            VM((length, ATT), f32),
            VM((length, 4 * ATT), bf16),
            VM((length, ATT), f32),
        ],
        compiler_params=pltpu.CompilerParams(vmem_limit_bytes=VMEM_LIMIT),
        name="row_backward",
    )(lengths, tokens, qkvc, kc, dep, ca, taps, joined, lse, gf, gj, wp, pw, kw, vec)


def local_layer(tokens, lengths, cotangent, gathered, rows):
    count = gathered.shape[0]
    wp, pw, dw, fi, fo, kw, vec = run_unpack(gathered, rows)
    saved = run_fwd(tokens, lengths, wp, pw, kw, vec)
    output, gf, gj, gdw, gfi, gfo, va = run_mid(tokens, lengths, saved[5], cotangent, dw, fi, fo, vec)
    gt, gp, gpw, gkw, vb = run_bwd(tokens, lengths, saved, gf, gj, wp, pw, kw, vec)
    send = run_pack(count, rows, gp, gpw, gdw, gfi, gfo, gkw, va, vb)
    return output, gt, send


def shards(tokens, doc_lengths, params, cotangent):
    rows = params.shape[0] // LANES
    outer, inner = lax.axis_size("dp"), lax.axis_size("fsdp")
    count = outer * inner
    pad = padded(rows)
    own = jnp.pad(params.reshape(rows, LANES), ((0, pad - rows), (0, 0)))
    gathered = lax.all_gather(own, ("dp", "fsdp"), axis=0, tiled=True).reshape(count, pad, LANES)
    output, gt, send = local_layer(tokens, doc_lengths, cotangent, gathered, rows)
    part = lax.psum_scatter(send.reshape(outer, inner, pad, LANES), "fsdp", scatter_dimension=1, tiled=True)
    part = lax.psum_scatter(part, "dp", scatter_dimension=0, tiled=True).astype(f32)
    part = lax.optimization_barrier(part.reshape(pad, LANES))
    return output, gt, part[:rows].reshape(rows * LANES)


def solution(mesh):
    axes = ("dp", "fsdp")
    placed = (P(axes, None), P(axes, None), P(axes), P(axes, None))
    return jax.shard_map(
        shards,
        mesh=mesh,
        in_specs=placed,
        out_specs=(P(axes, None), P(axes, None), P(axes)),
        check_vma=False,
    )
```

```python
import math

import jax
import jax.numpy as jnp
from jax import lax
from jax.experimental import pallas as pl
from jax.experimental.pallas import tpu as pltpu
from jax.sharding import PartitionSpec as P

D = 768
HEADS = 6
HEAD_DIM = 64
ATT = HEADS * HEAD_DIM
FF = 3072
GROUPS = 2
KS = 9
HALF = KS // 2
SLOTS = 16
EPS = 1e-12
LANES = 128
NEG = -1e30
BIG = 3e38
SCALE = HEAD_DIM ** (-0.5)

f32 = jnp.float32
bf16 = jnp.bfloat16
i32 = jnp.int32

PIECES = [
    ("proj", 4 * D, ATT),
    ("point", D, ATT),
    ("dense", D, D),
    ("ffn_in", D, FF // GROUPS),
    ("ffn_out", FF, D // GROUPS),
]
START = {}
_at = 0
for _name, _r, _c in PIECES:
    START[_name] = _at
    _at += _r * _c // LANES
START["depth"] = _at
START["kernel"] = _at + KS * D // LANES
START["bias4"] = START["kernel"] + ATT * HEADS * KS // LANES
START["tail"] = START["bias4"] + 4 * ATT // LANES
USED = START["tail"] + 61
KB = HEADS * KS

QB, VB, CB, PB, KBR, DB, N1G, N1S, FIB, FOB, N2G, N2S, DW = range(13)
VROWS = 24
TAIL = [(DB, 6), (N1G, 6), (N1S, 6), (FIB, 24), (FOB, 6), (N2G, 6), (N2S, 6)]

VM = pltpu.VMEM
VMEM_LIMIT = 62 * 1024 * 1024


def nn(a, b):
    return lax.dot_general(a, b, (((1,), (0,)), ((), ())), preferred_element_type=f32)


def nt(a, b):
    return lax.dot_general(a, b, (((1,), (1,)), ((), ())), preferred_element_type=f32)


def tn(a, b):
    return lax.dot_general(a, b, (((0,), (0,)), ((), ())), preferred_element_type=f32)


def iota(shape, axis):
    return lax.broadcasted_iota(i32, shape, axis)


def loop(count, body, unroll=1):
    def step(i, carry):
        body(i)
        return carry

    lax.fori_loop(0, count, step, 0, unroll=unroll)


def tap_perm():
    k, n = iota((LANES, LANES), 0), iota((LANES, LANES), 1)
    head, tap = n & 7, n >> 3
    return jnp.where((k == head * KS + tap) & (head < HEADS) & (tap < KS), 1.0, 0.0).astype(bf16)


def used_taps(shape):
    n = iota(shape, len(shape) - 1)
    return ((n & 7) < HEADS) & ((n >> 3) < KS)


def padded(rows):
    return -(-rows // 16) * 16


def unpack_kernel(count, rows, g_ref, wp_ref, pw_ref, dw_ref, fi_ref, fo_ref, kw_ref, vec_ref, flat, kwt):
    pad = padded(rows)

    def spread(i):
        flat[pl.ds(i * rows, pad), :] = g_ref[i].astype(f32)

    for i in range(count):
        spread(i)

    def piece(name, out, height, width, row0, col0, skip):
        per = width // LANES
        base = START[name] + skip
        for c in range(per):
            for r in range(0, height, 256):
                part = min(256, height - r)
                out[row0 + r : row0 + r + part, col0 + c * LANES : col0 + (c + 1) * LANES] = flat[
                    pl.ds(base + r * per + c, part, stride=per), :
                ].astype(bf16)

    for m in range(4):
        piece("proj", wp_ref, D, ATT, 0, m * ATT, m * D * ATT // LANES)
    piece("point", pw_ref, D, ATT, 0, 0, 0)
    piece("dense", dw_ref, D, D, 0, 0, 0)
    piece("ffn_in", fi_ref, D, FF // GROUPS, 0, 0, 0)
    piece("ffn_out", fo_ref, FF, D // GROUPS, 0, 0, 0)

    vec_ref[...] = jnp.zeros_like(vec_ref)
    for row in range(4):
        for c in range(3):
            at = START["bias4"] + row * 3 + c
            vec_ref[row : row + 1, c * LANES : (c + 1) * LANES] = flat[at : at + 1, :]
    for j in range(KS):
        for c in range(6):
            at = START["depth"] + j * 6 + c
            vec_ref[DW + j : DW + j + 1, c * LANES : (c + 1) * LANES] = flat[at : at + 1, :]
    at = START["tail"]
    lane = iota((64, LANES), 1)
    first = pltpu.roll(flat[at : at + 64, :], LANES - KB, 1)
    second = pltpu.roll(flat[at + 1 : at + 65, :], LANES - KB, 1)
    kwt[0:64, :] = jnp.where(lane < LANES - KB, first, second)
    at = 0
    for row, many in TAIL:
        for c in range(many):
            vec_ref[row : row + 1, c * LANES : (c + 1) * LANES] = kwt[at + c : at + c + 1, :]
        at += many
    perm = tap_perm()
    lane8 = iota((16, LANES), 1)
    kb = jnp.broadcast_to(flat[START["tail"] : START["tail"] + 1, :], (16, LANES))
    kb = nn(jnp.where(lane8 < KB, kb, 0.0).astype(bf16), perm)
    kb = jnp.where(used_taps((16, LANES)), kb, NEG)
    vec_ref[KBR : KBR + 1, 0:LANES] = kb[0:1]

    lane = iota((8, LANES), 1)
    for a in range(64):
        c0, ln = divmod(a * KB, LANES)
        at = START["kernel"] + c0
        x = pltpu.roll(flat[pl.ds(at, 8, stride=27), :], (LANES - ln) % LANES, 1)
        if ln + KB > LANES:
            y = pltpu.roll(flat[pl.ds(at + 1, 8, stride=27), :], (LANES - ln) % LANES, 1)
            x = jnp.where(lane < LANES - ln, x, y)
        kwt[pl.ds(a, 8, stride=64), :] = jnp.where(lane < KB, x, 0.0)
    kw_ref[...] = nn(kwt[0:ATT, :].astype(bf16), perm).astype(bf16)


def flat_rows(count, rows):
    return -(-(max((count - 1) * rows + padded(rows), USED + 240)) // 8) * 8


def run_unpack(gathered, rows):
    count = gathered.shape[0]
    shapes = [(D, 4 * ATT), (D, ATT), (D, D), (D, FF // GROUPS), (FF, D // GROUPS), (ATT, LANES)]
    out = [jax.ShapeDtypeStruct(s, bf16) for s in shapes] + [jax.ShapeDtypeStruct((VROWS, FF), f32)]

    def body(*refs):
        unpack_kernel(count, rows, *refs)

    return pl.pallas_call(
        body,
        out_shape=out,
        in_specs=[pl.BlockSpec(memory_space=VM)],
        out_specs=[pl.BlockSpec(memory_space=VM)] * len(out),
        scratch_shapes=[VM((flat_rows(count, rows), LANES), f32), VM((512, LANES), f32)],
        compiler_params=pltpu.CompilerParams(vmem_limit_bytes=VMEM_LIMIT),
        name="unpack",
    )(gathered)


def pack_kernel(count, rows, gp_ref, gpw_ref, gdw_ref, gfi_ref, gfo_ref, gkw_ref, va_ref, vb_ref, send_ref, flat, kwt, vec):
    total = flat.shape[0]
    used8 = START["depth"] // 8 * 8
    flat[used8:total, :] = jnp.zeros((total - used8, LANES), f32)
    vec[...] = va_ref[...] + vb_ref[...]

    def piece(name, src, height, width, row0, col0, skip):
        per = width // LANES
        base = START[name] + skip
        for c in range(per):
            for r in range(0, height, 256):
                part = min(256, height - r)
                flat[pl.ds(base + r * per + c, part, stride=per), :] = src[
                    row0 + r : row0 + r + part, col0 + c * LANES : col0 + (c + 1) * LANES
                ]

    for m in range(4):
        piece("proj", gp_ref, D, ATT, 0, m * ATT, m * D * ATT // LANES)
    piece("point", gpw_ref, D, ATT, 0, 0, 0)
    piece("dense", gdw_ref, D, D, 0, 0, 0)
    piece("ffn_in", gfi_ref, D, FF // GROUPS, 0, 0, 0)
    piece("ffn_out", gfo_ref, FF, D // GROUPS, 0, 0, 0)

    perm = tap_perm()
    kwt[...] = jnp.zeros_like(kwt)
    kwt[0:ATT, :] = nt(gkw_ref[...].astype(bf16), perm)
    lane = iota((8, LANES), 1)
    for a in range(64):
        c0, ln = divmod(a * KB, LANES)
        at = START["kernel"] + c0
        x = pltpu.roll(kwt[pl.ds(a, 8, stride=64), :], ln, 1)
        if ln + KB > LANES:
            flat[pl.ds(at, 8, stride=27), :] += jnp.where(lane >= ln, x, 0.0)
            flat[pl.ds(at + 1, 8, stride=27), :] += jnp.where(lane < ln, x, 0.0)
        else:
            flat[pl.ds(at, 8, stride=27), :] += x
    for row in range(4):
        for c in range(3):
            at = START["bias4"] + row * 3 + c
            flat[at : at + 1, :] = vec[row : row + 1, c * LANES : (c + 1) * LANES]
    for j in range(KS):
        for c in range(6):
            at = START["depth"] + j * 6 + c
            flat[at : at + 1, :] = vec[DW + j : DW + j + 1, c * LANES : (c + 1) * LANES]
    kwt[...] = jnp.zeros_like(kwt)
    at = 8
    for row, many in TAIL:
        for c in range(many):
            kwt[at + c : at + c + 1, :] = vec[row : row + 1, c * LANES : (c + 1) * LANES]
        at += many
    lane = iota((72, LANES), 1)
    before = pltpu.roll(kwt[7:79, :], KB, 1)
    here = pltpu.roll(kwt[8:80, :], KB, 1)
    at = START["tail"]
    flat[at : at + 72, :] = jnp.where(lane < KB, before, here)
    kb = jnp.broadcast_to(vec[KBR : KBR + 1, 0:LANES], (16, LANES))
    kb = nt(jnp.where(used_taps((16, LANES)), kb, 0.0).astype(bf16), perm)
    lane = iota((1, LANES), 1)
    flat[at : at + 1, :] = jnp.where(lane < KB, kb[0:1], flat[at : at + 1, :])

    pad = padded(rows)
    for i in range(count):
        send_ref[i] = flat[i * rows : i * rows + pad, :].astype(bf16)


def run_pack(count, rows, gp, gpw, gdw, gfi, gfo, gkw, va, vb):
    def body(*refs):
        pack_kernel(count, rows, *refs)

    return pl.pallas_call(
        body,
        out_shape=jax.ShapeDtypeStruct((count, padded(rows), LANES), bf16),
        in_specs=[pl.BlockSpec(memory_space=VM)] * 8,
        out_specs=pl.BlockSpec(memory_space=VM),
        scratch_shapes=[
            VM((flat_rows(count, rows), LANES), f32),
            VM((512, LANES), f32),
            VM((VROWS, FF), f32),
        ],
        compiler_params=pltpu.CompilerParams(vmem_limit_bytes=VMEM_LIMIT),
        name="pack",
    )(gp, gpw, gdw, gfi, gfo, gkw, va, vb)


def doc_marks(r, length, len_ref, dcol, tm, mb):
    t = iota((length, LANES), 0)
    u = iota((8, length), 1)
    ends = jnp.int32(0)
    d = jnp.zeros((length, LANES), i32)
    e = jnp.zeros((8, length), i32)
    for j in range(SLOTS):
        ends = ends + len_ref[r, j]
        d = d + (t >= ends).astype(i32)
        e = e + (u >= ends).astype(i32)
    dcol[0:8, :] = jnp.full((8, LANES), -1, i32)
    dcol[8 : 8 + length, :] = d
    dcol[8 + length : 16 + length, :] = jnp.full((8, LANES), -1, i32)
    for j in range(KS):
        at = 8 + j - HALF
        tm[j] = (dcol[at : at + length, :] == d).astype(f32)
    for c in range(length // LANES):
        mb[:, c * LANES : (c + 1) * LANES] = jnp.where(d == e[0:1, c * LANES : (c + 1) * LANES], BIG, NEG)


def tap_lanes(tm, length):
    tap = iota((length, LANES), 1) >> 3
    out = jnp.zeros((length, LANES), f32)
    for j in range(KS):
        out = jnp.where(tap == j, tm[j], out)
    return jnp.where(used_taps((length, LANES)), out, 0.0)


def over_taps(x, op):
    for s in (8, 16, 32, 64):
        x = op(x, pltpu.roll(x, s, 1))
    return x


def fill_emat(emat):
    k, c = iota((2 * LANES, ATT), 0) & (LANES - 1), iota((2 * LANES, ATT), 1)
    for j in range(KS):
        emat[:, j * ATT : (j + 1) * ATT] = jnp.where(k == j * 8 + (c >> 6), 1.0, 0.0).astype(bf16)


def two_parts(x):
    high = x.astype(bf16)
    return jnp.concatenate([high, (x - high.astype(f32)).astype(bf16)], axis=1)


def zero_pads(ref, length):
    for c in range(ref.shape[0]):
        ref[c, 0:8, :] = jnp.zeros((8, LANES), f32)
        ref[c, 8 + length : 16 + length, :] = jnp.zeros((8, LANES), f32)


def fwd_kernel(length, len_ref, tok_ref, wp_ref, pw_ref, kw_ref, vec_ref,
               qkvc_ref, kc_ref, dep_ref, ca_ref, tap_ref, join_ref, lse_ref,
               xs, cs, dcol, tm, mb, emat, acc):
    row = pl.program_id(0)

    @pl.when(row == 0)
    def _():
        fill_emat(emat)

    doc_marks(row, length, len_ref, dcol, tm, mb)
    tok = tok_ref[...]
    zero_pads(xs, length)
    zero_pads(cs, length)
    for c in range(6):
        xs[c, 8 : 8 + length, :] = tok[:, c * LANES : (c + 1) * LANES].astype(f32)
    for m, bias in ((0, QB), (1, None), (2, VB), (3, CB)):
        x = nn(tok, wp_ref[:, m * ATT : (m + 1) * ATT])
        if bias is not None:
            x = x + vec_ref[bias : bias + 1, 0:ATT]
        x = x.astype(bf16)
        qkvc_ref[:, m * ATT : (m + 1) * ATT] = x
        if m == 3:
            for c in range(3):
                cs[c, 8 : 8 + length, :] = x[:, c * LANES : (c + 1) * LANES].astype(f32)

    step = 64

    for c in range(6):
        w = [vec_ref[DW + j : DW + j + 1, c * LANES : (c + 1) * LANES] for j in range(KS)]
        for r in range(0, length, step):
            total = w[HALF] * xs[c, 8 + r : 8 + r + step, :]
            for j in range(KS):
                if j != HALF:
                    at = 8 + r + j - HALF
                    total = total + w[j] * (xs[c, at : at + step, :] * tm[j, r : r + step, :])
            dep_ref[r : r + step, c * LANES : (c + 1) * LANES] = total.astype(bf16)

    keyconv = nn(dep_ref[...], pw_ref[...]) + vec_ref[PB : PB + 1, 0:ATT]
    kc_ref[...] = keyconv.astype(bf16)
    ca = (keyconv * qkvc_ref[:, 0:ATT].astype(f32)).astype(bf16)
    ca_ref[...] = ca
    logits = nn(ca, kw_ref[...]) + vec_ref[KBR : KBR + 1, 0:LANES]
    e = jnp.exp(logits - over_taps(logits, jnp.maximum))
    taps = e / over_taps(e, jnp.add)
    tap_ref[...] = taps
    spread = two_parts(taps * tap_lanes(tm, length))
    for j in range(KS):
        t = nn(spread, emat[:, j * ATT : (j + 1) * ATT])
        for c in range(3):
            at = 8 + j - HALF
            part = t[:, c * LANES : (c + 1) * LANES] * cs[c, at : at + length, :]
            if j:
                part = part + acc[:, c * LANES : (c + 1) * LANES]
            if j < KS - 1:
                acc[:, c * LANES : (c + 1) * LANES] = part
            else:
                join_ref[:, ATT + c * LANES : ATT + (c + 1) * LANES] = part.astype(bf16)

    for p in range(3):
        cols = slice(p * LANES, (p + 1) * LANES)
        q, k, v = (qkvc_ref[:, m * ATT + p * LANES : m * ATT + (p + 1) * LANES] for m in range(3))
        qs = q.astype(f32) * SCALE
        vt = v.astype(f32).T
        lane, sub = iota((length, LANES), 1), iota((LANES, length), 0)
        halves = []
        for h in range(2):
            qh = jnp.where((lane >= HEAD_DIM) == bool(h), qs, 0.0).astype(bf16)
            vh = jnp.where((sub >= HEAD_DIM) == bool(h), vt, 1.0).astype(bf16)
            z = jnp.minimum(nt(k, qh), mb[...])
            top = jnp.max(z, axis=0, keepdims=True)
            o = nn(vh, jnp.exp(z - top).astype(bf16))
            s = o[(1 - h) * HEAD_DIM : (1 - h) * HEAD_DIM + 1, :]
            lse_ref[0, 2 * p + h : 2 * p + h + 1, :] = top + jnp.log(s)
            halves.append(o[h * HEAD_DIM : (h + 1) * HEAD_DIM, :] / s)
        join_ref[:, cols] = jnp.concatenate(halves, axis=0).T.astype(bf16)


def blocked(rows, cols):
    return pl.BlockSpec((rows, cols), lambda r: (r, 0))


def row_scratch(length):
    return [
        VM((6, length + 16, LANES), f32),
        VM((3, length + 16, LANES), f32),
        VM((length + 16, LANES), i32),
        VM((KS, length, LANES), f32),
        VM((length, length), f32),
        VM((2 * LANES, KS * ATT), bf16),
    ]


def run_fwd(tokens, lengths, wp, pw, kw, vec):
    rows, count = lengths.shape[0], tokens.shape[0]
    length = count // rows

    def body(*refs):
        fwd_kernel(length, *refs)

    full = pl.BlockSpec(memory_space=VM)
    return pl.pallas_call(
        body,
        grid=(rows,),
        out_shape=[
            jax.ShapeDtypeStruct((count, 4 * ATT), bf16),
            jax.ShapeDtypeStruct((count, ATT), bf16),
            jax.ShapeDtypeStruct((count, D), bf16),
            jax.ShapeDtypeStruct((count, ATT), bf16),
            jax.ShapeDtypeStruct((count, LANES), f32),
            jax.ShapeDtypeStruct((count, D), bf16),
            jax.ShapeDtypeStruct((rows, 8, length), f32),
        ],
        in_specs=[pl.BlockSpec(memory_space=pltpu.SMEM), blocked(length, D), full, full, full, full],
        out_specs=[
            blocked(length, 4 * ATT),
            blocked(length, ATT),
            blocked(length, D),
            blocked(length, ATT),
            blocked(length, LANES),
            blocked(length, D),
            pl.BlockSpec((1, 8, length), lambda r: (r, 0, 0)),
        ],
        scratch_shapes=row_scratch(length) + [VM((length, ATT), f32)],
        compiler_params=pltpu.CompilerParams(vmem_limit_bytes=VMEM_LIMIT),
        name="row_forward",
    )(lengths, tokens, wp, pw, kw, vec)


def mid_kernel(length, len_ref, tok_ref, join_ref, cot_ref, dw_ref, fi_ref, fo_ref, vec_ref,
               out_ref, gf_ref, gj_ref, gdw_ref, gfi_ref, gfo_ref, gv_ref,
               xh1, rs1, nl, act, slope, gsec, gsl):
    row = pl.program_id(0)
    fg, dg = FF // GROUPS, D // GROUPS

    @pl.when(row == 0)
    def _():
        for ref in (gdw_ref, gfi_ref, gfo_ref, gv_ref):
            ref[...] = jnp.zeros_like(ref)

    used = jnp.int32(0)
    for j in range(SLOTS):
        used = used + len_ref[row, j]

    def vec(r, n=D):
        return vec_ref[r : r + 1, 0:n]

    step = 64
    gsec[...] = nn(join_ref[...], dw_ref[...])

    def norm1(i):
        at = pl.ds(pl.multiple_of(i * step, step), step)
        z = gsec[at, :] + vec(DB) + tok_ref[at, :].astype(f32)
        z = z - jnp.mean(z, axis=1, keepdims=True)
        r = lax.rsqrt(jnp.mean(z * z, axis=1, keepdims=True) + EPS)
        x = z * r
        xh1[at, :] = x
        rs1[at, :] = jnp.broadcast_to(r, (step, LANES))
        nl[at, :] = (x * vec(N1G) + vec(N1S)).astype(bf16)

    loop(length // step, norm1)

    tile = 512
    per = fg // tile

    for g in range(GROUPS):
        def widen(i, g=g):
            col = pl.ds(pl.multiple_of(i * tile, tile), tile)
            col2 = pl.ds(pl.multiple_of(g * fg + i * tile, tile), tile)
            x = nn(nl[:, g * dg : (g + 1) * dg], fi_ref[g * dg : (g + 1) * dg, col]) + vec_ref[FIB : FIB + 1, col2]
            e = jnp.exp(x * x * -0.5)
            t = pl.reciprocal(1.0 + 0.2316419 * jnp.abs(x), approx=True)
            poly = t * 0.53070271450 - 0.72657601350
            poly = poly * t + 0.71070687050
            poly = poly * t - 0.14224836800
            poly = poly * t + 0.12741479600
            q = poly * t * e
            phi = jnp.where(x >= 0, 1.0 - q, q)
            act[:, col2] = (x * phi).astype(bf16)
            slope[:, col2] = (phi + x * 0.3989422804014327 * e).astype(bf16)

        loop(per, widen)

    for g in range(GROUPS):
        gsec[:, g * dg : (g + 1) * dg] = nn(act[:, g * fg : (g + 1) * fg], fo_ref[g * fg : (g + 1) * fg, :])

    def rows8(x):
        total = x[0:8]
        for k in range(8, x.shape[0], 8):
            total = total + x[k : k + 8]
        return total

    def norm2(i, carry):
        at = pl.ds(pl.multiple_of(i * step, step), step)
        norm = xh1[at, :] * vec(N1G) + vec(N1S)
        z = gsec[at, :] + vec(FOB) + norm
        z = z - jnp.mean(z, axis=1, keepdims=True)
        r = lax.rsqrt(jnp.mean(z * z, axis=1, keepdims=True) + EPS)
        x = z * r
        keep = ((iota((step, 1), 0) + i * step) < used).astype(f32)
        out_ref[at, :] = ((x * vec(N2G) + vec(N2S)) * keep).astype(bf16)
        gf = cot_ref[at, :].astype(f32) * keep
        gx = gf * x
        e = gf * vec(N2G)
        gz = r * (e - jnp.mean(e, axis=1, keepdims=True) - x * jnp.mean(e * x, axis=1, keepdims=True))
        gsec[at, :] = gz
        gsl[at, :] = gz.astype(bf16)
        return (carry[0] + rows8(gx), carry[1] + rows8(gf), carry[2] + rows8(gz))

    none = jnp.zeros((8, D), f32)
    sums = lax.fori_loop(0, length // step, norm2, (none, none, none))

    def add(r, value):
        gv_ref[r : r + 1, 0 : value.shape[1]] += jnp.sum(value, axis=0, keepdims=True)

    for r, value in zip((N2G, N2S, FOB), sums):
        add(r, value)

    for g in range(GROUPS):
        def narrow(i, g=g):
            r0 = pl.ds(pl.multiple_of(g * fg + i * tile, tile), tile)
            x = nt(gsl[:, g * dg : (g + 1) * dg], fo_ref[r0, :]) * slope[:, r0].astype(f32)
            gv_ref[FIB : FIB + 1, r0] += jnp.sum(x, axis=0, keepdims=True)
            slope[:, r0] = x.astype(bf16)
            gfo_ref[r0, :] += tn(act[:, r0], gsl[:, g * dg : (g + 1) * dg])
            col = pl.ds(pl.multiple_of(i * tile, tile), tile)
            gfi_ref[g * dg : (g + 1) * dg, col] += tn(nl[:, g * dg : (g + 1) * dg], slope[:, r0])

        loop(per, narrow)
    for g in range(GROUPS):
        gsec[:, g * dg : (g + 1) * dg] += nt(slope[:, g * fg : (g + 1) * fg], fi_ref[g * dg : (g + 1) * dg, :])

    def norm1_back(i, carry):
        at = pl.ds(pl.multiple_of(i * step, step), step)
        gn = gsec[at, :]
        x = xh1[at, :]
        e = gn * vec(N1G)
        r = rs1[at, :]
        r = jnp.concatenate([r] * (D // LANES), axis=1)
        gz = r * (e - jnp.mean(e, axis=1, keepdims=True) - x * jnp.mean(e * x, axis=1, keepdims=True))
        gf_ref[at, :] = gz.astype(bf16)
        return (carry[0] + rows8(gn * x), carry[1] + rows8(gn), carry[2] + rows8(gz))

    sums = lax.fori_loop(0, length // step, norm1_back, (none, none, none))
    for r, value in zip((N1G, N1S, DB), sums):
        add(r, value)
    low = gf_ref[...]
    gj_ref[...] = nt(low, dw_ref[...]).astype(bf16)
    gdw_ref[...] += tn(join_ref[...], low)


def run_mid(tokens, lengths, joined, cotangent, dw, fi, fo, vec):
    rows, count = lengths.shape[0], tokens.shape[0]
    length = count // rows

    def body(*refs):
        mid_kernel(length, *refs)

    full = pl.BlockSpec(memory_space=VM)
    return pl.pallas_call(
        body,
        grid=(rows,),
        out_shape=[
            jax.ShapeDtypeStruct((count, D), bf16),
            jax.ShapeDtypeStruct((count, D), bf16),
            jax.ShapeDtypeStruct((count, D), bf16),
            jax.ShapeDtypeStruct((D, D), f32),
            jax.ShapeDtypeStruct((D, FF // GROUPS), f32),
            jax.ShapeDtypeStruct((FF, D // GROUPS), f32),
            jax.ShapeDtypeStruct((VROWS, FF), f32),
        ],
        in_specs=[pl.BlockSpec(memory_space=pltpu.SMEM)] + [blocked(length, D)] * 3 + [full] * 4,
        out_specs=[blocked(length, D)] * 3 + [full] * 4,
        scratch_shapes=[
            VM((length, D), f32),
            VM((length, LANES), f32),
            VM((length, D), bf16),
            VM((length, FF), bf16),
            VM((length, FF), bf16),
            VM((length, D), f32),
            VM((length, D), bf16),
        ],
        compiler_params=pltpu.CompilerParams(vmem_limit_bytes=VMEM_LIMIT),
        name="mid",
    )(lengths, tokens, joined, cotangent, dw, fi, fo, vec)


def bwd_kernel(length, len_ref, tok_ref, qkvc_ref, kc_ref, dep_ref, ca_ref, tap_ref, join_ref, lse_ref, gf_ref, gj_ref,
               wp_ref, pw_ref, kw_ref, vec_ref,
               gt_ref, gp_ref, gpw_ref, gkw_ref, gv_ref,
               ds, cs, dcol, tm, mb, emat, gs, tp, prod, gq, gfour, acc):
    row = pl.program_id(0)

    @pl.when(row == 0)
    def _():
        fill_emat(emat)
        for ref in (gp_ref, gpw_ref, gkw_ref, gv_ref):
            ref[...] = jnp.zeros_like(ref)

    doc_marks(row, length, len_ref, dcol, tm, mb)
    for ref in (ds, cs, gs, tp):
        zero_pads(ref, length)

    def add(r, value):
        gv_ref[r : r + 1, 0 : value.shape[1]] += jnp.sum(value, axis=0, keepdims=True)

    for p in range(3):
        cols = slice(p * LANES, (p + 1) * LANES)
        q, k, v = (qkvc_ref[:, m * ATT + p * LANES : m * ATT + (p + 1) * LANES] for m in range(3))
        g = gj_ref[:, cols]
        lane, sub = iota((length, LANES), 1), iota((16, LANES), 1)
        which = iota((16, LANES), 0)
        marks = jnp.where((sub >= HEAD_DIM) == (which >= 8), 1.0, 0.0).astype(bf16)
        dots = g.astype(f32) * join_ref[:, cols].astype(f32)
        high = dots.astype(bf16)
        dots = nt(marks, high) + nt(marks, (dots - high.astype(f32)).astype(bf16))
        qs = q.astype(f32) * SCALE
        kt = k.astype(f32).T.astype(bf16)
        gk, gv, gqt = None, None, []
        for h in range(2):
            own = (lane >= HEAD_DIM) == bool(h)
            qh = jnp.where(own, qs, 0.0).astype(bf16)
            gh = jnp.where(own, g.astype(f32), 0.0).astype(bf16)
            prob = jnp.exp(jnp.minimum(nt(k, qh), mb[...]) - lse_ref[0, 2 * p + h : 2 * p + h + 1, :])
            dsc = (prob * (nt(v, gh) - dots[8 * h : 8 * h + 1, :])).astype(bf16)
            a, b = nn(prob.astype(bf16), gh), nn(dsc, qh)
            gv, gk = (a, b) if h == 0 else (gv + a, gk + b)
            gqt.append(nn(kt, dsc)[h * HEAD_DIM : (h + 1) * HEAD_DIM, :])
        gq[:, cols] = jnp.concatenate(gqt, axis=0).T * SCALE
        gfour[:, ATT + p * LANES : ATT + (p + 1) * LANES] = gk.astype(bf16)
        gfour[:, 2 * ATT + p * LANES : 2 * ATT + (p + 1) * LANES] = gv.astype(bf16)
        gv_ref[VB : VB + 1, cols] += jnp.sum(gv, axis=0, keepdims=True)

    for c in range(3):
        cs[c, 8 : 8 + length, :] = qkvc_ref[:, 3 * ATT + c * LANES : 3 * ATT + (c + 1) * LANES].astype(f32)
        gs[c, 8 : 8 + length, :] = gj_ref[:, ATT + c * LANES : ATT + (c + 1) * LANES].astype(f32)
    for j in range(KS):
        for c in range(3):
            at = 8 + j - HALF
            prod[:, j * ATT + c * LANES : j * ATT + (c + 1) * LANES] = (
                gs[c, 8 : 8 + length, :] * cs[c, at : at + length, :]
            ).astype(bf16)
    marks = tap_lanes(tm, length)
    gtaps = nt(prod[...], emat[0:LANES, :]) * marks
    taps = jnp.where(used_taps((length, LANES)), tap_ref[...], 0.0)
    glog = taps * (gtaps - over_taps(taps * gtaps, jnp.add))
    add(KBR, glog)
    glog = glog.astype(bf16)
    gkw_ref[...] += tn(ca_ref[...], glog)
    gca = nt(glog, kw_ref[...])

    tp[0, 8 : 8 + length, :] = taps * marks
    tap = iota((length, LANES), 1) >> 3
    moved = jnp.zeros((length, LANES), f32)
    for j in range(KS):
        at = 8 + HALF - j
        moved = jnp.where(tap == j, tp[0, at : at + length, :], moved)
    spread = two_parts(moved)
    for j in range(KS):
        t = nn(spread, emat[:, j * ATT : (j + 1) * ATT])
        for c in range(3):
            at = 8 + HALF - j
            part = t[:, c * LANES : (c + 1) * LANES] * gs[c, at : at + length, :]
            if j:
                part = part + acc[:, c * LANES : (c + 1) * LANES]
            if j < KS - 1:
                acc[:, c * LANES : (c + 1) * LANES] = part
            else:
                gfour[:, 3 * ATT + c * LANES : 3 * ATT + (c + 1) * LANES] = part.astype(bf16)
                gv_ref[CB : CB + 1, c * LANES : (c + 1) * LANES] += jnp.sum(part, axis=0, keepdims=True)

    gkc = gca * qkvc_ref[:, 0:ATT].astype(f32)
    gquery = gq[...] + gca * kc_ref[...].astype(f32)
    add(QB, gquery)
    gfour[:, 0:ATT] = gquery.astype(bf16)
    add(PB, gkc)
    gkc = gkc.astype(bf16)
    gpw_ref[...] += tn(dep_ref[...], gkc)
    for c in range(3):
        x = nt(gkc, pw_ref[c * 256 : (c + 1) * 256, :])
        ds[2 * c, 8 : 8 + length, :] = x[:, 0:LANES]
        ds[2 * c + 1, 8 : 8 + length, :] = x[:, LANES:]
    for m in range(4):
        gp_ref[:, m * ATT : (m + 1) * ATT] += tn(tok_ref[...], gfour[:, m * ATT : (m + 1) * ATT])

    step = 64
    for c in range(6):
        cols = slice(c * LANES, (c + 1) * LANES)
        w = [vec_ref[DW + j : DW + j + 1, cols] for j in range(KS)]
        sums = [None] * KS
        if c % 2 == 0:
            direct = nt(gfour[...], wp_ref[c * LANES : (c + 2) * LANES, :])
        for r in range(0, length, step):
            tok = tok_ref[r : r + step, cols].astype(f32)
            total = gf_ref[r : r + step, cols].astype(f32) + direct[r : r + step, (c % 2) * LANES : (c % 2 + 1) * LANES]
            for j in range(KS):
                at = 8 + r + j - HALF
                u = ds[c, at : at + step, :]
                if j != HALF:
                    u = u * tm[j, r : r + step, :]
                total = total + w[KS - 1 - j] * u
                u = tok * u
                part = u[0:8]
                for s in range(8, step, 8):
                    part = part + u[s : s + 8]
                sums[j] = part if r == 0 else sums[j] + part
            gt_ref[r : r + step, cols] = total.astype(bf16)
        for j in range(KS):
            gv_ref[DW + KS - 1 - j : DW + KS - j, cols] += jnp.sum(sums[j], axis=0, keepdims=True)


def run_bwd(tokens, lengths, saved, gf, gj, wp, pw, kw, vec):
    qkvc, kc, dep, ca, taps, joined, lse = saved
    rows, count = lengths.shape[0], tokens.shape[0]
    length = count // rows

    def body(*refs):
        bwd_kernel(length, *refs)

    full = pl.BlockSpec(memory_space=VM)
    return pl.pallas_call(
        body,
        grid=(rows,),
        out_shape=[
            jax.ShapeDtypeStruct((count, D), bf16),
            jax.ShapeDtypeStruct((D, 4 * ATT), f32),
            jax.ShapeDtypeStruct((D, ATT), f32),
            jax.ShapeDtypeStruct((ATT, LANES), f32),
            jax.ShapeDtypeStruct((VROWS, FF), f32),
        ],
        in_specs=[
            pl.BlockSpec(memory_space=pltpu.SMEM),
            blocked(length, D),
            blocked(length, 4 * ATT),
            blocked(length, ATT),
            blocked(length, D),
            blocked(length, ATT),
            blocked(length, LANES),
            blocked(length, D),
            pl.BlockSpec((1, 8, length), lambda r: (r, 0, 0)),
            blocked(length, D),
            blocked(length, D),
            full,
            full,
            full,
            full,
        ],
        out_specs=[blocked(length, D)] + [full] * 4,
        scratch_shapes=row_scratch(length)
        + [
            VM((3, length + 16, LANES), f32),
            VM((1, length + 16, LANES), f32),
            VM((length, KS * ATT), bf16),
            VM((length, ATT), f32),
            VM((length, 4 * ATT), bf16),
            VM((length, ATT), f32),
        ],
        compiler_params=pltpu.CompilerParams(vmem_limit_bytes=VMEM_LIMIT),
        name="row_backward",
    )(lengths, tokens, qkvc, kc, dep, ca, taps, joined, lse, gf, gj, wp, pw, kw, vec)


class Place:
    def __init__(self, outer, inner):
        self.outer, self.inner = outer, inner
        self.lines = inner // 2
        dp, fs = lax.axis_index("dp"), lax.axis_index("fsdp")
        self.y, self.x, self.z, self.c = dp // 2, lax.rem(dp, 2), fs // 2, lax.rem(fs, 2)

    def coords(self, dy=0, dx=0, dz=0, dc=0):
        def other(v, d):
            if d == 0:
                return v
            out, bit = 0, 1
            while bit <= max(d, self.lines - 1, 1):
                digit = lax.rem(v // bit, 2)
                out = out + bit * ((1 - digit) if d & bit else digit)
                bit *= 2
            return out

        return other(self.y, dy) * 2 + other(self.x, dx), other(self.z, dz) * 2 + other(self.c, dc)

    def index(self, **d):
        o, i = self.coords(**d)
        return o * self.inner + i


def greet(peers):
    barrier = pltpu.get_barrier_semaphore()
    for peer in peers:
        pl.semaphore_signal(barrier, inc=1, device_id=peer, device_id_type=pl.DeviceIdType.MESH)
    pl.semaphore_wait(barrier, len(peers))


def peers_of(place):
    return [place.coords(dz=d) for d in range(1, place.lines)] + [
        place.coords(dx=1),
        place.coords(dy=1),
        place.coords(dc=1),
    ]


class Copies:
    def __init__(self, send, recv):
        self.send, self.recv, self.used, self.made = send, recv, 0, []

    def start(self, src, dst, peer, slot):
        copy = pltpu.make_async_remote_copy(
            src_ref=src,
            dst_ref=dst,
            send_sem=self.send.at[self.used],
            recv_sem=self.recv.at[slot],
            device_id=peer,
            device_id_type=pl.DeviceIdType.MESH,
        )
        self.used += 1
        copy.start()
        self.made.append(copy)

    def arrived(self, dst, slot):
        pltpu.make_async_copy(dst, dst, self.recv.at[slot]).wait()

    def finish(self):
        for copy in self.made:
            copy.wait_send()


def gather_kernel(outer, inner, pad, own_ref, out_ref, send, recv):
    place = Place(outer, inner)
    lines = place.lines
    cut = -(-pad // 32) * 16
    parts = {"a": pl.ds(0, cut), "b": pl.ds(cut, pad - cut)}
    me = place.index()
    out_ref[me] = own_ref[...]
    greet(peers_of(place))
    xp, yp, cp = place.coords(dx=1), place.coords(dy=1), place.coords(dc=1)
    copies = Copies(send, recv)
    Z, X, Y, A, B, OTHER = (lines * k for k in range(6))

    def whole(at):
        return out_ref.at[at]

    def half(at, which):
        return out_ref.at[at, parts[which]]

    def on(ref, peer, slot):
        copies.start(ref, ref, peer, slot)

    for d in range(1, lines):
        on(whole(me), place.coords(dz=d), Z + d)
    on(whole(me), xp, X)
    on(whole(me), yp, Y)
    on(whole(me), cp, OTHER + Z)
    for d in range(1, lines):
        at = place.index(dz=d)
        copies.arrived(whole(at), Z + d)
        on(whole(at), xp, X + d)
        on(whole(at), yp, Y + d)
        on(whole(at), cp, OTHER + Z + d)
    for d in range(lines):
        at = place.index(dz=d, dx=1)
        copies.arrived(whole(at), X + d)
        on(half(at, "a"), yp, A + d)
        on(whole(at), cp, OTHER + X + d)
        at = place.index(dz=d, dy=1)
        copies.arrived(whole(at), Y + d)
        on(half(at, "b"), xp, B + d)
        on(whole(at), cp, OTHER + Y + d)
    for d in range(lines):
        at = place.index(dz=d, dy=1, dx=1)
        copies.arrived(half(at, "a"), A + d)
        on(half(at, "a"), cp, OTHER + A + d)
        copies.arrived(half(at, "b"), B + d)
        on(half(at, "b"), cp, OTHER + B + d)
    for d in range(lines):
        copies.arrived(whole(place.index(dz=d, dc=1)), OTHER + Z + d)
        copies.arrived(whole(place.index(dz=d, dx=1, dc=1)), OTHER + X + d)
        copies.arrived(whole(place.index(dz=d, dy=1, dc=1)), OTHER + Y + d)
        at = place.index(dz=d, dy=1, dx=1, dc=1)
        copies.arrived(half(at, "a"), OTHER + A + d)
        copies.arrived(half(at, "b"), OTHER + B + d)
    copies.finish()


def run_gather(own, outer, inner):
    pad = own.shape[0]
    lines = inner // 2

    def body(*refs):
        gather_kernel(outer, inner, pad, *refs)

    return pl.pallas_call(
        body,
        out_shape=jax.ShapeDtypeStruct((outer * inner, pad, LANES), bf16),
        in_specs=[pl.BlockSpec(memory_space=VM)],
        out_specs=pl.BlockSpec(memory_space=VM),
        scratch_shapes=[pltpu.SemaphoreType.DMA((11 * lines,)), pltpu.SemaphoreType.DMA((10 * lines,))],
        compiler_params=pltpu.CompilerParams(
            vmem_limit_bytes=VMEM_LIMIT, collective_id=0, has_side_effects=True
        ),
        name="gather",
    )(own)


def scatter_kernel(outer, inner, rows, pad, part_ref, out_ref, work, rc, ry, rx, ry2, rx2, rz, send, recv):
    place = Place(outer, inner)
    lines = place.lines
    cut = -(-pad // 32) * 16
    a, b = pl.ds(0, cut), pl.ds(cut, pad - cut)
    every = pl.ds(0, pad)
    greet(peers_of(place))
    xp, yp, cp = place.coords(dx=1), place.coords(dy=1), place.coords(dc=1)
    copies = Copies(send, recv)
    C, YA, XB, XA, YB, Z = (lines * k for k in (0, 4, 6, 8, 9, 10))

    def at(dy, dx, d):
        return (dy * 2 + dx) * lines + d

    order = [(dy, dx, d) for dy, dx in ((1, 1), (1, 0), (0, 1), (0, 0)) for d in range(lines)]
    for dy, dx, d in order:
        k = at(dy, dx, d)
        copies.start(part_ref.at[place.index(dy=dy, dx=dx, dz=d, dc=1)], rc.at[k], cp, C + k)

    def plus(k, rows_, other):
        work[k, rows_] = (work[k, rows_].astype(f32) + other.astype(f32)).astype(bf16)

    for dy, dx, d in order:
        k = at(dy, dx, d)
        copies.arrived(rc.at[k], C + k)
        work[k] = (part_ref[place.index(dy=dy, dx=dx, dz=d)].astype(f32) + rc[k].astype(f32)).astype(bf16)
        if dy:
            copies.start(work.at[k, a], ry.at[dx * lines + d], yp, YA + dx * lines + d)
        if dx:
            copies.start(work.at[k, b], rx.at[dy * lines + d], xp, XB + dy * lines + d)
    for d in range(lines):
        n = lines + d
        copies.arrived(ry.at[n], YA + n)
        plus(at(0, 1, d), a, ry[n])
        copies.start(work.at[at(0, 1, d), a], rx2.at[d], xp, XA + d)
        copies.arrived(rx.at[n], XB + n)
        plus(at(1, 0, d), b, rx[n])
        copies.start(work.at[at(1, 0, d), b], ry2.at[d], yp, YB + d)
    for d in reversed(range(lines)):
        k = at(0, 0, d)
        copies.arrived(ry.at[d], YA + d)
        copies.arrived(rx.at[d], XB + d)
        copies.arrived(rx2.at[d], XA + d)
        copies.arrived(ry2.at[d], YB + d)
        top = work[k, a].astype(f32) + ry[d].astype(f32) + rx2[d].astype(f32)
        low = work[k, b].astype(f32) + rx[d].astype(f32) + ry2[d].astype(f32)
        work[k, a] = top.astype(bf16)
        work[k, b] = low.astype(bf16)
        if d:
            copies.start(work.at[k], rz.at[d], place.coords(dz=d), Z + d)
    total = work[at(0, 0, 0)].astype(f32)
    for d in range(1, lines):
        copies.arrived(rz.at[d], Z + d)
        total = total + rz[d].astype(f32)
    out_ref[...] = total[0:rows]
    copies.finish()


def run_scatter(part, rows, outer, inner):
    pad = part.shape[1]
    lines = inner // 2
    cut = -(-pad // 32) * 16

    def body(*refs):
        scatter_kernel(outer, inner, rows, pad, *refs)

    return pl.pallas_call(
        body,
        out_shape=jax.ShapeDtypeStruct((rows, LANES), f32),
        in_specs=[pl.BlockSpec(memory_space=VM)],
        out_specs=pl.BlockSpec(memory_space=VM),
        scratch_shapes=[
            VM((4 * lines, pad, LANES), bf16),
            VM((4 * lines, pad, LANES), bf16),
            VM((2 * lines, cut, LANES), bf16),
            VM((2 * lines, pad - cut, LANES), bf16),
            VM((lines, pad - cut, LANES), bf16),
            VM((lines, cut, LANES), bf16),
            VM((lines, pad, LANES), bf16),
            pltpu.SemaphoreType.DMA((11 * lines,)),
            pltpu.SemaphoreType.DMA((11 * lines,)),
        ],
        compiler_params=pltpu.CompilerParams(
            vmem_limit_bytes=VMEM_LIMIT, collective_id=1, has_side_effects=True
        ),
        name="scatter",
    )(part)


def local_layer(tokens, lengths, cotangent, gathered, rows):
    count = gathered.shape[0]
    wp, pw, dw, fi, fo, kw, vec = run_unpack(gathered, rows)
    saved = run_fwd(tokens, lengths, wp, pw, kw, vec)
    output, gf, gj, gdw, gfi, gfo, va = run_mid(tokens, lengths, saved[5], cotangent, dw, fi, fo, vec)
    gt, gp, gpw, gkw, vb = run_bwd(tokens, lengths, saved, gf, gj, wp, pw, kw, vec)
    send = run_pack(count, rows, gp, gpw, gdw, gfi, gfo, gkw, va, vb)
    return output, gt, send


def shards(tokens, doc_lengths, params, cotangent):
    rows = params.shape[0] // LANES
    outer, inner = lax.axis_size("dp"), lax.axis_size("fsdp")
    own = jnp.pad(params.reshape(rows, LANES), ((0, padded(rows) - rows), (0, 0)))
    gathered = run_gather(own, outer, inner)
    output, gt, send = local_layer(tokens, doc_lengths, cotangent, gathered, rows)
    part = run_scatter(send, rows, outer, inner)
    return output, gt, part.reshape(rows * LANES)


def solution(mesh):
    axes = ("dp", "fsdp")
    placed = (P(axes, None), P(axes, None), P(axes), P(axes, None))
    return jax.shard_map(
        shards,
        mesh=mesh,
        in_specs=placed,
        out_specs=(P(axes, None), P(axes, None), P(axes)),
        check_vma=False,
    )
```

```python
import math

import jax
import jax.numpy as jnp
from jax import lax
from jax.experimental import pallas as pl
from jax.experimental.pallas import tpu as pltpu
from jax.sharding import PartitionSpec as P

D = 768
HEADS = 6
HEAD_DIM = 64
ATT = HEADS * HEAD_DIM
FF = 3072
GROUPS = 2
KS = 9
HALF = KS // 2
SLOTS = 16
EPS = 1e-12
LANES = 128
NEG = -1e30
BIG = 3e38
SCALE = HEAD_DIM ** (-0.5)

f32 = jnp.float32
bf16 = jnp.bfloat16
i32 = jnp.int32

FIRST = 5 * D * ATT // LANES
MATRICES = FIRST + (D * D + 2 * D * FF // GROUPS) // LANES
DEPTH_AT = 0
KERNEL_AT = KS * D // LANES
BIAS_AT = KERNEL_AT + ATT * HEADS * KS // LANES
TAIL_AT = BIAS_AT + 4 * ATT // LANES
SMALL = TAIL_AT + 61
KB = HEADS * KS

QB, VB, CB, PB, KBR, DB, N1G, N1S, FIB, FOB, N2G, N2S, DW = range(13)
VROWS = 24
TAIL = [(DB, 6), (N1G, 6), (N1S, 6), (FIB, 24), (FOB, 6), (N2G, 6), (N2S, 6)]

VM = pltpu.VMEM
VMEM_LIMIT = 62 * 1024 * 1024


def nn(a, b):
    return lax.dot_general(a, b, (((1,), (0,)), ((), ())), preferred_element_type=f32)


def nt(a, b):
    return lax.dot_general(a, b, (((1,), (1,)), ((), ())), preferred_element_type=f32)


def tn(a, b):
    return lax.dot_general(a, b, (((0,), (0,)), ((), ())), preferred_element_type=f32)


def iota(shape, axis):
    return lax.broadcasted_iota(i32, shape, axis)


def loop(count, body, unroll=1):
    def step(i, carry):
        body(i)
        return carry

    lax.fori_loop(0, count, step, 0, unroll=unroll)


def tap_perm():
    k, n = iota((LANES, LANES), 0), iota((LANES, LANES), 1)
    head, tap = n & 7, n >> 3
    return jnp.where((k == head * KS + tap) & (head < HEADS) & (tap < KS), 1.0, 0.0).astype(bf16)


def used_taps(shape):
    n = iota(shape, len(shape) - 1)
    return ((n & 7) < HEADS) & ((n >> 3) < KS)


def padded(rows):
    return -(-rows // 16) * 16


class Section:
    def __init__(self, base, kinds, chunk, small, rows, count, inner):
        self.base, self.chunk, self.rows, self.count, self.inner = base, chunk, rows, count, inner
        self.main = sum(n for n, _ in kinds)
        self.small = -(-SMALL // chunk) if small else 0
        self.kinds = kinds + ([(self.small, 1)] if small else [])
        self.used = self.main + self.small
        self.pieces = -(-rows // chunk) + 1
        self.slots = self.pieces + self.small
        self.sources = (chunk - 2) // rows + 2

    def start(self, v):
        at = self.base + v * self.chunk
        if self.small:
            at = jnp.where(v >= self.main, MATRICES + (v - self.main) * self.chunk, at)
        return at

    def first_piece(self, i):
        return jnp.maximum(self.rows * i - self.base, 0) // self.chunk

    def of_owner(self, i, k):
        if k < self.pieces:
            v = self.first_piece(i) + k
            ok = v < self.main
        else:
            v = self.main + k - self.pieces + 0 * i
            ok = v >= 0
        at = self.start(v)
        return v, ok & (at < self.rows * (i + 1)) & (at + self.chunk > self.rows * i)

    def of_chunk(self, v, s):
        i = self.start(v) // self.rows + s
        return i, (v < self.used) & (i < self.count) & (self.rows * i < self.start(v) + self.chunk)

    def source_of(self, v, i):
        return i - self.start(v) // self.rows

    def slot_of(self, v, i):
        return jnp.where(v < self.main, v - self.first_piece(i), self.pieces + v - self.main)

    def by_kind(self, v, action):
        at, seen = 0, {}
        for n, per in self.kinds:
            seen.setdefault(per, []).append((at, at + n))
            at += n
        for per, spans in seen.items():
            ok = False
            for lo, hi in spans:
                ok = ((v >= lo) & (v < hi)) | ok
            pl.when(ok)(lambda per=per: action(per))


def sections(count, rows, inner):
    big, little = 24576 // count, 12288 // count
    first = Section(0, [(FIRST // little, 3)], little, True, rows, count, inner)
    kinds = [(D * n // LANES // big, n // LANES) for n in (D, FF // GROUPS)] + [(FF * 3 // big, 3)]
    return first, Section(FIRST, kinds, big, False, rows, count, inner)


def to_frames(part, pieces):
    chunk, v = part.shape[1], 0
    for ref, height, width, col in pieces:
        per = width // LANES
        tall = chunk // per
        for r in range(0, height, tall):
            for c in range(per):
                part[v, c * tall : (c + 1) * tall, :] = ref[
                    r : r + tall, col + c * LANES : col + (c + 1) * LANES
                ].astype(bf16)
            v += 1
    if v < part.shape[0]:
        part[v:] = jnp.zeros((part.shape[0] - v, chunk, LANES), bf16)
    return v


def from_frames(buf, pieces):
    chunk, v = buf.shape[1], 0
    for ref, height, width, col in pieces:
        per = width // LANES
        tall = chunk // per
        for r in range(0, height, tall):
            for c in range(per):
                ref[r : r + tall, col + c * LANES : col + (c + 1) * LANES] = buf[v, c * tall : (c + 1) * tall, :]
            v += 1
    return v


def unpack_small(flat, kw_ref, vec_ref, kwt):
    vec_ref[...] = jnp.zeros_like(vec_ref)
    for row in range(4):
        for c in range(3):
            at = BIAS_AT + row * 3 + c
            vec_ref[row : row + 1, c * LANES : (c + 1) * LANES] = flat[at : at + 1, :]
    for j in range(KS):
        for c in range(6):
            at = DEPTH_AT + j * 6 + c
            vec_ref[DW + j : DW + j + 1, c * LANES : (c + 1) * LANES] = flat[at : at + 1, :]
    at = TAIL_AT
    lane = iota((64, LANES), 1)
    first = pltpu.roll(flat[at : at + 64, :], LANES - KB, 1)
    second = pltpu.roll(flat[at + 1 : at + 65, :], LANES - KB, 1)
    kwt[0:64, :] = jnp.where(lane < LANES - KB, first, second)
    at = 0
    for row, many in TAIL:
        for c in range(many):
            vec_ref[row : row + 1, c * LANES : (c + 1) * LANES] = kwt[at + c : at + c + 1, :]
        at += many
    perm = tap_perm()
    lane8 = iota((16, LANES), 1)
    kb = jnp.broadcast_to(flat[TAIL_AT : TAIL_AT + 1, :], (16, LANES))
    kb = nn(jnp.where(lane8 < KB, kb, 0.0).astype(bf16), perm)
    kb = jnp.where(used_taps((16, LANES)), kb, NEG)
    vec_ref[KBR : KBR + 1, 0:LANES] = kb[0:1]

    lane = iota((8, LANES), 1)
    for a in range(64):
        c0, ln = divmod(a * KB, LANES)
        at = KERNEL_AT + c0
        x = pltpu.roll(flat[pl.ds(at, 8, stride=27), :], (LANES - ln) % LANES, 1)
        if ln + KB > LANES:
            y = pltpu.roll(flat[pl.ds(at + 1, 8, stride=27), :], (LANES - ln) % LANES, 1)
            x = jnp.where(lane < LANES - ln, x, y)
        kwt[pl.ds(a, 8, stride=64), :] = jnp.where(lane < KB, x, 0.0)
    kw_ref[...] = nn(kwt[0:ATT, :].astype(bf16), perm).astype(bf16)


def pack_small(flat, gkw_ref, vec, kwt):
    flat[...] = jnp.zeros_like(flat)
    perm = tap_perm()
    kwt[...] = jnp.zeros_like(kwt)
    kwt[0:ATT, :] = nt(gkw_ref[...].astype(bf16), perm)
    lane = iota((8, LANES), 1)
    for a in range(64):
        c0, ln = divmod(a * KB, LANES)
        at = KERNEL_AT + c0
        x = pltpu.roll(kwt[pl.ds(a, 8, stride=64), :], ln, 1)
        if ln + KB > LANES:
            flat[pl.ds(at, 8, stride=27), :] += jnp.where(lane >= ln, x, 0.0)
            flat[pl.ds(at + 1, 8, stride=27), :] += jnp.where(lane < ln, x, 0.0)
        else:
            flat[pl.ds(at, 8, stride=27), :] += x
    for row in range(4):
        for c in range(3):
            at = BIAS_AT + row * 3 + c
            flat[at : at + 1, :] = vec[row : row + 1, c * LANES : (c + 1) * LANES]
    for j in range(KS):
        for c in range(6):
            at = DEPTH_AT + j * 6 + c
            flat[at : at + 1, :] = vec[DW + j : DW + j + 1, c * LANES : (c + 1) * LANES]
    kwt[...] = jnp.zeros_like(kwt)
    at = 8
    for row, many in TAIL:
        for c in range(many):
            kwt[at + c : at + c + 1, :] = vec[row : row + 1, c * LANES : (c + 1) * LANES]
        at += many
    lane = iota((72, LANES), 1)
    before = pltpu.roll(kwt[7:79, :], KB, 1)
    here = pltpu.roll(kwt[8:80, :], KB, 1)
    at = TAIL_AT
    flat[at : at + 72, :] = jnp.where(lane < KB, before, here)
    kb = jnp.broadcast_to(vec[KBR : KBR + 1, 0:LANES], (16, LANES))
    kb = nt(jnp.where(used_taps((16, LANES)), kb, 0.0).astype(bf16), perm)
    lane = iota((1, LANES), 1)
    flat[at : at + 1, :] = jnp.where(lane < KB, kb[0:1], flat[at : at + 1, :])


class Place:
    def __init__(self, outer, inner):
        self.outer, self.inner, self.count = outer, inner, outer * inner
        self.lines = inner // 2
        dp, fs = lax.axis_index("dp"), lax.axis_index("fsdp")
        self.y, self.x, self.z, self.c = dp // 2, lax.rem(dp, 2), fs // 2, lax.rem(fs, 2)
        self.me = dp * inner + fs

    def coords(self, dy=0, dx=0, z=None, dc=0):
        def flip(v, d):
            return 1 - v if d else v

        z = self.z if z is None else z
        return flip(self.y, dy) * 2 + flip(self.x, dx), z * 2 + flip(self.c, dc)

    def index(self, **d):
        o, i = self.coords(**d)
        return o * self.inner + i

    def device(self, n):
        return n // self.inner, lax.rem(n, self.inner)

    def item(self, t):
        s = (t + 1) // 2
        z = self.z - s if t % 2 else self.z + s
        return z, (z >= 0) & (z < self.lines), s, t % 2 == 1

    def greet_all(self):
        barrier = pltpu.get_barrier_semaphore()
        for n in range(1, self.count):
            peer = self.device(lax.rem(self.me + n, self.count))
            pl.semaphore_signal(barrier, inc=1, device_id=peer, device_id_type=pl.DeviceIdType.MESH)
        pl.semaphore_wait(barrier, self.count - 1)


class Copies:
    def __init__(self, send, recv):
        self.send, self.recv, self.used, self.made = send, recv, 0, []

    def start(self, src, dst, peer, slot, ok=None):
        number = self.used
        self.used += 1
        assert number < self.send.shape[0]

        def make():
            return pltpu.make_async_remote_copy(
                src_ref=src(),
                dst_ref=dst(),
                send_sem=self.send.at[number],
                recv_sem=self.recv.at[slot() if callable(slot) else slot],
                device_id=peer(),
                device_id_type=pl.DeviceIdType.MESH,
            )

        self.made.append((make, ok))
        guarded(ok, lambda: make().start())

    def arrived(self, dst, slot, ok=None):
        def wait():
            ref = dst()
            pltpu.make_async_copy(ref, ref, self.recv.at[slot]).wait()

        guarded(ok, wait)

    def finish(self):
        for make, ok in self.made:
            guarded(ok, lambda make=make: make().wait_send())


def guarded(ok, action):
    if ok is None:
        action()
    else:
        pl.when(ok())(action)


def half_of(chunk):
    return -(-chunk // 32) * 16


class Gather:
    @staticmethod
    def scratch(sect, inner):
        lines = inner // 2
        items = 2 * lines - 1
        return [
            VM((sect.count, sect.chunk, LANES), bf16),
            VM((sect.rows + 2 * sect.chunk + 16, LANES), f32),
            VM((sect.slots, sect.chunk, LANES), bf16),
            VM((sect.sources, sect.chunk, LANES), bf16),
            VM((sect.chunk, LANES), f32),
            pltpu.SemaphoreType.DMA((sect.slots + 10 * items + 4,)),
            pltpu.SemaphoreType.DMA((sect.sources + 9 * items,)),
        ]

    def __init__(self, sect, place, own_ref, scratch):
        self.sect, self.place, self.own = sect, place, own_ref
        self.buf, self.ownf, self.win, self.land, self.frame, send, recv = scratch
        self.copies = Copies(send, recv)
        n = 2 * place.lines - 1
        self.items = n
        self.Z, self.X, self.Y, self.A, self.B, self.CZ, self.CX, self.CY, self.CD = (sect.sources + n * k for k in range(9))
        cut = half_of(sect.chunk)
        self.half = {"a": pl.ds(0, cut), "b": pl.ds(cut, sect.chunk - cut)}
        self.steps = [self.offer, self.form]
        for s in range(1, place.lines):
            self.steps.append(lambda s=s: self.along(s))
            self.steps.append(lambda s=s: self.across(s - 1))
        self.steps.append(lambda: self.across(place.lines - 1))
        self.steps.append(self.diagonal)
        self.steps.append(self.rest)

    def greet(self):
        self.place.greet_all()

    def offer(self):
        sect, me = self.sect, self.place.me
        self.ownf[...] = jnp.zeros_like(self.ownf)
        self.ownf[sect.chunk : sect.chunk + sect.rows, :] = self.own[...].astype(f32)
        for k in range(sect.slots):
            self.give(k)

    def give(self, k):
        sect, place, me = self.sect, self.place, self.place.me
        v, ok = sect.of_owner(me, k)

        @pl.when(ok)
        def _():
            at = sect.chunk + sect.start(v) - sect.rows * me
            self.win[k] = self.ownf[pl.ds(at, sect.chunk), :].astype(bf16)

        @pl.when(ok & (v == me))
        def _():
            self.land[sect.source_of(v, me)] = self.win[k]

        def chunk():
            return sect.of_owner(me, k)[0]

        def away():
            v, ok = sect.of_owner(me, k)
            return ok & (v != me)

        self.copies.start(
            lambda: self.win.at[k],
            lambda: self.land.at[sect.source_of(chunk(), me)],
            lambda: place.device(chunk()),
            lambda: sect.source_of(chunk(), me),
            away,
        )

    def form(self):
        sect, me = self.sect, self.place.me
        row = iota((sect.chunk, LANES), 0) + sect.start(me)
        x = None
        for s in range(sect.sources):
            i, ok = sect.of_chunk(me, s)
            self.copies.arrived(lambda: self.land.at[s], s, lambda: ok & (i != me))
            here = self.land[s].astype(f32)
            x = here if x is None else jnp.where(row >= sect.rows * i, here, x)
        self.frame[...] = x

        def settle(per):
            tall = sect.chunk // per
            for c in range(per):
                self.buf[me, c * tall : (c + 1) * tall, :] = self.frame[pl.ds(c, tall, stride=per), :].astype(bf16)

        sect.by_kind(me, settle)

        @pl.when(me >= sect.used)
        def _():
            self.buf[me] = jnp.zeros((sect.chunk, LANES), bf16)

        self.pass_on(0)

    def ref(self, t, which=None, **way):
        def make():
            at = self.place.index(z=self.place.item(t)[0], **way)
            return self.buf.at[at] if which is None else self.buf.at[at, self.half[which]]

        return make

    def ok(self, t):
        return None if t == 0 else lambda: self.place.item(t)[1]

    def same(self, ref, peer, slot, ok):
        self.copies.start(ref, ref, peer, slot, ok)

    def beside(self, **way):
        return lambda: self.place.coords(**way)

    def pass_on(self, t):
        place = self.place
        _, _, s, below = place.item(t)
        for way in (1, -1) if t == 0 else ((1,) if below else (-1,)):
            slot = 2 * s + 1 if way > 0 else 2 * s + 2

            def inside(way=way):
                there = place.z + way
                good = (there >= 0) & (there < place.lines)
                return good if t == 0 else good & place.item(t)[1]

            if slot < self.items:
                self.same(self.ref(t), lambda way=way: place.coords(z=place.z + way), self.Z + slot, inside)
        ok = self.ok(t)
        self.same(self.ref(t), self.beside(dx=1), self.X + t, ok)
        self.same(self.ref(t), self.beside(dy=1), self.Y + t, ok)
        self.same(self.ref(t), self.beside(dc=1), self.CZ + t, ok)

    def at_distance(self, s):
        return [0] if s == 0 else [2 * s - 1, 2 * s]

    def along(self, s):
        for t in self.at_distance(s):
            self.copies.arrived(self.ref(t), self.Z + t, self.ok(t))
            self.pass_on(t)

    def across(self, s):
        for t in self.at_distance(s):
            ok = self.ok(t)
            self.copies.arrived(self.ref(t, dx=1), self.X + t, ok)
            self.same(self.ref(t, "a", dx=1), self.beside(dy=1), self.A + t, ok)
            self.same(self.ref(t, dx=1), self.beside(dc=1), self.CX + t, ok)
            self.copies.arrived(self.ref(t, dy=1), self.Y + t, ok)
            self.same(self.ref(t, "b", dy=1), self.beside(dx=1), self.B + t, ok)
            self.same(self.ref(t, dy=1), self.beside(dc=1), self.CY + t, ok)

    def diagonal(self):
        for t in range(self.items):
            ok = self.ok(t)
            self.copies.arrived(self.ref(t, "a", dy=1, dx=1), self.A + t, ok)
            self.copies.arrived(self.ref(t, "b", dy=1, dx=1), self.B + t, ok)
            self.same(self.ref(t, dy=1, dx=1), self.beside(dc=1), self.CD + t, ok)

    def rest(self):
        for t in range(self.items):
            for k, way in ((self.CZ, {}), (self.CX, {"dx": 1}), (self.CY, {"dy": 1}), (self.CD, {"dy": 1, "dx": 1})):
                self.copies.arrived(self.ref(t, dc=1, **way), k + t, self.ok(t))
        self.copies.finish()


class Scatter:
    @staticmethod
    def scratch(sect, inner):
        lines = inner // 2
        cut = half_of(sect.chunk)
        return [
            VM((4 * lines, sect.chunk, LANES), bf16),
            VM((4 * lines, sect.chunk, LANES), bf16),
            VM((2 * lines, cut, LANES), bf16),
            VM((2 * lines, sect.chunk - cut, LANES), bf16),
            VM((lines, sect.chunk - cut, LANES), bf16),
            VM((lines, cut, LANES), bf16),
            VM((lines, sect.chunk, LANES), bf16),
            VM((sect.chunk, LANES), f32),
            VM((sect.chunk, LANES), bf16),
            VM((sect.slots, sect.chunk, LANES), bf16),
            VM((sect.rows + 2 * sect.chunk + 16, LANES), f32),
            pltpu.SemaphoreType.DMA((11 * lines + sect.sources,)),
            pltpu.SemaphoreType.DMA((11 * lines + sect.slots,)),
        ]

    def __init__(self, sect, place, part_ref, scratch):
        self.sect, self.place, self.partial = sect, place, part_ref
        (self.work, self.rc, self.ry, self.rx, self.ry2, self.rx2, self.rz, self.frame, self.low, self.land, self.out,
         send, recv) = scratch
        self.copies = Copies(send, recv)
        lines = place.lines
        self.lines = lines
        cut = half_of(sect.chunk)
        self.a, self.b = pl.ds(0, cut), pl.ds(cut, sect.chunk - cut)
        self.C, self.YA, self.XB, self.XA, self.YB, self.Z, self.O = (lines * k for k in (0, 4, 6, 8, 9, 10, 11))
        self.order = [(dy, dx, d) for dy, dx in ((1, 1), (1, 0), (0, 1), (0, 0)) for d in self.far_first()]
        self.steps = [self.core, self.first, self.second, self.third, self.settle, self.take]

    def greet(self):
        self.place.greet_all()

    def far_first(self):
        return list(range(1, self.lines)) + [0]

    def z(self, d):
        return lax.rem(self.place.z + d, self.lines) if d else self.place.z

    def at(self, dy, dx, d):
        return (dy * 2 + dx) * self.lines + d

    def core(self):
        place = self.place

        def give(dy, dx, d):
            k = self.at(dy, dx, d)
            self.copies.start(
                lambda: self.partial.at[place.index(dy=dy, dx=dx, z=self.z(d), dc=1)],
                lambda: self.rc.at[k],
                lambda: place.coords(dc=1),
                self.C + k,
            )

        for spot in self.order:
            give(*spot)

    def send(self, k, rows, buf, n, way, slot):
        self.copies.start(lambda: self.work.at[k, rows], lambda: buf.at[n], lambda: self.place.coords(**way), slot)

    def got(self, buf, n, slot):
        self.copies.arrived(lambda: buf.at[n], slot)

    def plus(self, k, rows, other):
        self.work[k, rows] = (self.work[k, rows].astype(f32) + other.astype(f32)).astype(bf16)

    def first(self):
        place, lines = self.place, self.lines
        for dy, dx, d in self.order:
            k = self.at(dy, dx, d)
            self.got(self.rc, k, self.C + k)
            mine = self.partial[place.index(dy=dy, dx=dx, z=self.z(d))]
            self.work[k] = (mine.astype(f32) + self.rc[k].astype(f32)).astype(bf16)
            if dy:
                self.send(k, self.a, self.ry, dx * lines + d, {"dy": 1}, self.YA + dx * lines + d)
            if dx:
                self.send(k, self.b, self.rx, dy * lines + d, {"dx": 1}, self.XB + dy * lines + d)

    def second(self):
        lines = self.lines
        for d in self.far_first():
            n = lines + d
            self.got(self.ry, n, self.YA + n)
            self.plus(self.at(0, 1, d), self.a, self.ry[n])
            self.send(self.at(0, 1, d), self.a, self.rx2, d, {"dx": 1}, self.XA + d)
            self.got(self.rx, n, self.XB + n)
            self.plus(self.at(1, 0, d), self.b, self.rx[n])
            self.send(self.at(1, 0, d), self.b, self.ry2, d, {"dy": 1}, self.YB + d)

    def third(self):
        place = self.place
        for d in self.far_first():
            k = self.at(0, 0, d)
            self.got(self.ry, d, self.YA + d)
            self.got(self.rx, d, self.XB + d)
            self.got(self.rx2, d, self.XA + d)
            self.got(self.ry2, d, self.YB + d)
            top = self.work[k, self.a].astype(f32) + self.ry[d].astype(f32) + self.rx2[d].astype(f32)
            low = self.work[k, self.b].astype(f32) + self.rx[d].astype(f32) + self.ry2[d].astype(f32)
            self.work[k, self.a] = top.astype(bf16)
            self.work[k, self.b] = low.astype(bf16)
            if d:
                self.copies.start(
                    lambda k=k: self.work.at[k],
                    lambda d=d: self.rz.at[d],
                    lambda d=d: place.coords(z=self.z(d)),
                    self.Z + d,
                )

    def settle(self):
        sect, me = self.sect, self.place.me
        total = self.work[self.at(0, 0, 0)].astype(f32)
        for d in range(1, self.lines):
            self.got(self.rz, d, self.Z + d)
            total = total + self.rz[d].astype(f32)
        self.frame[...] = total
        self.low[...] = total.astype(bf16)

        def spread(per):
            if per == 1:
                return
            tall = sect.chunk // per
            for c in range(per):
                self.out[pl.ds(c, tall, stride=per), :] = self.frame[c * tall : (c + 1) * tall, :]
            self.low[...] = self.out[0 : sect.chunk, :].astype(bf16)

        sect.by_kind(me, spread)
        for s in range(sect.sources):
            self.give(s)

    def give(self, s):
        sect, me = self.sect, self.place.me
        i, ok = sect.of_chunk(me, s)

        @pl.when(ok & (i == me))
        def _():
            self.land[sect.slot_of(me, i)] = self.low[...]

        def owner():
            return jnp.minimum(sect.of_chunk(me, s)[0], sect.count - 1)

        def slot():
            return jnp.clip(sect.slot_of(me, owner()), 0, sect.slots - 1)

        def away():
            i, ok = sect.of_chunk(me, s)
            return ok & (i != me)

        self.copies.start(
            lambda: self.low, lambda: self.land.at[slot()], lambda: self.place.device(owner()), lambda: self.O + slot(), away
        )

    def take(self):
        sect, me = self.sect, self.place.me
        self.out[...] = jnp.zeros_like(self.out)
        for k in range(sect.slots):
            v, ok = sect.of_owner(me, k)
            self.copies.arrived(lambda: self.land.at[k], self.O + k, lambda: ok & (v != me))

            @pl.when(ok)
            def _():
                at = sect.chunk + sect.start(v) - sect.rows * me
                self.out[pl.ds(at, sect.chunk), :] = self.land[k].astype(f32)

        self.copies.finish()


def all_steps(job):
    for step in job.steps:
        step()


def pumped(steps, rows, points):
    total, row = rows * points, pl.program_id(0)
    due = {}
    for k, step in enumerate(steps):
        due.setdefault(k * (total - 1) // (len(steps) - 1), []).append(step)

    def pump(point):
        for r in range(rows):
            for step in due.get(r * points + point, []):
                pl.when(row == r)(step)

    return pump


def doc_marks(r, length, len_ref, dcol, tm, mb):
    t = iota((length, LANES), 0)
    u = iota((8, length), 1)
    ends = jnp.int32(0)
    d = jnp.zeros((length, LANES), i32)
    e = jnp.zeros((8, length), i32)
    for j in range(SLOTS):
        ends = ends + len_ref[r, j]
        d = d + (t >= ends).astype(i32)
        e = e + (u >= ends).astype(i32)
    dcol[0:8, :] = jnp.full((8, LANES), -1, i32)
    dcol[8 : 8 + length, :] = d
    dcol[8 + length : 16 + length, :] = jnp.full((8, LANES), -1, i32)
    for j in range(KS):
        at = 8 + j - HALF
        tm[j] = (dcol[at : at + length, :] == d).astype(f32)
    for c in range(length // LANES):
        mb[:, c * LANES : (c + 1) * LANES] = jnp.where(d == e[0:1, c * LANES : (c + 1) * LANES], BIG, NEG)


def tap_lanes(tm, length):
    tap = iota((length, LANES), 1) >> 3
    out = jnp.zeros((length, LANES), f32)
    for j in range(KS):
        out = jnp.where(tap == j, tm[j], out)
    return jnp.where(used_taps((length, LANES)), out, 0.0)


def over_taps(x, op):
    for s in (8, 16, 32, 64):
        x = op(x, pltpu.roll(x, s, 1))
    return x


def fill_emat(emat):
    k, c = iota((2 * LANES, ATT), 0) & (LANES - 1), iota((2 * LANES, ATT), 1)
    for j in range(KS):
        emat[:, j * ATT : (j + 1) * ATT] = jnp.where(k == j * 8 + (c >> 6), 1.0, 0.0).astype(bf16)


def two_parts(x):
    high = x.astype(bf16)
    return jnp.concatenate([high, (x - high.astype(f32)).astype(bf16)], axis=1)


def zero_pads(ref, length):
    for c in range(ref.shape[0]):
        ref[c, 0:8, :] = jnp.zeros((8, LANES), f32)
        ref[c, 8 + length : 16 + length, :] = jnp.zeros((8, LANES), f32)


def fwd_kernel(length, pump, len_ref, tok_ref, wp_ref, pw_ref, kw_ref, vec_ref,
               qkvc_ref, kc_ref, dep_ref, ca_ref, tap_ref, join_ref, lse_ref,
               xs, cs, dcol, tm, mb, emat, acc):
    row = pl.program_id(0)
    pump(0)

    @pl.when(row == 0)
    def _():
        fill_emat(emat)

    doc_marks(row, length, len_ref, dcol, tm, mb)
    tok = tok_ref[...]
    zero_pads(xs, length)
    zero_pads(cs, length)
    for c in range(6):
        xs[c, 8 : 8 + length, :] = tok[:, c * LANES : (c + 1) * LANES].astype(f32)
    for m, bias in ((0, QB), (1, None), (2, VB), (3, CB)):
        x = nn(tok, wp_ref[:, m * ATT : (m + 1) * ATT])
        if bias is not None:
            x = x + vec_ref[bias : bias + 1, 0:ATT]
        x = x.astype(bf16)
        qkvc_ref[:, m * ATT : (m + 1) * ATT] = x
        if m == 3:
            for c in range(3):
                cs[c, 8 : 8 + length, :] = x[:, c * LANES : (c + 1) * LANES].astype(f32)

    step = 64

    for c in range(6):
        w = [vec_ref[DW + j : DW + j + 1, c * LANES : (c + 1) * LANES] for j in range(KS)]
        for r in range(0, length, step):
            total = w[HALF] * xs[c, 8 + r : 8 + r + step, :]
            for j in range(KS):
                if j != HALF:
                    at = 8 + r + j - HALF
                    total = total + w[j] * (xs[c, at : at + step, :] * tm[j, r : r + step, :])
            dep_ref[r : r + step, c * LANES : (c + 1) * LANES] = total.astype(bf16)

    pump(1)
    keyconv = nn(dep_ref[...], pw_ref[...]) + vec_ref[PB : PB + 1, 0:ATT]
    kc_ref[...] = keyconv.astype(bf16)
    ca = (keyconv * qkvc_ref[:, 0:ATT].astype(f32)).astype(bf16)
    ca_ref[...] = ca
    logits = nn(ca, kw_ref[...]) + vec_ref[KBR : KBR + 1, 0:LANES]
    e = jnp.exp(logits - over_taps(logits, jnp.maximum))
    taps = e / over_taps(e, jnp.add)
    tap_ref[...] = taps
    spread = two_parts(taps * tap_lanes(tm, length))
    for j in range(KS):
        t = nn(spread, emat[:, j * ATT : (j + 1) * ATT])
        for c in range(3):
            at = 8 + j - HALF
            part = t[:, c * LANES : (c + 1) * LANES] * cs[c, at : at + length, :]
            if j:
                part = part + acc[:, c * LANES : (c + 1) * LANES]
            if j < KS - 1:
                acc[:, c * LANES : (c + 1) * LANES] = part
            else:
                join_ref[:, ATT + c * LANES : ATT + (c + 1) * LANES] = part.astype(bf16)

    for p in range(3):
        pump(2 + p)
        cols = slice(p * LANES, (p + 1) * LANES)
        q, k, v = (qkvc_ref[:, m * ATT + p * LANES : m * ATT + (p + 1) * LANES] for m in range(3))
        qs = q.astype(f32) * SCALE
        vt = v.astype(f32).T
        lane, sub = iota((length, LANES), 1), iota((LANES, length), 0)
        halves = []
        for h in range(2):
            qh = jnp.where((lane >= HEAD_DIM) == bool(h), qs, 0.0).astype(bf16)
            vh = jnp.where((sub >= HEAD_DIM) == bool(h), vt, 1.0).astype(bf16)
            z = jnp.minimum(nt(k, qh), mb[...])
            top = jnp.max(z, axis=0, keepdims=True)
            o = nn(vh, jnp.exp(z - top).astype(bf16))
            s = o[(1 - h) * HEAD_DIM : (1 - h) * HEAD_DIM + 1, :]
            lse_ref[0, 2 * p + h : 2 * p + h + 1, :] = top + jnp.log(s)
            halves.append(o[h * HEAD_DIM : (h + 1) * HEAD_DIM, :] / s)
        join_ref[:, cols] = jnp.concatenate(halves, axis=0).T.astype(bf16)
    pump(5)


def blocked(rows, cols):
    return pl.BlockSpec((rows, cols), lambda r: (r, 0))


def row_scratch(length):
    return [
        VM((6, length + 16, LANES), f32),
        VM((3, length + 16, LANES), f32),
        VM((length + 16, LANES), i32),
        VM((KS, length, LANES), f32),
        VM((length, length), f32),
        VM((2 * LANES, KS * ATT), bf16),
    ]


FWD_POINTS = 6


def run_fwd(sect, outer, inner, own, tokens, lengths, wp, pw, kw, vec):
    rows, count = lengths.shape[0], tokens.shape[0]
    length = count // rows
    scratch = row_scratch(length) + [VM((length, ATT), f32)]
    n = len(scratch)

    def body(own_ref, *refs):
        ours, (dw_ref, fi_ref, fo_ref) = refs[:13], refs[13:16]
        job = Gather(sect, Place(outer, inner), own_ref, refs[16 + n :])

        def begin():
            job.greet()
            job.steps[0]()

        def end():
            job.steps[-1]()
            from_frames(job.buf, ((dw_ref, D, D, 0), (fi_ref, D, FF // GROUPS, 0), (fo_ref, FF, D // GROUPS, 0)))

        pump = pumped([begin, *job.steps[1:-1], end], rows, FWD_POINTS)
        fwd_kernel(length, pump, *ours, *refs[16 : 16 + n])

    full = pl.BlockSpec(memory_space=VM)
    return pl.pallas_call(
        body,
        grid=(rows,),
        out_shape=[
            jax.ShapeDtypeStruct((count, 4 * ATT), bf16),
            jax.ShapeDtypeStruct((count, ATT), bf16),
            jax.ShapeDtypeStruct((count, D), bf16),
            jax.ShapeDtypeStruct((count, ATT), bf16),
            jax.ShapeDtypeStruct((count, LANES), f32),
            jax.ShapeDtypeStruct((count, D), bf16),
            jax.ShapeDtypeStruct((rows, 8, length), f32),
            jax.ShapeDtypeStruct((D, D), bf16),
            jax.ShapeDtypeStruct((D, FF // GROUPS), bf16),
            jax.ShapeDtypeStruct((FF, D // GROUPS), bf16),
        ],
        in_specs=[full, pl.BlockSpec(memory_space=pltpu.SMEM), blocked(length, D), full, full, full, full],
        out_specs=[
            blocked(length, 4 * ATT),
            blocked(length, ATT),
            blocked(length, D),
            blocked(length, ATT),
            blocked(length, LANES),
            blocked(length, D),
            pl.BlockSpec((1, 8, length), lambda r: (r, 0, 0)),
            full,
            full,
            full,
        ],
        scratch_shapes=scratch + Gather.scratch(sect, inner),
        compiler_params=pltpu.CompilerParams(vmem_limit_bytes=VMEM_LIMIT, collective_id=2, has_side_effects=True),
        name="row_forward",
    )(own, lengths, tokens, wp, pw, kw, vec)


def mid_kernel(length, len_ref, tok_ref, join_ref, cot_ref, dw_ref, fi_ref, fo_ref, vec_ref,
               out_ref, gf_ref, gj_ref, part_ref, gv_ref,
               gdw_ref, gfi_ref, gfo_ref, xh1, rs1, nl, act, slope, gsec, gsl, wide):
    row = pl.program_id(0)
    fg, dg = FF // GROUPS, D // GROUPS

    @pl.when(row == 0)
    def _():
        for ref in (gdw_ref, gfi_ref, gfo_ref, gv_ref):
            ref[...] = jnp.zeros_like(ref)

    used = jnp.int32(0)
    for j in range(SLOTS):
        used = used + len_ref[row, j]

    def vec(r, n=D):
        return vec_ref[r : r + 1, 0:n]

    step = 128
    gsec[...] = nn(join_ref[...], dw_ref[...])

    def norm1(i):
        at = pl.ds(pl.multiple_of(i * step, step), step)
        z = gsec[at, :] + vec(DB) + tok_ref[at, :].astype(f32)
        z = z - jnp.mean(z, axis=1, keepdims=True)
        r = lax.rsqrt(jnp.mean(z * z, axis=1, keepdims=True) + EPS)
        x = z * r
        xh1[at, :] = x
        rs1[at, :] = jnp.broadcast_to(r, (step, LANES))
        nl[at, :] = (x * vec(N1G) + vec(N1S)).astype(bf16)

    loop(length // step, norm1)

    tile = 512
    per = fg // tile

    tiles = [(g, i) for g in range(GROUPS) for i in range(per)]

    def inner(n):
        g, i = tiles[n]
        wide[n % 2] = nn(nl[:, g * dg : (g + 1) * dg], fi_ref[g * dg : (g + 1) * dg, i * tile : (i + 1) * tile])

    inner(0)
    for n, (g, i) in enumerate(tiles):
        if n + 1 < len(tiles):
            inner(n + 1)
        col = slice(g * fg + i * tile, g * fg + (i + 1) * tile)
        for r in range(0, length, 64):
            x = wide[n % 2, r : r + 64, :] + vec_ref[FIB : FIB + 1, col]
            phi = 0.5 * lax.erf(x * math.sqrt(0.5)) + 0.5
            e = jnp.exp2(x * x * (-0.5 / math.log(2.0)))
            act[r : r + 64, col] = (x * phi).astype(bf16)
            slope[r : r + 64, col] = (phi + x * (1.0 / math.sqrt(2.0 * math.pi)) * e).astype(bf16)

    for g in range(GROUPS):
        gsec[:, g * dg : (g + 1) * dg] = nn(act[:, g * fg : (g + 1) * fg], fo_ref[g * fg : (g + 1) * fg, :])

    def rows8(x):
        total = x[0:8]
        for k in range(8, x.shape[0], 8):
            total = total + x[k : k + 8]
        return total

    def norm2(i, carry):
        at = pl.ds(pl.multiple_of(i * step, step), step)
        norm = xh1[at, :] * vec(N1G) + vec(N1S)
        z = gsec[at, :] + vec(FOB) + norm
        z = z - jnp.mean(z, axis=1, keepdims=True)
        r = lax.rsqrt(jnp.mean(z * z, axis=1, keepdims=True) + EPS)
        x = z * r
        keep = ((iota((step, 1), 0) + i * step) < used).astype(f32)
        out_ref[at, :] = ((x * vec(N2G) + vec(N2S)) * keep).astype(bf16)
        gf = cot_ref[at, :].astype(f32) * keep
        gx = gf * x
        e = gf * vec(N2G)
        gz = r * (e - jnp.mean(e, axis=1, keepdims=True) - x * jnp.mean(e * x, axis=1, keepdims=True))
        gsec[at, :] = gz
        gsl[at, :] = gz.astype(bf16)
        return (carry[0] + rows8(gx), carry[1] + rows8(gf), carry[2] + rows8(gz))

    none = jnp.zeros((8, D), f32)
    sums = lax.fori_loop(0, length // step, norm2, (none, none, none))

    def add(r, value):
        gv_ref[r : r + 1, 0 : value.shape[1]] += jnp.sum(value, axis=0, keepdims=True)

    for r, value in zip((N2G, N2S, FOB), sums):
        add(r, value)

    for g in range(GROUPS):
        def narrow(i, g=g):
            r0 = pl.ds(pl.multiple_of(g * fg + i * tile, tile), tile)
            x = nt(gsl[:, g * dg : (g + 1) * dg], fo_ref[r0, :]) * slope[:, r0].astype(f32)
            gv_ref[FIB : FIB + 1, r0] += jnp.sum(x, axis=0, keepdims=True)
            slope[:, r0] = x.astype(bf16)
            gfo_ref[r0, :] += tn(act[:, r0], gsl[:, g * dg : (g + 1) * dg])
            col = pl.ds(pl.multiple_of(i * tile, tile), tile)
            gfi_ref[g * dg : (g + 1) * dg, col] += tn(nl[:, g * dg : (g + 1) * dg], slope[:, r0])

        loop(per, narrow)
    for g in range(GROUPS):
        gsec[:, g * dg : (g + 1) * dg] += nt(slope[:, g * fg : (g + 1) * fg], fi_ref[g * dg : (g + 1) * dg, :])

    def norm1_back(i, carry):
        at = pl.ds(pl.multiple_of(i * step, step), step)
        gn = gsec[at, :]
        x = xh1[at, :]
        e = gn * vec(N1G)
        r = rs1[at, :]
        r = jnp.concatenate([r] * (D // LANES), axis=1)
        gz = r * (e - jnp.mean(e, axis=1, keepdims=True) - x * jnp.mean(e * x, axis=1, keepdims=True))
        gf_ref[at, :] = gz.astype(bf16)
        return (carry[0] + rows8(gn * x), carry[1] + rows8(gn), carry[2] + rows8(gz))

    sums = lax.fori_loop(0, length // step, norm1_back, (none, none, none))
    for r, value in zip((N1G, N1S, DB), sums):
        add(r, value)
    low = gf_ref[...]
    gj_ref[...] = nt(low, dw_ref[...]).astype(bf16)
    gdw_ref[...] += tn(join_ref[...], low)

    @pl.when(row == pl.num_programs(0) - 1)
    def _():
        to_frames(part_ref, ((gdw_ref, D, D, 0), (gfi_ref, D, FF // GROUPS, 0), (gfo_ref, FF, D // GROUPS, 0)))


def run_mid(sect, tokens, lengths, joined, cotangent, dw, fi, fo, vec):
    rows, count = lengths.shape[0], tokens.shape[0]
    length = count // rows

    def body(*refs):
        mid_kernel(length, *refs)

    full = pl.BlockSpec(memory_space=VM)
    return pl.pallas_call(
        body,
        grid=(rows,),
        out_shape=[
            jax.ShapeDtypeStruct((count, D), bf16),
            jax.ShapeDtypeStruct((count, D), bf16),
            jax.ShapeDtypeStruct((count, D), bf16),
            jax.ShapeDtypeStruct((sect.count, sect.chunk, LANES), bf16),
            jax.ShapeDtypeStruct((VROWS, FF), f32),
        ],
        in_specs=[pl.BlockSpec(memory_space=pltpu.SMEM)] + [blocked(length, D)] * 3 + [full] * 4,
        out_specs=[blocked(length, D)] * 3 + [full] * 2,
        scratch_shapes=[
            VM((D, D), f32),
            VM((D, FF // GROUPS), f32),
            VM((FF, D // GROUPS), f32),
            VM((length, D), f32),
            VM((length, LANES), f32),
            VM((length, D), bf16),
            VM((length, FF), bf16),
            VM((length, FF), bf16),
            VM((length, D), f32),
            VM((length, D), bf16),
            VM((2, length, 512), f32),
        ],
        compiler_params=pltpu.CompilerParams(vmem_limit_bytes=VMEM_LIMIT),
        name="mid",
    )(lengths, tokens, joined, cotangent, dw, fi, fo, vec)


def bwd_kernel(length, pump, len_ref, tok_ref, qkvc_ref, kc_ref, dep_ref, ca_ref, tap_ref, join_ref, lse_ref, gf_ref, gj_ref,
               wp_ref, pw_ref, kw_ref, vec_ref,
               gt_ref, gp_ref, gpw_ref, gkw_ref, gv_ref,
               ds, cs, dcol, tm, mb, emat, gs, tp, prod, gq, gfour, acc):
    row = pl.program_id(0)
    pump(0)

    @pl.when(row == 0)
    def _():
        fill_emat(emat)
        for ref in (gp_ref, gpw_ref, gkw_ref, gv_ref):
            ref[...] = jnp.zeros_like(ref)

    doc_marks(row, length, len_ref, dcol, tm, mb)
    for ref in (ds, cs, gs, tp):
        zero_pads(ref, length)

    def add(r, value):
        gv_ref[r : r + 1, 0 : value.shape[1]] += jnp.sum(value, axis=0, keepdims=True)

    for p in range(3):
        if p:
            pump(p)
        cols = slice(p * LANES, (p + 1) * LANES)
        q, k, v = (qkvc_ref[:, m * ATT + p * LANES : m * ATT + (p + 1) * LANES] for m in range(3))
        g = gj_ref[:, cols]
        lane, sub = iota((length, LANES), 1), iota((16, LANES), 1)
        which = iota((16, LANES), 0)
        marks = jnp.where((sub >= HEAD_DIM) == (which >= 8), 1.0, 0.0).astype(bf16)
        dots = g.astype(f32) * join_ref[:, cols].astype(f32)
        high = dots.astype(bf16)
        dots = nt(marks, high) + nt(marks, (dots - high.astype(f32)).astype(bf16))
        qs = q.astype(f32) * SCALE
        kt = k.astype(f32).T.astype(bf16)
        gk, gv, gqt = None, None, []
        for h in range(2):
            own = (lane >= HEAD_DIM) == bool(h)
            qh = jnp.where(own, qs, 0.0).astype(bf16)
            gh = jnp.where(own, g.astype(f32), 0.0).astype(bf16)
            prob = jnp.exp(jnp.minimum(nt(k, qh), mb[...]) - lse_ref[0, 2 * p + h : 2 * p + h + 1, :])
            dsc = (prob * (nt(v, gh) - dots[8 * h : 8 * h + 1, :])).astype(bf16)
            a, b = nn(prob.astype(bf16), gh), nn(dsc, qh)
            gv, gk = (a, b) if h == 0 else (gv + a, gk + b)
            gqt.append(nn(kt, dsc)[h * HEAD_DIM : (h + 1) * HEAD_DIM, :])
        gq[:, cols] = jnp.concatenate(gqt, axis=0).T * SCALE
        gfour[:, ATT + p * LANES : ATT + (p + 1) * LANES] = gk.astype(bf16)
        gfour[:, 2 * ATT + p * LANES : 2 * ATT + (p + 1) * LANES] = gv.astype(bf16)
        gv_ref[VB : VB + 1, cols] += jnp.sum(gv, axis=0, keepdims=True)

    pump(3)
    for c in range(3):
        cs[c, 8 : 8 + length, :] = qkvc_ref[:, 3 * ATT + c * LANES : 3 * ATT + (c + 1) * LANES].astype(f32)
        gs[c, 8 : 8 + length, :] = gj_ref[:, ATT + c * LANES : ATT + (c + 1) * LANES].astype(f32)
    for j in range(KS):
        for c in range(3):
            at = 8 + j - HALF
            prod[:, j * ATT + c * LANES : j * ATT + (c + 1) * LANES] = (
                gs[c, 8 : 8 + length, :] * cs[c, at : at + length, :]
            ).astype(bf16)
    marks = tap_lanes(tm, length)
    gtaps = nt(prod[...], emat[0:LANES, :]) * marks
    taps = jnp.where(used_taps((length, LANES)), tap_ref[...], 0.0)
    glog = taps * (gtaps - over_taps(taps * gtaps, jnp.add))
    add(KBR, glog)
    glog = glog.astype(bf16)
    gkw_ref[...] += tn(ca_ref[...], glog)
    gca = nt(glog, kw_ref[...])

    tp[0, 8 : 8 + length, :] = taps * marks
    tap = iota((length, LANES), 1) >> 3
    moved = jnp.zeros((length, LANES), f32)
    for j in range(KS):
        at = 8 + HALF - j
        moved = jnp.where(tap == j, tp[0, at : at + length, :], moved)
    spread = two_parts(moved)
    for j in range(KS):
        t = nn(spread, emat[:, j * ATT : (j + 1) * ATT])
        for c in range(3):
            at = 8 + HALF - j
            part = t[:, c * LANES : (c + 1) * LANES] * gs[c, at : at + length, :]
            if j:
                part = part + acc[:, c * LANES : (c + 1) * LANES]
            if j < KS - 1:
                acc[:, c * LANES : (c + 1) * LANES] = part
            else:
                gfour[:, 3 * ATT + c * LANES : 3 * ATT + (c + 1) * LANES] = part.astype(bf16)
                gv_ref[CB : CB + 1, c * LANES : (c + 1) * LANES] += jnp.sum(part, axis=0, keepdims=True)

    pump(4)
    gkc = gca * qkvc_ref[:, 0:ATT].astype(f32)
    gquery = gq[...] + gca * kc_ref[...].astype(f32)
    add(QB, gquery)
    gfour[:, 0:ATT] = gquery.astype(bf16)
    add(PB, gkc)
    gkc = gkc.astype(bf16)
    gpw_ref[...] += tn(dep_ref[...], gkc)
    for c in range(3):
        x = nt(gkc, pw_ref[c * 256 : (c + 1) * 256, :])
        ds[2 * c, 8 : 8 + length, :] = x[:, 0:LANES]
        ds[2 * c + 1, 8 : 8 + length, :] = x[:, LANES:]
    for m in range(4):
        gp_ref[:, m * ATT : (m + 1) * ATT] += tn(tok_ref[...], gfour[:, m * ATT : (m + 1) * ATT])

    pump(5)
    step = 64
    for c in range(6):
        cols = slice(c * LANES, (c + 1) * LANES)
        w = [vec_ref[DW + j : DW + j + 1, cols] for j in range(KS)]
        sums = [None] * KS
        if c % 2 == 0:
            direct = nt(gfour[...], wp_ref[c * LANES : (c + 2) * LANES, :])
        for r in range(0, length, step):
            tok = tok_ref[r : r + step, cols].astype(f32)
            total = gf_ref[r : r + step, cols].astype(f32) + direct[r : r + step, (c % 2) * LANES : (c % 2 + 1) * LANES]
            for j in range(KS):
                at = 8 + r + j - HALF
                u = ds[c, at : at + step, :]
                if j != HALF:
                    u = u * tm[j, r : r + step, :]
                total = total + w[KS - 1 - j] * u
                u = tok * u
                part = u[0:8]
                for s in range(8, step, 8):
                    part = part + u[s : s + 8]
                sums[j] = part if r == 0 else sums[j] + part
            gt_ref[r : r + step, cols] = total.astype(bf16)
        for j in range(KS):
            gv_ref[DW + KS - 1 - j : DW + KS - j, cols] += jnp.sum(sums[j], axis=0, keepdims=True)
    pump(6)


BWD_POINTS = 7


def run_bwd(sect, outer, inner, part, tokens, lengths, saved, gf, gj, wp, pw, kw, vec):
    qkvc, kc, dep, ca, taps, joined, lse = saved
    rows, count = lengths.shape[0], tokens.shape[0]
    length = count // rows
    scratch = row_scratch(length) + [
        VM((3, length + 16, LANES), f32),
        VM((1, length + 16, LANES), f32),
        VM((length, KS * ATT), bf16),
        VM((length, ATT), f32),
        VM((length, 4 * ATT), bf16),
        VM((length, ATT), f32),
    ]
    n = len(scratch)

    def body(part_ref, *refs):
        ours, own_ref = refs[:20], refs[20]
        job = Scatter(sect, Place(outer, inner), part_ref, refs[21 + n :])

        def begin():
            job.greet()
            job.steps[0]()

        def end():
            job.steps[-1]()
            own_ref[...] = job.out[sect.chunk : sect.chunk + sect.rows, :]

        pump = pumped([begin, *job.steps[1:-1], end], rows, BWD_POINTS)
        bwd_kernel(length, pump, *ours, *refs[21 : 21 + n])

    full = pl.BlockSpec(memory_space=VM)
    return pl.pallas_call(
        body,
        grid=(rows,),
        out_shape=[
            jax.ShapeDtypeStruct((count, D), bf16),
            jax.ShapeDtypeStruct((D, 4 * ATT), f32),
            jax.ShapeDtypeStruct((D, ATT), f32),
            jax.ShapeDtypeStruct((ATT, LANES), f32),
            jax.ShapeDtypeStruct((VROWS, FF), f32),
            jax.ShapeDtypeStruct((sect.rows, LANES), f32),
        ],
        in_specs=[
            full,
            pl.BlockSpec(memory_space=pltpu.SMEM),
            blocked(length, D),
            blocked(length, 4 * ATT),
            blocked(length, ATT),
            blocked(length, D),
            blocked(length, ATT),
            blocked(length, LANES),
            blocked(length, D),
            pl.BlockSpec((1, 8, length), lambda r: (r, 0, 0)),
            blocked(length, D),
            blocked(length, D),
            full,
            full,
            full,
            full,
        ],
        out_specs=[blocked(length, D)] + [full] * 5,
        scratch_shapes=scratch + Scatter.scratch(sect, inner),
        compiler_params=pltpu.CompilerParams(vmem_limit_bytes=VMEM_LIMIT, collective_id=3, has_side_effects=True),
        name="row_backward",
    )(part, lengths, tokens, qkvc, kc, dep, ca, taps, joined, lse, gf, gj, wp, pw, kw, vec)


def gather_kernel(sect, outer, inner, own_ref, wp_ref, pw_ref, kw_ref, vec_ref, flat, kwt, *scratch):
    place = Place(outer, inner)
    job = Gather(sect, place, own_ref, scratch)
    job.greet()
    all_steps(job)
    pieces = [(wp_ref, D, ATT, m * ATT) for m in range(4)] + [(pw_ref, D, ATT, 0)]
    v = from_frames(job.buf, pieces)
    for n in range(sect.small):
        flat[n * sect.chunk : (n + 1) * sect.chunk, :] = job.buf[v + n].astype(f32)
    unpack_small(flat, kw_ref, vec_ref, kwt)


def run_gather(sect, own, outer, inner):
    def body(*refs):
        gather_kernel(sect, outer, inner, *refs)

    full = pl.BlockSpec(memory_space=VM)
    return pl.pallas_call(
        body,
        out_shape=[
            jax.ShapeDtypeStruct((D, 4 * ATT), bf16),
            jax.ShapeDtypeStruct((D, ATT), bf16),
            jax.ShapeDtypeStruct((ATT, LANES), bf16),
            jax.ShapeDtypeStruct((VROWS, FF), f32),
        ],
        in_specs=[full],
        out_specs=[full] * 4,
        scratch_shapes=[VM((sect.small * sect.chunk, LANES), f32), VM((512, LANES), f32)] + Gather.scratch(sect, inner),
        compiler_params=pltpu.CompilerParams(vmem_limit_bytes=VMEM_LIMIT, collective_id=0, has_side_effects=True),
        name="gather",
    )(own)


def scatter_kernel(sect, outer, inner, gp_ref, gpw_ref, gkw_ref, va_ref, vb_ref, other_ref, out_ref, part, vec, flat, kwt, *scratch):
    place = Place(outer, inner)
    job = Scatter(sect, place, part, scratch)
    vec[...] = va_ref[...] + vb_ref[...]
    v = to_frames(part, [(gp_ref, D, ATT, m * ATT) for m in range(4)] + [(gpw_ref, D, ATT, 0)])
    pack_small(flat, gkw_ref, vec, kwt)
    for n in range(sect.small):
        part[v + n] = flat[n * sect.chunk : (n + 1) * sect.chunk, :].astype(bf16)
    job.greet()
    all_steps(job)
    out_ref[...] = job.out[sect.chunk : sect.chunk + sect.rows, :] + other_ref[...]


def run_scatter(sect, outer, inner, gp, gpw, gkw, va, vb, other):
    def body(*refs):
        scatter_kernel(sect, outer, inner, *refs)

    full = pl.BlockSpec(memory_space=VM)
    return pl.pallas_call(
        body,
        out_shape=jax.ShapeDtypeStruct((sect.rows, LANES), f32),
        in_specs=[full] * 6,
        out_specs=full,
        scratch_shapes=[
            VM((sect.count, sect.chunk, LANES), bf16),
            VM((VROWS, FF), f32),
            VM((max(sect.small * sect.chunk, 384), LANES), f32),
            VM((512, LANES), f32),
        ]
        + Scatter.scratch(sect, inner),
        compiler_params=pltpu.CompilerParams(vmem_limit_bytes=VMEM_LIMIT, collective_id=1, has_side_effects=True),
        name="scatter",
    )(gp, gpw, gkw, va, vb, other)


def shards(tokens, doc_lengths, params, cotangent):
    rows = params.shape[0] // LANES
    outer, inner = lax.axis_size("dp"), lax.axis_size("fsdp")
    own = params.reshape(rows, LANES)
    first, second = sections(outer * inner, rows, inner)
    wp, pw, kw, vec = run_gather(first, own, outer, inner)
    *saved, dw, fi, fo = run_fwd(second, outer, inner, own, tokens, doc_lengths, wp, pw, kw, vec)
    output, gf, gj, part, va = run_mid(second, tokens, doc_lengths, saved[5], cotangent, dw, fi, fo, vec)
    gt, gp, gpw, gkw, vb, some = run_bwd(second, outer, inner, part, tokens, doc_lengths, saved, gf, gj, wp, pw, kw, vec)
    own_grad = run_scatter(first, outer, inner, gp, gpw, gkw, va, vb, some)
    return output, gt, own_grad.reshape(rows * LANES)


def solution(mesh):
    axes = ("dp", "fsdp")
    placed = (P(axes, None), P(axes, None), P(axes), P(axes, None))
    return jax.shard_map(
        shards,
        mesh=mesh,
        in_specs=placed,
        out_specs=(P(axes, None), P(axes, None), P(axes)),
        check_vma=False,
    )
```

```python
import math

import jax
import jax.numpy as jnp
from jax import lax
from jax.experimental import pallas as pl
from jax.experimental.pallas import tpu as pltpu
from jax.sharding import PartitionSpec as P

D = 768
HEADS = 6
HEAD_DIM = 64
ATT = HEADS * HEAD_DIM
FF = 3072
GROUPS = 2
KS = 9
HALF = KS // 2
SLOTS = 16
EPS = 1e-12
LANES = 128
NEG = -1e30
BIG = 3e38
SCALE = HEAD_DIM ** (-0.5)

f32 = jnp.float32
bf16 = jnp.bfloat16
i32 = jnp.int32

FIRST = 5 * D * ATT // LANES
MATRICES = FIRST + (D * D + 2 * D * FF // GROUPS) // LANES
DEPTH_AT = 0
KERNEL_AT = KS * D // LANES
BIAS_AT = KERNEL_AT + ATT * HEADS * KS // LANES
TAIL_AT = BIAS_AT + 4 * ATT // LANES
SMALL = TAIL_AT + 61
KB = HEADS * KS

QB, VB, CB, PB, KBR, DB, N1G, N1S, FIB, FOB, N2G, N2S, DW = range(13)
VROWS = 24
TAIL = [(DB, 6), (N1G, 6), (N1S, 6), (FIB, 24), (FOB, 6), (N2G, 6), (N2S, 6)]

VM = pltpu.VMEM
VMEM_LIMIT = 62 * 1024 * 1024


def nn(a, b):
    return lax.dot_general(a, b, (((1,), (0,)), ((), ())), preferred_element_type=f32)


def nt(a, b):
    return lax.dot_general(a, b, (((1,), (1,)), ((), ())), preferred_element_type=f32)


def tn(a, b):
    return lax.dot_general(a, b, (((0,), (0,)), ((), ())), preferred_element_type=f32)


def iota(shape, axis):
    return lax.broadcasted_iota(i32, shape, axis)


def loop(count, body, unroll=1):
    def step(i, carry):
        body(i)
        return carry

    lax.fori_loop(0, count, step, 0, unroll=unroll)


def tap_perm():
    k, n = iota((LANES, LANES), 0), iota((LANES, LANES), 1)
    head, tap = n & 7, n >> 3
    return jnp.where((k == head * KS + tap) & (head < HEADS) & (tap < KS), 1.0, 0.0).astype(bf16)


def used_taps(shape):
    n = iota(shape, len(shape) - 1)
    return ((n & 7) < HEADS) & ((n >> 3) < KS)


def padded(rows):
    return -(-rows // 16) * 16


class Section:
    def __init__(self, base, kinds, chunk, small, rows, count, inner):
        self.base, self.chunk, self.rows, self.count, self.inner = base, chunk, rows, count, inner
        self.main = sum(n for n, _ in kinds)
        self.small = -(-SMALL // chunk) if small else 0
        self.kinds = kinds + ([(self.small, 1)] if small else [])
        self.used = self.main + self.small
        self.pieces = -(-rows // chunk) + 1
        self.slots = self.pieces + self.small
        self.sources = (chunk - 2) // rows + 2
        self.lead = -(-base // rows)

    def seat(self, v, pick=jnp.where):
        q, r, n = v // 3, v % 3, self.count
        if self.small:
            near = pick(q < n // 4, r * (n // 4) + q, 3 * (n // 4) + v - 3 * (n // 4))
            return pick(v < self.main, near, n - self.small + v - self.main)
        return pick(r < 2, self.lead + 2 * q + r, q)

    def chunk_at(self, d):
        n = self.count
        if self.small:
            quarter = n // 4
            v = jnp.where(d < 3 * quarter, 3 * lax.rem(d, quarter) + d // quarter, d)
            v = jnp.where(v < self.main, v, self.used)
            return jnp.where(d >= n - self.small, self.main + d - (n - self.small), v)
        t = d - self.lead
        v = jnp.where(d < self.main // 3, 3 * d + 2, self.used)
        return jnp.where((t >= 0) & (t < 2 * self.main // 3), 3 * (t // 2) + lax.rem(t, 2), v)

    def start(self, v):
        at = self.base + v * self.chunk
        if self.small:
            at = jnp.where(v >= self.main, MATRICES + (v - self.main) * self.chunk, at)
        return at

    def first_piece(self, i):
        return jnp.maximum(self.rows * i - self.base, 0) // self.chunk

    def of_owner(self, i, k):
        if k < self.pieces:
            v = self.first_piece(i) + k
            ok = v < self.main
        else:
            v = self.main + k - self.pieces + 0 * i
            ok = v >= 0
        at = self.start(v)
        return v, ok & (at < self.rows * (i + 1)) & (at + self.chunk > self.rows * i)

    def of_chunk(self, v, s):
        i = self.start(v) // self.rows + s
        return i, (v < self.used) & (i < self.count) & (self.rows * i < self.start(v) + self.chunk)

    def source_of(self, v, i):
        return i - self.start(v) // self.rows

    def slot_of(self, v, i):
        return jnp.where(v < self.main, v - self.first_piece(i), self.pieces + v - self.main)

    def by_kind(self, v, action):
        at, seen = 0, {}
        for n, per in self.kinds:
            seen.setdefault(per, []).append((at, at + n))
            at += n
        for per, spans in seen.items():
            ok = False
            for lo, hi in spans:
                ok = ((v >= lo) & (v < hi)) | ok
            pl.when(ok)(lambda per=per: action(per))


def sections(count, rows, inner):
    big, little = 24576 // count, 12288 // count
    first = Section(0, [(FIRST // little, 3)], little, True, rows, count, inner)
    kinds = [(D * n // LANES // big, n // LANES) for n in (D, FF // GROUPS)] + [(FF * 3 // big, 3)]
    return first, Section(FIRST, kinds, big, False, rows, count, inner)


class Rows:
    def __init__(self, ref, chunk):
        self.ref, self.chunk = ref, chunk

    def __setitem__(self, where, value):
        v, rows, _ = where
        self.ref[v * self.chunk + rows.start : v * self.chunk + rows.stop, :] = value


def choose(ok, a, b):
    return a if ok else b


def pieces_of(sect, matrices):
    v = 0
    for ref, height, width, col in matrices:
        per = width // LANES
        tall = sect.chunk // per
        for r in range(0, height, tall):
            for c in range(per):
                cols = slice(col + c * LANES, col + (c + 1) * LANES)
                yield sect.seat(v, choose), slice(c * tall, (c + 1) * tall), ref, slice(r, r + tall), cols
            v += 1


def to_frames(sect, part, matrices, small=None):
    for seat, rows, ref, r, c in pieces_of(sect, matrices):
        part[seat, rows, :] = ref[r, c].astype(bf16)
    for k in range(sect.small):
        part[sect.seat(sect.main + k, choose), slice(0, sect.chunk), :] = small[
            k * sect.chunk : (k + 1) * sect.chunk, :
        ].astype(bf16)
    for d in set(range(sect.count)) - {sect.seat(v, choose) for v in range(sect.used)}:
        part[d, slice(0, sect.chunk), :] = jnp.zeros((sect.chunk, LANES), bf16)


def from_frames(sect, buf, matrices, small=None):
    for seat, rows, ref, r, c in pieces_of(sect, matrices):
        ref[r, c] = buf[seat, rows, :]
    for k in range(sect.small):
        small[k * sect.chunk : (k + 1) * sect.chunk, :] = buf[sect.seat(sect.main + k, choose)].astype(f32)


def unpack_small(flat, kw_ref, vec_ref, kwt):
    vec_ref[...] = jnp.zeros_like(vec_ref)
    for row in range(4):
        for c in range(3):
            at = BIAS_AT + row * 3 + c
            vec_ref[row : row + 1, c * LANES : (c + 1) * LANES] = flat[at : at + 1, :]
    for j in range(KS):
        for c in range(6):
            at = DEPTH_AT + j * 6 + c
            vec_ref[DW + j : DW + j + 1, c * LANES : (c + 1) * LANES] = flat[at : at + 1, :]
    at = TAIL_AT
    lane = iota((64, LANES), 1)
    first = pltpu.roll(flat[at : at + 64, :], LANES - KB, 1)
    second = pltpu.roll(flat[at + 1 : at + 65, :], LANES - KB, 1)
    kwt[0:64, :] = jnp.where(lane < LANES - KB, first, second)
    at = 0
    for row, many in TAIL:
        for c in range(many):
            vec_ref[row : row + 1, c * LANES : (c + 1) * LANES] = kwt[at + c : at + c + 1, :]
        at += many
    perm = tap_perm()
    lane8 = iota((16, LANES), 1)
    kb = jnp.broadcast_to(flat[TAIL_AT : TAIL_AT + 1, :], (16, LANES))
    kb = nn(jnp.where(lane8 < KB, kb, 0.0).astype(bf16), perm)
    kb = jnp.where(used_taps((16, LANES)), kb, NEG)
    vec_ref[KBR : KBR + 1, 0:LANES] = kb[0:1]

    lane = iota((8, LANES), 1)
    for a in range(64):
        c0, ln = divmod(a * KB, LANES)
        at = KERNEL_AT + c0
        x = pltpu.roll(flat[pl.ds(at, 8, stride=27), :], (LANES - ln) % LANES, 1)
        if ln + KB > LANES:
            y = pltpu.roll(flat[pl.ds(at + 1, 8, stride=27), :], (LANES - ln) % LANES, 1)
            x = jnp.where(lane < LANES - ln, x, y)
        kwt[pl.ds(a, 8, stride=64), :] = jnp.where(lane < KB, x, 0.0)
    kw_ref[...] = nn(kwt[0:ATT, :].astype(bf16), perm).astype(bf16)


def pack_small(flat, gkw_ref, vec, kwt):
    flat[...] = jnp.zeros_like(flat)
    perm = tap_perm()
    kwt[...] = jnp.zeros_like(kwt)
    kwt[0:ATT, :] = nt(gkw_ref[...].astype(bf16), perm)
    lane = iota((8, LANES), 1)
    for a in range(64):
        c0, ln = divmod(a * KB, LANES)
        at = KERNEL_AT + c0
        x = pltpu.roll(kwt[pl.ds(a, 8, stride=64), :], ln, 1)
        if ln + KB > LANES:
            flat[pl.ds(at, 8, stride=27), :] += jnp.where(lane >= ln, x, 0.0)
            flat[pl.ds(at + 1, 8, stride=27), :] += jnp.where(lane < ln, x, 0.0)
        else:
            flat[pl.ds(at, 8, stride=27), :] += x
    for row in range(4):
        for c in range(3):
            at = BIAS_AT + row * 3 + c
            flat[at : at + 1, :] = vec[row : row + 1, c * LANES : (c + 1) * LANES]
    for j in range(KS):
        for c in range(6):
            at = DEPTH_AT + j * 6 + c
            flat[at : at + 1, :] = vec[DW + j : DW + j + 1, c * LANES : (c + 1) * LANES]
    kwt[...] = jnp.zeros_like(kwt)
    at = 8
    for row, many in TAIL:
        for c in range(many):
            kwt[at + c : at + c + 1, :] = vec[row : row + 1, c * LANES : (c + 1) * LANES]
        at += many
    lane = iota((72, LANES), 1)
    before = pltpu.roll(kwt[7:79, :], KB, 1)
    here = pltpu.roll(kwt[8:80, :], KB, 1)
    at = TAIL_AT
    flat[at : at + 72, :] = jnp.where(lane < KB, before, here)
    kb = jnp.broadcast_to(vec[KBR : KBR + 1, 0:LANES], (16, LANES))
    kb = nt(jnp.where(used_taps((16, LANES)), kb, 0.0).astype(bf16), perm)
    lane = iota((1, LANES), 1)
    flat[at : at + 1, :] = jnp.where(lane < KB, kb[0:1], flat[at : at + 1, :])


class Place:
    def __init__(self, outer, inner):
        self.outer, self.inner, self.count = outer, inner, outer * inner
        self.lines = inner // 2
        dp, fs = lax.axis_index("dp"), lax.axis_index("fsdp")
        self.y, self.x, self.z, self.c = dp // 2, lax.rem(dp, 2), fs // 2, lax.rem(fs, 2)
        self.me = dp * inner + fs

    def coords(self, dy=0, dx=0, z=None, dc=0):
        def flip(v, d):
            return 1 - v if d else v

        z = self.z if z is None else z
        return flip(self.y, dy) * 2 + flip(self.x, dx), z * 2 + flip(self.c, dc)

    def index(self, **d):
        o, i = self.coords(**d)
        return o * self.inner + i

    def device(self, n):
        return n // self.inner, lax.rem(n, self.inner)

    def item(self, t):
        s = (t + 1) // 2
        z = self.z - s if t % 2 else self.z + s
        return z, (z >= 0) & (z < self.lines), s, t % 2 == 1

    def greet_all(self):
        barrier = pltpu.get_barrier_semaphore()
        for n in range(1, self.count):
            peer = self.device(lax.rem(self.me + n, self.count))
            pl.semaphore_signal(barrier, inc=1, device_id=peer, device_id_type=pl.DeviceIdType.MESH)
        pl.semaphore_wait(barrier, self.count - 1)


class Copies:
    def __init__(self, send, recv):
        self.send, self.recv, self.used, self.made = send, recv, 0, []

    def start(self, src, dst, peer, slot, ok=None):
        number = self.used
        self.used += 1
        assert number < self.send.shape[0]

        def make():
            return pltpu.make_async_remote_copy(
                src_ref=src(),
                dst_ref=dst(),
                send_sem=self.send.at[number],
                recv_sem=self.recv.at[slot() if callable(slot) else slot],
                device_id=peer(),
                device_id_type=pl.DeviceIdType.MESH,
            )

        self.made.append((make, ok))
        guarded(ok, lambda: make().start())

    def arrived(self, dst, slot, ok=None):
        def wait():
            ref = dst()
            pltpu.make_async_copy(ref, ref, self.recv.at[slot]).wait()

        guarded(ok, wait)

    def finish(self):
        for make, ok in self.made:
            guarded(ok, lambda make=make: make().wait_send())


def guarded(ok, action):
    if ok is None:
        action()
    else:
        pl.when(ok())(action)


def half_of(chunk):
    return -(-chunk // 32) * 16


class Gather:
    @staticmethod
    def scratch(sect, inner):
        lines = inner // 2
        items = 2 * lines - 1
        return [
            VM((sect.count, sect.chunk, LANES), bf16),
            VM((sect.slots, sect.chunk, LANES), bf16),
            VM((sect.sources, sect.chunk, LANES), bf16),
            VM((sect.chunk, LANES), f32),
            pltpu.SemaphoreType.DMA((sect.slots + 10 * items + 4,)),
            pltpu.SemaphoreType.DMA((sect.sources + 9 * items,)),
        ]

    def __init__(self, sect, place, ownf, lead, scratch):
        self.sect, self.place, self.ownf, self.lead = sect, place, ownf, lead
        self.buf, self.win, self.land, self.frame, send, recv = scratch
        self.copies = Copies(send, recv)
        n = 2 * place.lines - 1
        self.items = n
        self.Z, self.X, self.Y, self.A, self.B, self.CZ, self.CX, self.CY, self.CD = (sect.sources + n * k for k in range(9))
        cut = half_of(sect.chunk)
        self.half = {"a": pl.ds(0, cut), "b": pl.ds(cut, sect.chunk - cut)}

    def offer(self):
        for k in range(self.sect.slots):
            self.give(k)

    def give(self, k):
        sect, place, me = self.sect, self.place, self.place.me
        v, ok = sect.of_owner(me, k)

        @pl.when(ok)
        def _():
            at = self.lead + sect.start(v) - sect.rows * me
            self.win[k] = self.ownf[pl.ds(at, sect.chunk), :].astype(bf16)

        @pl.when(ok & (sect.seat(v) == me))
        def _():
            self.land[sect.source_of(v, me)] = self.win[k]

        def chunk():
            return sect.of_owner(me, k)[0]

        def away():
            v, ok = sect.of_owner(me, k)
            return ok & (sect.seat(v) != me)

        def source():
            return jnp.clip(sect.source_of(chunk(), me), 0, sect.sources - 1)

        def seat():
            return jnp.clip(sect.seat(chunk()), 0, sect.count - 1)

        self.copies.start(lambda: self.win.at[k], lambda: self.land.at[source()], lambda: place.device(seat()), source, away)

    def form(self):
        sect, me = self.sect, self.place.me
        v = sect.chunk_at(me)
        row = iota((sect.chunk, LANES), 0) + sect.start(v)
        x = None
        for s in range(sect.sources):
            i, ok = sect.of_chunk(v, s)
            self.copies.arrived(lambda: self.land.at[s], s, lambda: ok & (i != me))
            here = self.land[s].astype(f32)
            x = here if x is None else jnp.where(row >= sect.rows * i, here, x)
        self.frame[...] = x

        def settle(per):
            tall = sect.chunk // per
            for c in range(per):
                self.buf[me, c * tall : (c + 1) * tall, :] = self.frame[pl.ds(c, tall, stride=per), :].astype(bf16)

        sect.by_kind(v, settle)

        @pl.when(v >= sect.used)
        def _():
            self.buf[me] = jnp.zeros((sect.chunk, LANES), bf16)

        self.pass_on(0)

    def ref(self, t, which=None, **way):
        def make():
            at = self.place.index(z=self.place.item(t)[0], **way)
            return self.buf.at[at] if which is None else self.buf.at[at, self.half[which]]

        return make

    def ok(self, t):
        return None if t == 0 else lambda: self.place.item(t)[1]

    def same(self, ref, peer, slot, ok):
        self.copies.start(ref, ref, peer, slot, ok)

    def beside(self, **way):
        return lambda: self.place.coords(**way)

    def pass_on(self, t):
        place = self.place
        _, _, s, below = place.item(t)
        for way in (1, -1) if t == 0 else ((1,) if below else (-1,)):
            slot = 2 * s + 1 if way > 0 else 2 * s + 2

            def inside(way=way):
                there = place.z + way
                good = (there >= 0) & (there < place.lines)
                return good if t == 0 else good & place.item(t)[1]

            if slot < self.items:
                self.same(self.ref(t), lambda way=way: place.coords(z=place.z + way), self.Z + slot, inside)
        ok = self.ok(t)
        self.same(self.ref(t), self.beside(dx=1), self.X + t, ok)
        self.same(self.ref(t), self.beside(dy=1), self.Y + t, ok)
        self.same(self.ref(t), self.beside(dc=1), self.CZ + t, ok)

    def at_distance(self, s):
        return [0] if s == 0 else [2 * s - 1, 2 * s]

    def along(self, s):
        for t in self.at_distance(s):
            self.copies.arrived(self.ref(t), self.Z + t, self.ok(t))
            self.pass_on(t)

    def across(self, s):
        for t in self.at_distance(s):
            ok = self.ok(t)
            self.copies.arrived(self.ref(t, dx=1), self.X + t, ok)
            self.same(self.ref(t, "a", dx=1), self.beside(dy=1), self.A + t, ok)
            self.same(self.ref(t, dx=1), self.beside(dc=1), self.CX + t, ok)
            self.copies.arrived(self.ref(t, dy=1), self.Y + t, ok)
            self.same(self.ref(t, "b", dy=1), self.beside(dx=1), self.B + t, ok)
            self.same(self.ref(t, dy=1), self.beside(dc=1), self.CY + t, ok)

    def diagonal(self):
        for t in range(self.items):
            ok = self.ok(t)
            self.copies.arrived(self.ref(t, "a", dy=1, dx=1), self.A + t, ok)
            self.copies.arrived(self.ref(t, "b", dy=1, dx=1), self.B + t, ok)
            self.same(self.ref(t, dy=1, dx=1), self.beside(dc=1), self.CD + t, ok)

    def rest(self):
        for t in range(self.items):
            for k, way in ((self.CZ, {}), (self.CX, {"dx": 1}), (self.CY, {"dy": 1}), (self.CD, {"dy": 1, "dx": 1})):
                self.copies.arrived(self.ref(t, dc=1, **way), k + t, self.ok(t))
        self.copies.finish()


class Scatter:
    @staticmethod
    def scratch(sect, inner):
        lines = inner // 2
        cut = half_of(sect.chunk)
        return [
            VM((4 * lines, sect.chunk, LANES), bf16),
            VM((4 * lines, sect.chunk, LANES), bf16),
            VM((2 * lines, cut, LANES), bf16),
            VM((2 * lines, sect.chunk - cut, LANES), bf16),
            VM((lines, sect.chunk - cut, LANES), bf16),
            VM((lines, cut, LANES), bf16),
            VM((lines, sect.chunk, LANES), bf16),
            VM((sect.chunk, LANES), f32),
            VM((sect.chunk, LANES), f32),
            VM((sect.chunk, LANES), bf16),
            VM((sect.slots, sect.chunk, LANES), bf16),
            pltpu.SemaphoreType.DMA((11 * lines + sect.sources,)),
            pltpu.SemaphoreType.DMA((11 * lines + sect.slots,)),
            pltpu.SemaphoreType.DMA((4 * lines,)),
        ]

    def __init__(self, sect, place, part, out, lead, scratch):
        self.sect, self.place, self.part, self.out, self.lead = sect, place, part, out, lead
        (self.work, self.rc, self.ry, self.rx, self.ry2, self.rx2, self.rz, self.frame, self.flat, self.low, self.land,
         send, recv, self.near) = scratch
        self.copies = Copies(send, recv)
        lines = place.lines
        self.lines = lines
        cut = half_of(sect.chunk)
        self.a, self.b = pl.ds(0, cut), pl.ds(cut, sect.chunk - cut)
        self.C, self.YA, self.XB, self.XA, self.YB, self.Z, self.O = (lines * k for k in (0, 4, 6, 8, 9, 10, 11))
        self.far = list(range(1, lines)) + [0]

    def sums(self):
        out = []
        for n in range(self.lines + 2):
            for lag, step in ((0, self.first), (1, self.second), (2, self.third)):
                if 0 <= n - lag < self.lines:
                    out.append(lambda step=step, d=self.far[n - lag]: step(d))
        return out

    def z(self, d):
        return lax.rem(self.place.z + d, self.lines) if d else self.place.z

    def at(self, dy, dx, d):
        return (dy * 2 + dx) * self.lines + d

    def own(self, dy, dx, d):
        k = self.at(dy, dx, d)
        there = self.place.index(dy=dy, dx=dx, z=self.z(d))
        return pltpu.make_async_copy(self.part(there), self.work.at[k], self.near.at[k])

    def core(self):
        place = self.place

        def give(dy, dx, d):
            k = self.at(dy, dx, d)
            self.copies.start(
                lambda: self.part(place.index(dy=dy, dx=dx, z=self.z(d), dc=1)),
                lambda: self.rc.at[k],
                lambda: place.coords(dc=1),
                self.C + k,
            )
            self.own(dy, dx, d).start()

        for d in self.far:
            for dy, dx in ((1, 1), (1, 0), (0, 1), (0, 0)):
                give(dy, dx, d)

    def send(self, k, rows, buf, n, way, slot):
        self.copies.start(lambda: self.work.at[k, rows], lambda: buf.at[n], lambda: self.place.coords(**way), slot)

    def got(self, buf, n, slot):
        self.copies.arrived(lambda: buf.at[n], slot)

    def plus(self, k, rows, other):
        self.work[k, rows] = (self.work[k, rows].astype(f32) + other.astype(f32)).astype(bf16)

    def first(self, d):
        lines = self.lines
        for dy, dx in ((1, 1), (1, 0), (0, 1), (0, 0)):
            k = self.at(dy, dx, d)
            self.own(dy, dx, d).wait()
            self.got(self.rc, k, self.C + k)
            self.plus(k, pl.ds(0, self.sect.chunk), self.rc[k])
            if dy:
                self.send(k, self.a, self.ry, dx * lines + d, {"dy": 1}, self.YA + dx * lines + d)
            if dx:
                self.send(k, self.b, self.rx, dy * lines + d, {"dx": 1}, self.XB + dy * lines + d)

    def second(self, d):
        n = self.lines + d
        self.got(self.ry, n, self.YA + n)
        self.plus(self.at(0, 1, d), self.a, self.ry[n])
        self.send(self.at(0, 1, d), self.a, self.rx2, d, {"dx": 1}, self.XA + d)
        self.got(self.rx, n, self.XB + n)
        self.plus(self.at(1, 0, d), self.b, self.rx[n])
        self.send(self.at(1, 0, d), self.b, self.ry2, d, {"dy": 1}, self.YB + d)

    def third(self, d):
        k = self.at(0, 0, d)
        self.got(self.ry, d, self.YA + d)
        self.got(self.rx, d, self.XB + d)
        self.got(self.rx2, d, self.XA + d)
        self.got(self.ry2, d, self.YB + d)
        self.plus(k, self.a, self.ry[d].astype(f32) + self.rx2[d].astype(f32))
        self.plus(k, self.b, self.rx[d].astype(f32) + self.ry2[d].astype(f32))
        if d:
            self.copies.start(
                lambda: self.work.at[k], lambda: self.rz.at[d], lambda: self.place.coords(z=self.z(d)), self.Z + d
            )

    def settle(self):
        sect, me = self.sect, self.place.me
        total = self.work[self.at(0, 0, 0)].astype(f32)
        for d in range(1, self.lines):
            self.got(self.rz, d, self.Z + d)
            total = total + self.rz[d].astype(f32)
        self.frame[...] = total

        def spread(per):
            tall = sect.chunk // per
            for c in range(per):
                self.flat[pl.ds(c, tall, stride=per), :] = self.frame[c * tall : (c + 1) * tall, :]

        self.flat[...] = total
        sect.by_kind(sect.chunk_at(me), spread)
        self.low[...] = self.flat[...].astype(bf16)
        for s in range(sect.sources):
            self.give(s)

    def give(self, s):
        sect, me = self.sect, self.place.me
        i, ok = sect.of_chunk(sect.chunk_at(me), s)

        @pl.when(ok & (i == me))
        def _():
            self.land[sect.slot_of(sect.chunk_at(me), i)] = self.low[...]

        def owner():
            return jnp.minimum(sect.of_chunk(sect.chunk_at(me), s)[0], sect.count - 1)

        def slot():
            return jnp.clip(sect.slot_of(sect.chunk_at(me), owner()), 0, sect.slots - 1)

        def away():
            i, ok = sect.of_chunk(sect.chunk_at(me), s)
            return ok & (i != me)

        self.copies.start(
            lambda: self.low, lambda: self.land.at[slot()], lambda: self.place.device(owner()), lambda: self.O + slot(), away
        )

    def take(self):
        sect, me = self.sect, self.place.me
        for k in range(sect.slots):
            v, ok = sect.of_owner(me, k)
            self.copies.arrived(lambda: self.land.at[k], self.O + k, lambda: ok & (sect.seat(v) != me))

            @pl.when(ok)
            def _():
                at = self.lead + sect.start(v) - sect.rows * me
                self.out[pl.ds(at, sect.chunk), :] = self.land[k].astype(f32)


def pumped(due):
    row = pl.program_id(0)

    def pump(point):
        for r, p, step in due:
            if p == point:
                pl.when(row == r)(step)

    return pump


def spread_over(steps, rows, points, spots):
    end = rows * points - 1
    return [(min(n, end) // points, min(n, end) % points, step) for step, n in zip(steps, spots)]


def doc_marks(r, length, len_ref, dcol, tm, mb):
    t = iota((length, LANES), 0)
    u = iota((8, length), 1)
    ends = jnp.int32(0)
    d = jnp.zeros((length, LANES), i32)
    e = jnp.zeros((8, length), i32)
    for j in range(SLOTS):
        ends = ends + len_ref[r, j]
        d = d + (t >= ends).astype(i32)
        e = e + (u >= ends).astype(i32)
    dcol[0:8, :] = jnp.full((8, LANES), -1, i32)
    dcol[8 : 8 + length, :] = d
    dcol[8 + length : 16 + length, :] = jnp.full((8, LANES), -1, i32)
    for j in range(KS):
        at = 8 + j - HALF
        tm[j] = (dcol[at : at + length, :] == d).astype(f32)
    for c in range(length // LANES):
        mb[:, c * LANES : (c + 1) * LANES] = jnp.where(d == e[0:1, c * LANES : (c + 1) * LANES], BIG, NEG)


def tap_lanes(tm, length):
    tap = iota((length, LANES), 1) >> 3
    out = jnp.zeros((length, LANES), f32)
    for j in range(KS):
        out = jnp.where(tap == j, tm[j], out)
    return jnp.where(used_taps((length, LANES)), out, 0.0)


def over_taps(x, op):
    for s in (8, 16, 32, 64):
        x = op(x, pltpu.roll(x, s, 1))
    return x


def fill_emat(emat):
    k, c = iota((2 * LANES, ATT), 0) & (LANES - 1), iota((2 * LANES, ATT), 1)
    for j in range(KS):
        emat[:, j * ATT : (j + 1) * ATT] = jnp.where(k == j * 8 + (c >> 6), 1.0, 0.0).astype(bf16)


def two_parts(x):
    high = x.astype(bf16)
    return jnp.concatenate([high, (x - high.astype(f32)).astype(bf16)], axis=1)


def zero_pads(ref, length):
    for c in range(ref.shape[0]):
        ref[c, 0:8, :] = jnp.zeros((8, LANES), f32)
        ref[c, 8 + length : 16 + length, :] = jnp.zeros((8, LANES), f32)


def fwd_kernel(length, pump, len_ref, tok_ref, wp_ref, pw_ref, kw_ref, vec_ref,
               qkvc_ref, kc_ref, dep_ref, ca_ref, tap_ref, join_ref, lse_ref,
               xs, cs, dcol, tm, mb, emat, acc):
    row = pl.program_id(0)
    pump(0)
    pl.when(row > 0)(lambda: doc_marks(row, length, len_ref, dcol, tm, mb))
    pump(1)
    tok = tok_ref[...]
    zero_pads(xs, length)
    zero_pads(cs, length)
    for c in range(6):
        xs[c, 8 : 8 + length, :] = tok[:, c * LANES : (c + 1) * LANES].astype(f32)
    for m, bias in ((0, QB), (1, None), (2, VB), (3, CB)):
        x = nn(tok, wp_ref[:, m * ATT : (m + 1) * ATT])
        if bias is not None:
            x = x + vec_ref[bias : bias + 1, 0:ATT]
        x = x.astype(bf16)
        qkvc_ref[:, m * ATT : (m + 1) * ATT] = x
        if m == 3:
            for c in range(3):
                cs[c, 8 : 8 + length, :] = x[:, c * LANES : (c + 1) * LANES].astype(f32)

    pump(2)
    step = 64

    for c in range(6):
        w = [vec_ref[DW + j : DW + j + 1, c * LANES : (c + 1) * LANES] for j in range(KS)]
        for r in range(0, length, step):
            total = w[HALF] * xs[c, 8 + r : 8 + r + step, :]
            for j in range(KS):
                if j != HALF:
                    at = 8 + r + j - HALF
                    total = total + w[j] * (xs[c, at : at + step, :] * tm[j, r : r + step, :])
            dep_ref[r : r + step, c * LANES : (c + 1) * LANES] = total.astype(bf16)

    pump(3)
    keyconv = nn(dep_ref[...], pw_ref[...]) + vec_ref[PB : PB + 1, 0:ATT]
    kc_ref[...] = keyconv.astype(bf16)
    ca = (keyconv * qkvc_ref[:, 0:ATT].astype(f32)).astype(bf16)
    ca_ref[...] = ca
    logits = nn(ca, kw_ref[...]) + vec_ref[KBR : KBR + 1, 0:LANES]
    e = jnp.exp(logits - over_taps(logits, jnp.maximum))
    taps = e / over_taps(e, jnp.add)
    tap_ref[...] = taps
    spread = two_parts(taps * tap_lanes(tm, length))
    for j in range(KS):
        if j % 3 == 0:
            pump(4 + j // 3)
        t = nn(spread, emat[:, j * ATT : (j + 1) * ATT])
        for c in range(3):
            at = 8 + j - HALF
            part = t[:, c * LANES : (c + 1) * LANES] * cs[c, at : at + length, :]
            if j:
                part = part + acc[:, c * LANES : (c + 1) * LANES]
            if j < KS - 1:
                acc[:, c * LANES : (c + 1) * LANES] = part
            else:
                join_ref[:, ATT + c * LANES : ATT + (c + 1) * LANES] = part.astype(bf16)

    for p in range(3):
        pump(7 + p)
        cols = slice(p * LANES, (p + 1) * LANES)
        q, k, v = (qkvc_ref[:, m * ATT + p * LANES : m * ATT + (p + 1) * LANES] for m in range(3))
        qs = q.astype(f32) * SCALE
        vt = v.astype(f32).T
        lane, sub = iota((length, LANES), 1), iota((LANES, length), 0)
        halves = []
        for h in range(2):
            qh = jnp.where((lane >= HEAD_DIM) == bool(h), qs, 0.0).astype(bf16)
            vh = jnp.where((sub >= HEAD_DIM) == bool(h), vt, 1.0).astype(bf16)
            z = jnp.minimum(nt(k, qh), mb[...])
            top = jnp.max(z, axis=0, keepdims=True)
            o = nn(vh, jnp.exp(z - top).astype(bf16))
            s = o[(1 - h) * HEAD_DIM : (1 - h) * HEAD_DIM + 1, :]
            lse_ref[0, 2 * p + h : 2 * p + h + 1, :] = top + jnp.log(s)
            halves.append(o[h * HEAD_DIM : (h + 1) * HEAD_DIM, :] / s)
        join_ref[:, cols] = jnp.concatenate(halves, axis=0).T.astype(bf16)
    pump(10)


def blocked(rows, cols):
    return pl.BlockSpec((rows, cols), lambda r: (r, 0))


def row_scratch(length):
    return [
        VM((6, length + 16, LANES), f32),
        VM((3, length + 16, LANES), f32),
        VM((length + 16, LANES), i32),
        VM((KS, length, LANES), f32),
        VM((length, length), f32),
        VM((2 * LANES, KS * ATT), bf16),
    ]


FWD_POINTS = 11
FWD_SPOTS = (4, 5, 10, 11, 16, 17, 22, 27, 99)


def run_front(first, second, own, tokens, lengths):
    outer, inner = lax.axis_size("dp"), lax.axis_size("fsdp")
    rows, count = lengths.shape[0], tokens.shape[0]
    length = count // rows
    scratch = row_scratch(length) + [VM((length, ATT), f32)]
    n = len(scratch)
    lead = max(first.chunk, second.chunk)
    more = [
        VM((first.rows + 2 * lead + 16, LANES), f32),
        VM((first.small * first.chunk, LANES), f32),
        VM((512, LANES), f32),
    ]
    m = len(Gather.scratch(first, inner))

    def body(own_ref, len_ref, tok_ref, *refs):
        outs, (dw_ref, fi_ref, fo_ref, wp_ref, pw_ref, kw_ref, vec_ref), refs = refs[:7], refs[7:14], refs[14:]
        rows_refs, (ownf, flat, kwt), refs = refs[:n], refs[n : n + 3], refs[n + 3 :]
        place = Place(outer, inner)
        a = Gather(first, place, ownf, lead, refs[:m])
        b = Gather(second, place, ownf, lead, refs[m:])

        def begin():
            ownf[...] = jnp.zeros_like(ownf)
            ownf[lead : lead + first.rows, :] = own_ref[...].astype(f32)
            place.greet_all()
            a.offer()
            b.offer()
            _, _, dcol, tm, mb, emat, _ = rows_refs
            fill_emat(emat)
            doc_marks(0, length, len_ref, dcol, tm, mb)
            a.form()
            for s in range(1, place.lines):
                a.along(s)
                a.across(s - 1)
            a.across(place.lines - 1)
            b.form()
            a.diagonal()
            a.rest()
            from_frames(first, a.buf, [(wp_ref, D, ATT, k * ATT) for k in range(4)] + [(pw_ref, D, ATT, 0)], flat)
            unpack_small(flat, kw_ref, vec_ref, kwt)

        def end():
            b.rest()
            from_frames(second, b.buf, ((dw_ref, D, D, 0), (fi_ref, D, FF // GROUPS, 0), (fo_ref, FF, D // GROUPS, 0)))

        steps = []
        for s in range(1, place.lines):
            steps.append(lambda s=s: b.along(s))
            steps.append(lambda s=s: b.across(s - 1))
        steps += [lambda: b.across(place.lines - 1), b.diagonal, end]
        spots = FWD_SPOTS if len(steps) == len(FWD_SPOTS) else [99] * len(steps)
        pump = pumped([(0, 0, begin)] + spread_over(steps, rows, FWD_POINTS, spots))
        fwd_kernel(length, pump, len_ref, tok_ref, wp_ref, pw_ref, kw_ref, vec_ref, *outs, *rows_refs)

    full = pl.BlockSpec(memory_space=VM)
    return pl.pallas_call(
        body,
        grid=(rows,),
        out_shape=[
            jax.ShapeDtypeStruct((count, 4 * ATT), bf16),
            jax.ShapeDtypeStruct((count, ATT), bf16),
            jax.ShapeDtypeStruct((count, D), bf16),
            jax.ShapeDtypeStruct((count, ATT), bf16),
            jax.ShapeDtypeStruct((count, LANES), f32),
            jax.ShapeDtypeStruct((count, D), bf16),
            jax.ShapeDtypeStruct((rows, 8, length), f32),
            jax.ShapeDtypeStruct((D, D), bf16),
            jax.ShapeDtypeStruct((D, FF // GROUPS), bf16),
            jax.ShapeDtypeStruct((FF, D // GROUPS), bf16),
            jax.ShapeDtypeStruct((D, 4 * ATT), bf16),
            jax.ShapeDtypeStruct((D, ATT), bf16),
            jax.ShapeDtypeStruct((ATT, LANES), bf16),
            jax.ShapeDtypeStruct((VROWS, FF), f32),
        ],
        in_specs=[full, pl.BlockSpec(memory_space=pltpu.SMEM), blocked(length, D)],
        out_specs=[
            blocked(length, 4 * ATT),
            blocked(length, ATT),
            blocked(length, D),
            blocked(length, ATT),
            blocked(length, LANES),
            blocked(length, D),
            pl.BlockSpec((1, 8, length), lambda r: (r, 0, 0)),
        ]
        + [full] * 7,
        scratch_shapes=scratch + more + Gather.scratch(first, inner) + Gather.scratch(second, inner),
        compiler_params=pltpu.CompilerParams(vmem_limit_bytes=VMEM_LIMIT, collective_id=0, has_side_effects=True),
        name="front",
    )(own, lengths, tokens)


def mid_kernel(sect, length, len_ref, tok_ref, join_ref, cot_ref, dw_ref, fi_ref, fo_ref, vec_ref,
               out_ref, gf_ref, gj_ref, part_ref, gv_ref,
               gdw_ref, gfi_ref, gfo_ref, xh1, rs1, nl, act, slope, gsec, gsl, wide):
    row = pl.program_id(0)
    fg, dg = FF // GROUPS, D // GROUPS

    @pl.when(row == 0)
    def _():
        for ref in (gdw_ref, gfi_ref, gfo_ref, gv_ref):
            ref[...] = jnp.zeros_like(ref)

    used = jnp.int32(0)
    for j in range(SLOTS):
        used = used + len_ref[row, j]

    def vec(r, n=D):
        return vec_ref[r : r + 1, 0:n]

    step = 128
    gsec[...] = nn(join_ref[...], dw_ref[...])

    def norm1(i):
        at = pl.ds(pl.multiple_of(i * step, step), step)
        z = gsec[at, :] + vec(DB) + tok_ref[at, :].astype(f32)
        z = z - jnp.mean(z, axis=1, keepdims=True)
        r = lax.rsqrt(jnp.mean(z * z, axis=1, keepdims=True) + EPS)
        x = z * r
        xh1[at, :] = x
        rs1[at, :] = jnp.broadcast_to(r, (step, LANES))
        nl[at, :] = (x * vec(N1G) + vec(N1S)).astype(bf16)

    loop(length // step, norm1)

    tile = 512
    per = fg // tile

    tiles = [(g, i) for g in range(GROUPS) for i in range(per)]

    def inner(n):
        g, i = tiles[n]
        wide[n % 2] = nn(nl[:, g * dg : (g + 1) * dg], fi_ref[g * dg : (g + 1) * dg, i * tile : (i + 1) * tile])

    inner(0)
    for n, (g, i) in enumerate(tiles):
        if n + 1 < len(tiles):
            inner(n + 1)
        col = slice(g * fg + i * tile, g * fg + (i + 1) * tile)
        for r in range(0, length, 64):
            x = wide[n % 2, r : r + 64, :] + vec_ref[FIB : FIB + 1, col]
            phi = 0.5 * lax.erf(x * math.sqrt(0.5)) + 0.5
            e = jnp.exp2(x * x * (-0.5 / math.log(2.0)))
            act[r : r + 64, col] = (x * phi).astype(bf16)
            slope[r : r + 64, col] = (phi + x * (1.0 / math.sqrt(2.0 * math.pi)) * e).astype(bf16)

    for g in range(GROUPS):
        gsec[:, g * dg : (g + 1) * dg] = nn(act[:, g * fg : (g + 1) * fg], fo_ref[g * fg : (g + 1) * fg, :])

    def rows8(x):
        total = x[0:8]
        for k in range(8, x.shape[0], 8):
            total = total + x[k : k + 8]
        return total

    def norm2(i, carry):
        at = pl.ds(pl.multiple_of(i * step, step), step)
        norm = xh1[at, :] * vec(N1G) + vec(N1S)
        z = gsec[at, :] + vec(FOB) + norm
        z = z - jnp.mean(z, axis=1, keepdims=True)
        r = lax.rsqrt(jnp.mean(z * z, axis=1, keepdims=True) + EPS)
        x = z * r
        keep = ((iota((step, 1), 0) + i * step) < used).astype(f32)
        out_ref[at, :] = ((x * vec(N2G) + vec(N2S)) * keep).astype(bf16)
        gf = cot_ref[at, :].astype(f32) * keep
        gx = gf * x
        e = gf * vec(N2G)
        gz = r * (e - jnp.mean(e, axis=1, keepdims=True) - x * jnp.mean(e * x, axis=1, keepdims=True))
        gsec[at, :] = gz
        gsl[at, :] = gz.astype(bf16)
        return (carry[0] + rows8(gx), carry[1] + rows8(gf), carry[2] + rows8(gz))

    none = jnp.zeros((8, D), f32)
    sums = lax.fori_loop(0, length // step, norm2, (none, none, none))

    def add(r, value):
        gv_ref[r : r + 1, 0 : value.shape[1]] += jnp.sum(value, axis=0, keepdims=True)

    for r, value in zip((N2G, N2S, FOB), sums):
        add(r, value)

    for g in range(GROUPS):
        def narrow(i, g=g):
            r0 = pl.ds(pl.multiple_of(g * fg + i * tile, tile), tile)
            x = nt(gsl[:, g * dg : (g + 1) * dg], fo_ref[r0, :]) * slope[:, r0].astype(f32)
            gv_ref[FIB : FIB + 1, r0] += jnp.sum(x, axis=0, keepdims=True)
            slope[:, r0] = x.astype(bf16)
            gfo_ref[r0, :] += tn(act[:, r0], gsl[:, g * dg : (g + 1) * dg])
            col = pl.ds(pl.multiple_of(i * tile, tile), tile)
            gfi_ref[g * dg : (g + 1) * dg, col] += tn(nl[:, g * dg : (g + 1) * dg], slope[:, r0])

        loop(per, narrow)
    for g in range(GROUPS):
        gsec[:, g * dg : (g + 1) * dg] += nt(slope[:, g * fg : (g + 1) * fg], fi_ref[g * dg : (g + 1) * dg, :])

    def norm1_back(i, carry):
        at = pl.ds(pl.multiple_of(i * step, step), step)
        gn = gsec[at, :]
        x = xh1[at, :]
        e = gn * vec(N1G)
        r = rs1[at, :]
        r = jnp.concatenate([r] * (D // LANES), axis=1)
        gz = r * (e - jnp.mean(e, axis=1, keepdims=True) - x * jnp.mean(e * x, axis=1, keepdims=True))
        gf_ref[at, :] = gz.astype(bf16)
        return (carry[0] + rows8(gn * x), carry[1] + rows8(gn), carry[2] + rows8(gz))

    sums = lax.fori_loop(0, length // step, norm1_back, (none, none, none))
    for r, value in zip((N1G, N1S, DB), sums):
        add(r, value)
    low = gf_ref[...]
    gj_ref[...] = nt(low, dw_ref[...]).astype(bf16)
    gdw_ref[...] += tn(join_ref[...], low)

    @pl.when(row == pl.num_programs(0) - 1)
    def _():
        to_frames(sect, part_ref, ((gdw_ref, D, D, 0), (gfi_ref, D, FF // GROUPS, 0), (gfo_ref, FF, D // GROUPS, 0)))


def run_mid(sect, tokens, lengths, joined, cotangent, dw, fi, fo, vec):
    rows, count = lengths.shape[0], tokens.shape[0]
    length = count // rows

    def body(*refs):
        mid_kernel(sect, length, *refs)

    full = pl.BlockSpec(memory_space=VM)
    return pl.pallas_call(
        body,
        grid=(rows,),
        out_shape=[
            jax.ShapeDtypeStruct((count, D), bf16),
            jax.ShapeDtypeStruct((count, D), bf16),
            jax.ShapeDtypeStruct((count, D), bf16),
            jax.ShapeDtypeStruct((sect.count, sect.chunk, LANES), bf16),
            jax.ShapeDtypeStruct((VROWS, FF), f32),
        ],
        in_specs=[pl.BlockSpec(memory_space=pltpu.SMEM)] + [blocked(length, D)] * 3 + [full] * 4,
        out_specs=[blocked(length, D)] * 3 + [full] * 2,
        scratch_shapes=[
            VM((D, D), f32),
            VM((D, FF // GROUPS), f32),
            VM((FF, D // GROUPS), f32),
            VM((length, D), f32),
            VM((length, LANES), f32),
            VM((length, D), bf16),
            VM((length, FF), bf16),
            VM((length, FF), bf16),
            VM((length, D), f32),
            VM((length, D), bf16),
            VM((2, length, 512), f32),
        ],
        compiler_params=pltpu.CompilerParams(vmem_limit_bytes=VMEM_LIMIT),
        name="mid",
    )(lengths, tokens, joined, cotangent, dw, fi, fo, vec)


def bwd_kernel(length, pump, len_ref, tok_ref, qkvc_ref, kc_ref, dep_ref, ca_ref, tap_ref, join_ref, lse_ref, gf_ref, gj_ref,
               wp_ref, pw_ref, kw_ref, vec_ref,
               gt_ref, gp_ref, gpw_ref, gkw_ref, gv_ref,
               ds, cs, dcol, tm, mb, emat, gs, tp, prod, gq, gfour, acc):
    row = pl.program_id(0)

    @pl.when(row == 0)
    def _():
        fill_emat(emat)
        for ref in (gp_ref, gpw_ref, gkw_ref, gv_ref):
            ref[...] = jnp.zeros_like(ref)

    doc_marks(row, length, len_ref, dcol, tm, mb)
    pump(0)
    for ref in (ds, cs, gs, tp):
        zero_pads(ref, length)

    def add(r, value):
        gv_ref[r : r + 1, 0 : value.shape[1]] += jnp.sum(value, axis=0, keepdims=True)

    for p in range(3):
        pump(1 + p)
        cols = slice(p * LANES, (p + 1) * LANES)
        q, k, v = (qkvc_ref[:, m * ATT + p * LANES : m * ATT + (p + 1) * LANES] for m in range(3))
        g = gj_ref[:, cols]
        lane, sub = iota((length, LANES), 1), iota((16, LANES), 1)
        which = iota((16, LANES), 0)
        marks = jnp.where((sub >= HEAD_DIM) == (which >= 8), 1.0, 0.0).astype(bf16)
        dots = g.astype(f32) * join_ref[:, cols].astype(f32)
        high = dots.astype(bf16)
        dots = nt(marks, high) + nt(marks, (dots - high.astype(f32)).astype(bf16))
        qs = q.astype(f32) * SCALE
        kt = k.astype(f32).T.astype(bf16)
        gk, gv, gqt = None, None, []
        for h in range(2):
            own = (lane >= HEAD_DIM) == bool(h)
            qh = jnp.where(own, qs, 0.0).astype(bf16)
            gh = jnp.where(own, g.astype(f32), 0.0).astype(bf16)
            prob = jnp.exp(jnp.minimum(nt(k, qh), mb[...]) - lse_ref[0, 2 * p + h : 2 * p + h + 1, :])
            dsc = (prob * (nt(v, gh) - dots[8 * h : 8 * h + 1, :])).astype(bf16)
            a, b = nn(prob.astype(bf16), gh), nn(dsc, qh)
            gv, gk = (a, b) if h == 0 else (gv + a, gk + b)
            gqt.append(nn(kt, dsc)[h * HEAD_DIM : (h + 1) * HEAD_DIM, :])
        gq[:, cols] = jnp.concatenate(gqt, axis=0).T * SCALE
        gfour[:, ATT + p * LANES : ATT + (p + 1) * LANES] = gk.astype(bf16)
        gfour[:, 2 * ATT + p * LANES : 2 * ATT + (p + 1) * LANES] = gv.astype(bf16)
        gv_ref[VB : VB + 1, cols] += jnp.sum(gv, axis=0, keepdims=True)

    pump(4)
    for c in range(3):
        cs[c, 8 : 8 + length, :] = qkvc_ref[:, 3 * ATT + c * LANES : 3 * ATT + (c + 1) * LANES].astype(f32)
        gs[c, 8 : 8 + length, :] = gj_ref[:, ATT + c * LANES : ATT + (c + 1) * LANES].astype(f32)
    gtaps = None
    for j in range(0, KS, 3):
        for k in range(3):
            for c in range(3):
                at, spot = 8 + j + k - HALF, ((j + k) * 3 + c) * length
                prod[spot : spot + length, :] = (gs[c, 8 : 8 + length, :] * cs[c, at : at + length, :]).astype(bf16)
        blocks = [prod[n * length : (n + 1) * length, :] for n in range(j * 3, j * 3 + 9)]
        x = nt(jnp.concatenate(blocks, axis=1), emat[0:LANES, j * ATT : (j + 3) * ATT])
        gtaps = x if gtaps is None else gtaps + x
    marks = tap_lanes(tm, length)
    gtaps = gtaps * marks
    pump(5)
    taps = jnp.where(used_taps((length, LANES)), tap_ref[...], 0.0)
    glog = taps * (gtaps - over_taps(taps * gtaps, jnp.add))
    add(KBR, glog)
    glog = glog.astype(bf16)
    gkw_ref[...] += tn(ca_ref[...], glog)
    gca = nt(glog, kw_ref[...])

    tp[0, 8 : 8 + length, :] = taps * marks
    tap = iota((length, LANES), 1) >> 3
    moved = jnp.zeros((length, LANES), f32)
    for j in range(KS):
        at = 8 + HALF - j
        moved = jnp.where(tap == j, tp[0, at : at + length, :], moved)
    spread = two_parts(moved)
    for j in range(KS):
        t = nn(spread, emat[:, j * ATT : (j + 1) * ATT])
        for c in range(3):
            at = 8 + HALF - j
            part = t[:, c * LANES : (c + 1) * LANES] * gs[c, at : at + length, :]
            if j:
                part = part + acc[:, c * LANES : (c + 1) * LANES]
            if j < KS - 1:
                acc[:, c * LANES : (c + 1) * LANES] = part
            else:
                gfour[:, 3 * ATT + c * LANES : 3 * ATT + (c + 1) * LANES] = part.astype(bf16)
                gv_ref[CB : CB + 1, c * LANES : (c + 1) * LANES] += jnp.sum(part, axis=0, keepdims=True)

    pump(6)
    gkc = gca * qkvc_ref[:, 0:ATT].astype(f32)
    gquery = gq[...] + gca * kc_ref[...].astype(f32)
    add(QB, gquery)
    gfour[:, 0:ATT] = gquery.astype(bf16)
    add(PB, gkc)
    gkc = gkc.astype(bf16)
    gpw_ref[...] += tn(dep_ref[...], gkc)
    for c in range(3):
        x = nt(gkc, pw_ref[c * 256 : (c + 1) * 256, :])
        ds[2 * c, 8 : 8 + length, :] = x[:, 0:LANES]
        ds[2 * c + 1, 8 : 8 + length, :] = x[:, LANES:]
    pump(7)
    for m in range(4):
        gp_ref[:, m * ATT : (m + 1) * ATT] += tn(tok_ref[...], gfour[:, m * ATT : (m + 1) * ATT])

    pump(8)
    step = 64
    for c in range(6):
        cols = slice(c * LANES, (c + 1) * LANES)
        w = [vec_ref[DW + j : DW + j + 1, cols] for j in range(KS)]
        sums = [None] * KS
        if c % 2 == 0:
            direct = nt(gfour[...], wp_ref[c * LANES : (c + 2) * LANES, :])
        for r in range(0, length, step):
            tok = tok_ref[r : r + step, cols].astype(f32)
            total = gf_ref[r : r + step, cols].astype(f32) + direct[r : r + step, (c % 2) * LANES : (c % 2 + 1) * LANES]
            for j in range(KS):
                at = 8 + r + j - HALF
                u = ds[c, at : at + step, :]
                if j != HALF:
                    u = u * tm[j, r : r + step, :]
                total = total + w[KS - 1 - j] * u
                u = tok * u
                part = u[0:8]
                for s in range(8, step, 8):
                    part = part + u[s : s + 8]
                sums[j] = part if r == 0 else sums[j] + part
            gt_ref[r : r + step, cols] = total.astype(bf16)
        for j in range(KS):
            gv_ref[DW + KS - 1 - j : DW + KS - j, cols] += jnp.sum(sums[j], axis=0, keepdims=True)
    pump(9)


BWD_POINTS = 10
FIRST_AT, SECOND_AT, THIRD_AT = (2, 3, 6, 10), (5, 9, 13, 15), (9, 13, 16, 17)
SETTLE_AT, TAKE_AT = 21, 26


def run_back(first, second, part, va, tokens, lengths, saved, gf, gj, wp, pw, kw, vec):
    outer, inner = lax.axis_size("dp"), lax.axis_size("fsdp")
    qkvc, kc, dep, ca, taps, joined, lse = saved
    rows, count = lengths.shape[0], tokens.shape[0]
    length = count // rows
    lead = max(first.chunk, second.chunk)
    tall = -(-max(3 * KS * length, first.count * first.chunk) // 16) * 16
    scratch = row_scratch(length) + [
        VM((3, length + 16, LANES), f32),
        VM((1, length + 16, LANES), f32),
        VM((tall, LANES), bf16),
        VM((length, ATT), f32),
        VM((length, 4 * ATT), bf16),
        VM((length, ATT), f32),
    ]
    grads = [VM((D, 4 * ATT), f32), VM((D, ATT), f32), VM((ATT, LANES), f32), VM((VROWS, FF), f32)]
    more = [
        VM((first.rows + 2 * lead + 16, LANES), f32),
        VM((max(first.small * first.chunk, 384), LANES), f32),
        VM((512, LANES), f32),
    ]
    n, m = len(scratch), len(Scatter.scratch(first, inner))

    def body(part_ref, va_ref, *refs):
        ours, (gt_ref, own_ref), refs = refs[:15], refs[15:17], refs[17:]
        rows_refs, sums, refs = refs[:n], refs[n : n + 4], refs[n + 4 :]
        (out, flat, kwt), refs = refs[:3], refs[3:]
        gp_ref, gpw_ref, gkw_ref, gv_ref = sums
        stage = rows_refs[8]
        place = Place(outer, inner)
        a = Scatter(first, place, lambda v: stage.at[pl.ds(v * first.chunk, first.chunk)], out, lead, refs[:m])
        b = Scatter(second, place, lambda v: part_ref.at[v], out, lead, refs[m:])

        def begin():
            out[...] = jnp.zeros_like(out)
            place.greet_all()
            b.core()

        def end():
            gv_ref[...] += va_ref[...]
            pack_small(flat, gkw_ref, gv_ref, kwt)
            to_frames(
                first,
                Rows(stage, first.chunk),
                [(gp_ref, D, ATT, k * ATT) for k in range(4)] + [(gpw_ref, D, ATT, 0)],
                flat,
            )
            a.core()
            for step in a.sums():
                step()
            a.settle()
            a.take()
            a.copies.finish()
            b.copies.finish()
            own_ref[...] = out[lead : lead + first.rows, :]

        due = [(0, 0, begin)]
        for step, spots in ((b.first, FIRST_AT), (b.second, SECOND_AT), (b.third, THIRD_AT)):
            steps = [lambda step=step, d=d: step(d) for d in b.far]
            due += spread_over(steps, rows, BWD_POINTS, list(spots) + [spots[-1]] * (len(steps) - len(spots)))
        due += spread_over([b.settle, b.take], rows, BWD_POINTS, (SETTLE_AT, TAKE_AT))
        pump = pumped(due + [(rows - 1, BWD_POINTS - 1, end)])
        bwd_kernel(length, pump, *ours, gt_ref, *sums, *rows_refs)

    full = pl.BlockSpec(memory_space=VM)
    return pl.pallas_call(
        body,
        grid=(rows,),
        out_shape=[jax.ShapeDtypeStruct((count, D), bf16), jax.ShapeDtypeStruct((first.rows, LANES), f32)],
        in_specs=[
            pl.BlockSpec(memory_space=pl.ANY),
            full,
            pl.BlockSpec(memory_space=pltpu.SMEM),
            blocked(length, D),
            blocked(length, 4 * ATT),
            blocked(length, ATT),
            blocked(length, D),
            blocked(length, ATT),
            blocked(length, LANES),
            blocked(length, D),
            pl.BlockSpec((1, 8, length), lambda r: (r, 0, 0)),
            blocked(length, D),
            blocked(length, D),
            full,
            full,
            full,
            full,
        ],
        out_specs=[blocked(length, D), full],
        scratch_shapes=scratch + grads + more + Scatter.scratch(first, inner) + Scatter.scratch(second, inner),
        compiler_params=pltpu.CompilerParams(vmem_limit_bytes=VMEM_LIMIT, collective_id=1, has_side_effects=True),
        name="back",
    )(part, va, lengths, tokens, qkvc, kc, dep, ca, taps, joined, lse, gf, gj, wp, pw, kw, vec)


def shards(tokens, doc_lengths, params, cotangent):
    rows = params.shape[0] // LANES
    outer, inner = lax.axis_size("dp"), lax.axis_size("fsdp")
    first, second = sections(outer * inner, rows, inner)
    *saved, dw, fi, fo, wp, pw, kw, vec = run_front(first, second, params.reshape(rows, LANES), tokens, doc_lengths)
    output, gf, gj, part, va = run_mid(second, tokens, doc_lengths, saved[5], cotangent, dw, fi, fo, vec)
    gt, own_grad = run_back(first, second, part, va, tokens, doc_lengths, saved, gf, gj, wp, pw, kw, vec)
    return output, gt, own_grad.reshape(rows * LANES)


def solution(mesh):
    axes = ("dp", "fsdp")
    placed = (P(axes, None), P(axes, None), P(axes), P(axes, None))
    return jax.shard_map(
        shards,
        mesh=mesh,
        in_specs=placed,
        out_specs=(P(axes, None), P(axes, None), P(axes)),
        check_vma=False,
    )
```

```python
import math

import jax
import jax.numpy as jnp
from jax import lax
from jax.experimental import pallas as pl
from jax.experimental.pallas import tpu as pltpu
from jax.sharding import PartitionSpec as P

D = 768
HEADS = 6
HEAD_DIM = 64
ATT = HEADS * HEAD_DIM
FF = 3072
GROUPS = 2
KS = 9
HALF = KS // 2
SLOTS = 16
EPS = 1e-12
LANES = 128
NEG = -1e30
BIG = 3e38
SCALE = HEAD_DIM ** (-0.5)

f32 = jnp.float32
bf16 = jnp.bfloat16
i32 = jnp.int32

FIRST = 5 * D * ATT // LANES
MATRICES = FIRST + (D * D + 2 * D * FF // GROUPS) // LANES
DEPTH_AT = 0
KERNEL_AT = KS * D // LANES
BIAS_AT = KERNEL_AT + ATT * HEADS * KS // LANES
TAIL_AT = BIAS_AT + 4 * ATT // LANES
SMALL = TAIL_AT + 61
KB = HEADS * KS

QB, VB, CB, PB, KBR, DB, N1G, N1S, FIB, FOB, N2G, N2S, DW = range(13)
VROWS = 24
TAIL = [(DB, 6), (N1G, 6), (N1S, 6), (FIB, 24), (FOB, 6), (N2G, 6), (N2S, 6)]

VM = pltpu.VMEM
VMEM_LIMIT = 62 * 1024 * 1024


def nn(a, b):
    return lax.dot_general(a, b, (((1,), (0,)), ((), ())), preferred_element_type=f32)


def nt(a, b):
    return lax.dot_general(a, b, (((1,), (1,)), ((), ())), preferred_element_type=f32)


def tn(a, b):
    return lax.dot_general(a, b, (((0,), (0,)), ((), ())), preferred_element_type=f32)


def iota(shape, axis):
    return lax.broadcasted_iota(i32, shape, axis)


def loop(count, body, unroll=1):
    def step(i, carry):
        body(i)
        return carry

    lax.fori_loop(0, count, step, 0, unroll=unroll)


def tap_perm():
    k, n = iota((LANES, LANES), 0), iota((LANES, LANES), 1)
    head, tap = n & 7, n >> 3
    return jnp.where((k == head * KS + tap) & (head < HEADS) & (tap < KS), 1.0, 0.0).astype(bf16)


def used_taps(shape):
    n = iota(shape, len(shape) - 1)
    return ((n & 7) < HEADS) & ((n >> 3) < KS)


def padded(rows):
    return -(-rows // 16) * 16


class Section:
    def __init__(self, base, kinds, chunk, small, rows, count, inner):
        self.base, self.chunk, self.rows, self.count, self.inner = base, chunk, rows, count, inner
        self.main = sum(n for n, _ in kinds)
        self.small = -(-SMALL // chunk) if small else 0
        self.kinds = kinds + ([(self.small, 1)] if small else [])
        self.used = self.main + self.small
        self.pieces = -(-rows // chunk) + 1
        self.slots = self.pieces + self.small
        self.sources = (chunk - 2) // rows + 2
        self.lead = -(-base // rows)

    def seat(self, v, pick=jnp.where):
        q, r, n = v // 3, v % 3, self.count
        if self.small:
            near = pick(q < n // 4, r * (n // 4) + q, 3 * (n // 4) + v - 3 * (n // 4))
            return pick(v < self.main, near, n - self.small + v - self.main)
        return pick(r < 2, self.lead + 2 * q + r, q)

    def chunk_at(self, d):
        n = self.count
        if self.small:
            quarter = n // 4
            v = jnp.where(d < 3 * quarter, 3 * lax.rem(d, quarter) + d // quarter, d)
            v = jnp.where(v < self.main, v, self.used)
            return jnp.where(d >= n - self.small, self.main + d - (n - self.small), v)
        t = d - self.lead
        v = jnp.where(d < self.main // 3, 3 * d + 2, self.used)
        return jnp.where((t >= 0) & (t < 2 * self.main // 3), 3 * (t // 2) + lax.rem(t, 2), v)

    def start(self, v):
        at = self.base + v * self.chunk
        if self.small:
            at = jnp.where(v >= self.main, MATRICES + (v - self.main) * self.chunk, at)
        return at

    def first_piece(self, i):
        return jnp.maximum(self.rows * i - self.base, 0) // self.chunk

    def of_owner(self, i, k):
        if k < self.pieces:
            v = self.first_piece(i) + k
            ok = v < self.main
        else:
            v = self.main + k - self.pieces + 0 * i
            ok = v >= 0
        at = self.start(v)
        return v, ok & (at < self.rows * (i + 1)) & (at + self.chunk > self.rows * i)

    def of_chunk(self, v, s):
        i = self.start(v) // self.rows + s
        return i, (v < self.used) & (i < self.count) & (self.rows * i < self.start(v) + self.chunk)

    def source_of(self, v, i):
        return i - self.start(v) // self.rows

    def slot_of(self, v, i):
        return jnp.where(v < self.main, v - self.first_piece(i), self.pieces + v - self.main)

    def by_kind(self, v, action):
        at, seen = 0, {}
        for n, per in self.kinds:
            seen.setdefault(per, []).append((at, at + n))
            at += n
        for per, spans in seen.items():
            ok = False
            for lo, hi in spans:
                ok = ((v >= lo) & (v < hi)) | ok
            pl.when(ok)(lambda per=per: action(per))


def sections(count, rows, inner):
    big, little = 24576 // count, 12288 // count
    first = Section(0, [(FIRST // little, 3)], little, True, rows, count, inner)
    kinds = [(D * n // LANES // big, n // LANES) for n in (D, FF // GROUPS)] + [(FF * 3 // big, 3)]
    return first, Section(FIRST, kinds, big, False, rows, count, inner)


class Rows:
    def __init__(self, ref, chunk):
        self.ref, self.chunk = ref, chunk

    def __setitem__(self, where, value):
        v, rows, _ = where
        self.ref[v * self.chunk + rows.start : v * self.chunk + rows.stop, :] = value


def choose(ok, a, b):
    return a if ok else b


def pieces_of(sect, matrices):
    v = 0
    for ref, height, width, col in matrices:
        per = width // LANES
        tall = sect.chunk // per
        for r in range(0, height, tall):
            for c in range(per):
                cols = slice(col + c * LANES, col + (c + 1) * LANES)
                yield sect.seat(v, choose), slice(c * tall, (c + 1) * tall), ref, slice(r, r + tall), cols
            v += 1


def to_frames(sect, part, matrices, small=None):
    for seat, rows, ref, r, c in pieces_of(sect, matrices):
        part[seat, rows, :] = ref[r, c].astype(bf16)
    for k in range(sect.small):
        part[sect.seat(sect.main + k, choose), slice(0, sect.chunk), :] = small[
            k * sect.chunk : (k + 1) * sect.chunk, :
        ].astype(bf16)
    for d in set(range(sect.count)) - {sect.seat(v, choose) for v in range(sect.used)}:
        part[d, slice(0, sect.chunk), :] = jnp.zeros((sect.chunk, LANES), bf16)


def from_frames(sect, buf, matrices, small=None):
    for seat, rows, ref, r, c in pieces_of(sect, matrices):
        ref[r, c] = buf[seat, rows, :]
    for k in range(sect.small):
        small[k * sect.chunk : (k + 1) * sect.chunk, :] = buf[sect.seat(sect.main + k, choose)].astype(f32)


def unpack_small(flat, kw_ref, vec_ref, kwt):
    vec_ref[...] = jnp.zeros_like(vec_ref)
    for row in range(4):
        for c in range(3):
            at = BIAS_AT + row * 3 + c
            vec_ref[row : row + 1, c * LANES : (c + 1) * LANES] = flat[at : at + 1, :]
    for j in range(KS):
        for c in range(6):
            at = DEPTH_AT + j * 6 + c
            vec_ref[DW + j : DW + j + 1, c * LANES : (c + 1) * LANES] = flat[at : at + 1, :]
    at = TAIL_AT
    lane = iota((64, LANES), 1)
    first = pltpu.roll(flat[at : at + 64, :], LANES - KB, 1)
    second = pltpu.roll(flat[at + 1 : at + 65, :], LANES - KB, 1)
    kwt[0:64, :] = jnp.where(lane < LANES - KB, first, second)
    at = 0
    for row, many in TAIL:
        for c in range(many):
            vec_ref[row : row + 1, c * LANES : (c + 1) * LANES] = kwt[at + c : at + c + 1, :]
        at += many
    perm = tap_perm()
    lane8 = iota((16, LANES), 1)
    kb = jnp.broadcast_to(flat[TAIL_AT : TAIL_AT + 1, :], (16, LANES))
    kb = nn(jnp.where(lane8 < KB, kb, 0.0).astype(bf16), perm)
    kb = jnp.where(used_taps((16, LANES)), kb, NEG)
    vec_ref[KBR : KBR + 1, 0:LANES] = kb[0:1]

    lane = iota((8, LANES), 1)
    for a in range(64):
        c0, ln = divmod(a * KB, LANES)
        at = KERNEL_AT + c0
        x = pltpu.roll(flat[pl.ds(at, 8, stride=27), :], (LANES - ln) % LANES, 1)
        if ln + KB > LANES:
            y = pltpu.roll(flat[pl.ds(at + 1, 8, stride=27), :], (LANES - ln) % LANES, 1)
            x = jnp.where(lane < LANES - ln, x, y)
        kwt[pl.ds(a, 8, stride=64), :] = jnp.where(lane < KB, x, 0.0)
    kw_ref[...] = nn(kwt[0:ATT, :].astype(bf16), perm).astype(bf16)


def pack_small(flat, gkw_ref, vec, kwt):
    flat[...] = jnp.zeros_like(flat)
    perm = tap_perm()
    kwt[...] = jnp.zeros_like(kwt)
    kwt[0:ATT, :] = nt(gkw_ref[...].astype(bf16), perm)
    lane = iota((8, LANES), 1)
    for a in range(64):
        c0, ln = divmod(a * KB, LANES)
        at = KERNEL_AT + c0
        x = pltpu.roll(kwt[pl.ds(a, 8, stride=64), :], ln, 1)
        if ln + KB > LANES:
            flat[pl.ds(at, 8, stride=27), :] += jnp.where(lane >= ln, x, 0.0)
            flat[pl.ds(at + 1, 8, stride=27), :] += jnp.where(lane < ln, x, 0.0)
        else:
            flat[pl.ds(at, 8, stride=27), :] += x
    for row in range(4):
        for c in range(3):
            at = BIAS_AT + row * 3 + c
            flat[at : at + 1, :] = vec[row : row + 1, c * LANES : (c + 1) * LANES]
    for j in range(KS):
        for c in range(6):
            at = DEPTH_AT + j * 6 + c
            flat[at : at + 1, :] = vec[DW + j : DW + j + 1, c * LANES : (c + 1) * LANES]
    kwt[...] = jnp.zeros_like(kwt)
    at = 8
    for row, many in TAIL:
        for c in range(many):
            kwt[at + c : at + c + 1, :] = vec[row : row + 1, c * LANES : (c + 1) * LANES]
        at += many
    lane = iota((72, LANES), 1)
    before = pltpu.roll(kwt[7:79, :], KB, 1)
    here = pltpu.roll(kwt[8:80, :], KB, 1)
    at = TAIL_AT
    flat[at : at + 72, :] = jnp.where(lane < KB, before, here)
    kb = jnp.broadcast_to(vec[KBR : KBR + 1, 0:LANES], (16, LANES))
    kb = nt(jnp.where(used_taps((16, LANES)), kb, 0.0).astype(bf16), perm)
    lane = iota((1, LANES), 1)
    flat[at : at + 1, :] = jnp.where(lane < KB, kb[0:1], flat[at : at + 1, :])


class Place:
    def __init__(self, outer, inner):
        self.outer, self.inner, self.count = outer, inner, outer * inner
        self.lines = inner // 2
        dp, fs = lax.axis_index("dp"), lax.axis_index("fsdp")
        self.y, self.x, self.z, self.c = dp // 2, lax.rem(dp, 2), fs // 2, lax.rem(fs, 2)
        self.me = dp * inner + fs

    def coords(self, dy=0, dx=0, z=None, dc=0):
        def flip(v, d):
            return 1 - v if d else v

        z = self.z if z is None else z
        return flip(self.y, dy) * 2 + flip(self.x, dx), z * 2 + flip(self.c, dc)

    def index(self, **d):
        o, i = self.coords(**d)
        return o * self.inner + i

    def device(self, n):
        return n // self.inner, lax.rem(n, self.inner)

    def item(self, t):
        s = (t + 1) // 2
        z = self.z - s if t % 2 else self.z + s
        return z, (z >= 0) & (z < self.lines), s, t % 2 == 1

    def call(self):
        barrier = pltpu.get_barrier_semaphore()
        for n in range(1, self.count):
            peer = self.device(lax.rem(self.me + n, self.count))
            pl.semaphore_signal(barrier, inc=1, device_id=peer, device_id_type=pl.DeviceIdType.MESH)

    def all_here(self):
        pl.semaphore_wait(pltpu.get_barrier_semaphore(), self.count - 1)


class Copies:
    def __init__(self, send, recv):
        self.send, self.recv, self.used, self.made = send, recv, 0, []

    def start(self, src, dst, peer, slot, ok=None, group=None):
        number = self.used if group is None else group
        if group is None:
            self.used += 1
        assert number < self.send.shape[0]

        def make():
            return pltpu.make_async_remote_copy(
                src_ref=src(),
                dst_ref=dst(),
                send_sem=self.send.at[number],
                recv_sem=self.recv.at[slot() if callable(slot) else slot],
                device_id=peer(),
                device_id_type=pl.DeviceIdType.MESH,
            )

        if group is None:
            self.made.append((make, ok))
        guarded(ok, lambda: make().start())

    def sent(self, ref, group):
        pltpu.make_async_copy(ref, ref, self.send.at[group]).wait()

    def arrived(self, dst, slot, ok=None):
        def wait():
            ref = dst()
            pltpu.make_async_copy(ref, ref, self.recv.at[slot]).wait()

        guarded(ok, wait)

    def finish(self):
        for make, ok in self.made:
            guarded(ok, lambda make=make: make().wait_send())


def guarded(ok, action):
    if ok is None:
        action()
    else:
        pl.when(ok())(action)


def half_of(chunk):
    return -(-chunk // 32) * 16


class Gather:
    @staticmethod
    def scratch(sect, inner):
        lines = inner // 2
        items = 2 * lines - 1
        return [
            VM((sect.count, sect.chunk, LANES), bf16),
            VM((sect.slots, sect.chunk, LANES), bf16),
            VM((sect.sources, sect.chunk, LANES), bf16),
            VM((sect.chunk, LANES), f32),
            pltpu.SemaphoreType.DMA((sect.slots + 10 * items + 4,)),
            pltpu.SemaphoreType.DMA((sect.sources + 9 * items,)),
        ]

    def __init__(self, sect, place, ownf, lead, scratch):
        self.sect, self.place, self.ownf, self.lead = sect, place, ownf, lead
        self.buf, self.win, self.land, self.frame, send, recv = scratch
        self.copies = Copies(send, recv)
        n = 2 * place.lines - 1
        self.items = n
        self.Z, self.X, self.Y, self.A, self.B, self.CZ, self.CX, self.CY, self.CD = (sect.sources + n * k for k in range(9))
        cut = half_of(sect.chunk)
        self.half = {"a": pl.ds(0, cut), "b": pl.ds(cut, sect.chunk - cut)}

    def offer(self):
        for k in range(self.sect.slots):
            self.give(k)

    def give(self, k):
        sect, place, me = self.sect, self.place, self.place.me
        v, ok = sect.of_owner(me, k)

        @pl.when(ok)
        def _():
            at = self.lead + sect.start(v) - sect.rows * me
            self.win[k] = self.ownf[pl.ds(at, sect.chunk), :].astype(bf16)

        @pl.when(ok & (sect.seat(v) == me))
        def _():
            self.land[sect.source_of(v, me)] = self.win[k]

        def chunk():
            return sect.of_owner(me, k)[0]

        def away():
            v, ok = sect.of_owner(me, k)
            return ok & (sect.seat(v) != me)

        def source():
            return jnp.clip(sect.source_of(chunk(), me), 0, sect.sources - 1)

        def seat():
            return jnp.clip(sect.seat(chunk()), 0, sect.count - 1)

        self.copies.start(lambda: self.win.at[k], lambda: self.land.at[source()], lambda: place.device(seat()), source, away)

    def form(self):
        sect, me = self.sect, self.place.me
        v = sect.chunk_at(me)
        row = iota((sect.chunk, LANES), 0) + sect.start(v)
        x = None
        for s in range(sect.sources):
            i, ok = sect.of_chunk(v, s)
            self.copies.arrived(lambda: self.land.at[s], s, lambda: ok & (i != me))
            here = self.land[s].astype(f32)
            x = here if x is None else jnp.where(row >= sect.rows * i, here, x)
        self.frame[...] = x

        def settle(per):
            tall = sect.chunk // per
            for c in range(per):
                self.buf[me, c * tall : (c + 1) * tall, :] = self.frame[pl.ds(c, tall, stride=per), :].astype(bf16)

        sect.by_kind(v, settle)

        @pl.when(v >= sect.used)
        def _():
            self.buf[me] = jnp.zeros((sect.chunk, LANES), bf16)

        self.pass_on(0)

    def ref(self, t, which=None, **way):
        def make():
            at = self.place.index(z=self.place.item(t)[0], **way)
            return self.buf.at[at] if which is None else self.buf.at[at, self.half[which]]

        return make

    def ok(self, t):
        return None if t == 0 else lambda: self.place.item(t)[1]

    def same(self, ref, peer, slot, ok):
        self.copies.start(ref, ref, peer, slot, ok)

    def beside(self, **way):
        return lambda: self.place.coords(**way)

    def pass_on(self, t):
        place = self.place
        _, _, s, below = place.item(t)
        for way in (1, -1) if t == 0 else ((1,) if below else (-1,)):
            slot = 2 * s + 1 if way > 0 else 2 * s + 2

            def inside(way=way):
                there = place.z + way
                good = (there >= 0) & (there < place.lines)
                return good if t == 0 else good & place.item(t)[1]

            if slot < self.items:
                self.same(self.ref(t), lambda way=way: place.coords(z=place.z + way), self.Z + slot, inside)
        ok = self.ok(t)
        self.same(self.ref(t), self.beside(dx=1), self.X + t, ok)
        self.same(self.ref(t), self.beside(dy=1), self.Y + t, ok)
        self.same(self.ref(t), self.beside(dc=1), self.CZ + t, ok)

    def at_distance(self, s):
        return [0] if s == 0 else [2 * s - 1, 2 * s]

    def along(self, s):
        for t in self.at_distance(s):
            self.copies.arrived(self.ref(t), self.Z + t, self.ok(t))
            self.pass_on(t)

    def across(self, s):
        for t in self.at_distance(s):
            ok = self.ok(t)
            self.copies.arrived(self.ref(t, dx=1), self.X + t, ok)
            self.same(self.ref(t, "a", dx=1), self.beside(dy=1), self.A + t, ok)
            self.same(self.ref(t, dx=1), self.beside(dc=1), self.CX + t, ok)
            self.copies.arrived(self.ref(t, dy=1), self.Y + t, ok)
            self.same(self.ref(t, "b", dy=1), self.beside(dx=1), self.B + t, ok)
            self.same(self.ref(t, dy=1), self.beside(dc=1), self.CY + t, ok)

    def diagonal(self):
        for t in range(self.items):
            ok = self.ok(t)
            self.copies.arrived(self.ref(t, "a", dy=1, dx=1), self.A + t, ok)
            self.copies.arrived(self.ref(t, "b", dy=1, dx=1), self.B + t, ok)
            self.same(self.ref(t, dy=1, dx=1), self.beside(dc=1), self.CD + t, ok)

    def rest(self):
        for t in range(self.items):
            for k, way in ((self.CZ, {}), (self.CX, {"dx": 1}), (self.CY, {"dy": 1}), (self.CD, {"dy": 1, "dx": 1})):
                self.copies.arrived(self.ref(t, dc=1, **way), k + t, self.ok(t))


class Scatter:
    @staticmethod
    def scratch(sect, inner):
        lines = inner // 2
        cut = half_of(sect.chunk)
        return [
            VM((4 * lines, sect.chunk, LANES), bf16),
            VM((4 * lines, sect.chunk, LANES), bf16),
            VM((2 * lines, cut, LANES), bf16),
            VM((2 * lines, sect.chunk - cut, LANES), bf16),
            VM((lines, sect.chunk - cut, LANES), bf16),
            VM((lines, cut, LANES), bf16),
            VM((lines, sect.chunk, LANES), bf16),
            VM((sect.chunk, LANES), f32),
            VM((sect.chunk, LANES), f32),
            VM((sect.chunk, LANES), bf16),
            VM((sect.slots, sect.chunk, LANES), bf16),
            pltpu.SemaphoreType.DMA((sect.sources + 6,)),
            pltpu.SemaphoreType.DMA((11 * lines + sect.slots,)),
            pltpu.SemaphoreType.DMA((4 * lines,)),
        ]

    def __init__(self, sect, place, part, out, lead, scratch, close):
        self.close = close
        self.sect, self.place, self.part, self.out, self.lead = sect, place, part, out, lead
        (self.work, self.rc, self.ry, self.rx, self.ry2, self.rx2, self.rz, self.frame, self.flat, self.low, self.land,
         send, recv, self.near) = scratch
        self.copies = Copies(send, recv)
        lines = place.lines
        self.lines = lines
        cut = half_of(sect.chunk)
        self.a, self.b = pl.ds(0, cut), pl.ds(cut, sect.chunk - cut)
        self.C, self.YA, self.XB, self.XA, self.YB, self.Z, self.O = (lines * k for k in (0, 4, 6, 8, 9, 10, 11))
        self.far = list(range(1, lines)) + [0]
        self.group = sect.sources

    def sums(self):
        out = []
        for n in range(self.lines + 2):
            for lag, step in ((0, self.first), (1, self.second), (2, self.third)):
                if 0 <= n - lag < self.lines:
                    out.append(lambda step=step, d=self.far[n - lag]: step(d))
        return out

    def z(self, d):
        return lax.rem(self.place.z + d, self.lines) if d else self.place.z

    def at(self, dy, dx, d):
        return (dy * 2 + dx) * self.lines + d

    def own(self, dy, dx, d):
        k = self.at(dy, dx, d)
        there = self.place.index(dy=dy, dx=dx, z=self.z(d))
        return pltpu.make_async_copy(self.part(there), self.work.at[k], self.near.at[k])

    def core(self, *places):
        place = self.place

        def give(dy, dx, d):
            k = self.at(dy, dx, d)
            self.copies.start(
                lambda: self.part(place.index(dy=dy, dx=dx, z=self.z(d), dc=1)),
                lambda: self.rc.at[k],
                lambda: place.coords(dc=1),
                self.C + k,
                group=self.group,
            )
            if not self.close:
                self.own(dy, dx, d).start()

        for d in places or self.far:
            for dy, dx in ((1, 1), (1, 0), (0, 1), (0, 0)):
                give(dy, dx, d)

    def send(self, k, rows, buf, n, way, slot, group):
        self.copies.start(
            lambda: self.work.at[k, rows],
            lambda: buf.at[n],
            lambda: self.place.coords(**way),
            slot,
            group=self.group + group,
        )

    def finish(self):
        for k, ref in enumerate((self.rc, self.ry, self.rx, self.rx2, self.ry2, self.rz.at[pl.ds(1, self.lines - 1)])):
            self.copies.sent(ref, self.group + k)
        self.copies.finish()

    def got(self, buf, n, slot):
        self.copies.arrived(lambda: buf.at[n], slot)

    def plus(self, k, rows, other):
        self.work[k, rows] = (self.work[k, rows].astype(f32) + other.astype(f32)).astype(bf16)

    def first(self, d):
        lines = self.lines
        for dy, dx in ((1, 1), (1, 0), (0, 1), (0, 0)):
            k = self.at(dy, dx, d)
            if self.close:
                self.got(self.rc, k, self.C + k)
                mine = self.part(self.place.index(dy=dy, dx=dx, z=self.z(d)))[...]
                self.work[k] = (mine.astype(f32) + self.rc[k].astype(f32)).astype(bf16)
            else:
                self.own(dy, dx, d).wait()
                self.got(self.rc, k, self.C + k)
                self.plus(k, pl.ds(0, self.sect.chunk), self.rc[k])
            if dy:
                self.send(k, self.a, self.ry, dx * lines + d, {"dy": 1}, self.YA + dx * lines + d, 1)
            if dx:
                self.send(k, self.b, self.rx, dy * lines + d, {"dx": 1}, self.XB + dy * lines + d, 2)

    def second(self, d):
        n = self.lines + d
        self.got(self.ry, n, self.YA + n)
        self.plus(self.at(0, 1, d), self.a, self.ry[n])
        self.send(self.at(0, 1, d), self.a, self.rx2, d, {"dx": 1}, self.XA + d, 3)
        self.got(self.rx, n, self.XB + n)
        self.plus(self.at(1, 0, d), self.b, self.rx[n])
        self.send(self.at(1, 0, d), self.b, self.ry2, d, {"dy": 1}, self.YB + d, 4)

    def third(self, d):
        k = self.at(0, 0, d)
        self.got(self.ry, d, self.YA + d)
        self.got(self.rx, d, self.XB + d)
        self.got(self.rx2, d, self.XA + d)
        self.got(self.ry2, d, self.YB + d)
        self.plus(k, self.a, self.ry[d].astype(f32) + self.rx2[d].astype(f32))
        self.plus(k, self.b, self.rx[d].astype(f32) + self.ry2[d].astype(f32))
        if d:
            self.copies.start(
                lambda: self.work.at[k],
                lambda: self.rz.at[d],
                lambda: self.place.coords(z=self.z(d)),
                self.Z + d,
                group=self.group + 5,
            )

    def settle(self):
        sect, me = self.sect, self.place.me
        total = self.work[self.at(0, 0, 0)].astype(f32)
        for d in range(1, self.lines):
            self.got(self.rz, d, self.Z + d)
            total = total + self.rz[d].astype(f32)
        self.frame[...] = total

        def spread(per):
            tall = sect.chunk // per
            for c in range(per):
                self.flat[pl.ds(c, tall, stride=per), :] = self.frame[c * tall : (c + 1) * tall, :]

        self.flat[...] = total
        sect.by_kind(sect.chunk_at(me), spread)
        self.low[...] = self.flat[...].astype(bf16)
        for s in range(sect.sources):
            self.give(s)

    def give(self, s):
        sect, me = self.sect, self.place.me
        i, ok = sect.of_chunk(sect.chunk_at(me), s)

        @pl.when(ok & (i == me))
        def _():
            self.land[sect.slot_of(sect.chunk_at(me), i)] = self.low[...]

        def owner():
            return jnp.minimum(sect.of_chunk(sect.chunk_at(me), s)[0], sect.count - 1)

        def slot():
            return jnp.clip(sect.slot_of(sect.chunk_at(me), owner()), 0, sect.slots - 1)

        def away():
            i, ok = sect.of_chunk(sect.chunk_at(me), s)
            return ok & (i != me)

        self.copies.start(
            lambda: self.low, lambda: self.land.at[slot()], lambda: self.place.device(owner()), lambda: self.O + slot(), away
        )

    def take(self):
        sect, me = self.sect, self.place.me
        for k in range(sect.slots):
            v, ok = sect.of_owner(me, k)
            self.copies.arrived(lambda: self.land.at[k], self.O + k, lambda: ok & (sect.seat(v) != me))

            @pl.when(ok)
            def _():
                at = self.lead + sect.start(v) - sect.rows * me
                self.out[pl.ds(at, sect.chunk), :] = self.land[k].astype(f32)


def pumped(due):
    row = pl.program_id(0)

    def pump(point):
        for r, p, step in due:
            if p == point:
                pl.when(row == r)(step)

    return pump


def spread_over(steps, rows, points, spots):
    end = rows * points - 1
    return [(min(n, end) // points, min(n, end) % points, step) for step, n in zip(steps, spots)]


def doc_marks(r, length, len_ref, dcol, tm, mb):
    t = iota((length, LANES), 0)
    u = iota((8, length), 1)
    ends = jnp.int32(0)
    d = jnp.zeros((length, LANES), i32)
    e = jnp.zeros((8, length), i32)
    for j in range(SLOTS):
        ends = ends + len_ref[r, j]
        d = d + (t >= ends).astype(i32)
        e = e + (u >= ends).astype(i32)
    dcol[0:8, :] = jnp.full((8, LANES), -1, i32)
    dcol[8 : 8 + length, :] = d
    dcol[8 + length : 16 + length, :] = jnp.full((8, LANES), -1, i32)
    for j in range(KS):
        at = 8 + j - HALF
        tm[j] = (dcol[at : at + length, :] == d).astype(f32)
    for c in range(length // LANES):
        mb[:, c * LANES : (c + 1) * LANES] = jnp.where(d == e[0:1, c * LANES : (c + 1) * LANES], BIG, NEG)


def tap_lanes(tm, length):
    tap = iota((length, LANES), 1) >> 3
    out = jnp.zeros((length, LANES), f32)
    for j in range(KS):
        out = jnp.where(tap == j, tm[j], out)
    return jnp.where(used_taps((length, LANES)), out, 0.0)


def over_taps(x, op):
    for s in (8, 16, 32, 64):
        x = op(x, pltpu.roll(x, s, 1))
    return x


def fill_emat(emat):
    k, c = iota((2 * LANES, ATT), 0) & (LANES - 1), iota((2 * LANES, ATT), 1)
    for j in range(KS):
        emat[:, j * ATT : (j + 1) * ATT] = jnp.where(k == j * 8 + (c >> 6), 1.0, 0.0).astype(bf16)


def two_parts(x):
    high = x.astype(bf16)
    return jnp.concatenate([high, (x - high.astype(f32)).astype(bf16)], axis=1)


def zero_pads(ref, length):
    for c in range(ref.shape[0]):
        ref[c, 0:8, :] = jnp.zeros((8, LANES), f32)
        ref[c, 8 + length : 16 + length, :] = jnp.zeros((8, LANES), f32)


def fwd_kernel(length, pump, len_ref, tok_ref, wp_ref, pw_ref, kw_ref, vec_ref,
               qkvc_ref, kc_ref, dep_ref, ca_ref, tap_ref, join_ref, lse_ref,
               xs, cs, dcol, tm, mb, emat, acc):
    row = pl.program_id(0)
    pump(0)
    pl.when(row > 0)(lambda: doc_marks(row, length, len_ref, dcol, tm, mb))
    pump(1)
    tok = tok_ref[...]
    zero_pads(xs, length)
    zero_pads(cs, length)
    for c in range(6):
        xs[c, 8 : 8 + length, :] = tok[:, c * LANES : (c + 1) * LANES].astype(f32)
    for m, bias in ((0, QB), (1, None), (2, VB), (3, CB)):
        x = nn(tok, wp_ref[:, m * ATT : (m + 1) * ATT])
        if bias is not None:
            x = x + vec_ref[bias : bias + 1, 0:ATT]
        x = x.astype(bf16)
        qkvc_ref[:, m * ATT : (m + 1) * ATT] = x
        if m == 3:
            for c in range(3):
                cs[c, 8 : 8 + length, :] = x[:, c * LANES : (c + 1) * LANES].astype(f32)

    pump(2)
    step = 64

    for c in range(6):
        w = [vec_ref[DW + j : DW + j + 1, c * LANES : (c + 1) * LANES] for j in range(KS)]
        for r in range(0, length, step):
            total = w[HALF] * xs[c, 8 + r : 8 + r + step, :]
            for j in range(KS):
                if j != HALF:
                    at = 8 + r + j - HALF
                    total = total + w[j] * (xs[c, at : at + step, :] * tm[j, r : r + step, :])
            dep_ref[r : r + step, c * LANES : (c + 1) * LANES] = total.astype(bf16)

    pump(3)
    keyconv = nn(dep_ref[...], pw_ref[...]) + vec_ref[PB : PB + 1, 0:ATT]
    kc_ref[...] = keyconv.astype(bf16)
    ca = (keyconv * qkvc_ref[:, 0:ATT].astype(f32)).astype(bf16)
    ca_ref[...] = ca
    logits = nn(ca, kw_ref[...]) + vec_ref[KBR : KBR + 1, 0:LANES]
    e = jnp.exp(logits - over_taps(logits, jnp.maximum))
    taps = e / over_taps(e, jnp.add)
    tap_ref[...] = taps
    spread = two_parts(taps * tap_lanes(tm, length))
    for j in range(KS):
        if j % 3 == 0:
            pump(4 + j // 3)
        t = nn(spread, emat[:, j * ATT : (j + 1) * ATT])
        for c in range(3):
            at = 8 + j - HALF
            part = t[:, c * LANES : (c + 1) * LANES] * cs[c, at : at + length, :]
            if j:
                part = part + acc[:, c * LANES : (c + 1) * LANES]
            if j < KS - 1:
                acc[:, c * LANES : (c + 1) * LANES] = part
            else:
                join_ref[:, ATT + c * LANES : ATT + (c + 1) * LANES] = part.astype(bf16)

    for p in range(3):
        pump(7 + p)
        cols = slice(p * LANES, (p + 1) * LANES)
        q, k, v = (qkvc_ref[:, m * ATT + p * LANES : m * ATT + (p + 1) * LANES] for m in range(3))
        qs = q.astype(f32) * SCALE
        vt = v.astype(f32).T
        lane, sub = iota((length, LANES), 1), iota((LANES, length), 0)
        halves = []
        for h in range(2):
            qh = jnp.where((lane >= HEAD_DIM) == bool(h), qs, 0.0).astype(bf16)
            vh = jnp.where((sub >= HEAD_DIM) == bool(h), vt, 1.0).astype(bf16)
            z = jnp.minimum(nt(k, qh), mb[...])
            top = jnp.max(z, axis=0, keepdims=True)
            o = nn(vh, jnp.exp(z - top).astype(bf16))
            s = o[(1 - h) * HEAD_DIM : (1 - h) * HEAD_DIM + 1, :]
            lse_ref[0, 2 * p + h : 2 * p + h + 1, :] = top + jnp.log(s)
            halves.append(o[h * HEAD_DIM : (h + 1) * HEAD_DIM, :] / s)
        join_ref[:, cols] = jnp.concatenate(halves, axis=0).T.astype(bf16)
    pump(10)


def blocked(rows, cols):
    return pl.BlockSpec((rows, cols), lambda r: (r, 0))


def row_scratch(length):
    return [
        VM((6, length + 16, LANES), f32),
        VM((3, length + 16, LANES), f32),
        VM((length + 16, LANES), i32),
        VM((KS, length, LANES), f32),
        VM((length, length), f32),
        VM((2 * LANES, KS * ATT), bf16),
    ]


FWD_POINTS = 11
FWD_SPOTS = (4, 5, 10, 11, 16, 17, 22, 27, 99)


def run_front(first, second, own, tokens, lengths):
    outer, inner = lax.axis_size("dp"), lax.axis_size("fsdp")
    rows, count = lengths.shape[0], tokens.shape[0]
    length = count // rows
    scratch = row_scratch(length) + [VM((length, ATT), f32)]
    n = len(scratch)
    lead = max(first.chunk, second.chunk)
    more = [
        VM((first.rows + 2 * lead + 16, LANES), f32),
        VM((first.small * first.chunk, LANES), f32),
        VM((512, LANES), f32),
    ]
    m = len(Gather.scratch(first, inner))

    def body(own_ref, len_ref, tok_ref, *refs):
        outs, (dw_ref, fi_ref, fo_ref, wp_ref, pw_ref, kw_ref, vec_ref), refs = refs[:7], refs[7:14], refs[14:]
        rows_refs, (ownf, flat, kwt), refs = refs[:n], refs[n : n + 3], refs[n + 3 :]
        place = Place(outer, inner)
        a = Gather(first, place, ownf, lead, refs[:m])
        b = Gather(second, place, ownf, lead, refs[m:])

        def begin():
            place.call()
            ownf[...] = jnp.zeros_like(ownf)
            ownf[lead : lead + first.rows, :] = own_ref[...].astype(f32)
            _, _, dcol, tm, mb, emat, _ = rows_refs
            fill_emat(emat)
            place.all_here()
            a.offer()
            b.offer()
            doc_marks(0, length, len_ref, dcol, tm, mb)
            a.form()
            for s in range(1, place.lines):
                a.along(s)
                a.across(s - 1)
            a.across(place.lines - 1)
            b.form()
            a.diagonal()
            a.rest()
            from_frames(first, a.buf, [(wp_ref, D, ATT, k * ATT) for k in range(4)] + [(pw_ref, D, ATT, 0)], flat)
            unpack_small(flat, kw_ref, vec_ref, kwt)

        def end():
            a.copies.finish()
            b.rest()
            b.copies.finish()
            from_frames(second, b.buf, ((dw_ref, D, D, 0), (fi_ref, D, FF // GROUPS, 0), (fo_ref, FF, D // GROUPS, 0)))

        steps = []
        for s in range(1, place.lines):
            steps.append(lambda s=s: b.along(s))
            steps.append(lambda s=s: b.across(s - 1))
        steps += [lambda: b.across(place.lines - 1), b.diagonal, end]
        spots = FWD_SPOTS if len(steps) == len(FWD_SPOTS) else [99] * len(steps)
        pump = pumped([(0, 0, begin)] + spread_over(steps, rows, FWD_POINTS, spots))
        fwd_kernel(length, pump, len_ref, tok_ref, wp_ref, pw_ref, kw_ref, vec_ref, *outs, *rows_refs)

    full = pl.BlockSpec(memory_space=VM)
    return pl.pallas_call(
        body,
        grid=(rows,),
        out_shape=[
            jax.ShapeDtypeStruct((count, 4 * ATT), bf16),
            jax.ShapeDtypeStruct((count, ATT), bf16),
            jax.ShapeDtypeStruct((count, D), bf16),
            jax.ShapeDtypeStruct((count, ATT), bf16),
            jax.ShapeDtypeStruct((count, LANES), f32),
            jax.ShapeDtypeStruct((count, D), bf16),
            jax.ShapeDtypeStruct((rows, 8, length), f32),
            jax.ShapeDtypeStruct((D, D), bf16),
            jax.ShapeDtypeStruct((D, FF // GROUPS), bf16),
            jax.ShapeDtypeStruct((FF, D // GROUPS), bf16),
            jax.ShapeDtypeStruct((D, 4 * ATT), bf16),
            jax.ShapeDtypeStruct((D, ATT), bf16),
            jax.ShapeDtypeStruct((ATT, LANES), bf16),
            jax.ShapeDtypeStruct((VROWS, FF), f32),
        ],
        in_specs=[full, pl.BlockSpec(memory_space=pltpu.SMEM), blocked(length, D)],
        out_specs=[
            blocked(length, 4 * ATT),
            blocked(length, ATT),
            blocked(length, D),
            blocked(length, ATT),
            blocked(length, LANES),
            blocked(length, D),
            pl.BlockSpec((1, 8, length), lambda r: (r, 0, 0)),
        ]
        + [full] * 7,
        scratch_shapes=scratch + more + Gather.scratch(first, inner) + Gather.scratch(second, inner),
        compiler_params=pltpu.CompilerParams(vmem_limit_bytes=VMEM_LIMIT, collective_id=0, has_side_effects=True),
        name="front",
    )(own, lengths, tokens)


def mid_kernel(sect, length, len_ref, tok_ref, join_ref, cot_ref, dw_ref, fi_ref, fo_ref, vec_ref,
               out_ref, gf_ref, gj_ref, part_ref, gv_ref,
               gdw_ref, gfi_ref, gfo_ref, xh1, rs1, nl, act, slope, gsec, gsl, wide):
    row = pl.program_id(0)
    fg, dg = FF // GROUPS, D // GROUPS

    @pl.when(row == 0)
    def _():
        for ref in (gdw_ref, gfi_ref, gfo_ref, gv_ref):
            ref[...] = jnp.zeros_like(ref)

    used = jnp.int32(0)
    for j in range(SLOTS):
        used = used + len_ref[row, j]

    def vec(r, n=D):
        return vec_ref[r : r + 1, 0:n]

    step = 128
    halves = [slice(k * (length // 2), (k + 1) * (length // 2)) for k in range(2)]
    for rows in halves:
        gsec[rows, :] = nn(join_ref[rows, :], dw_ref[...])

    def norm1(i):
        at = slice(i * step, (i + 1) * step)
        z = gsec[at, :] + vec(DB) + tok_ref[at, :].astype(f32)
        z = z - jnp.mean(z, axis=1, keepdims=True)
        r = lax.rsqrt(jnp.mean(z * z, axis=1, keepdims=True) + EPS)
        x = z * r
        xh1[at, :] = x
        rs1[at, :] = jnp.broadcast_to(r, (step, LANES))
        nl[at, :] = (x * vec(N1G) + vec(N1S)).astype(bf16)

    for k in range(length // step):
        norm1(k)

    tile = 768
    per = fg // tile

    tiles = [(g, i) for g in range(GROUPS) for i in range(per)]

    def inner(n):
        g, i = tiles[n]
        wide[n % 2] = nn(nl[:, g * dg : (g + 1) * dg], fi_ref[g * dg : (g + 1) * dg, i * tile : (i + 1) * tile])

    inner(0)
    for n, (g, i) in enumerate(tiles):
        if n + 1 < len(tiles):
            inner(n + 1)
        col = slice(g * fg + i * tile, g * fg + (i + 1) * tile)
        for r in range(0, length, 64):
            x = wide[n % 2, r : r + 64, :] + vec_ref[FIB : FIB + 1, col]
            phi = 0.5 * lax.erf(x * math.sqrt(0.5)) + 0.5
            e = jnp.exp2(x * x * (-0.5 / math.log(2.0)))
            act[r : r + 64, col] = (x * phi).astype(bf16)
            slope[r : r + 64, col] = (phi + x * (1.0 / math.sqrt(2.0 * math.pi)) * e).astype(bf16)

    for rows in halves:
        for g in range(GROUPS):
            gsec[rows, g * dg : (g + 1) * dg] = nn(act[rows, g * fg : (g + 1) * fg], fo_ref[g * fg : (g + 1) * fg, :])

    def rows8(x):
        total = x[0:8]
        for k in range(8, x.shape[0], 8):
            total = total + x[k : k + 8]
        return total

    def norm2(i, carry):
        at = slice(i * step, (i + 1) * step)
        norm = xh1[at, :] * vec(N1G) + vec(N1S)
        z = gsec[at, :] + vec(FOB) + norm
        z = z - jnp.mean(z, axis=1, keepdims=True)
        r = lax.rsqrt(jnp.mean(z * z, axis=1, keepdims=True) + EPS)
        x = z * r
        keep = ((iota((step, 1), 0) + i * step) < used).astype(f32)
        out_ref[at, :] = ((x * vec(N2G) + vec(N2S)) * keep).astype(bf16)
        gf = cot_ref[at, :].astype(f32) * keep
        gx = gf * x
        e = gf * vec(N2G)
        gz = r * (e - jnp.mean(e, axis=1, keepdims=True) - x * jnp.mean(e * x, axis=1, keepdims=True))
        gsec[at, :] = gz
        gsl[at, :] = gz.astype(bf16)
        return (carry[0] + rows8(gx), carry[1] + rows8(gf), carry[2] + rows8(gz))

    none = jnp.zeros((8, D), f32)
    sums = (none, none, none)
    for k in range(length // step):
        sums = norm2(k, sums)

    def add(r, value):
        gv_ref[r : r + 1, 0 : value.shape[1]] += jnp.sum(value, axis=0, keepdims=True)

    for r, value in zip((N2G, N2S, FOB), sums):
        add(r, value)

    def slopes(n):
        g, i = tiles[n]
        at = slice(g * fg + i * tile, g * fg + (i + 1) * tile)
        wide[n % 2] = nt(gsl[:, g * dg : (g + 1) * dg], fo_ref[at, :])

    slopes(0)
    for n, (g, i) in enumerate(tiles):
        if n + 1 < len(tiles):
            slopes(n + 1)
        at = slice(g * fg + i * tile, g * fg + (i + 1) * tile)
        total = jnp.zeros((8, tile), f32)
        for r in range(0, length, 64):
            x = wide[n % 2, r : r + 64, :] * slope[r : r + 64, at].astype(f32)
            slope[r : r + 64, at] = x.astype(bf16)
            total = total + rows8(x)
        gv_ref[FIB : FIB + 1, at] += jnp.sum(total, axis=0, keepdims=True)
    for rows in halves:
        for g in range(GROUPS):
            gsec[rows, g * dg : (g + 1) * dg] += nt(slope[rows, g * fg : (g + 1) * fg], fi_ref[g * dg : (g + 1) * dg, :])

    def norm1_back(i, carry):
        at = slice(i * step, (i + 1) * step)
        gn = gsec[at, :]
        x = xh1[at, :]
        e = gn * vec(N1G)
        r = rs1[at, :]
        r = jnp.concatenate([r] * (D // LANES), axis=1)
        gz = r * (e - jnp.mean(e, axis=1, keepdims=True) - x * jnp.mean(e * x, axis=1, keepdims=True))
        gf_ref[at, :] = gz.astype(bf16)
        return (carry[0] + rows8(gn * x), carry[1] + rows8(gn), carry[2] + rows8(gz))

    sums = (none, none, none)
    todo = list(enumerate(tiles))
    for k in range(length // step):
        sums = norm1_back(k, sums)
        if k % 2:
            rows = slice((k - 1) * step, (k + 1) * step)
            gj_ref[rows, :] = nt(gf_ref[rows, :], dw_ref[...]).astype(bf16)
        for n, (g, i) in todo[k * len(todo) // (length // step) : (k + 1) * len(todo) // (length // step)]:
            at = slice(g * fg + i * tile, g * fg + (i + 1) * tile)
            gfo_ref[at, :] += tn(act[:, at], gsl[:, g * dg : (g + 1) * dg])
            gfi_ref[g * dg : (g + 1) * dg, i * tile : (i + 1) * tile] += tn(nl[:, g * dg : (g + 1) * dg], slope[:, at])
    for r, value in zip((N1G, N1S, DB), sums):
        add(r, value)
    gdw_ref[...] += tn(join_ref[...], gf_ref[...])

    @pl.when(row == pl.num_programs(0) - 1)
    def _():
        to_frames(sect, part_ref, ((gdw_ref, D, D, 0), (gfi_ref, D, FF // GROUPS, 0), (gfo_ref, FF, D // GROUPS, 0)))


def run_mid(sect, tokens, lengths, joined, cotangent, dw, fi, fo, vec):
    rows, count = lengths.shape[0], tokens.shape[0]
    length = count // rows

    def body(*refs):
        mid_kernel(sect, length, *refs)

    full = pl.BlockSpec(memory_space=VM)
    return pl.pallas_call(
        body,
        grid=(rows,),
        out_shape=[
            jax.ShapeDtypeStruct((count, D), bf16),
            jax.ShapeDtypeStruct((count, D), bf16),
            jax.ShapeDtypeStruct((count, D), bf16),
            jax.ShapeDtypeStruct((sect.count, sect.chunk, LANES), bf16),
            jax.ShapeDtypeStruct((VROWS, FF), f32),
        ],
        in_specs=[pl.BlockSpec(memory_space=pltpu.SMEM)] + [blocked(length, D)] * 3 + [full] * 4,
        out_specs=[blocked(length, D)] * 3 + [full] * 2,
        scratch_shapes=[
            VM((D, D), f32),
            VM((D, FF // GROUPS), f32),
            VM((FF, D // GROUPS), f32),
            VM((length, D), f32),
            VM((length, LANES), f32),
            VM((length, D), bf16),
            VM((length, FF), bf16),
            VM((length, FF), bf16),
            VM((length, D), f32),
            VM((length, D), bf16),
            VM((2, length, 768), f32),
        ],
        compiler_params=pltpu.CompilerParams(vmem_limit_bytes=VMEM_LIMIT),
        name="mid",
    )(lengths, tokens, joined, cotangent, dw, fi, fo, vec)


def bwd_kernel(length, pump, len_ref, tok_ref, qkvc_ref, kc_ref, dep_ref, ca_ref, tap_ref, join_ref, lse_ref, gf_ref, gj_ref,
               wp_ref, pw_ref, kw_ref, vec_ref,
               gt_ref, gp_ref, gpw_ref, gkw_ref, gv_ref,
               ds, cs, dcol, tm, mb, emat, gs, tp, prod, gq, gfour, acc):
    row = pl.program_id(0)

    @pl.when(row == 0)
    def _():
        fill_emat(emat)
        for ref in (gp_ref, gpw_ref, gkw_ref, gv_ref):
            ref[...] = jnp.zeros_like(ref)

    doc_marks(row, length, len_ref, dcol, tm, mb)
    pump(0)
    for ref in (ds, cs, gs, tp):
        zero_pads(ref, length)

    def add(r, value):
        gv_ref[r : r + 1, 0 : value.shape[1]] += jnp.sum(value, axis=0, keepdims=True)

    for p in range(3):
        pump(1 + p)
        cols = slice(p * LANES, (p + 1) * LANES)
        q, k, v = (qkvc_ref[:, m * ATT + p * LANES : m * ATT + (p + 1) * LANES] for m in range(3))
        g = gj_ref[:, cols]
        lane, sub = iota((length, LANES), 1), iota((16, LANES), 1)
        which = iota((16, LANES), 0)
        marks = jnp.where((sub >= HEAD_DIM) == (which >= 8), 1.0, 0.0).astype(bf16)
        dots = g.astype(f32) * join_ref[:, cols].astype(f32)
        high = dots.astype(bf16)
        dots = nt(marks, high) + nt(marks, (dots - high.astype(f32)).astype(bf16))
        qs = q.astype(f32) * SCALE
        kt = k.astype(f32).T.astype(bf16)
        gk, gv, gqt = None, None, []
        for h in range(2):
            own = (lane >= HEAD_DIM) == bool(h)
            qh = jnp.where(own, qs, 0.0).astype(bf16)
            gh = jnp.where(own, g.astype(f32), 0.0).astype(bf16)
            prob = jnp.exp(jnp.minimum(nt(k, qh), mb[...]) - lse_ref[0, 2 * p + h : 2 * p + h + 1, :])
            dsc = (prob * (nt(v, gh) - dots[8 * h : 8 * h + 1, :])).astype(bf16)
            a, b = nn(prob.astype(bf16), gh), nn(dsc, qh)
            gv, gk = (a, b) if h == 0 else (gv + a, gk + b)
            gqt.append(nn(kt, dsc)[h * HEAD_DIM : (h + 1) * HEAD_DIM, :])
        gq[:, cols] = jnp.concatenate(gqt, axis=0).T * SCALE
        gfour[:, ATT + p * LANES : ATT + (p + 1) * LANES] = gk.astype(bf16)
        gfour[:, 2 * ATT + p * LANES : 2 * ATT + (p + 1) * LANES] = gv.astype(bf16)
        gv_ref[VB : VB + 1, cols] += jnp.sum(gv, axis=0, keepdims=True)

    pump(4)
    for c in range(3):
        cs[c, 8 : 8 + length, :] = qkvc_ref[:, 3 * ATT + c * LANES : 3 * ATT + (c + 1) * LANES].astype(f32)
        gs[c, 8 : 8 + length, :] = gj_ref[:, ATT + c * LANES : ATT + (c + 1) * LANES].astype(f32)
    gtaps = None
    for j in range(0, KS, 3):
        for k in range(3):
            for c in range(3):
                at, spot = 8 + j + k - HALF, ((j + k) * 3 + c) * length
                prod[spot : spot + length, :] = (gs[c, 8 : 8 + length, :] * cs[c, at : at + length, :]).astype(bf16)
        blocks = [prod[n * length : (n + 1) * length, :] for n in range(j * 3, j * 3 + 9)]
        x = nt(jnp.concatenate(blocks, axis=1), emat[0:LANES, j * ATT : (j + 3) * ATT])
        gtaps = x if gtaps is None else gtaps + x
    marks = tap_lanes(tm, length)
    gtaps = gtaps * marks
    pump(5)
    taps = jnp.where(used_taps((length, LANES)), tap_ref[...], 0.0)
    glog = taps * (gtaps - over_taps(taps * gtaps, jnp.add))
    add(KBR, glog)
    glog = glog.astype(bf16)
    gkw_ref[...] += tn(ca_ref[...], glog)
    gca = nt(glog, kw_ref[...])

    tp[0, 8 : 8 + length, :] = taps * marks
    tap = iota((length, LANES), 1) >> 3
    moved = jnp.zeros((length, LANES), f32)
    for j in range(KS):
        at = 8 + HALF - j
        moved = jnp.where(tap == j, tp[0, at : at + length, :], moved)
    spread = two_parts(moved)
    for j in range(KS):
        t = nn(spread, emat[:, j * ATT : (j + 1) * ATT])
        for c in range(3):
            at = 8 + HALF - j
            part = t[:, c * LANES : (c + 1) * LANES] * gs[c, at : at + length, :]
            if j:
                part = part + acc[:, c * LANES : (c + 1) * LANES]
            if j < KS - 1:
                acc[:, c * LANES : (c + 1) * LANES] = part
            else:
                gfour[:, 3 * ATT + c * LANES : 3 * ATT + (c + 1) * LANES] = part.astype(bf16)
                gv_ref[CB : CB + 1, c * LANES : (c + 1) * LANES] += jnp.sum(part, axis=0, keepdims=True)

    pump(6)
    gkc = gca * qkvc_ref[:, 0:ATT].astype(f32)
    gquery = gq[...] + gca * kc_ref[...].astype(f32)
    add(QB, gquery)
    gfour[:, 0:ATT] = gquery.astype(bf16)
    add(PB, gkc)
    gkc = gkc.astype(bf16)
    gpw_ref[...] += tn(dep_ref[...], gkc)
    for c in range(3):
        x = nt(gkc, pw_ref[c * 256 : (c + 1) * 256, :])
        ds[2 * c, 8 : 8 + length, :] = x[:, 0:LANES]
        ds[2 * c + 1, 8 : 8 + length, :] = x[:, LANES:]
    pump(7)
    for m in range(4):
        gp_ref[:, m * ATT : (m + 1) * ATT] += tn(tok_ref[...], gfour[:, m * ATT : (m + 1) * ATT])

    pump(8)
    step = 64
    for c in range(6):
        cols = slice(c * LANES, (c + 1) * LANES)
        w = [vec_ref[DW + j : DW + j + 1, cols] for j in range(KS)]
        sums = [None] * KS
        if c % 2 == 0:
            direct = nt(gfour[...], wp_ref[c * LANES : (c + 2) * LANES, :])
        for r in range(0, length, step):
            tok = tok_ref[r : r + step, cols].astype(f32)
            total = gf_ref[r : r + step, cols].astype(f32) + direct[r : r + step, (c % 2) * LANES : (c % 2 + 1) * LANES]
            for j in range(KS):
                at = 8 + r + j - HALF
                u = ds[c, at : at + step, :]
                if j != HALF:
                    u = u * tm[j, r : r + step, :]
                total = total + w[KS - 1 - j] * u
                u = tok * u
                part = u[0:8]
                for s in range(8, step, 8):
                    part = part + u[s : s + 8]
                sums[j] = part if r == 0 else sums[j] + part
            gt_ref[r : r + step, cols] = total.astype(bf16)
        for j in range(KS):
            gv_ref[DW + KS - 1 - j : DW + KS - j, cols] += jnp.sum(sums[j], axis=0, keepdims=True)
    pump(9)


BWD_POINTS = 10
FIRST_AT, SECOND_AT, THIRD_AT = (2, 3, 6, 10), (5, 9, 13, 15), (9, 13, 16, 17)
SETTLE_AT, TAKE_AT = 21, 26


def run_back(first, second, part, va, tokens, lengths, saved, gf, gj, wp, pw, kw, vec):
    outer, inner = lax.axis_size("dp"), lax.axis_size("fsdp")
    qkvc, kc, dep, ca, taps, joined, lse = saved
    rows, count = lengths.shape[0], tokens.shape[0]
    length = count // rows
    lead = max(first.chunk, second.chunk)
    tall = -(-max(3 * KS * length, first.count * first.chunk) // 16) * 16
    scratch = row_scratch(length) + [
        VM((3, length + 16, LANES), f32),
        VM((1, length + 16, LANES), f32),
        VM((tall, LANES), bf16),
        VM((length, ATT), f32),
        VM((length, 4 * ATT), bf16),
        VM((length, ATT), f32),
    ]
    grads = [VM((D, 4 * ATT), f32), VM((D, ATT), f32), VM((ATT, LANES), f32), VM((VROWS, FF), f32)]
    more = [
        VM((first.rows + 2 * lead + 16, LANES), f32),
        VM((max(first.small * first.chunk, 384), LANES), f32),
        VM((512, LANES), f32),
    ]
    n, m = len(scratch), len(Scatter.scratch(first, inner))

    def body(part_ref, va_ref, *refs):
        ours, (gt_ref, own_ref), refs = refs[:15], refs[15:17], refs[17:]
        rows_refs, sums, refs = refs[:n], refs[n : n + 4], refs[n + 4 :]
        (out, flat, kwt), refs = refs[:3], refs[3:]
        gp_ref, gpw_ref, gkw_ref, gv_ref = sums
        stage = rows_refs[8]
        place = Place(outer, inner)
        a = Scatter(first, place, lambda v: stage.at[pl.ds(v * first.chunk, first.chunk)], out, lead, refs[:m], True)
        b = Scatter(second, place, lambda v: part_ref.at[v], out, lead, refs[m:], False)

        def begin():
            out[...] = jnp.zeros_like(out)
            place.all_here()
            b.core()

        def end():
            gv_ref[...] += va_ref[...]
            pack_small(flat, gkw_ref, gv_ref, kwt)
            to_frames(
                first,
                Rows(stage, first.chunk),
                [(gp_ref, D, ATT, k * ATT) for k in range(4)] + [(gpw_ref, D, ATT, 0)],
                flat,
            )
            steps = a.sums()
            a.core(*a.far[:2])
            for k, step in enumerate(steps):
                if k < len(a.far) - 2:
                    a.core(a.far[2 + k])
                step()
            b.finish()
            a.settle()
            a.take()
            a.finish()
            own_ref[...] = out[lead : lead + first.rows, :]

        due = [(0, 0, begin)]
        for step, spots in ((b.first, FIRST_AT), (b.second, SECOND_AT), (b.third, THIRD_AT)):
            steps = [lambda step=step, d=d: step(d) for d in b.far]
            due += spread_over(steps, rows, BWD_POINTS, list(spots) + [spots[-1]] * (len(steps) - len(spots)))
        due += spread_over([b.settle, b.take], rows, BWD_POINTS, (SETTLE_AT, TAKE_AT))
        pump = pumped(due + [(rows - 1, BWD_POINTS - 1, end)])
        pl.when(pl.program_id(0) == 0)(place.call)
        bwd_kernel(length, pump, *ours, gt_ref, *sums, *rows_refs)

    full = pl.BlockSpec(memory_space=VM)
    return pl.pallas_call(
        body,
        grid=(rows,),
        out_shape=[jax.ShapeDtypeStruct((count, D), bf16), jax.ShapeDtypeStruct((first.rows, LANES), f32)],
        in_specs=[
            pl.BlockSpec(memory_space=pl.ANY),
            full,
            pl.BlockSpec(memory_space=pltpu.SMEM),
            blocked(length, D),
            blocked(length, 4 * ATT),
            blocked(length, ATT),
            blocked(length, D),
            blocked(length, ATT),
            blocked(length, LANES),
            blocked(length, D),
            pl.BlockSpec((1, 8, length), lambda r: (r, 0, 0)),
            blocked(length, D),
            blocked(length, D),
            full,
            full,
            full,
            full,
        ],
        out_specs=[blocked(length, D), full],
        scratch_shapes=scratch + grads + more + Scatter.scratch(first, inner) + Scatter.scratch(second, inner),
        compiler_params=pltpu.CompilerParams(vmem_limit_bytes=VMEM_LIMIT, collective_id=1, has_side_effects=True),
        name="back",
    )(part, va, lengths, tokens, qkvc, kc, dep, ca, taps, joined, lse, gf, gj, wp, pw, kw, vec)


def shards(tokens, doc_lengths, params, cotangent):
    rows = params.shape[0] // LANES
    outer, inner = lax.axis_size("dp"), lax.axis_size("fsdp")
    first, second = sections(outer * inner, rows, inner)
    *saved, dw, fi, fo, wp, pw, kw, vec = run_front(first, second, params.reshape(rows, LANES), tokens, doc_lengths)
    output, gf, gj, part, va = run_mid(second, tokens, doc_lengths, saved[5], cotangent, dw, fi, fo, vec)
    gt, own_grad = run_back(first, second, part, va, tokens, doc_lengths, saved, gf, gj, wp, pw, kw, vec)
    return output, gt, own_grad.reshape(rows * LANES)


def solution(mesh):
    axes = ("dp", "fsdp")
    placed = (P(axes, None), P(axes, None), P(axes), P(axes, None))
    return jax.shard_map(
        shards,
        mesh=mesh,
        in_specs=placed,
        out_specs=(P(axes, None), P(axes, None), P(axes)),
        check_vma=False,
    )
```

```python
import math

import jax
import jax.numpy as jnp
from jax import lax
from jax.experimental import pallas as pl
from jax.experimental.pallas import tpu as pltpu
from jax.sharding import PartitionSpec as P

D = 768
HEADS = 6
HEAD_DIM = 64
ATT = HEADS * HEAD_DIM
FF = 3072
GROUPS = 2
KS = 9
HALF = KS // 2
SLOTS = 16
EPS = 1e-12
LANES = 128
NEG = -1e30
BIG = 3e38
SCALE = HEAD_DIM ** (-0.5)

f32 = jnp.float32
bf16 = jnp.bfloat16
i32 = jnp.int32

FIRST = 5 * D * ATT // LANES
MATRICES = FIRST + (D * D + 2 * D * FF // GROUPS) // LANES
DEPTH_AT = 0
KERNEL_AT = KS * D // LANES
BIAS_AT = KERNEL_AT + ATT * HEADS * KS // LANES
TAIL_AT = BIAS_AT + 4 * ATT // LANES
SMALL = TAIL_AT + 61
KB = HEADS * KS

QB, VB, CB, PB, KBR, DB, N1G, N1S, FIB, FOB, N2G, N2S, DW = range(13)
VROWS = 24
TAIL = [(DB, 6), (N1G, 6), (N1S, 6), (FIB, 24), (FOB, 6), (N2G, 6), (N2S, 6)]

VM = pltpu.VMEM
VMEM_LIMIT = 62 * 1024 * 1024


def nn(a, b):
    return lax.dot_general(a, b, (((1,), (0,)), ((), ())), preferred_element_type=f32)


def nt(a, b):
    return lax.dot_general(a, b, (((1,), (1,)), ((), ())), preferred_element_type=f32)


def tn(a, b):
    return lax.dot_general(a, b, (((0,), (0,)), ((), ())), preferred_element_type=f32)


def iota(shape, axis):
    return lax.broadcasted_iota(i32, shape, axis)


def loop(count, body, unroll=1):
    def step(i, carry):
        body(i)
        return carry

    lax.fori_loop(0, count, step, 0, unroll=unroll)


def tap_perm():
    k, n = iota((LANES, LANES), 0), iota((LANES, LANES), 1)
    head, tap = n & 7, n >> 3
    return jnp.where((k == head * KS + tap) & (head < HEADS) & (tap < KS), 1.0, 0.0).astype(bf16)


def used_taps(shape):
    n = iota(shape, len(shape) - 1)
    return ((n & 7) < HEADS) & ((n >> 3) < KS)


def padded(rows):
    return -(-rows // 16) * 16


class Section:
    def __init__(self, base, kinds, chunk, small, rows, count, inner):
        self.base, self.chunk, self.rows, self.count, self.inner = base, chunk, rows, count, inner
        self.main = sum(n for n, _ in kinds)
        self.small = -(-SMALL // chunk) if small else 0
        self.kinds = kinds + ([(self.small, 1)] if small else [])
        self.used = self.main + self.small
        self.pieces = -(-rows // chunk) + 1
        self.slots = self.pieces + self.small
        self.sources = (chunk - 2) // rows + 2
        self.lead = -(-base // rows)

    def seat(self, v, pick=jnp.where):
        q, r, n = v // 3, v % 3, self.count
        if self.small:
            near = pick(q < n // 4, r * (n // 4) + q, 3 * (n // 4) + v - 3 * (n // 4))
            return pick(v < self.main, near, n - self.small + v - self.main)
        return pick(r < 2, self.lead + 2 * q + r, q)

    def chunk_at(self, d):
        n = self.count
        if self.small:
            quarter = n // 4
            v = jnp.where(d < 3 * quarter, 3 * lax.rem(d, quarter) + d // quarter, d)
            v = jnp.where(v < self.main, v, self.used)
            return jnp.where(d >= n - self.small, self.main + d - (n - self.small), v)
        t = d - self.lead
        v = jnp.where(d < self.main // 3, 3 * d + 2, self.used)
        return jnp.where((t >= 0) & (t < 2 * self.main // 3), 3 * (t // 2) + lax.rem(t, 2), v)

    def start(self, v):
        at = self.base + v * self.chunk
        if self.small:
            at = jnp.where(v >= self.main, MATRICES + (v - self.main) * self.chunk, at)
        return at

    def first_piece(self, i):
        return jnp.maximum(self.rows * i - self.base, 0) // self.chunk

    def of_owner(self, i, k):
        if k < self.pieces:
            v = self.first_piece(i) + k
            ok = v < self.main
        else:
            v = self.main + k - self.pieces + 0 * i
            ok = v >= 0
        at = self.start(v)
        return v, ok & (at < self.rows * (i + 1)) & (at + self.chunk > self.rows * i)

    def of_chunk(self, v, s):
        i = self.start(v) // self.rows + s
        return i, (v < self.used) & (i < self.count) & (self.rows * i < self.start(v) + self.chunk)

    def source_of(self, v, i):
        return i - self.start(v) // self.rows

    def slot_of(self, v, i):
        return jnp.where(v < self.main, v - self.first_piece(i), self.pieces + v - self.main)

    def by_kind(self, v, action):
        at, seen = 0, {}
        for n, per in self.kinds:
            seen.setdefault(per, []).append((at, at + n))
            at += n
        for per, spans in seen.items():
            ok = False
            for lo, hi in spans:
                ok = ((v >= lo) & (v < hi)) | ok
            pl.when(ok)(lambda per=per: action(per))


def sections(count, rows, inner):
    big, little = 24576 // count, 12288 // count
    first = Section(0, [(FIRST // little, 3)], little, True, rows, count, inner)
    kinds = [(D * n // LANES // big, n // LANES) for n in (D, FF // GROUPS)] + [(FF * 3 // big, 3)]
    return first, Section(FIRST, kinds, big, False, rows, count, inner)


class Rows:
    def __init__(self, ref, chunk):
        self.ref, self.chunk = ref, chunk

    def __setitem__(self, where, value):
        v, rows, _ = where
        self.ref[v * self.chunk + rows.start : v * self.chunk + rows.stop, :] = value


def choose(ok, a, b):
    return a if ok else b


def pieces_of(sect, matrices):
    v = 0
    for ref, height, width, col in matrices:
        per = width // LANES
        tall = sect.chunk // per
        for r in range(0, height, tall):
            for c in range(per):
                cols = slice(col + c * LANES, col + (c + 1) * LANES)
                yield sect.seat(v, choose), slice(c * tall, (c + 1) * tall), ref, slice(r, r + tall), cols
            v += 1


def to_frames(sect, part, matrices, small=None):
    for seat, rows, ref, r, c in pieces_of(sect, matrices):
        part[seat, rows, :] = ref[r, c].astype(bf16)
    for k in range(sect.small):
        part[sect.seat(sect.main + k, choose), slice(0, sect.chunk), :] = small[
            k * sect.chunk : (k + 1) * sect.chunk, :
        ].astype(bf16)
    for d in set(range(sect.count)) - {sect.seat(v, choose) for v in range(sect.used)}:
        part[d, slice(0, sect.chunk), :] = jnp.zeros((sect.chunk, LANES), bf16)


def from_frames(sect, buf, matrices, small=None):
    for seat, rows, ref, r, c in pieces_of(sect, matrices):
        ref[r, c] = buf[seat, rows, :]
    for k in range(sect.small):
        small[k * sect.chunk : (k + 1) * sect.chunk, :] = buf[sect.seat(sect.main + k, choose)].astype(f32)


def unpack_small(flat, kw_ref, vec_ref, kwt):
    vec_ref[...] = jnp.zeros_like(vec_ref)
    for row in range(4):
        for c in range(3):
            at = BIAS_AT + row * 3 + c
            vec_ref[row : row + 1, c * LANES : (c + 1) * LANES] = flat[at : at + 1, :]
    for j in range(KS):
        for c in range(6):
            at = DEPTH_AT + j * 6 + c
            vec_ref[DW + j : DW + j + 1, c * LANES : (c + 1) * LANES] = flat[at : at + 1, :]
    at = TAIL_AT
    lane = iota((64, LANES), 1)
    first = pltpu.roll(flat[at : at + 64, :], LANES - KB, 1)
    second = pltpu.roll(flat[at + 1 : at + 65, :], LANES - KB, 1)
    kwt[0:64, :] = jnp.where(lane < LANES - KB, first, second)
    at = 0
    for row, many in TAIL:
        for c in range(many):
            vec_ref[row : row + 1, c * LANES : (c + 1) * LANES] = kwt[at + c : at + c + 1, :]
        at += many
    perm = tap_perm()
    lane8 = iota((16, LANES), 1)
    kb = jnp.broadcast_to(flat[TAIL_AT : TAIL_AT + 1, :], (16, LANES))
    kb = nn(jnp.where(lane8 < KB, kb, 0.0).astype(bf16), perm)
    kb = jnp.where(used_taps((16, LANES)), kb, NEG)
    vec_ref[KBR : KBR + 1, 0:LANES] = kb[0:1]

    lane = iota((8, LANES), 1)
    for a in range(64):
        c0, ln = divmod(a * KB, LANES)
        at = KERNEL_AT + c0
        x = pltpu.roll(flat[pl.ds(at, 8, stride=27), :], (LANES - ln) % LANES, 1)
        if ln + KB > LANES:
            y = pltpu.roll(flat[pl.ds(at + 1, 8, stride=27), :], (LANES - ln) % LANES, 1)
            x = jnp.where(lane < LANES - ln, x, y)
        kwt[pl.ds(a, 8, stride=64), :] = jnp.where(lane < KB, x, 0.0)
    kw_ref[...] = nn(kwt[0:ATT, :].astype(bf16), perm).astype(bf16)


def pack_small(flat, gkw_ref, vec, kwt):
    flat[...] = jnp.zeros_like(flat)
    perm = tap_perm()
    kwt[...] = jnp.zeros_like(kwt)
    kwt[0:ATT, :] = nt(gkw_ref[...].astype(bf16), perm)
    lane = iota((8, LANES), 1)
    for a in range(64):
        c0, ln = divmod(a * KB, LANES)
        at = KERNEL_AT + c0
        x = pltpu.roll(kwt[pl.ds(a, 8, stride=64), :], ln, 1)
        if ln + KB > LANES:
            flat[pl.ds(at, 8, stride=27), :] += jnp.where(lane >= ln, x, 0.0)
            flat[pl.ds(at + 1, 8, stride=27), :] += jnp.where(lane < ln, x, 0.0)
        else:
            flat[pl.ds(at, 8, stride=27), :] += x
    for row in range(4):
        for c in range(3):
            at = BIAS_AT + row * 3 + c
            flat[at : at + 1, :] = vec[row : row + 1, c * LANES : (c + 1) * LANES]
    for j in range(KS):
        for c in range(6):
            at = DEPTH_AT + j * 6 + c
            flat[at : at + 1, :] = vec[DW + j : DW + j + 1, c * LANES : (c + 1) * LANES]
    kwt[...] = jnp.zeros_like(kwt)
    at = 8
    for row, many in TAIL:
        for c in range(many):
            kwt[at + c : at + c + 1, :] = vec[row : row + 1, c * LANES : (c + 1) * LANES]
        at += many
    lane = iota((72, LANES), 1)
    before = pltpu.roll(kwt[7:79, :], KB, 1)
    here = pltpu.roll(kwt[8:80, :], KB, 1)
    at = TAIL_AT
    flat[at : at + 72, :] = jnp.where(lane < KB, before, here)
    kb = jnp.broadcast_to(vec[KBR : KBR + 1, 0:LANES], (16, LANES))
    kb = nt(jnp.where(used_taps((16, LANES)), kb, 0.0).astype(bf16), perm)
    lane = iota((1, LANES), 1)
    flat[at : at + 1, :] = jnp.where(lane < KB, kb[0:1], flat[at : at + 1, :])


class Place:
    def __init__(self, outer, inner):
        self.outer, self.inner, self.count = outer, inner, outer * inner
        self.lines = inner // 2
        dp, fs = lax.axis_index("dp"), lax.axis_index("fsdp")
        self.y, self.x, self.z, self.c = dp // 2, lax.rem(dp, 2), fs // 2, lax.rem(fs, 2)
        self.me = dp * inner + fs

    def coords(self, dy=0, dx=0, z=None, dc=0):
        def flip(v, d):
            return 1 - v if d else v

        z = self.z if z is None else z
        return flip(self.y, dy) * 2 + flip(self.x, dx), z * 2 + flip(self.c, dc)

    def index(self, **d):
        o, i = self.coords(**d)
        return o * self.inner + i

    def device(self, n):
        return n // self.inner, lax.rem(n, self.inner)

    def item(self, t):
        s = (t + 1) // 2
        z = self.z - s if t % 2 else self.z + s
        return z, (z >= 0) & (z < self.lines), s, t % 2 == 1

    def call(self):
        barrier = pltpu.get_barrier_semaphore()
        for n in range(1, self.count):
            peer = self.device(lax.rem(self.me + n, self.count))
            pl.semaphore_signal(barrier, inc=1, device_id=peer, device_id_type=pl.DeviceIdType.MESH)

    def all_here(self):
        pl.semaphore_wait(pltpu.get_barrier_semaphore(), self.count - 1)


class Copies:
    def __init__(self, send, recv):
        self.send, self.recv, self.used, self.made = send, recv, 0, []

    def start(self, src, dst, peer, slot, ok=None, group=None):
        number = self.used if group is None else group
        if group is None:
            self.used += 1
        assert number < self.send.shape[0]

        def make():
            return pltpu.make_async_remote_copy(
                src_ref=src(),
                dst_ref=dst(),
                send_sem=self.send.at[number],
                recv_sem=self.recv.at[slot() if callable(slot) else slot],
                device_id=peer(),
                device_id_type=pl.DeviceIdType.MESH,
            )

        if group is None:
            self.made.append((make, ok))
        guarded(ok, lambda: make().start())

    def sent(self, ref, group):
        pltpu.make_async_copy(ref, ref, self.send.at[group]).wait()

    def arrived(self, dst, slot, ok=None):
        def wait():
            ref = dst()
            pltpu.make_async_copy(ref, ref, self.recv.at[slot]).wait()

        guarded(ok, wait)

    def finish(self):
        for make, ok in self.made:
            guarded(ok, lambda make=make: make().wait_send())


def guarded(ok, action):
    if ok is None:
        action()
    else:
        pl.when(ok())(action)


def half_of(chunk):
    return -(-chunk // 32) * 16


class Gather:
    @staticmethod
    def scratch(sect, inner):
        lines = inner // 2
        items = 2 * lines - 1
        return [
            VM((sect.count, sect.chunk, LANES), bf16),
            VM((sect.slots, sect.chunk, LANES), bf16),
            VM((sect.sources, sect.chunk, LANES), bf16),
            VM((sect.chunk, LANES), f32),
            pltpu.SemaphoreType.DMA((sect.slots + 10 * items + 4,)),
            pltpu.SemaphoreType.DMA((sect.sources + 9 * items,)),
        ]

    def __init__(self, sect, place, ownf, lead, scratch):
        self.sect, self.place, self.ownf, self.lead = sect, place, ownf, lead
        self.buf, self.win, self.land, self.frame, send, recv = scratch
        self.copies = Copies(send, recv)
        n = 2 * place.lines - 1
        self.items = n
        self.Z, self.X, self.Y, self.A, self.B, self.CZ, self.CX, self.CY, self.CD = (sect.sources + n * k for k in range(9))
        cut = half_of(sect.chunk)
        self.half = {"a": pl.ds(0, cut), "b": pl.ds(cut, sect.chunk - cut)}

    def offer(self):
        for k in range(self.sect.slots):
            self.give(k)

    def give(self, k):
        sect, place, me = self.sect, self.place, self.place.me
        v, ok = sect.of_owner(me, k)

        @pl.when(ok)
        def _():
            at = self.lead + sect.start(v) - sect.rows * me
            self.win[k] = self.ownf[pl.ds(at, sect.chunk), :].astype(bf16)

        @pl.when(ok & (sect.seat(v) == me))
        def _():
            self.land[sect.source_of(v, me)] = self.win[k]

        def chunk():
            return sect.of_owner(me, k)[0]

        def away():
            v, ok = sect.of_owner(me, k)
            return ok & (sect.seat(v) != me)

        def source():
            return jnp.clip(sect.source_of(chunk(), me), 0, sect.sources - 1)

        def seat():
            return jnp.clip(sect.seat(chunk()), 0, sect.count - 1)

        self.copies.start(lambda: self.win.at[k], lambda: self.land.at[source()], lambda: place.device(seat()), source, away)

    def form(self):
        sect, me = self.sect, self.place.me
        v = sect.chunk_at(me)
        row = iota((sect.chunk, LANES), 0) + sect.start(v)
        x = None
        for s in range(sect.sources):
            i, ok = sect.of_chunk(v, s)
            self.copies.arrived(lambda: self.land.at[s], s, lambda: ok & (i != me))
            here = self.land[s].astype(f32)
            x = here if x is None else jnp.where(row >= sect.rows * i, here, x)
        self.frame[...] = x

        def settle(per):
            tall = sect.chunk // per
            for c in range(per):
                self.buf[me, c * tall : (c + 1) * tall, :] = self.frame[pl.ds(c, tall, stride=per), :].astype(bf16)

        sect.by_kind(v, settle)

        @pl.when(v >= sect.used)
        def _():
            self.buf[me] = jnp.zeros((sect.chunk, LANES), bf16)

        self.pass_on(0)

    def ref(self, t, which=None, **way):
        def make():
            at = self.place.index(z=self.place.item(t)[0], **way)
            return self.buf.at[at] if which is None else self.buf.at[at, self.half[which]]

        return make

    def ok(self, t):
        return None if t == 0 else lambda: self.place.item(t)[1]

    def same(self, ref, peer, slot, ok):
        self.copies.start(ref, ref, peer, slot, ok)

    def beside(self, **way):
        return lambda: self.place.coords(**way)

    def pass_on(self, t):
        place = self.place
        _, _, s, below = place.item(t)
        for way in (1, -1) if t == 0 else ((1,) if below else (-1,)):
            slot = 2 * s + 1 if way > 0 else 2 * s + 2

            def inside(way=way):
                there = place.z + way
                good = (there >= 0) & (there < place.lines)
                return good if t == 0 else good & place.item(t)[1]

            if slot < self.items:
                self.same(self.ref(t), lambda way=way: place.coords(z=place.z + way), self.Z + slot, inside)
        ok = self.ok(t)
        self.same(self.ref(t), self.beside(dx=1), self.X + t, ok)
        self.same(self.ref(t), self.beside(dy=1), self.Y + t, ok)
        self.same(self.ref(t), self.beside(dc=1), self.CZ + t, ok)

    def at_distance(self, s):
        return [0] if s == 0 else [2 * s - 1, 2 * s]

    def along(self, s):
        for t in self.at_distance(s):
            self.copies.arrived(self.ref(t), self.Z + t, self.ok(t))
            self.pass_on(t)

    def across(self, s):
        for t in self.at_distance(s):
            ok = self.ok(t)
            self.copies.arrived(self.ref(t, dx=1), self.X + t, ok)
            self.same(self.ref(t, "a", dx=1), self.beside(dy=1), self.A + t, ok)
            self.same(self.ref(t, dx=1), self.beside(dc=1), self.CX + t, ok)
            self.copies.arrived(self.ref(t, dy=1), self.Y + t, ok)
            self.same(self.ref(t, "b", dy=1), self.beside(dx=1), self.B + t, ok)
            self.same(self.ref(t, dy=1), self.beside(dc=1), self.CY + t, ok)

    def diagonal(self):
        for t in range(self.items):
            ok = self.ok(t)
            self.copies.arrived(self.ref(t, "a", dy=1, dx=1), self.A + t, ok)
            self.copies.arrived(self.ref(t, "b", dy=1, dx=1), self.B + t, ok)
            self.same(self.ref(t, dy=1, dx=1), self.beside(dc=1), self.CD + t, ok)

    def rest(self):
        for t in range(self.items):
            for k, way in ((self.CZ, {}), (self.CX, {"dx": 1}), (self.CY, {"dy": 1}), (self.CD, {"dy": 1, "dx": 1})):
                self.copies.arrived(self.ref(t, dc=1, **way), k + t, self.ok(t))


class Scatter:
    @staticmethod
    def scratch(sect, inner):
        lines = inner // 2
        cut = half_of(sect.chunk)
        return [
            VM((4 * lines, sect.chunk, LANES), bf16),
            VM((4 * lines, sect.chunk, LANES), bf16),
            VM((2 * lines, cut, LANES), bf16),
            VM((2 * lines, sect.chunk - cut, LANES), bf16),
            VM((lines, sect.chunk - cut, LANES), bf16),
            VM((lines, cut, LANES), bf16),
            VM((lines, sect.chunk, LANES), bf16),
            VM((sect.chunk, LANES), f32),
            VM((sect.chunk, LANES), f32),
            VM((sect.chunk, LANES), bf16),
            VM((sect.slots, sect.chunk, LANES), bf16),
            pltpu.SemaphoreType.DMA((sect.sources + 6,)),
            pltpu.SemaphoreType.DMA((11 * lines + sect.slots,)),
            pltpu.SemaphoreType.DMA((4 * lines,)),
        ]

    def __init__(self, sect, place, part, out, lead, scratch, close):
        self.close = close
        self.sect, self.place, self.part, self.out, self.lead = sect, place, part, out, lead
        (self.work, self.rc, self.ry, self.rx, self.ry2, self.rx2, self.rz, self.frame, self.flat, self.low, self.land,
         send, recv, self.near) = scratch
        self.copies = Copies(send, recv)
        lines = place.lines
        self.lines = lines
        cut = half_of(sect.chunk)
        self.a, self.b = pl.ds(0, cut), pl.ds(cut, sect.chunk - cut)
        self.C, self.YA, self.XB, self.XA, self.YB, self.Z, self.O = (lines * k for k in (0, 4, 6, 8, 9, 10, 11))
        self.far = list(range(1, lines)) + [0]
        self.group = sect.sources

    def sums(self):
        out = []
        for n in range(self.lines + 2):
            for lag, step in ((0, self.first), (1, self.second), (2, self.third)):
                if 0 <= n - lag < self.lines:
                    out.append(lambda step=step, d=self.far[n - lag]: step(d))
        return out

    def z(self, d):
        return lax.rem(self.place.z + d, self.lines) if d else self.place.z

    def at(self, dy, dx, d):
        return (dy * 2 + dx) * self.lines + d

    def own(self, dy, dx, d):
        k = self.at(dy, dx, d)
        there = self.place.index(dy=dy, dx=dx, z=self.z(d))
        return pltpu.make_async_copy(self.part(there), self.work.at[k], self.near.at[k])

    def core(self, *places):
        place = self.place

        def give(dy, dx, d):
            k = self.at(dy, dx, d)
            self.copies.start(
                lambda: self.part(place.index(dy=dy, dx=dx, z=self.z(d), dc=1)),
                lambda: self.rc.at[k],
                lambda: place.coords(dc=1),
                self.C + k,
                group=self.group,
            )
            if not self.close:
                self.own(dy, dx, d).start()

        for d in places or self.far:
            for dy, dx in ((1, 1), (1, 0), (0, 1), (0, 0)):
                give(dy, dx, d)

    def send(self, k, rows, buf, n, way, slot, group):
        self.copies.start(
            lambda: self.work.at[k, rows],
            lambda: buf.at[n],
            lambda: self.place.coords(**way),
            slot,
            group=self.group + group,
        )

    def finish(self):
        for k, ref in enumerate((self.rc, self.ry, self.rx, self.rx2, self.ry2, self.rz.at[pl.ds(1, self.lines - 1)])):
            self.copies.sent(ref, self.group + k)
        self.copies.finish()

    def got(self, buf, n, slot):
        self.copies.arrived(lambda: buf.at[n], slot)

    def plus(self, k, rows, other):
        self.work[k, rows] = (self.work[k, rows].astype(f32) + other.astype(f32)).astype(bf16)

    def first(self, d):
        lines = self.lines
        for dy, dx in ((1, 1), (1, 0), (0, 1), (0, 0)):
            k = self.at(dy, dx, d)
            if self.close:
                self.got(self.rc, k, self.C + k)
                mine = self.part(self.place.index(dy=dy, dx=dx, z=self.z(d)))[...]
                self.work[k] = (mine.astype(f32) + self.rc[k].astype(f32)).astype(bf16)
            else:
                self.own(dy, dx, d).wait()
                self.got(self.rc, k, self.C + k)
                self.plus(k, pl.ds(0, self.sect.chunk), self.rc[k])
            if dy:
                self.send(k, self.a, self.ry, dx * lines + d, {"dy": 1}, self.YA + dx * lines + d, 1)
            if dx:
                self.send(k, self.b, self.rx, dy * lines + d, {"dx": 1}, self.XB + dy * lines + d, 2)

    def second(self, d):
        n = self.lines + d
        self.got(self.ry, n, self.YA + n)
        self.plus(self.at(0, 1, d), self.a, self.ry[n])
        self.send(self.at(0, 1, d), self.a, self.rx2, d, {"dx": 1}, self.XA + d, 3)
        self.got(self.rx, n, self.XB + n)
        self.plus(self.at(1, 0, d), self.b, self.rx[n])
        self.send(self.at(1, 0, d), self.b, self.ry2, d, {"dy": 1}, self.YB + d, 4)

    def third(self, d):
        k = self.at(0, 0, d)
        self.got(self.ry, d, self.YA + d)
        self.got(self.rx, d, self.XB + d)
        self.got(self.rx2, d, self.XA + d)
        self.got(self.ry2, d, self.YB + d)
        self.plus(k, self.a, self.ry[d].astype(f32) + self.rx2[d].astype(f32))
        self.plus(k, self.b, self.rx[d].astype(f32) + self.ry2[d].astype(f32))
        if d:
            self.copies.start(
                lambda: self.work.at[k],
                lambda: self.rz.at[d],
                lambda: self.place.coords(z=self.z(d)),
                self.Z + d,
                group=self.group + 5,
            )

    def settle(self):
        sect, me = self.sect, self.place.me
        total = self.work[self.at(0, 0, 0)].astype(f32)
        for d in range(1, self.lines):
            self.got(self.rz, d, self.Z + d)
            total = total + self.rz[d].astype(f32)
        self.frame[...] = total

        def spread(per):
            tall = sect.chunk // per
            for c in range(per):
                self.flat[pl.ds(c, tall, stride=per), :] = self.frame[c * tall : (c + 1) * tall, :]

        self.flat[...] = total
        sect.by_kind(sect.chunk_at(me), spread)
        self.low[...] = self.flat[...].astype(bf16)
        for s in range(sect.sources):
            self.give(s)

    def give(self, s):
        sect, me = self.sect, self.place.me
        i, ok = sect.of_chunk(sect.chunk_at(me), s)

        @pl.when(ok & (i == me))
        def _():
            self.land[sect.slot_of(sect.chunk_at(me), i)] = self.low[...]

        def owner():
            return jnp.minimum(sect.of_chunk(sect.chunk_at(me), s)[0], sect.count - 1)

        def slot():
            return jnp.clip(sect.slot_of(sect.chunk_at(me), owner()), 0, sect.slots - 1)

        def away():
            i, ok = sect.of_chunk(sect.chunk_at(me), s)
            return ok & (i != me)

        self.copies.start(
            lambda: self.low, lambda: self.land.at[slot()], lambda: self.place.device(owner()), lambda: self.O + slot(), away
        )

    def take(self):
        sect, me = self.sect, self.place.me
        for k in range(sect.slots):
            v, ok = sect.of_owner(me, k)
            self.copies.arrived(lambda: self.land.at[k], self.O + k, lambda: ok & (sect.seat(v) != me))

            @pl.when(ok)
            def _():
                at = self.lead + sect.start(v) - sect.rows * me
                self.out[pl.ds(at, sect.chunk), :] = self.land[k].astype(f32)


def pumped(due):
    row = pl.program_id(0)

    def pump(point):
        for r, p, step in due:
            if p == point:
                pl.when(row == r)(step)

    return pump


def spread_over(steps, rows, points, spots):
    end = rows * points - 1
    return [(min(n, end) // points, min(n, end) % points, step) for step, n in zip(steps, spots)]


def doc_marks(r, length, len_ref, dcol, tm, mb):
    t = iota((length, LANES), 0)
    u = iota((8, length), 1)
    ends = jnp.int32(0)
    d = jnp.zeros((length, LANES), i32)
    e = jnp.zeros((8, length), i32)
    for j in range(SLOTS):
        ends = ends + len_ref[r, j]
        d = d + (t >= ends).astype(i32)
        e = e + (u >= ends).astype(i32)
    dcol[0:8, :] = jnp.full((8, LANES), -1, i32)
    dcol[8 : 8 + length, :] = d
    dcol[8 + length : 16 + length, :] = jnp.full((8, LANES), -1, i32)
    for j in range(KS):
        at = 8 + j - HALF
        tm[j] = (dcol[at : at + length, :] == d).astype(f32)
    for c in range(length // LANES):
        mb[:, c * LANES : (c + 1) * LANES] = jnp.where(d == e[0:1, c * LANES : (c + 1) * LANES], BIG, NEG)


def tap_lanes(tm, length):
    tap = iota((length, LANES), 1) >> 3
    out = jnp.zeros((length, LANES), f32)
    for j in range(KS):
        out = jnp.where(tap == j, tm[j], out)
    return jnp.where(used_taps((length, LANES)), out, 0.0)


def over_taps(x, op):
    for s in (8, 16, 32, 64):
        x = op(x, pltpu.roll(x, s, 1))
    return x


def fill_emat(emat):
    k, c = iota((2 * LANES, ATT), 0) & (LANES - 1), iota((2 * LANES, ATT), 1)
    for j in range(KS):
        emat[:, j * ATT : (j + 1) * ATT] = jnp.where(k == j * 8 + (c >> 6), 1.0, 0.0).astype(bf16)


def two_parts(x):
    high = x.astype(bf16)
    return jnp.concatenate([high, (x - high.astype(f32)).astype(bf16)], axis=1)


def zero_pads(ref, length):
    for c in range(ref.shape[0]):
        ref[c, 0:8, :] = jnp.zeros((8, LANES), f32)
        ref[c, 8 + length : 16 + length, :] = jnp.zeros((8, LANES), f32)


def fwd_kernel(length, pump, len_ref, tok_ref, wp_ref, pw_ref, kw_ref, vec_ref,
               qkvc_ref, kc_ref, dep_ref, ca_ref, tap_ref, join_ref, lse_ref,
               xs, cs, dcol, tm, mb, emat, acc):
    row = pl.program_id(0)
    pump(0)
    pl.when(row > 0)(lambda: doc_marks(row, length, len_ref, dcol, tm, mb))
    pump(1)
    tok = tok_ref[...]
    zero_pads(xs, length)
    zero_pads(cs, length)
    for c in range(6):
        xs[c, 8 : 8 + length, :] = tok[:, c * LANES : (c + 1) * LANES].astype(f32)
    for m, bias in ((0, QB), (1, None), (2, VB), (3, CB)):
        x = nn(tok, wp_ref[:, m * ATT : (m + 1) * ATT])
        if bias is not None:
            x = x + vec_ref[bias : bias + 1, 0:ATT]
        x = x.astype(bf16)
        qkvc_ref[:, m * ATT : (m + 1) * ATT] = x
        if m == 3:
            for c in range(3):
                cs[c, 8 : 8 + length, :] = x[:, c * LANES : (c + 1) * LANES].astype(f32)

    pump(2)
    step = 64

    for c in range(6):
        w = [vec_ref[DW + j : DW + j + 1, c * LANES : (c + 1) * LANES] for j in range(KS)]
        for r in range(0, length, step):
            total = w[HALF] * xs[c, 8 + r : 8 + r + step, :]
            for j in range(KS):
                if j != HALF:
                    at = 8 + r + j - HALF
                    total = total + w[j] * (xs[c, at : at + step, :] * tm[j, r : r + step, :])
            dep_ref[r : r + step, c * LANES : (c + 1) * LANES] = total.astype(bf16)

    pump(3)
    keyconv = nn(dep_ref[...], pw_ref[...]) + vec_ref[PB : PB + 1, 0:ATT]
    kc_ref[...] = keyconv.astype(bf16)
    ca = (keyconv * qkvc_ref[:, 0:ATT].astype(f32)).astype(bf16)
    ca_ref[...] = ca
    logits = nn(ca, kw_ref[...]) + vec_ref[KBR : KBR + 1, 0:LANES]
    e = jnp.exp(logits - over_taps(logits, jnp.maximum))
    taps = e / over_taps(e, jnp.add)
    tap_ref[...] = taps
    spread = two_parts(taps * tap_lanes(tm, length))
    for j in range(KS):
        if j in (0, 4, 8):
            pump(4 + j // 4)
        if j % 2 == 0:
            t = nn(spread, emat[:, j * ATT : min(j + 2, KS) * ATT])
        for c in range(3):
            at, k = 8 + j - HALF, (j % 2 * 3 + c) * LANES
            part = t[:, k : k + LANES] * cs[c, at : at + length, :]
            if j:
                part = part + acc[:, c * LANES : (c + 1) * LANES]
            if j < KS - 1:
                acc[:, c * LANES : (c + 1) * LANES] = part
            else:
                join_ref[:, ATT + c * LANES : ATT + (c + 1) * LANES] = part.astype(bf16)

    for p in range(3):
        pump(7 + p)
        cols = slice(p * LANES, (p + 1) * LANES)
        q, k, v = (qkvc_ref[:, m * ATT + p * LANES : m * ATT + (p + 1) * LANES] for m in range(3))
        qs = q.astype(f32) * SCALE
        vt = v.astype(f32).T
        lane, sub = iota((length, LANES), 1), iota((LANES, length), 0)
        halves = []
        for h in range(2):
            qh = jnp.where((lane >= HEAD_DIM) == bool(h), qs, 0.0).astype(bf16)
            vh = jnp.where((sub >= HEAD_DIM) == bool(h), vt, 1.0).astype(bf16)
            z = jnp.minimum(nt(k, qh), mb[...])
            top = jnp.max(z, axis=0, keepdims=True)
            o = nn(vh, jnp.exp(z - top).astype(bf16))
            s = o[(1 - h) * HEAD_DIM : (1 - h) * HEAD_DIM + 1, :]
            lse_ref[0, 2 * p + h : 2 * p + h + 1, :] = top + jnp.log(s)
            halves.append(o[h * HEAD_DIM : (h + 1) * HEAD_DIM, :] / s)
        join_ref[:, cols] = jnp.concatenate(halves, axis=0).T.astype(bf16)
    pump(10)


def blocked(rows, cols):
    return pl.BlockSpec((rows, cols), lambda r: (r, 0))


def row_scratch(length):
    return [
        VM((6, length + 16, LANES), f32),
        VM((3, length + 16, LANES), f32),
        VM((length + 16, LANES), i32),
        VM((KS, length, LANES), f32),
        VM((length, length), f32),
        VM((2 * LANES, KS * ATT), bf16),
    ]


FWD_POINTS = 11
FWD_SPOTS = (2, 4, 8, 10, 14, 16, 20, 25, 99)


def run_front(first, second, own, tokens, lengths):
    outer, inner = lax.axis_size("dp"), lax.axis_size("fsdp")
    rows, count = lengths.shape[0], tokens.shape[0]
    length = count // rows
    scratch = row_scratch(length) + [VM((length, ATT), f32)]
    n = len(scratch)
    lead = max(first.chunk, second.chunk)
    more = [
        VM((first.rows + 2 * lead + 16, LANES), f32),
        VM((first.small * first.chunk, LANES), f32),
        VM((512, LANES), f32),
    ]
    m = len(Gather.scratch(first, inner))

    def body(own_ref, len_ref, tok_ref, *refs):
        outs, (dw_ref, fi_ref, fo_ref, wp_ref, pw_ref, kw_ref, vec_ref), refs = refs[:7], refs[7:14], refs[14:]
        rows_refs, (ownf, flat, kwt), refs = refs[:n], refs[n : n + 3], refs[n + 3 :]
        place = Place(outer, inner)
        a = Gather(first, place, ownf, lead, refs[:m])
        b = Gather(second, place, ownf, lead, refs[m:])

        def begin():
            place.call()
            ownf[...] = jnp.zeros_like(ownf)
            ownf[lead : lead + first.rows, :] = own_ref[...].astype(f32)
            _, _, dcol, tm, mb, emat, _ = rows_refs
            fill_emat(emat)
            place.all_here()
            a.offer()
            b.offer()
            doc_marks(0, length, len_ref, dcol, tm, mb)
            a.form()
            for s in range(1, place.lines):
                a.along(s)
                a.across(s - 1)
            a.across(place.lines - 1)
            b.form()
            a.diagonal()
            a.rest()
            from_frames(first, a.buf, [(wp_ref, D, ATT, k * ATT) for k in range(4)] + [(pw_ref, D, ATT, 0)], flat)
            unpack_small(flat, kw_ref, vec_ref, kwt)

        def end():
            a.copies.finish()
            b.rest()
            b.copies.finish()
            from_frames(second, b.buf, ((dw_ref, D, D, 0), (fi_ref, D, FF // GROUPS, 0), (fo_ref, FF, D // GROUPS, 0)))

        steps = []
        for s in range(1, place.lines):
            steps.append(lambda s=s: b.along(s))
            steps.append(lambda s=s: b.across(s - 1))
        steps += [lambda: b.across(place.lines - 1), b.diagonal, end]
        spots = FWD_SPOTS if len(steps) == len(FWD_SPOTS) else [99] * len(steps)
        pump = pumped([(0, 0, begin)] + spread_over(steps, rows, FWD_POINTS, spots))
        fwd_kernel(length, pump, len_ref, tok_ref, wp_ref, pw_ref, kw_ref, vec_ref, *outs, *rows_refs)

    full = pl.BlockSpec(memory_space=VM)
    return pl.pallas_call(
        body,
        grid=(rows,),
        out_shape=[
            jax.ShapeDtypeStruct((count, 4 * ATT), bf16),
            jax.ShapeDtypeStruct((count, ATT), bf16),
            jax.ShapeDtypeStruct((count, D), bf16),
            jax.ShapeDtypeStruct((count, ATT), bf16),
            jax.ShapeDtypeStruct((count, LANES), f32),
            jax.ShapeDtypeStruct((count, D), bf16),
            jax.ShapeDtypeStruct((rows, 8, length), f32),
            jax.ShapeDtypeStruct((D, D), bf16),
            jax.ShapeDtypeStruct((D, FF // GROUPS), bf16),
            jax.ShapeDtypeStruct((FF, D // GROUPS), bf16),
            jax.ShapeDtypeStruct((D, 4 * ATT), bf16),
            jax.ShapeDtypeStruct((D, ATT), bf16),
            jax.ShapeDtypeStruct((ATT, LANES), bf16),
            jax.ShapeDtypeStruct((VROWS, FF), f32),
        ],
        in_specs=[full, pl.BlockSpec(memory_space=pltpu.SMEM), blocked(length, D)],
        out_specs=[
            blocked(length, 4 * ATT),
            blocked(length, ATT),
            blocked(length, D),
            blocked(length, ATT),
            blocked(length, LANES),
            blocked(length, D),
            pl.BlockSpec((1, 8, length), lambda r: (r, 0, 0)),
        ]
        + [full] * 7,
        scratch_shapes=scratch + more + Gather.scratch(first, inner) + Gather.scratch(second, inner),
        compiler_params=pltpu.CompilerParams(vmem_limit_bytes=VMEM_LIMIT, collective_id=0, has_side_effects=True),
        name="front",
    )(own, lengths, tokens)


def mid_kernel(sect, length, len_ref, tok_ref, join_ref, cot_ref, dw_ref, fi_ref, fo_ref, vec_ref,
               out_ref, gf_ref, gj_ref, part_ref, gv_ref,
               gdw_ref, gfi_ref, gfo_ref, xh1, rs1, nl, act, slope, gsec, gsl, wide):
    row = pl.program_id(0)
    fg, dg = FF // GROUPS, D // GROUPS

    @pl.when(row == 0)
    def _():
        for ref in (gdw_ref, gfi_ref, gfo_ref, gv_ref):
            ref[...] = jnp.zeros_like(ref)

    used = jnp.int32(0)
    for j in range(SLOTS):
        used = used + len_ref[row, j]

    def vec(r, n=D):
        return vec_ref[r : r + 1, 0:n]

    step = 128
    halves = [slice(k * (length // 2), (k + 1) * (length // 2)) for k in range(2)]
    for rows in halves:
        gsec[rows, :] = nn(join_ref[rows, :], dw_ref[...])

    def norm1(i):
        at = slice(i * step, (i + 1) * step)
        z = gsec[at, :] + vec(DB) + tok_ref[at, :].astype(f32)
        z = z - jnp.mean(z, axis=1, keepdims=True)
        r = lax.rsqrt(jnp.mean(z * z, axis=1, keepdims=True) + EPS)
        x = z * r
        xh1[at, :] = x
        rs1[at, :] = jnp.broadcast_to(r, (step, LANES))
        nl[at, :] = (x * vec(N1G) + vec(N1S)).astype(bf16)

    for k in range(length // step):
        norm1(k)

    tile = 768
    per = fg // tile

    tiles = [(g, i) for g in range(GROUPS) for i in range(per)]

    def inner(n):
        g, i = tiles[n]
        for rows in halves if n == 0 else [slice(0, length)]:
            wide[n % 2, rows, :] = nn(nl[rows, g * dg : (g + 1) * dg], fi_ref[g * dg : (g + 1) * dg, i * tile : (i + 1) * tile])

    inner(0)
    for n, (g, i) in enumerate(tiles):
        if n + 1 < len(tiles):
            inner(n + 1)
        col = slice(g * fg + i * tile, g * fg + (i + 1) * tile)
        for r in range(0, length, 64):
            x = wide[n % 2, r : r + 64, :] + vec_ref[FIB : FIB + 1, col]
            phi = 0.5 * lax.erf(x * math.sqrt(0.5)) + 0.5
            e = jnp.exp2(x * x * (-0.5 / math.log(2.0)))
            act[r : r + 64, col] = (x * phi).astype(bf16)
            slope[r : r + 64, col] = (phi + x * (1.0 / math.sqrt(2.0 * math.pi)) * e).astype(bf16)

    for rows in halves:
        for g in range(GROUPS):
            gsec[rows, g * dg : (g + 1) * dg] = nn(act[rows, g * fg : (g + 1) * fg], fo_ref[g * fg : (g + 1) * fg, :])

    def rows8(x):
        total = x[0:8]
        for k in range(8, x.shape[0], 8):
            total = total + x[k : k + 8]
        return total

    def norm2(i, carry):
        at = slice(i * step, (i + 1) * step)
        norm = xh1[at, :] * vec(N1G) + vec(N1S)
        z = gsec[at, :] + vec(FOB) + norm
        z = z - jnp.mean(z, axis=1, keepdims=True)
        r = lax.rsqrt(jnp.mean(z * z, axis=1, keepdims=True) + EPS)
        x = z * r
        keep = ((iota((step, 1), 0) + i * step) < used).astype(f32)
        out_ref[at, :] = ((x * vec(N2G) + vec(N2S)) * keep).astype(bf16)
        gf = cot_ref[at, :].astype(f32) * keep
        gx = gf * x
        e = gf * vec(N2G)
        gz = r * (e - jnp.mean(e, axis=1, keepdims=True) - x * jnp.mean(e * x, axis=1, keepdims=True))
        gsec[at, :] = gz
        gsl[at, :] = gz.astype(bf16)
        return (carry[0] + rows8(gx), carry[1] + rows8(gf), carry[2] + rows8(gz))

    none = jnp.zeros((8, D), f32)
    sums = (none, none, none)
    for k in range(length // step):
        sums = norm2(k, sums)

    def add(r, value):
        gv_ref[r : r + 1, 0 : value.shape[1]] += jnp.sum(value, axis=0, keepdims=True)

    for r, value in zip((N2G, N2S, FOB), sums):
        add(r, value)

    def slopes(n):
        g, i = tiles[n]
        at = slice(g * fg + i * tile, g * fg + (i + 1) * tile)
        for rows in halves if n == 0 else [slice(0, length)]:
            wide[n % 2, rows, :] = nt(gsl[rows, g * dg : (g + 1) * dg], fo_ref[at, :])

    slopes(0)
    for n, (g, i) in enumerate(tiles):
        if n + 1 < len(tiles):
            slopes(n + 1)
        at = slice(g * fg + i * tile, g * fg + (i + 1) * tile)
        total = jnp.zeros((8, tile), f32)
        for r in range(0, length, 64):
            x = wide[n % 2, r : r + 64, :] * slope[r : r + 64, at].astype(f32)
            slope[r : r + 64, at] = x.astype(bf16)
            total = total + rows8(x)
        gv_ref[FIB : FIB + 1, at] += jnp.sum(total, axis=0, keepdims=True)
    for rows in halves:
        for g in range(GROUPS):
            gsec[rows, g * dg : (g + 1) * dg] += nt(slope[rows, g * fg : (g + 1) * fg], fi_ref[g * dg : (g + 1) * dg, :])

    def norm1_back(i, carry):
        at = slice(i * step, (i + 1) * step)
        gn = gsec[at, :]
        x = xh1[at, :]
        e = gn * vec(N1G)
        r = rs1[at, :]
        r = jnp.concatenate([r] * (D // LANES), axis=1)
        gz = r * (e - jnp.mean(e, axis=1, keepdims=True) - x * jnp.mean(e * x, axis=1, keepdims=True))
        gf_ref[at, :] = gz.astype(bf16)
        return (carry[0] + rows8(gn * x), carry[1] + rows8(gn), carry[2] + rows8(gz))

    sums = (none, none, none)
    todo = list(enumerate(tiles))
    for k in range(length // step):
        sums = norm1_back(k, sums)
        if k % 2:
            rows = slice((k - 1) * step, (k + 1) * step)
            gj_ref[rows, :] = nt(gf_ref[rows, :], dw_ref[...]).astype(bf16)
        for n, (g, i) in todo[k * len(todo) // (length // step) : (k + 1) * len(todo) // (length // step)]:
            at = slice(g * fg + i * tile, g * fg + (i + 1) * tile)
            gfo_ref[at, :] += tn(act[:, at], gsl[:, g * dg : (g + 1) * dg])
            gfi_ref[g * dg : (g + 1) * dg, i * tile : (i + 1) * tile] += tn(nl[:, g * dg : (g + 1) * dg], slope[:, at])
    for r, value in zip((N1G, N1S, DB), sums):
        add(r, value)
    gdw_ref[...] += tn(join_ref[...], gf_ref[...])

    @pl.when(row == pl.num_programs(0) - 1)
    def _():
        to_frames(sect, part_ref, ((gdw_ref, D, D, 0), (gfi_ref, D, FF // GROUPS, 0), (gfo_ref, FF, D // GROUPS, 0)))


def run_mid(sect, tokens, lengths, joined, cotangent, dw, fi, fo, vec):
    rows, count = lengths.shape[0], tokens.shape[0]
    length = count // rows

    def body(*refs):
        mid_kernel(sect, length, *refs)

    full = pl.BlockSpec(memory_space=VM)
    return pl.pallas_call(
        body,
        grid=(rows,),
        out_shape=[
            jax.ShapeDtypeStruct((count, D), bf16),
            jax.ShapeDtypeStruct((count, D), bf16),
            jax.ShapeDtypeStruct((count, D), bf16),
            jax.ShapeDtypeStruct((sect.count, sect.chunk, LANES), bf16),
            jax.ShapeDtypeStruct((VROWS, FF), f32),
        ],
        in_specs=[pl.BlockSpec(memory_space=pltpu.SMEM)] + [blocked(length, D)] * 3 + [full] * 4,
        out_specs=[blocked(length, D)] * 3 + [full] * 2,
        scratch_shapes=[
            VM((D, D), f32),
            VM((D, FF // GROUPS), f32),
            VM((FF, D // GROUPS), f32),
            VM((length, D), f32),
            VM((length, LANES), f32),
            VM((length, D), bf16),
            VM((length, FF), bf16),
            VM((length, FF), bf16),
            VM((length, D), f32),
            VM((length, D), bf16),
            VM((2, length, 768), f32),
        ],
        compiler_params=pltpu.CompilerParams(vmem_limit_bytes=VMEM_LIMIT),
        name="mid",
    )(lengths, tokens, joined, cotangent, dw, fi, fo, vec)


def bwd_kernel(length, pump, len_ref, tok_ref, qkvc_ref, kc_ref, dep_ref, ca_ref, tap_ref, join_ref, lse_ref, gf_ref, gj_ref,
               wp_ref, pw_ref, kw_ref, vec_ref,
               gt_ref, gp_ref, gpw_ref, gkw_ref, gv_ref,
               ds, cs, dcol, tm, mb, emat, gs, tp, prod, gq, gfour, acc):
    row = pl.program_id(0)

    @pl.when(row == 0)
    def _():
        fill_emat(emat)
        for ref in (gp_ref, gpw_ref, gkw_ref, gv_ref):
            ref[...] = jnp.zeros_like(ref)

    doc_marks(row, length, len_ref, dcol, tm, mb)
    pump(0)
    for ref in (ds, cs, gs, tp):
        zero_pads(ref, length)

    def add(r, value):
        gv_ref[r : r + 1, 0 : value.shape[1]] += jnp.sum(value, axis=0, keepdims=True)

    for p in range(3):
        pump(1 + p)
        cols = slice(p * LANES, (p + 1) * LANES)
        q, k, v = (qkvc_ref[:, m * ATT + p * LANES : m * ATT + (p + 1) * LANES] for m in range(3))
        g = gj_ref[:, cols]
        lane, sub = iota((length, LANES), 1), iota((16, LANES), 1)
        which = iota((16, LANES), 0)
        marks = jnp.where((sub >= HEAD_DIM) == (which >= 8), 1.0, 0.0).astype(bf16)
        dots = g.astype(f32) * join_ref[:, cols].astype(f32)
        high = dots.astype(bf16)
        dots = nt(marks, high) + nt(marks, (dots - high.astype(f32)).astype(bf16))
        qs = q.astype(f32) * SCALE
        kt = k.astype(f32).T.astype(bf16)
        gk, gv, gqt = None, None, []
        for h in range(2):
            own = (lane >= HEAD_DIM) == bool(h)
            qh = jnp.where(own, qs, 0.0).astype(bf16)
            gh = jnp.where(own, g.astype(f32), 0.0).astype(bf16)
            prob = jnp.exp(jnp.minimum(nt(k, qh), mb[...]) - lse_ref[0, 2 * p + h : 2 * p + h + 1, :])
            dsc = (prob * (nt(v, gh) - dots[8 * h : 8 * h + 1, :])).astype(bf16)
            a, b = nn(prob.astype(bf16), gh), nn(dsc, qh)
            gv, gk = (a, b) if h == 0 else (gv + a, gk + b)
            gqt.append(nn(kt, dsc)[h * HEAD_DIM : (h + 1) * HEAD_DIM, :])
        gq[:, cols] = jnp.concatenate(gqt, axis=0).T * SCALE
        gfour[:, ATT + p * LANES : ATT + (p + 1) * LANES] = gk.astype(bf16)
        gfour[:, 2 * ATT + p * LANES : 2 * ATT + (p + 1) * LANES] = gv.astype(bf16)
        gv_ref[VB : VB + 1, cols] += jnp.sum(gv, axis=0, keepdims=True)

    pump(4)
    for c in range(3):
        cs[c, 8 : 8 + length, :] = qkvc_ref[:, 3 * ATT + c * LANES : 3 * ATT + (c + 1) * LANES].astype(f32)
        gs[c, 8 : 8 + length, :] = gj_ref[:, ATT + c * LANES : ATT + (c + 1) * LANES].astype(f32)
    gtaps = None
    for j in range(0, KS, 3):
        for k in range(3):
            for c in range(3):
                at, spot = 8 + j + k - HALF, ((j + k) * 3 + c) * length
                prod[spot : spot + length, :] = (gs[c, 8 : 8 + length, :] * cs[c, at : at + length, :]).astype(bf16)
        blocks = [prod[n * length : (n + 1) * length, :] for n in range(j * 3, j * 3 + 9)]
        x = nt(jnp.concatenate(blocks, axis=1), emat[0:LANES, j * ATT : (j + 3) * ATT])
        gtaps = x if gtaps is None else gtaps + x
    marks = tap_lanes(tm, length)
    gtaps = gtaps * marks
    pump(5)
    taps = jnp.where(used_taps((length, LANES)), tap_ref[...], 0.0)
    glog = taps * (gtaps - over_taps(taps * gtaps, jnp.add))
    add(KBR, glog)
    glog = glog.astype(bf16)
    gkw_ref[...] += tn(ca_ref[...], glog)
    gca = nt(glog, kw_ref[...])

    tp[0, 8 : 8 + length, :] = taps * marks
    tap = iota((length, LANES), 1) >> 3
    moved = jnp.zeros((length, LANES), f32)
    for j in range(KS):
        at = 8 + HALF - j
        moved = jnp.where(tap == j, tp[0, at : at + length, :], moved)
    spread = two_parts(moved)
    for j in range(KS):
        if j % 2 == 0:
            t = nn(spread, emat[:, j * ATT : min(j + 2, KS) * ATT])
        for c in range(3):
            at, k = 8 + HALF - j, (j % 2 * 3 + c) * LANES
            part = t[:, k : k + LANES] * gs[c, at : at + length, :]
            if j:
                part = part + acc[:, c * LANES : (c + 1) * LANES]
            if j < KS - 1:
                acc[:, c * LANES : (c + 1) * LANES] = part
            else:
                gfour[:, 3 * ATT + c * LANES : 3 * ATT + (c + 1) * LANES] = part.astype(bf16)
                gv_ref[CB : CB + 1, c * LANES : (c + 1) * LANES] += jnp.sum(part, axis=0, keepdims=True)

    pump(6)
    gkc = gca * qkvc_ref[:, 0:ATT].astype(f32)
    gquery = gq[...] + gca * kc_ref[...].astype(f32)
    add(QB, gquery)
    gfour[:, 0:ATT] = gquery.astype(bf16)
    add(PB, gkc)
    gkc = gkc.astype(bf16)
    gpw_ref[...] += tn(dep_ref[...], gkc)
    for c in range(3):
        x = nt(gkc, pw_ref[c * 256 : (c + 1) * 256, :])
        ds[2 * c, 8 : 8 + length, :] = x[:, 0:LANES]
        ds[2 * c + 1, 8 : 8 + length, :] = x[:, LANES:]
    pump(7)
    for m in range(2):
        cols = slice(2 * m * ATT, 2 * (m + 1) * ATT)
        gp_ref[:, cols] += tn(tok_ref[...], gfour[:, cols])

    pump(8)
    step = 64
    for c in range(6):
        cols = slice(c * LANES, (c + 1) * LANES)
        w = [vec_ref[DW + j : DW + j + 1, cols] for j in range(KS)]
        sums = [None] * KS
        if c % 2 == 0:
            direct = nt(gfour[...], wp_ref[c * LANES : (c + 2) * LANES, :])
        for r in range(0, length, step):
            tok = tok_ref[r : r + step, cols].astype(f32)
            total = gf_ref[r : r + step, cols].astype(f32) + direct[r : r + step, (c % 2) * LANES : (c % 2 + 1) * LANES]
            for j in range(KS):
                at = 8 + r + j - HALF
                u = ds[c, at : at + step, :]
                if j != HALF:
                    u = u * tm[j, r : r + step, :]
                total = total + w[KS - 1 - j] * u
                u = tok * u
                part = u[0:8]
                for s in range(8, step, 8):
                    part = part + u[s : s + 8]
                sums[j] = part if r == 0 else sums[j] + part
            gt_ref[r : r + step, cols] = total.astype(bf16)
        for j in range(KS):
            gv_ref[DW + KS - 1 - j : DW + KS - j, cols] += jnp.sum(sums[j], axis=0, keepdims=True)
    pump(9)


BWD_POINTS = 10
FIRST_AT, SECOND_AT, THIRD_AT = (2, 3, 6, 10), (5, 9, 13, 15), (9, 13, 16, 17)
SETTLE_AT, TAKE_AT = 21, 26


def run_back(first, second, part, va, tokens, lengths, saved, gf, gj, wp, pw, kw, vec):
    outer, inner = lax.axis_size("dp"), lax.axis_size("fsdp")
    qkvc, kc, dep, ca, taps, joined, lse = saved
    rows, count = lengths.shape[0], tokens.shape[0]
    length = count // rows
    lead = max(first.chunk, second.chunk)
    tall = -(-max(3 * KS * length, first.count * first.chunk) // 16) * 16
    scratch = row_scratch(length) + [
        VM((3, length + 16, LANES), f32),
        VM((1, length + 16, LANES), f32),
        VM((tall, LANES), bf16),
        VM((length, ATT), f32),
        VM((length, 4 * ATT), bf16),
        VM((length, ATT), f32),
    ]
    grads = [VM((D, 4 * ATT), f32), VM((D, ATT), f32), VM((ATT, LANES), f32), VM((VROWS, FF), f32)]
    more = [
        VM((first.rows + 2 * lead + 16, LANES), f32),
        VM((max(first.small * first.chunk, 384), LANES), f32),
        VM((512, LANES), f32),
    ]
    n, m = len(scratch), len(Scatter.scratch(first, inner))

    def body(part_ref, va_ref, *refs):
        ours, (gt_ref, own_ref), refs = refs[:15], refs[15:17], refs[17:]
        rows_refs, sums, refs = refs[:n], refs[n : n + 4], refs[n + 4 :]
        (out, flat, kwt), refs = refs[:3], refs[3:]
        gp_ref, gpw_ref, gkw_ref, gv_ref = sums
        stage = rows_refs[8]
        place = Place(outer, inner)
        a = Scatter(first, place, lambda v: stage.at[pl.ds(v * first.chunk, first.chunk)], out, lead, refs[:m], True)
        b = Scatter(second, place, lambda v: part_ref.at[v], out, lead, refs[m:], False)

        def begin():
            out[...] = jnp.zeros_like(out)
            place.all_here()
            b.core()

        def end():
            gv_ref[...] += va_ref[...]
            pack_small(flat, gkw_ref, gv_ref, kwt)
            to_frames(
                first,
                Rows(stage, first.chunk),
                [(gp_ref, D, ATT, k * ATT) for k in range(4)] + [(gpw_ref, D, ATT, 0)],
                flat,
            )
            steps = a.sums()
            a.core(*a.far[:2])
            for k, step in enumerate(steps):
                if k < len(a.far) - 2:
                    a.core(a.far[2 + k])
                step()
            b.finish()
            a.settle()
            a.take()
            a.finish()
            own_ref[...] = out[lead : lead + first.rows, :]

        due = [(0, 0, begin)]
        for step, spots in ((b.first, FIRST_AT), (b.second, SECOND_AT), (b.third, THIRD_AT)):
            steps = [lambda step=step, d=d: step(d) for d in b.far]
            due += spread_over(steps, rows, BWD_POINTS, list(spots) + [spots[-1]] * (len(steps) - len(spots)))
        due += spread_over([b.settle, b.take], rows, BWD_POINTS, (SETTLE_AT, TAKE_AT))
        pump = pumped(due + [(rows - 1, BWD_POINTS - 1, end)])
        pl.when(pl.program_id(0) == 0)(place.call)
        bwd_kernel(length, pump, *ours, gt_ref, *sums, *rows_refs)

    full = pl.BlockSpec(memory_space=VM)
    return pl.pallas_call(
        body,
        grid=(rows,),
        out_shape=[jax.ShapeDtypeStruct((count, D), bf16), jax.ShapeDtypeStruct((first.rows, LANES), f32)],
        in_specs=[
            pl.BlockSpec(memory_space=pl.ANY),
            full,
            pl.BlockSpec(memory_space=pltpu.SMEM),
            blocked(length, D),
            blocked(length, 4 * ATT),
            blocked(length, ATT),
            blocked(length, D),
            blocked(length, ATT),
            blocked(length, LANES),
            blocked(length, D),
            pl.BlockSpec((1, 8, length), lambda r: (r, 0, 0)),
            blocked(length, D),
            blocked(length, D),
            full,
            full,
            full,
            full,
        ],
        out_specs=[blocked(length, D), full],
        scratch_shapes=scratch + grads + more + Scatter.scratch(first, inner) + Scatter.scratch(second, inner),
        compiler_params=pltpu.CompilerParams(vmem_limit_bytes=VMEM_LIMIT, collective_id=1, has_side_effects=True),
        name="back",
    )(part, va, lengths, tokens, qkvc, kc, dep, ca, taps, joined, lse, gf, gj, wp, pw, kw, vec)


def shards(tokens, doc_lengths, params, cotangent):
    rows = params.shape[0] // LANES
    outer, inner = lax.axis_size("dp"), lax.axis_size("fsdp")
    first, second = sections(outer * inner, rows, inner)
    *saved, dw, fi, fo, wp, pw, kw, vec = run_front(first, second, params.reshape(rows, LANES), tokens, doc_lengths)
    output, gf, gj, part, va = run_mid(second, tokens, doc_lengths, saved[5], cotangent, dw, fi, fo, vec)
    gt, own_grad = run_back(first, second, part, va, tokens, doc_lengths, saved, gf, gj, wp, pw, kw, vec)
    return output, gt, own_grad.reshape(rows * LANES)


def solution(mesh):
    axes = ("dp", "fsdp")
    placed = (P(axes, None), P(axes, None), P(axes), P(axes, None))
    return jax.shard_map(
        shards,
        mesh=mesh,
        in_specs=placed,
        out_specs=(P(axes, None), P(axes, None), P(axes)),
        check_vma=False,
    )
```

```python
import math

import jax
import jax.numpy as jnp
from jax import lax
from jax.experimental import pallas as pl
from jax.experimental.pallas import tpu as pltpu
from jax.sharding import PartitionSpec as P

D = 768
HEADS = 6
HEAD_DIM = 64
ATT = HEADS * HEAD_DIM
FF = 3072
GROUPS = 2
KS = 9
HALF = KS // 2
SLOTS = 16
EPS = 1e-12
LANES = 128
NEG = -1e30
BIG = 3e38
SCALE = HEAD_DIM ** (-0.5)

f32 = jnp.float32
bf16 = jnp.bfloat16
i32 = jnp.int32

FIRST = 5 * D * ATT // LANES
MATRICES = FIRST + (D * D + 2 * D * FF // GROUPS) // LANES
DEPTH_AT = 0
KERNEL_AT = KS * D // LANES
BIAS_AT = KERNEL_AT + ATT * HEADS * KS // LANES
TAIL_AT = BIAS_AT + 4 * ATT // LANES
SMALL = TAIL_AT + 61
KB = HEADS * KS

QB, VB, CB, PB, KBR, DB, N1G, N1S, FIB, FOB, N2G, N2S, DW = range(13)
VROWS = 24
TAIL = [(DB, 6), (N1G, 6), (N1S, 6), (FIB, 24), (FOB, 6), (N2G, 6), (N2S, 6)]

VM = pltpu.VMEM
VMEM_LIMIT = 62 * 1024 * 1024


def nn(a, b):
    return lax.dot_general(a, b, (((1,), (0,)), ((), ())), preferred_element_type=f32)


def nt(a, b):
    return lax.dot_general(a, b, (((1,), (1,)), ((), ())), preferred_element_type=f32)


def tn(a, b):
    return lax.dot_general(a, b, (((0,), (0,)), ((), ())), preferred_element_type=f32)


def iota(shape, axis):
    return lax.broadcasted_iota(i32, shape, axis)


def loop(count, body, unroll=1):
    def step(i, carry):
        body(i)
        return carry

    lax.fori_loop(0, count, step, 0, unroll=unroll)


def tap_perm():
    k, n = iota((LANES, LANES), 0), iota((LANES, LANES), 1)
    head, tap = n & 7, n >> 3
    return jnp.where((k == head * KS + tap) & (head < HEADS) & (tap < KS), 1.0, 0.0).astype(bf16)


def used_taps(shape):
    n = iota(shape, len(shape) - 1)
    return ((n & 7) < HEADS) & ((n >> 3) < KS)


def padded(rows):
    return -(-rows // 16) * 16


class Section:
    def __init__(self, base, kinds, chunk, small, rows, count, inner):
        self.base, self.chunk, self.rows, self.count, self.inner = base, chunk, rows, count, inner
        self.main = sum(n for n, _ in kinds)
        self.small = -(-SMALL // chunk) if small else 0
        self.kinds = kinds + ([(self.small, 1)] if small else [])
        self.used = self.main + self.small
        self.pieces = -(-rows // chunk) + 1
        self.slots = self.pieces + self.small
        self.sources = (chunk - 2) // rows + 2
        self.lead = -(-base // rows)

    def seat(self, v, pick=jnp.where):
        q, r, n = v // 3, v % 3, self.count
        if self.small:
            near = pick(q < n // 4, r * (n // 4) + q, 3 * (n // 4) + v - 3 * (n // 4))
            return pick(v < self.main, near, n - self.small + v - self.main)
        return pick(r < 2, self.lead + 2 * q + r, q)

    def chunk_at(self, d):
        n = self.count
        if self.small:
            quarter = n // 4
            v = jnp.where(d < 3 * quarter, 3 * lax.rem(d, quarter) + d // quarter, d)
            v = jnp.where(v < self.main, v, self.used)
            return jnp.where(d >= n - self.small, self.main + d - (n - self.small), v)
        t = d - self.lead
        v = jnp.where(d < self.main // 3, 3 * d + 2, self.used)
        return jnp.where((t >= 0) & (t < 2 * self.main // 3), 3 * (t // 2) + lax.rem(t, 2), v)

    def start(self, v):
        at = self.base + v * self.chunk
        if self.small:
            at = jnp.where(v >= self.main, MATRICES + (v - self.main) * self.chunk, at)
        return at

    def first_piece(self, i):
        return jnp.maximum(self.rows * i - self.base, 0) // self.chunk

    def of_owner(self, i, k):
        if k < self.pieces:
            v = self.first_piece(i) + k
            ok = v < self.main
        else:
            v = self.main + k - self.pieces + 0 * i
            ok = v >= 0
        at = self.start(v)
        return v, ok & (at < self.rows * (i + 1)) & (at + self.chunk > self.rows * i)

    def of_chunk(self, v, s):
        i = self.start(v) // self.rows + s
        return i, (v < self.used) & (i < self.count) & (self.rows * i < self.start(v) + self.chunk)

    def source_of(self, v, i):
        return i - self.start(v) // self.rows

    def slot_of(self, v, i):
        return jnp.where(v < self.main, v - self.first_piece(i), self.pieces + v - self.main)

    def by_kind(self, v, action):
        at, seen = 0, {}
        for n, per in self.kinds:
            seen.setdefault(per, []).append((at, at + n))
            at += n
        for per, spans in seen.items():
            ok = False
            for lo, hi in spans:
                ok = ((v >= lo) & (v < hi)) | ok
            pl.when(ok)(lambda per=per: action(per))


def sections(count, rows, inner):
    big, little = 24576 // count, 12288 // count
    first = Section(0, [(FIRST // little, 3)], little, True, rows, count, inner)
    kinds = [(D * n // LANES // big, n // LANES) for n in (D, FF // GROUPS)] + [(FF * 3 // big, 3)]
    return first, Section(FIRST, kinds, big, False, rows, count, inner)


class Rows:
    def __init__(self, ref, chunk):
        self.ref, self.chunk = ref, chunk

    def __setitem__(self, where, value):
        v, rows, _ = where
        self.ref[v * self.chunk + rows.start : v * self.chunk + rows.stop, :] = value


def choose(ok, a, b):
    return a if ok else b


def pieces_of(sect, matrices):
    v = 0
    for ref, height, width, col in matrices:
        per = width // LANES
        tall = sect.chunk // per
        for r in range(0, height, tall):
            for c in range(per):
                cols = slice(col + c * LANES, col + (c + 1) * LANES)
                yield sect.seat(v, choose), slice(c * tall, (c + 1) * tall), ref, slice(r, r + tall), cols
            v += 1


def to_frames(sect, part, matrices, small=None):
    for seat, rows, ref, r, c in pieces_of(sect, matrices):
        part[seat, rows, :] = ref[r, c].astype(bf16)
    for k in range(sect.small):
        part[sect.seat(sect.main + k, choose), slice(0, sect.chunk), :] = small[
            k * sect.chunk : (k + 1) * sect.chunk, :
        ].astype(bf16)
    for d in set(range(sect.count)) - {sect.seat(v, choose) for v in range(sect.used)}:
        part[d, slice(0, sect.chunk), :] = jnp.zeros((sect.chunk, LANES), bf16)


def from_frames(sect, buf, matrices, small=None):
    for seat, rows, ref, r, c in pieces_of(sect, matrices):
        ref[r, c] = buf[seat, rows, :]
    for k in range(sect.small):
        small[k * sect.chunk : (k + 1) * sect.chunk, :] = buf[sect.seat(sect.main + k, choose)].astype(f32)


def unpack_small(flat, kw_ref, vec_ref, kwt):
    vec_ref[...] = jnp.zeros_like(vec_ref)
    for row in range(4):
        for c in range(3):
            at = BIAS_AT + row * 3 + c
            vec_ref[row : row + 1, c * LANES : (c + 1) * LANES] = flat[at : at + 1, :]
    for j in range(KS):
        for c in range(6):
            at = DEPTH_AT + j * 6 + c
            vec_ref[DW + j : DW + j + 1, c * LANES : (c + 1) * LANES] = flat[at : at + 1, :]
    at = TAIL_AT
    lane = iota((64, LANES), 1)
    first = pltpu.roll(flat[at : at + 64, :], LANES - KB, 1)
    second = pltpu.roll(flat[at + 1 : at + 65, :], LANES - KB, 1)
    kwt[0:64, :] = jnp.where(lane < LANES - KB, first, second)
    at = 0
    for row, many in TAIL:
        for c in range(many):
            vec_ref[row : row + 1, c * LANES : (c + 1) * LANES] = kwt[at + c : at + c + 1, :]
        at += many
    perm = tap_perm()
    lane8 = iota((16, LANES), 1)
    kb = jnp.broadcast_to(flat[TAIL_AT : TAIL_AT + 1, :], (16, LANES))
    kb = nn(jnp.where(lane8 < KB, kb, 0.0).astype(bf16), perm)
    kb = jnp.where(used_taps((16, LANES)), kb, NEG)
    vec_ref[KBR : KBR + 1, 0:LANES] = kb[0:1]

    lane = iota((8, LANES), 1)
    for a in range(64):
        c0, ln = divmod(a * KB, LANES)
        at = KERNEL_AT + c0
        x = pltpu.roll(flat[pl.ds(at, 8, stride=27), :], (LANES - ln) % LANES, 1)
        if ln + KB > LANES:
            y = pltpu.roll(flat[pl.ds(at + 1, 8, stride=27), :], (LANES - ln) % LANES, 1)
            x = jnp.where(lane < LANES - ln, x, y)
        kwt[pl.ds(a, 8, stride=64), :] = jnp.where(lane < KB, x, 0.0)
    kw_ref[...] = nn(kwt[0:ATT, :].astype(bf16), perm).astype(bf16)


def pack_small(flat, gkw_ref, vec, kwt):
    flat[...] = jnp.zeros_like(flat)
    perm = tap_perm()
    kwt[...] = jnp.zeros_like(kwt)
    kwt[0:ATT, :] = nt(gkw_ref[...].astype(bf16), perm)
    lane = iota((8, LANES), 1)
    for a in range(64):
        c0, ln = divmod(a * KB, LANES)
        at = KERNEL_AT + c0
        x = pltpu.roll(kwt[pl.ds(a, 8, stride=64), :], ln, 1)
        if ln + KB > LANES:
            flat[pl.ds(at, 8, stride=27), :] += jnp.where(lane >= ln, x, 0.0)
            flat[pl.ds(at + 1, 8, stride=27), :] += jnp.where(lane < ln, x, 0.0)
        else:
            flat[pl.ds(at, 8, stride=27), :] += x
    for row in range(4):
        for c in range(3):
            at = BIAS_AT + row * 3 + c
            flat[at : at + 1, :] = vec[row : row + 1, c * LANES : (c + 1) * LANES]
    for j in range(KS):
        for c in range(6):
            at = DEPTH_AT + j * 6 + c
            flat[at : at + 1, :] = vec[DW + j : DW + j + 1, c * LANES : (c + 1) * LANES]
    kwt[...] = jnp.zeros_like(kwt)
    at = 8
    for row, many in TAIL:
        for c in range(many):
            kwt[at + c : at + c + 1, :] = vec[row : row + 1, c * LANES : (c + 1) * LANES]
        at += many
    lane = iota((72, LANES), 1)
    before = pltpu.roll(kwt[7:79, :], KB, 1)
    here = pltpu.roll(kwt[8:80, :], KB, 1)
    at = TAIL_AT
    flat[at : at + 72, :] = jnp.where(lane < KB, before, here)
    kb = jnp.broadcast_to(vec[KBR : KBR + 1, 0:LANES], (16, LANES))
    kb = nt(jnp.where(used_taps((16, LANES)), kb, 0.0).astype(bf16), perm)
    lane = iota((1, LANES), 1)
    flat[at : at + 1, :] = jnp.where(lane < KB, kb[0:1], flat[at : at + 1, :])


class Place:
    def __init__(self, outer, inner):
        self.outer, self.inner, self.count = outer, inner, outer * inner
        self.lines = inner // 2
        dp, fs = lax.axis_index("dp"), lax.axis_index("fsdp")
        self.y, self.x, self.z, self.c = dp // 2, lax.rem(dp, 2), fs // 2, lax.rem(fs, 2)
        self.me = dp * inner + fs

    def coords(self, dy=0, dx=0, z=None, dc=0):
        def flip(v, d):
            return 1 - v if d else v

        z = self.z if z is None else z
        return flip(self.y, dy) * 2 + flip(self.x, dx), z * 2 + flip(self.c, dc)

    def index(self, **d):
        o, i = self.coords(**d)
        return o * self.inner + i

    def device(self, n):
        return n // self.inner, lax.rem(n, self.inner)

    def item(self, t):
        s = (t + 1) // 2
        z = self.z - s if t % 2 else self.z + s
        return z, (z >= 0) & (z < self.lines), s, t % 2 == 1

    def call(self):
        barrier = pltpu.get_barrier_semaphore()
        for n in range(1, self.count):
            peer = self.device(lax.rem(self.me + n, self.count))
            pl.semaphore_signal(barrier, inc=1, device_id=peer, device_id_type=pl.DeviceIdType.MESH)

    def all_here(self):
        pl.semaphore_wait(pltpu.get_barrier_semaphore(), self.count - 1)


class Copies:
    def __init__(self, send, recv):
        self.send, self.recv, self.used, self.made = send, recv, 0, []

    def start(self, src, dst, peer, slot, ok=None, group=None):
        number = self.used if group is None else group
        if group is None:
            self.used += 1
        assert number < self.send.shape[0]

        def make():
            return pltpu.make_async_remote_copy(
                src_ref=src(),
                dst_ref=dst(),
                send_sem=self.send.at[number],
                recv_sem=self.recv.at[slot() if callable(slot) else slot],
                device_id=peer(),
                device_id_type=pl.DeviceIdType.MESH,
            )

        if group is None:
            self.made.append((make, ok))
        guarded(ok, lambda: make().start())

    def sent(self, ref, group):
        pltpu.make_async_copy(ref, ref, self.send.at[group]).wait()

    def arrived(self, dst, slot, ok=None):
        def wait():
            ref = dst()
            pltpu.make_async_copy(ref, ref, self.recv.at[slot]).wait()

        guarded(ok, wait)

    def finish(self):
        for make, ok in self.made:
            guarded(ok, lambda make=make: make().wait_send())


def guarded(ok, action):
    if ok is None:
        action()
    else:
        pl.when(ok())(action)


def half_of(chunk):
    return -(-chunk // 32) * 16


class Gather:
    @staticmethod
    def scratch(sect, inner):
        lines = inner // 2
        items = 2 * lines - 1
        return [
            VM((sect.count, sect.chunk, LANES), bf16),
            VM((sect.slots, sect.chunk, LANES), bf16),
            VM((sect.sources, sect.chunk, LANES), bf16),
            VM((sect.chunk, LANES), f32),
            pltpu.SemaphoreType.DMA((sect.slots + items + 3,)),
            pltpu.SemaphoreType.DMA((sect.sources + 9 * items,)),
        ]

    def __init__(self, sect, place, ownf, lead, scratch):
        self.sect, self.place, self.ownf, self.lead = sect, place, ownf, lead
        self.buf, self.win, self.land, self.frame, send, recv = scratch
        self.copies = Copies(send, recv)
        n = 2 * place.lines - 1
        self.items = n
        self.group = sect.slots + n + 2
        self.Z, self.X, self.Y, self.A, self.B, self.CZ, self.CX, self.CY, self.CD = (sect.sources + n * k for k in range(9))
        cut = half_of(sect.chunk)
        self.half = {"a": pl.ds(0, cut), "b": pl.ds(cut, sect.chunk - cut)}

    def offer(self):
        for k in range(self.sect.slots):
            self.give(k)

    def give(self, k):
        sect, place, me = self.sect, self.place, self.place.me
        v, ok = sect.of_owner(me, k)

        @pl.when(ok)
        def _():
            at = self.lead + sect.start(v) - sect.rows * me
            self.win[k] = self.ownf[pl.ds(at, sect.chunk), :].astype(bf16)

        @pl.when(ok & (sect.seat(v) == me))
        def _():
            self.land[sect.source_of(v, me)] = self.win[k]

        def chunk():
            return sect.of_owner(me, k)[0]

        def away():
            v, ok = sect.of_owner(me, k)
            return ok & (sect.seat(v) != me)

        def source():
            return jnp.clip(sect.source_of(chunk(), me), 0, sect.sources - 1)

        def seat():
            return jnp.clip(sect.seat(chunk()), 0, sect.count - 1)

        self.copies.start(lambda: self.win.at[k], lambda: self.land.at[source()], lambda: place.device(seat()), source, away)

    def form(self):
        sect, me = self.sect, self.place.me
        v = sect.chunk_at(me)
        row = iota((sect.chunk, LANES), 0) + sect.start(v)
        x = None
        for s in range(sect.sources):
            i, ok = sect.of_chunk(v, s)
            self.copies.arrived(lambda: self.land.at[s], s, lambda: ok & (i != me))
            here = self.land[s].astype(f32)
            x = here if x is None else jnp.where(row >= sect.rows * i, here, x)
        self.frame[...] = x

        def settle(per):
            tall = sect.chunk // per
            for c in range(per):
                self.buf[me, c * tall : (c + 1) * tall, :] = self.frame[pl.ds(c, tall, stride=per), :].astype(bf16)

        sect.by_kind(v, settle)

        @pl.when(v >= sect.used)
        def _():
            self.buf[me] = jnp.zeros((sect.chunk, LANES), bf16)

        self.pass_on(0)

    def ref(self, t, which=None, **way):
        def make():
            at = self.place.index(z=self.place.item(t)[0], **way)
            return self.buf.at[at] if which is None else self.buf.at[at, self.half[which]]

        return make

    def ok(self, t):
        return None if t == 0 else lambda: self.place.item(t)[1]

    def same(self, ref, peer, slot, ok, group=True):
        self.copies.start(ref, ref, peer, slot, ok, self.group if group else None)

    def finish(self):
        self.copies.sent(self.buf.at[pl.ds(0, 7 * self.place.lines)], self.group)
        self.copies.finish()

    def beside(self, **way):
        return lambda: self.place.coords(**way)

    def pass_on(self, t):
        place = self.place
        _, _, s, below = place.item(t)
        for way in (1, -1) if t == 0 else ((1,) if below else (-1,)):
            slot = 2 * s + 1 if way > 0 else 2 * s + 2

            def inside(way=way):
                there = place.z + way
                good = (there >= 0) & (there < place.lines)
                return good if t == 0 else good & place.item(t)[1]

            if slot < self.items:
                self.same(self.ref(t), lambda way=way: place.coords(z=place.z + way), self.Z + slot, inside, False)
        ok = self.ok(t)
        self.same(self.ref(t), self.beside(dx=1), self.X + t, ok)
        self.same(self.ref(t), self.beside(dy=1), self.Y + t, ok)
        self.same(self.ref(t), self.beside(dc=1), self.CZ + t, ok)

    def at_distance(self, s):
        return [0] if s == 0 else [2 * s - 1, 2 * s]

    def along(self, s):
        for t in self.at_distance(s):
            self.copies.arrived(self.ref(t), self.Z + t, self.ok(t))
            self.pass_on(t)

    def across(self, s):
        for t in self.at_distance(s):
            ok = self.ok(t)
            self.copies.arrived(self.ref(t, dx=1), self.X + t, ok)
            self.same(self.ref(t, "a", dx=1), self.beside(dy=1), self.A + t, ok)
            self.same(self.ref(t, dx=1), self.beside(dc=1), self.CX + t, ok)
            self.copies.arrived(self.ref(t, dy=1), self.Y + t, ok)
            self.same(self.ref(t, "b", dy=1), self.beside(dx=1), self.B + t, ok)
            self.same(self.ref(t, dy=1), self.beside(dc=1), self.CY + t, ok)

    def diagonal(self):
        for t in range(self.items):
            ok = self.ok(t)
            self.copies.arrived(self.ref(t, "a", dy=1, dx=1), self.A + t, ok)
            self.copies.arrived(self.ref(t, "b", dy=1, dx=1), self.B + t, ok)
            self.same(self.ref(t, dy=1, dx=1), self.beside(dc=1), self.CD + t, ok)

    def rest(self):
        for t in range(self.items):
            for k, way in ((self.CZ, {}), (self.CX, {"dx": 1}), (self.CY, {"dy": 1}), (self.CD, {"dy": 1, "dx": 1})):
                self.copies.arrived(self.ref(t, dc=1, **way), k + t, self.ok(t))


class Scatter:
    @staticmethod
    def scratch(sect, inner):
        lines = inner // 2
        cut = half_of(sect.chunk)
        return [
            VM((4 * lines, sect.chunk, LANES), bf16),
            VM((4 * lines, sect.chunk, LANES), bf16),
            VM((2 * lines, cut, LANES), bf16),
            VM((2 * lines, sect.chunk - cut, LANES), bf16),
            VM((lines, sect.chunk - cut, LANES), bf16),
            VM((lines, cut, LANES), bf16),
            VM((lines, sect.chunk, LANES), bf16),
            VM((sect.chunk, LANES), f32),
            VM((sect.chunk, LANES), f32),
            VM((sect.chunk, LANES), bf16),
            VM((sect.slots, sect.chunk, LANES), bf16),
            pltpu.SemaphoreType.DMA((sect.sources + 6,)),
            pltpu.SemaphoreType.DMA((11 * lines + sect.slots,)),
            pltpu.SemaphoreType.DMA((4 * lines,)),
        ]

    def __init__(self, sect, place, part, out, lead, scratch, close):
        self.close = close
        self.sect, self.place, self.part, self.out, self.lead = sect, place, part, out, lead
        (self.work, self.rc, self.ry, self.rx, self.ry2, self.rx2, self.rz, self.frame, self.flat, self.low, self.land,
         send, recv, self.near) = scratch
        self.copies = Copies(send, recv)
        lines = place.lines
        self.lines = lines
        cut = half_of(sect.chunk)
        self.a, self.b = pl.ds(0, cut), pl.ds(cut, sect.chunk - cut)
        self.C, self.YA, self.XB, self.XA, self.YB, self.Z, self.O = (lines * k for k in (0, 4, 6, 8, 9, 10, 11))
        self.far = list(range(1, lines)) + [0]
        self.group = sect.sources

    def sums(self):
        out = []
        for n in range(self.lines + 2):
            for lag, step in ((0, self.first), (1, self.second), (2, self.third)):
                if 0 <= n - lag < self.lines:
                    out.append(lambda step=step, d=self.far[n - lag]: step(d))
        return out

    def z(self, d):
        return lax.rem(self.place.z + d, self.lines) if d else self.place.z

    def at(self, dy, dx, d):
        return (dy * 2 + dx) * self.lines + d

    def own(self, dy, dx, d):
        k = self.at(dy, dx, d)
        there = self.place.index(dy=dy, dx=dx, z=self.z(d))
        return pltpu.make_async_copy(self.part(there), self.work.at[k], self.near.at[k])

    def core(self, *places):
        place = self.place

        def give(dy, dx, d):
            k = self.at(dy, dx, d)
            self.copies.start(
                lambda: self.part(place.index(dy=dy, dx=dx, z=self.z(d), dc=1)),
                lambda: self.rc.at[k],
                lambda: place.coords(dc=1),
                self.C + k,
                group=self.group,
            )
            if not self.close:
                self.own(dy, dx, d).start()

        for d in places or self.far:
            for dy, dx in ((1, 1), (1, 0), (0, 1), (0, 0)):
                give(dy, dx, d)

    def send(self, k, rows, buf, n, way, slot, group):
        self.copies.start(
            lambda: self.work.at[k, rows],
            lambda: buf.at[n],
            lambda: self.place.coords(**way),
            slot,
            group=self.group + group,
        )

    def finish(self):
        for k, ref in enumerate((self.rc, self.ry, self.rx, self.rx2, self.ry2, self.rz.at[pl.ds(1, self.lines - 1)])):
            self.copies.sent(ref, self.group + k)
        self.copies.finish()

    def got(self, buf, n, slot):
        self.copies.arrived(lambda: buf.at[n], slot)

    def plus(self, k, rows, other):
        self.work[k, rows] = (self.work[k, rows].astype(f32) + other.astype(f32)).astype(bf16)

    def first(self, d):
        lines = self.lines
        for dy, dx in ((1, 1), (1, 0), (0, 1), (0, 0)):
            k = self.at(dy, dx, d)
            if self.close:
                self.got(self.rc, k, self.C + k)
                mine = self.part(self.place.index(dy=dy, dx=dx, z=self.z(d)))[...]
                self.work[k] = (mine.astype(f32) + self.rc[k].astype(f32)).astype(bf16)
            else:
                self.own(dy, dx, d).wait()
                self.got(self.rc, k, self.C + k)
                self.plus(k, pl.ds(0, self.sect.chunk), self.rc[k])
            if dy:
                self.send(k, self.a, self.ry, dx * lines + d, {"dy": 1}, self.YA + dx * lines + d, 1)
            if dx:
                self.send(k, self.b, self.rx, dy * lines + d, {"dx": 1}, self.XB + dy * lines + d, 2)

    def second(self, d):
        n = self.lines + d
        self.got(self.ry, n, self.YA + n)
        self.plus(self.at(0, 1, d), self.a, self.ry[n])
        self.send(self.at(0, 1, d), self.a, self.rx2, d, {"dx": 1}, self.XA + d, 3)
        self.got(self.rx, n, self.XB + n)
        self.plus(self.at(1, 0, d), self.b, self.rx[n])
        self.send(self.at(1, 0, d), self.b, self.ry2, d, {"dy": 1}, self.YB + d, 4)

    def third(self, d):
        k = self.at(0, 0, d)
        self.got(self.ry, d, self.YA + d)
        self.got(self.rx, d, self.XB + d)
        self.got(self.rx2, d, self.XA + d)
        self.got(self.ry2, d, self.YB + d)
        self.plus(k, self.a, self.ry[d].astype(f32) + self.rx2[d].astype(f32))
        self.plus(k, self.b, self.rx[d].astype(f32) + self.ry2[d].astype(f32))
        if d:
            self.copies.start(
                lambda: self.work.at[k],
                lambda: self.rz.at[d],
                lambda: self.place.coords(z=self.z(d)),
                self.Z + d,
                group=self.group + 5,
            )

    def settle(self):
        sect, me = self.sect, self.place.me
        total = self.work[self.at(0, 0, 0)].astype(f32)
        for d in range(1, self.lines):
            self.got(self.rz, d, self.Z + d)
            total = total + self.rz[d].astype(f32)
        self.frame[...] = total

        def spread(per):
            tall = sect.chunk // per
            for c in range(per):
                self.flat[pl.ds(c, tall, stride=per), :] = self.frame[c * tall : (c + 1) * tall, :]

        self.flat[...] = total
        sect.by_kind(sect.chunk_at(me), spread)
        self.low[...] = self.flat[...].astype(bf16)
        for s in range(sect.sources):
            self.give(s)

    def give(self, s):
        sect, me = self.sect, self.place.me
        i, ok = sect.of_chunk(sect.chunk_at(me), s)

        @pl.when(ok & (i == me))
        def _():
            self.land[sect.slot_of(sect.chunk_at(me), i)] = self.low[...]

        def owner():
            return jnp.minimum(sect.of_chunk(sect.chunk_at(me), s)[0], sect.count - 1)

        def slot():
            return jnp.clip(sect.slot_of(sect.chunk_at(me), owner()), 0, sect.slots - 1)

        def away():
            i, ok = sect.of_chunk(sect.chunk_at(me), s)
            return ok & (i != me)

        self.copies.start(
            lambda: self.low, lambda: self.land.at[slot()], lambda: self.place.device(owner()), lambda: self.O + slot(), away
        )

    def take(self):
        sect, me = self.sect, self.place.me
        for k in range(sect.slots):
            v, ok = sect.of_owner(me, k)
            self.copies.arrived(lambda: self.land.at[k], self.O + k, lambda: ok & (sect.seat(v) != me))

            @pl.when(ok)
            def _():
                at = self.lead + sect.start(v) - sect.rows * me
                self.out[pl.ds(at, sect.chunk), :] = self.land[k].astype(f32)


def pumped(due):
    row = pl.program_id(0)

    def pump(point):
        for r, p, step in due:
            if p == point:
                pl.when(row == r)(step)

    return pump


def spread_over(steps, rows, points, spots):
    end = rows * points - 1
    return [(min(n, end) // points, min(n, end) % points, step) for step, n in zip(steps, spots)]


def doc_marks(r, length, len_ref, dcol, tm, mb):
    t = iota((length, LANES), 0)
    u = iota((8, length), 1)
    ends = jnp.int32(0)
    d = jnp.zeros((length, LANES), i32)
    e = jnp.zeros((8, length), i32)
    for j in range(SLOTS):
        ends = ends + len_ref[r, j]
        d = d + (t >= ends).astype(i32)
        e = e + (u >= ends).astype(i32)
    dcol[0:8, :] = jnp.full((8, LANES), -1, i32)
    dcol[8 : 8 + length, :] = d
    dcol[8 + length : 16 + length, :] = jnp.full((8, LANES), -1, i32)
    for j in range(KS):
        at = 8 + j - HALF
        tm[j] = (dcol[at : at + length, :] == d).astype(f32)
    for c in range(length // LANES):
        mb[:, c * LANES : (c + 1) * LANES] = jnp.where(d == e[0:1, c * LANES : (c + 1) * LANES], BIG, NEG)


def tap_lanes(tm, length):
    tap = iota((length, LANES), 1) >> 3
    out = jnp.zeros((length, LANES), f32)
    for j in range(KS):
        out = jnp.where(tap == j, tm[j], out)
    return jnp.where(used_taps((length, LANES)), out, 0.0)


def over_taps(x, op):
    for s in (8, 16, 32, 64):
        x = op(x, pltpu.roll(x, s, 1))
    return x


def fill_emat(emat):
    k, c = iota((2 * LANES, ATT), 0) & (LANES - 1), iota((2 * LANES, ATT), 1)
    for j in range(KS):
        emat[:, j * ATT : (j + 1) * ATT] = jnp.where(k == j * 8 + (c >> 6), 1.0, 0.0).astype(bf16)


def two_parts(x):
    high = x.astype(bf16)
    return jnp.concatenate([high, (x - high.astype(f32)).astype(bf16)], axis=1)


def zero_pads(ref, length):
    for c in range(ref.shape[0]):
        ref[c, 0:8, :] = jnp.zeros((8, LANES), f32)
        ref[c, 8 + length : 16 + length, :] = jnp.zeros((8, LANES), f32)


def fwd_kernel(length, pump, len_ref, tok_ref, wp_ref, pw_ref, kw_ref, vec_ref,
               qkvc_ref, kc_ref, dep_ref, ca_ref, tap_ref, join_ref, lse_ref,
               xs, cs, dcol, tm, mb, emat, acc):
    row = pl.program_id(0)
    pump(0)
    pl.when(row > 0)(lambda: doc_marks(row, length, len_ref, dcol, tm, mb))
    pump(1)
    tok = tok_ref[...]
    zero_pads(xs, length)
    zero_pads(cs, length)
    for c in range(6):
        xs[c, 8 : 8 + length, :] = tok[:, c * LANES : (c + 1) * LANES].astype(f32)
    for m, bias in ((0, QB), (1, None), (2, VB), (3, CB)):
        x = nn(tok, wp_ref[:, m * ATT : (m + 1) * ATT])
        if bias is not None:
            x = x + vec_ref[bias : bias + 1, 0:ATT]
        x = x.astype(bf16)
        qkvc_ref[:, m * ATT : (m + 1) * ATT] = x
        if m == 3:
            for c in range(3):
                cs[c, 8 : 8 + length, :] = x[:, c * LANES : (c + 1) * LANES].astype(f32)

    pump(2)
    step = 64

    for c in range(6):
        w = [vec_ref[DW + j : DW + j + 1, c * LANES : (c + 1) * LANES] for j in range(KS)]
        for r in range(0, length, step):
            total = w[HALF] * xs[c, 8 + r : 8 + r + step, :]
            for j in range(KS):
                if j != HALF:
                    at = 8 + r + j - HALF
                    total = total + w[j] * (xs[c, at : at + step, :] * tm[j, r : r + step, :])
            dep_ref[r : r + step, c * LANES : (c + 1) * LANES] = total.astype(bf16)

    pump(3)
    keyconv = nn(dep_ref[...], pw_ref[...]) + vec_ref[PB : PB + 1, 0:ATT]
    kc_ref[...] = keyconv.astype(bf16)
    ca = (keyconv * qkvc_ref[:, 0:ATT].astype(f32)).astype(bf16)
    ca_ref[...] = ca
    logits = nn(ca, kw_ref[...]) + vec_ref[KBR : KBR + 1, 0:LANES]
    e = jnp.exp(logits - over_taps(logits, jnp.maximum))
    taps = e / over_taps(e, jnp.add)
    tap_ref[...] = taps
    spread = two_parts(taps * tap_lanes(tm, length))
    for j in range(KS):
        if j in (0, 4, 8):
            pump(4 + j // 4)
        if j % 2 == 0:
            t = nn(spread, emat[:, j * ATT : min(j + 2, KS) * ATT])
        for c in range(3):
            at, k = 8 + j - HALF, (j % 2 * 3 + c) * LANES
            part = t[:, k : k + LANES] * cs[c, at : at + length, :]
            if j:
                part = part + acc[:, c * LANES : (c + 1) * LANES]
            if j < KS - 1:
                acc[:, c * LANES : (c + 1) * LANES] = part
            else:
                join_ref[:, ATT + c * LANES : ATT + (c + 1) * LANES] = part.astype(bf16)

    for p in range(3):
        pump(7 + p)
        cols = slice(p * LANES, (p + 1) * LANES)
        q, k, v = (qkvc_ref[:, m * ATT + p * LANES : m * ATT + (p + 1) * LANES] for m in range(3))
        qs = q.astype(f32) * SCALE
        vt = v.astype(f32).T
        lane, sub = iota((length, LANES), 1), iota((LANES, length), 0)
        halves = []
        for h in range(2):
            qh = jnp.where((lane >= HEAD_DIM) == bool(h), qs, 0.0).astype(bf16)
            vh = jnp.where((sub >= HEAD_DIM) == bool(h), vt, 1.0).astype(bf16)
            z = jnp.minimum(nt(k, qh), mb[...])
            top = jnp.max(z, axis=0, keepdims=True)
            o = nn(vh, jnp.exp(z - top).astype(bf16))
            s = o[(1 - h) * HEAD_DIM : (1 - h) * HEAD_DIM + 1, :]
            lse_ref[0, 2 * p + h : 2 * p + h + 1, :] = top + jnp.log(s)
            halves.append(o[h * HEAD_DIM : (h + 1) * HEAD_DIM, :] / s)
        join_ref[:, cols] = jnp.concatenate(halves, axis=0).T.astype(bf16)
    pump(10)


def blocked(rows, cols):
    return pl.BlockSpec((rows, cols), lambda r: (r, 0))


def row_scratch(length):
    return [
        VM((6, length + 16, LANES), f32),
        VM((3, length + 16, LANES), f32),
        VM((length + 16, LANES), i32),
        VM((KS, length, LANES), f32),
        VM((length, length), f32),
        VM((2 * LANES, KS * ATT), bf16),
    ]


FWD_POINTS = 11
FWD_SPOTS = (2, 4, 8, 10, 14, 16, 20, 25, 99)


def run_front(first, second, own, tokens, lengths):
    outer, inner = lax.axis_size("dp"), lax.axis_size("fsdp")
    rows, count = lengths.shape[0], tokens.shape[0]
    length = count // rows
    scratch = row_scratch(length) + [VM((length, ATT), f32)]
    n = len(scratch)
    lead = max(first.chunk, second.chunk)
    more = [
        VM((first.rows + 2 * lead + 16, LANES), f32),
        VM((first.small * first.chunk, LANES), f32),
        VM((512, LANES), f32),
    ]
    m = len(Gather.scratch(first, inner))

    def body(own_ref, len_ref, tok_ref, *refs):
        outs, (dw_ref, fi_ref, fo_ref, wp_ref, pw_ref, kw_ref, vec_ref), refs = refs[:7], refs[7:14], refs[14:]
        rows_refs, (ownf, flat, kwt), refs = refs[:n], refs[n : n + 3], refs[n + 3 :]
        place = Place(outer, inner)
        a = Gather(first, place, ownf, lead, refs[:m])
        b = Gather(second, place, ownf, lead, refs[m:])

        def begin():
            place.call()
            ownf[...] = jnp.zeros_like(ownf)
            ownf[lead : lead + first.rows, :] = own_ref[...].astype(f32)
            _, _, dcol, tm, mb, emat, _ = rows_refs
            fill_emat(emat)
            place.all_here()
            a.offer()
            b.offer()
            doc_marks(0, length, len_ref, dcol, tm, mb)
            a.form()
            for s in range(1, place.lines):
                a.along(s)
                a.across(s - 1)
            a.across(place.lines - 1)
            b.form()
            a.diagonal()
            a.rest()
            from_frames(first, a.buf, [(wp_ref, D, ATT, k * ATT) for k in range(4)] + [(pw_ref, D, ATT, 0)], flat)
            unpack_small(flat, kw_ref, vec_ref, kwt)

        def end():
            a.finish()
            b.rest()
            b.finish()
            from_frames(second, b.buf, ((dw_ref, D, D, 0), (fi_ref, D, FF // GROUPS, 0), (fo_ref, FF, D // GROUPS, 0)))

        steps = []
        for s in range(1, place.lines):
            steps.append(lambda s=s: b.along(s))
            steps.append(lambda s=s: b.across(s - 1))
        steps += [lambda: b.across(place.lines - 1), b.diagonal, end]
        spots = FWD_SPOTS if len(steps) == len(FWD_SPOTS) else [99] * len(steps)
        pump = pumped([(0, 0, begin)] + spread_over(steps, rows, FWD_POINTS, spots))
        fwd_kernel(length, pump, len_ref, tok_ref, wp_ref, pw_ref, kw_ref, vec_ref, *outs, *rows_refs)

    full = pl.BlockSpec(memory_space=VM)
    return pl.pallas_call(
        body,
        grid=(rows,),
        out_shape=[
            jax.ShapeDtypeStruct((count, 4 * ATT), bf16),
            jax.ShapeDtypeStruct((count, ATT), bf16),
            jax.ShapeDtypeStruct((count, D), bf16),
            jax.ShapeDtypeStruct((count, ATT), bf16),
            jax.ShapeDtypeStruct((count, LANES), f32),
            jax.ShapeDtypeStruct((count, D), bf16),
            jax.ShapeDtypeStruct((rows, 8, length), f32),
            jax.ShapeDtypeStruct((D, D), bf16),
            jax.ShapeDtypeStruct((D, FF // GROUPS), bf16),
            jax.ShapeDtypeStruct((FF, D // GROUPS), bf16),
            jax.ShapeDtypeStruct((D, 4 * ATT), bf16),
            jax.ShapeDtypeStruct((D, ATT), bf16),
            jax.ShapeDtypeStruct((ATT, LANES), bf16),
            jax.ShapeDtypeStruct((VROWS, FF), f32),
        ],
        in_specs=[full, pl.BlockSpec(memory_space=pltpu.SMEM), blocked(length, D)],
        out_specs=[
            blocked(length, 4 * ATT),
            blocked(length, ATT),
            blocked(length, D),
            blocked(length, ATT),
            blocked(length, LANES),
            blocked(length, D),
            pl.BlockSpec((1, 8, length), lambda r: (r, 0, 0)),
        ]
        + [full] * 7,
        scratch_shapes=scratch + more + Gather.scratch(first, inner) + Gather.scratch(second, inner),
        compiler_params=pltpu.CompilerParams(vmem_limit_bytes=VMEM_LIMIT, collective_id=0, has_side_effects=True),
        name="front",
    )(own, lengths, tokens)


def mid_kernel(sect, length, len_ref, tok_ref, join_ref, cot_ref, dw_ref, fi_ref, fo_ref, vec_ref,
               out_ref, gf_ref, gj_ref, part_ref, gv_ref,
               gdw_ref, gfi_ref, gfo_ref, xh1, rs1, nl, act, slope, gsec, gsl, wide):
    row = pl.program_id(0)
    fg, dg = FF // GROUPS, D // GROUPS

    @pl.when(row == 0)
    def _():
        for ref in (gdw_ref, gfi_ref, gfo_ref, gv_ref):
            ref[...] = jnp.zeros_like(ref)

    used = jnp.int32(0)
    for j in range(SLOTS):
        used = used + len_ref[row, j]

    def vec(r, n=D):
        return vec_ref[r : r + 1, 0:n]

    step = 128
    halves = [slice(k * (length // 2), (k + 1) * (length // 2)) for k in range(2)]
    for rows in halves:
        gsec[rows, :] = nn(join_ref[rows, :], dw_ref[...])

    def norm1(i):
        at = slice(i * step, (i + 1) * step)
        z = gsec[at, :] + vec(DB) + tok_ref[at, :].astype(f32)
        z = z - jnp.mean(z, axis=1, keepdims=True)
        r = lax.rsqrt(jnp.mean(z * z, axis=1, keepdims=True) + EPS)
        x = z * r
        xh1[at, :] = x
        rs1[at, :] = jnp.broadcast_to(r, (step, LANES))
        nl[at, :] = (x * vec(N1G) + vec(N1S)).astype(bf16)

    for k in range(length // step):
        norm1(k)

    tile = 768
    per = fg // tile

    tiles = [(g, i) for g in range(GROUPS) for i in range(per)]

    def inner(n):
        g, i = tiles[n]
        for rows in halves if n == 0 else [slice(0, length)]:
            wide[n % 2, rows, :] = nn(nl[rows, g * dg : (g + 1) * dg], fi_ref[g * dg : (g + 1) * dg, i * tile : (i + 1) * tile])

    inner(0)
    for n, (g, i) in enumerate(tiles):
        if n + 1 < len(tiles):
            inner(n + 1)
        col = slice(g * fg + i * tile, g * fg + (i + 1) * tile)
        for r in range(0, length, 64):
            x = wide[n % 2, r : r + 64, :] + vec_ref[FIB : FIB + 1, col]
            phi = 0.5 * lax.erf(x * math.sqrt(0.5)) + 0.5
            e = jnp.exp2(x * x * (-0.5 / math.log(2.0)))
            act[r : r + 64, col] = (x * phi).astype(bf16)
            slope[r : r + 64, col] = (phi + x * (1.0 / math.sqrt(2.0 * math.pi)) * e).astype(bf16)

    for rows in halves:
        for g in range(GROUPS):
            gsec[rows, g * dg : (g + 1) * dg] = nn(act[rows, g * fg : (g + 1) * fg], fo_ref[g * fg : (g + 1) * fg, :])

    def rows8(x):
        total = x[0:8]
        for k in range(8, x.shape[0], 8):
            total = total + x[k : k + 8]
        return total

    def norm2(i, carry):
        at = slice(i * step, (i + 1) * step)
        norm = xh1[at, :] * vec(N1G) + vec(N1S)
        z = gsec[at, :] + vec(FOB) + norm
        z = z - jnp.mean(z, axis=1, keepdims=True)
        r = lax.rsqrt(jnp.mean(z * z, axis=1, keepdims=True) + EPS)
        x = z * r
        keep = ((iota((step, 1), 0) + i * step) < used).astype(f32)
        out_ref[at, :] = ((x * vec(N2G) + vec(N2S)) * keep).astype(bf16)
        gf = cot_ref[at, :].astype(f32) * keep
        gx = gf * x
        e = gf * vec(N2G)
        gz = r * (e - jnp.mean(e, axis=1, keepdims=True) - x * jnp.mean(e * x, axis=1, keepdims=True))
        gsec[at, :] = gz
        gsl[at, :] = gz.astype(bf16)
        return (carry[0] + rows8(gx), carry[1] + rows8(gf), carry[2] + rows8(gz))

    none = jnp.zeros((8, D), f32)
    sums = (none, none, none)
    for k in range(length // step):
        sums = norm2(k, sums)

    def add(r, value):
        gv_ref[r : r + 1, 0 : value.shape[1]] += jnp.sum(value, axis=0, keepdims=True)

    for r, value in zip((N2G, N2S, FOB), sums):
        add(r, value)

    def slopes(n):
        g, i = tiles[n]
        at = slice(g * fg + i * tile, g * fg + (i + 1) * tile)
        for rows in halves if n == 0 else [slice(0, length)]:
            wide[n % 2, rows, :] = nt(gsl[rows, g * dg : (g + 1) * dg], fo_ref[at, :])

    slopes(0)
    for n, (g, i) in enumerate(tiles):
        if n + 1 < len(tiles):
            slopes(n + 1)
        at = slice(g * fg + i * tile, g * fg + (i + 1) * tile)
        total = jnp.zeros((8, tile), f32)
        for r in range(0, length, 64):
            x = wide[n % 2, r : r + 64, :] * slope[r : r + 64, at].astype(f32)
            slope[r : r + 64, at] = x.astype(bf16)
            total = total + rows8(x)
        gv_ref[FIB : FIB + 1, at] += jnp.sum(total, axis=0, keepdims=True)
    for rows in halves:
        for g in range(GROUPS):
            gsec[rows, g * dg : (g + 1) * dg] += nt(slope[rows, g * fg : (g + 1) * fg], fi_ref[g * dg : (g + 1) * dg, :])

    def norm1_back(i, carry):
        at = slice(i * step, (i + 1) * step)
        gn = gsec[at, :]
        x = xh1[at, :]
        e = gn * vec(N1G)
        r = rs1[at, :]
        r = jnp.concatenate([r] * (D // LANES), axis=1)
        gz = r * (e - jnp.mean(e, axis=1, keepdims=True) - x * jnp.mean(e * x, axis=1, keepdims=True))
        gf_ref[at, :] = gz.astype(bf16)
        return (carry[0] + rows8(gn * x), carry[1] + rows8(gn), carry[2] + rows8(gz))

    sums = (none, none, none)
    todo = list(enumerate(tiles))
    for k in range(length // step):
        sums = norm1_back(k, sums)
        if k % 2:
            rows = slice((k - 1) * step, (k + 1) * step)
            gj_ref[rows, :] = nt(gf_ref[rows, :], dw_ref[...]).astype(bf16)
        for n, (g, i) in todo[k * len(todo) // (length // step) : (k + 1) * len(todo) // (length // step)]:
            at = slice(g * fg + i * tile, g * fg + (i + 1) * tile)
            gfo_ref[at, :] += tn(act[:, at], gsl[:, g * dg : (g + 1) * dg])
            gfi_ref[g * dg : (g + 1) * dg, i * tile : (i + 1) * tile] += tn(nl[:, g * dg : (g + 1) * dg], slope[:, at])
    for r, value in zip((N1G, N1S, DB), sums):
        add(r, value)
    gdw_ref[...] += tn(join_ref[...], gf_ref[...])

    @pl.when(row == pl.num_programs(0) - 1)
    def _():
        to_frames(sect, part_ref, ((gdw_ref, D, D, 0), (gfi_ref, D, FF // GROUPS, 0), (gfo_ref, FF, D // GROUPS, 0)))


def run_mid(sect, tokens, lengths, joined, cotangent, dw, fi, fo, vec):
    rows, count = lengths.shape[0], tokens.shape[0]
    length = count // rows

    def body(*refs):
        mid_kernel(sect, length, *refs)

    full = pl.BlockSpec(memory_space=VM)
    return pl.pallas_call(
        body,
        grid=(rows,),
        out_shape=[
            jax.ShapeDtypeStruct((count, D), bf16),
            jax.ShapeDtypeStruct((count, D), bf16),
            jax.ShapeDtypeStruct((count, D), bf16),
            jax.ShapeDtypeStruct((sect.count, sect.chunk, LANES), bf16),
            jax.ShapeDtypeStruct((VROWS, FF), f32),
        ],
        in_specs=[pl.BlockSpec(memory_space=pltpu.SMEM)] + [blocked(length, D)] * 3 + [full] * 4,
        out_specs=[blocked(length, D)] * 3 + [full] * 2,
        scratch_shapes=[
            VM((D, D), f32),
            VM((D, FF // GROUPS), f32),
            VM((FF, D // GROUPS), f32),
            VM((length, D), f32),
            VM((length, LANES), f32),
            VM((length, D), bf16),
            VM((length, FF), bf16),
            VM((length, FF), bf16),
            VM((length, D), f32),
            VM((length, D), bf16),
            VM((2, length, 768), f32),
        ],
        compiler_params=pltpu.CompilerParams(vmem_limit_bytes=VMEM_LIMIT),
        name="mid",
    )(lengths, tokens, joined, cotangent, dw, fi, fo, vec)


def bwd_kernel(length, pump, len_ref, tok_ref, qkvc_ref, kc_ref, dep_ref, ca_ref, tap_ref, join_ref, lse_ref, gf_ref, gj_ref,
               wp_ref, pw_ref, kw_ref, vec_ref,
               gt_ref, gp_ref, gpw_ref, gkw_ref, gv_ref,
               ds, cs, dcol, tm, mb, emat, gs, tp, prod, gq, gfour, acc):
    row = pl.program_id(0)

    @pl.when(row == 0)
    def _():
        fill_emat(emat)
        for ref in (gp_ref, gpw_ref, gkw_ref, gv_ref):
            ref[...] = jnp.zeros_like(ref)

    doc_marks(row, length, len_ref, dcol, tm, mb)
    pump(0)
    for ref in (ds, cs, gs, tp):
        zero_pads(ref, length)

    def add(r, value):
        gv_ref[r : r + 1, 0 : value.shape[1]] += jnp.sum(value, axis=0, keepdims=True)

    for p in range(3):
        pump(1 + p)
        cols = slice(p * LANES, (p + 1) * LANES)
        q, k, v = (qkvc_ref[:, m * ATT + p * LANES : m * ATT + (p + 1) * LANES] for m in range(3))
        g = gj_ref[:, cols]
        lane, sub = iota((length, LANES), 1), iota((16, LANES), 1)
        which = iota((16, LANES), 0)
        marks = jnp.where((sub >= HEAD_DIM) == (which >= 8), 1.0, 0.0).astype(bf16)
        dots = g.astype(f32) * join_ref[:, cols].astype(f32)
        high = dots.astype(bf16)
        dots = nt(marks, high) + nt(marks, (dots - high.astype(f32)).astype(bf16))
        qs = q.astype(f32) * SCALE
        kt = k.astype(f32).T.astype(bf16)
        gk, gv, gqt = None, None, []
        for h in range(2):
            own = (lane >= HEAD_DIM) == bool(h)
            qh = jnp.where(own, qs, 0.0).astype(bf16)
            gh = jnp.where(own, g.astype(f32), 0.0).astype(bf16)
            prob = jnp.exp(jnp.minimum(nt(k, qh), mb[...]) - lse_ref[0, 2 * p + h : 2 * p + h + 1, :])
            dsc = (prob * (nt(v, gh) - dots[8 * h : 8 * h + 1, :])).astype(bf16)
            a, b = nn(prob.astype(bf16), gh), nn(dsc, qh)
            gv, gk = (a, b) if h == 0 else (gv + a, gk + b)
            gqt.append(nn(kt, dsc)[h * HEAD_DIM : (h + 1) * HEAD_DIM, :])
        gq[:, cols] = jnp.concatenate(gqt, axis=0).T * SCALE
        gfour[:, ATT + p * LANES : ATT + (p + 1) * LANES] = gk.astype(bf16)
        gfour[:, 2 * ATT + p * LANES : 2 * ATT + (p + 1) * LANES] = gv.astype(bf16)
        gv_ref[VB : VB + 1, cols] += jnp.sum(gv, axis=0, keepdims=True)

    pump(4)
    for c in range(3):
        cs[c, 8 : 8 + length, :] = qkvc_ref[:, 3 * ATT + c * LANES : 3 * ATT + (c + 1) * LANES].astype(f32)
        gs[c, 8 : 8 + length, :] = gj_ref[:, ATT + c * LANES : ATT + (c + 1) * LANES].astype(f32)
    gtaps = None
    for j in range(0, KS, 3):
        for k in range(3):
            for c in range(3):
                at, spot = 8 + j + k - HALF, ((j + k) * 3 + c) * length
                prod[spot : spot + length, :] = (gs[c, 8 : 8 + length, :] * cs[c, at : at + length, :]).astype(bf16)
        blocks = [prod[n * length : (n + 1) * length, :] for n in range(j * 3, j * 3 + 9)]
        x = nt(jnp.concatenate(blocks, axis=1), emat[0:LANES, j * ATT : (j + 3) * ATT])
        gtaps = x if gtaps is None else gtaps + x
    marks = tap_lanes(tm, length)
    gtaps = gtaps * marks
    pump(5)
    taps = jnp.where(used_taps((length, LANES)), tap_ref[...], 0.0)
    glog = taps * (gtaps - over_taps(taps * gtaps, jnp.add))
    add(KBR, glog)
    glog = glog.astype(bf16)
    gkw_ref[...] += tn(ca_ref[...], glog)
    gca = nt(glog, kw_ref[...])

    tp[0, 8 : 8 + length, :] = taps * marks
    tap = iota((length, LANES), 1) >> 3
    moved = jnp.zeros((length, LANES), f32)
    for j in range(KS):
        at = 8 + HALF - j
        moved = jnp.where(tap == j, tp[0, at : at + length, :], moved)
    spread = two_parts(moved)
    for j in range(KS):
        if j % 2 == 0:
            t = nn(spread, emat[:, j * ATT : min(j + 2, KS) * ATT])
        for c in range(3):
            at, k = 8 + HALF - j, (j % 2 * 3 + c) * LANES
            part = t[:, k : k + LANES] * gs[c, at : at + length, :]
            if j:
                part = part + acc[:, c * LANES : (c + 1) * LANES]
            if j < KS - 1:
                acc[:, c * LANES : (c + 1) * LANES] = part
            else:
                gfour[:, 3 * ATT + c * LANES : 3 * ATT + (c + 1) * LANES] = part.astype(bf16)
                gv_ref[CB : CB + 1, c * LANES : (c + 1) * LANES] += jnp.sum(part, axis=0, keepdims=True)

    pump(6)
    gkc = gca * qkvc_ref[:, 0:ATT].astype(f32)
    gquery = gq[...] + gca * kc_ref[...].astype(f32)
    add(QB, gquery)
    gfour[:, 0:ATT] = gquery.astype(bf16)
    add(PB, gkc)
    gkc = gkc.astype(bf16)
    gpw_ref[...] += tn(dep_ref[...], gkc)
    for c in range(3):
        x = nt(gkc, pw_ref[c * 256 : (c + 1) * 256, :])
        ds[2 * c, 8 : 8 + length, :] = x[:, 0:LANES]
        ds[2 * c + 1, 8 : 8 + length, :] = x[:, LANES:]
    pump(7)
    for m in range(2):
        cols = slice(2 * m * ATT, 2 * (m + 1) * ATT)
        gp_ref[:, cols] += tn(tok_ref[...], gfour[:, cols])

    pump(8)
    step = 64
    for c in range(6):
        cols = slice(c * LANES, (c + 1) * LANES)
        w = [vec_ref[DW + j : DW + j + 1, cols] for j in range(KS)]
        sums = [None] * KS
        if c % 2 == 0:
            direct = nt(gfour[...], wp_ref[c * LANES : (c + 2) * LANES, :])
        for r in range(0, length, step):
            tok = tok_ref[r : r + step, cols].astype(f32)
            total = gf_ref[r : r + step, cols].astype(f32) + direct[r : r + step, (c % 2) * LANES : (c % 2 + 1) * LANES]
            for j in range(KS):
                at = 8 + r + j - HALF
                u = ds[c, at : at + step, :]
                if j != HALF:
                    u = u * tm[j, r : r + step, :]
                total = total + w[KS - 1 - j] * u
                u = tok * u
                part = u[0:8]
                for s in range(8, step, 8):
                    part = part + u[s : s + 8]
                sums[j] = part if r == 0 else sums[j] + part
            gt_ref[r : r + step, cols] = total.astype(bf16)
        for j in range(KS):
            gv_ref[DW + KS - 1 - j : DW + KS - j, cols] += jnp.sum(sums[j], axis=0, keepdims=True)
    pump(9)


BWD_POINTS = 10
FIRST_AT, SECOND_AT, THIRD_AT = (2, 3, 6, 10), (5, 9, 13, 15), (9, 13, 16, 17)
SETTLE_AT, TAKE_AT = 21, 26


def run_back(first, second, part, va, tokens, lengths, saved, gf, gj, wp, pw, kw, vec):
    outer, inner = lax.axis_size("dp"), lax.axis_size("fsdp")
    qkvc, kc, dep, ca, taps, joined, lse = saved
    rows, count = lengths.shape[0], tokens.shape[0]
    length = count // rows
    lead = max(first.chunk, second.chunk)
    tall = -(-max(3 * KS * length, first.count * first.chunk) // 16) * 16
    scratch = row_scratch(length) + [
        VM((3, length + 16, LANES), f32),
        VM((1, length + 16, LANES), f32),
        VM((tall, LANES), bf16),
        VM((length, ATT), f32),
        VM((length, 4 * ATT), bf16),
        VM((length, ATT), f32),
    ]
    grads = [VM((D, 4 * ATT), f32), VM((D, ATT), f32), VM((ATT, LANES), f32), VM((VROWS, FF), f32)]
    more = [
        VM((first.rows + 2 * lead + 16, LANES), f32),
        VM((max(first.small * first.chunk, 384), LANES), f32),
        VM((512, LANES), f32),
    ]
    n, m = len(scratch), len(Scatter.scratch(first, inner))

    def body(part_ref, va_ref, *refs):
        ours, (gt_ref, own_ref), refs = refs[:15], refs[15:17], refs[17:]
        rows_refs, sums, refs = refs[:n], refs[n : n + 4], refs[n + 4 :]
        (out, flat, kwt), refs = refs[:3], refs[3:]
        gp_ref, gpw_ref, gkw_ref, gv_ref = sums
        stage = rows_refs[8]
        place = Place(outer, inner)
        a = Scatter(first, place, lambda v: stage.at[pl.ds(v * first.chunk, first.chunk)], out, lead, refs[:m], True)
        b = Scatter(second, place, lambda v: part_ref.at[v], out, lead, refs[m:], False)

        def begin():
            out[...] = jnp.zeros_like(out)
            place.all_here()
            b.core()

        def end():
            gv_ref[...] += va_ref[...]
            pack_small(flat, gkw_ref, gv_ref, kwt)
            to_frames(
                first,
                Rows(stage, first.chunk),
                [(gp_ref, D, ATT, k * ATT) for k in range(4)] + [(gpw_ref, D, ATT, 0)],
                flat,
            )
            steps = a.sums()
            a.core(*a.far[:2])
            for k, step in enumerate(steps):
                if k < len(a.far) - 2:
                    a.core(a.far[2 + k])
                step()
            b.finish()
            a.settle()
            a.take()
            a.finish()
            own_ref[...] = out[lead : lead + first.rows, :]

        due = [(0, 0, begin)]
        for step, spots in ((b.first, FIRST_AT), (b.second, SECOND_AT), (b.third, THIRD_AT)):
            steps = [lambda step=step, d=d: step(d) for d in b.far]
            due += spread_over(steps, rows, BWD_POINTS, list(spots) + [spots[-1]] * (len(steps) - len(spots)))
        due += spread_over([b.settle, b.take], rows, BWD_POINTS, (SETTLE_AT, TAKE_AT))
        pump = pumped(due + [(rows - 1, BWD_POINTS - 1, end)])
        pl.when(pl.program_id(0) == 0)(place.call)
        bwd_kernel(length, pump, *ours, gt_ref, *sums, *rows_refs)

    full = pl.BlockSpec(memory_space=VM)
    return pl.pallas_call(
        body,
        grid=(rows,),
        out_shape=[jax.ShapeDtypeStruct((count, D), bf16), jax.ShapeDtypeStruct((first.rows, LANES), f32)],
        in_specs=[
            pl.BlockSpec(memory_space=pl.ANY),
            full,
            pl.BlockSpec(memory_space=pltpu.SMEM),
            blocked(length, D),
            blocked(length, 4 * ATT),
            blocked(length, ATT),
            blocked(length, D),
            blocked(length, ATT),
            blocked(length, LANES),
            blocked(length, D),
            pl.BlockSpec((1, 8, length), lambda r: (r, 0, 0)),
            blocked(length, D),
            blocked(length, D),
            full,
            full,
            full,
            full,
        ],
        out_specs=[blocked(length, D), full],
        scratch_shapes=scratch + grads + more + Scatter.scratch(first, inner) + Scatter.scratch(second, inner),
        compiler_params=pltpu.CompilerParams(vmem_limit_bytes=VMEM_LIMIT, collective_id=1, has_side_effects=True),
        name="back",
    )(part, va, lengths, tokens, qkvc, kc, dep, ca, taps, joined, lse, gf, gj, wp, pw, kw, vec)


def shards(tokens, doc_lengths, params, cotangent):
    rows = params.shape[0] // LANES
    outer, inner = lax.axis_size("dp"), lax.axis_size("fsdp")
    first, second = sections(outer * inner, rows, inner)
    *saved, dw, fi, fo, wp, pw, kw, vec = run_front(first, second, params.reshape(rows, LANES), tokens, doc_lengths)
    output, gf, gj, part, va = run_mid(second, tokens, doc_lengths, saved[5], cotangent, dw, fi, fo, vec)
    gt, own_grad = run_back(first, second, part, va, tokens, doc_lengths, saved, gf, gj, wp, pw, kw, vec)
    return output, gt, own_grad.reshape(rows * LANES)


def solution(mesh):
    axes = ("dp", "fsdp")
    placed = (P(axes, None), P(axes, None), P(axes), P(axes, None))
    return jax.shard_map(
        shards,
        mesh=mesh,
        in_specs=placed,
        out_specs=(P(axes, None), P(axes, None), P(axes)),
        check_vma=False,
    )
```

```python
import math

import jax
import jax.numpy as jnp
from jax import lax
from jax.experimental import pallas as pl
from jax.experimental.pallas import tpu as pltpu
from jax.sharding import PartitionSpec as P

D = 768
HEADS = 6
HEAD_DIM = 64
ATT = HEADS * HEAD_DIM
FF = 3072
GROUPS = 2
KS = 9
HALF = KS // 2
SLOTS = 16
EPS = 1e-12
LANES = 128
NEG = -1e30
BIG = 3e38
SCALE = HEAD_DIM ** (-0.5)

f32 = jnp.float32
bf16 = jnp.bfloat16
i32 = jnp.int32

FIRST = 5 * D * ATT // LANES
MATRICES = FIRST + (D * D + 2 * D * FF // GROUPS) // LANES
DEPTH_AT = 0
KERNEL_AT = KS * D // LANES
BIAS_AT = KERNEL_AT + ATT * HEADS * KS // LANES
TAIL_AT = BIAS_AT + 4 * ATT // LANES
SMALL = TAIL_AT + 61
KB = HEADS * KS

QB, VB, CB, PB, KBR, DB, N1G, N1S, FIB, FOB, N2G, N2S, DW = range(13)
VROWS = 24
TAIL = [(DB, 6), (N1G, 6), (N1S, 6), (FIB, 24), (FOB, 6), (N2G, 6), (N2S, 6)]

VM = pltpu.VMEM
VMEM_LIMIT = 62 * 1024 * 1024


def nn(a, b):
    return lax.dot_general(a, b, (((1,), (0,)), ((), ())), preferred_element_type=f32)


def nt(a, b):
    return lax.dot_general(a, b, (((1,), (1,)), ((), ())), preferred_element_type=f32)


def tn(a, b):
    return lax.dot_general(a, b, (((0,), (0,)), ((), ())), preferred_element_type=f32)


def iota(shape, axis):
    return lax.broadcasted_iota(i32, shape, axis)


def loop(count, body, unroll=1):
    def step(i, carry):
        body(i)
        return carry

    lax.fori_loop(0, count, step, 0, unroll=unroll)


def tap_perm():
    k, n = iota((LANES, LANES), 0), iota((LANES, LANES), 1)
    head, tap = n & 7, n >> 3
    return jnp.where((k == head * KS + tap) & (head < HEADS) & (tap < KS), 1.0, 0.0).astype(bf16)


def used_taps(shape):
    n = iota(shape, len(shape) - 1)
    return ((n & 7) < HEADS) & ((n >> 3) < KS)


def padded(rows):
    return -(-rows // 16) * 16


class Section:
    def __init__(self, base, kinds, chunk, small, rows, count, inner):
        self.base, self.chunk, self.rows, self.count, self.inner = base, chunk, rows, count, inner
        self.main = sum(n for n, _ in kinds)
        self.small = -(-SMALL // chunk) if small else 0
        self.kinds = kinds + ([(self.small, 1)] if small else [])
        self.used = self.main + self.small
        self.pieces = -(-rows // chunk) + 1
        self.slots = self.pieces + self.small
        self.sources = (chunk - 2) // rows + 2
        self.lead = -(-base // rows)

    def seat(self, v, pick=jnp.where):
        q, r, n = v // 3, v % 3, self.count
        if self.small:
            near = pick(q < n // 4, r * (n // 4) + q, 3 * (n // 4) + v - 3 * (n // 4))
            return pick(v < self.main, near, n - self.small + v - self.main)
        return pick(r < 2, self.lead + 2 * q + r, q)

    def chunk_at(self, d):
        n = self.count
        if self.small:
            quarter = n // 4
            v = jnp.where(d < 3 * quarter, 3 * lax.rem(d, quarter) + d // quarter, d)
            v = jnp.where(v < self.main, v, self.used)
            return jnp.where(d >= n - self.small, self.main + d - (n - self.small), v)
        t = d - self.lead
        v = jnp.where(d < self.main // 3, 3 * d + 2, self.used)
        return jnp.where((t >= 0) & (t < 2 * self.main // 3), 3 * (t // 2) + lax.rem(t, 2), v)

    def start(self, v):
        at = self.base + v * self.chunk
        if self.small:
            at = jnp.where(v >= self.main, MATRICES + (v - self.main) * self.chunk, at)
        return at

    def first_piece(self, i):
        return jnp.maximum(self.rows * i - self.base, 0) // self.chunk

    def of_owner(self, i, k):
        if k < self.pieces:
            v = self.first_piece(i) + k
            ok = v < self.main
        else:
            v = self.main + k - self.pieces + 0 * i
            ok = v >= 0
        at = self.start(v)
        return v, ok & (at < self.rows * (i + 1)) & (at + self.chunk > self.rows * i)

    def of_chunk(self, v, s):
        i = self.start(v) // self.rows + s
        return i, (v < self.used) & (i < self.count) & (self.rows * i < self.start(v) + self.chunk)

    def source_of(self, v, i):
        return i - self.start(v) // self.rows

    def slot_of(self, v, i):
        return jnp.where(v < self.main, v - self.first_piece(i), self.pieces + v - self.main)

    def by_kind(self, v, action):
        at, seen = 0, {}
        for n, per in self.kinds:
            seen.setdefault(per, []).append((at, at + n))
            at += n
        for per, spans in seen.items():
            ok = False
            for lo, hi in spans:
                ok = ((v >= lo) & (v < hi)) | ok
            pl.when(ok)(lambda per=per: action(per))


def sections(count, rows, inner):
    big, little = 24576 // count, 12288 // count
    first = Section(0, [(FIRST // little, 3)], little, True, rows, count, inner)
    kinds = [(D * n // LANES // big, n // LANES) for n in (D, FF // GROUPS)] + [(FF * 3 // big, 3)]
    return first, Section(FIRST, kinds, big, False, rows, count, inner)


class Rows:
    def __init__(self, ref, chunk):
        self.ref, self.chunk = ref, chunk

    def __setitem__(self, where, value):
        v, rows, _ = where
        self.ref[v * self.chunk + rows.start : v * self.chunk + rows.stop, :] = value


def choose(ok, a, b):
    return a if ok else b


def pieces_of(sect, matrices):
    v = 0
    for ref, height, width, col in matrices:
        per = width // LANES
        tall = sect.chunk // per
        for r in range(0, height, tall):
            for c in range(per):
                cols = slice(col + c * LANES, col + (c + 1) * LANES)
                yield sect.seat(v, choose), slice(c * tall, (c + 1) * tall), ref, slice(r, r + tall), cols
            v += 1


def to_frames(sect, part, matrices, small=None):
    for seat, rows, ref, r, c in pieces_of(sect, matrices):
        part[seat, rows, :] = ref[r, c].astype(bf16)
    for k in range(sect.small):
        part[sect.seat(sect.main + k, choose), slice(0, sect.chunk), :] = small[
            k * sect.chunk : (k + 1) * sect.chunk, :
        ].astype(bf16)
    for d in set(range(sect.count)) - {sect.seat(v, choose) for v in range(sect.used)}:
        part[d, slice(0, sect.chunk), :] = jnp.zeros((sect.chunk, LANES), bf16)


def from_frames(sect, buf, matrices, small=None):
    for seat, rows, ref, r, c in pieces_of(sect, matrices):
        ref[r, c] = buf[seat, rows, :]
    for k in range(sect.small):
        small[k * sect.chunk : (k + 1) * sect.chunk, :] = buf[sect.seat(sect.main + k, choose)].astype(f32)


def unpack_small(flat, kw_ref, vec_ref, kwt):
    vec_ref[...] = jnp.zeros_like(vec_ref)
    for row in range(4):
        for c in range(3):
            at = BIAS_AT + row * 3 + c
            vec_ref[row : row + 1, c * LANES : (c + 1) * LANES] = flat[at : at + 1, :]
    for j in range(KS):
        for c in range(6):
            at = DEPTH_AT + j * 6 + c
            vec_ref[DW + j : DW + j + 1, c * LANES : (c + 1) * LANES] = flat[at : at + 1, :]
    at = TAIL_AT
    lane = iota((64, LANES), 1)
    first = pltpu.roll(flat[at : at + 64, :], LANES - KB, 1)
    second = pltpu.roll(flat[at + 1 : at + 65, :], LANES - KB, 1)
    kwt[0:64, :] = jnp.where(lane < LANES - KB, first, second)
    at = 0
    for row, many in TAIL:
        for c in range(many):
            vec_ref[row : row + 1, c * LANES : (c + 1) * LANES] = kwt[at + c : at + c + 1, :]
        at += many
    perm = tap_perm()
    lane8 = iota((16, LANES), 1)
    kb = jnp.broadcast_to(flat[TAIL_AT : TAIL_AT + 1, :], (16, LANES))
    kb = nn(jnp.where(lane8 < KB, kb, 0.0).astype(bf16), perm)
    kb = jnp.where(used_taps((16, LANES)), kb, NEG)
    vec_ref[KBR : KBR + 1, 0:LANES] = kb[0:1]

    lane = iota((8, LANES), 1)
    for a in range(64):
        c0, ln = divmod(a * KB, LANES)
        at = KERNEL_AT + c0
        x = pltpu.roll(flat[pl.ds(at, 8, stride=27), :], (LANES - ln) % LANES, 1)
        if ln + KB > LANES:
            y = pltpu.roll(flat[pl.ds(at + 1, 8, stride=27), :], (LANES - ln) % LANES, 1)
            x = jnp.where(lane < LANES - ln, x, y)
        kwt[pl.ds(a, 8, stride=64), :] = jnp.where(lane < KB, x, 0.0)
    kw_ref[...] = nn(kwt[0:ATT, :].astype(bf16), perm).astype(bf16)


def pack_small(flat, gkw_ref, vec, kwt):
    flat[...] = jnp.zeros_like(flat)
    perm = tap_perm()
    kwt[...] = jnp.zeros_like(kwt)
    kwt[0:ATT, :] = nt(gkw_ref[...].astype(bf16), perm)
    lane = iota((8, LANES), 1)
    for a in range(64):
        c0, ln = divmod(a * KB, LANES)
        at = KERNEL_AT + c0
        x = pltpu.roll(kwt[pl.ds(a, 8, stride=64), :], ln, 1)
        if ln + KB > LANES:
            flat[pl.ds(at, 8, stride=27), :] += jnp.where(lane >= ln, x, 0.0)
            flat[pl.ds(at + 1, 8, stride=27), :] += jnp.where(lane < ln, x, 0.0)
        else:
            flat[pl.ds(at, 8, stride=27), :] += x
    for row in range(4):
        for c in range(3):
            at = BIAS_AT + row * 3 + c
            flat[at : at + 1, :] = vec[row : row + 1, c * LANES : (c + 1) * LANES]
    for j in range(KS):
        for c in range(6):
            at = DEPTH_AT + j * 6 + c
            flat[at : at + 1, :] = vec[DW + j : DW + j + 1, c * LANES : (c + 1) * LANES]
    kwt[...] = jnp.zeros_like(kwt)
    at = 8
    for row, many in TAIL:
        for c in range(many):
            kwt[at + c : at + c + 1, :] = vec[row : row + 1, c * LANES : (c + 1) * LANES]
        at += many
    lane = iota((72, LANES), 1)
    before = pltpu.roll(kwt[7:79, :], KB, 1)
    here = pltpu.roll(kwt[8:80, :], KB, 1)
    at = TAIL_AT
    flat[at : at + 72, :] = jnp.where(lane < KB, before, here)
    kb = jnp.broadcast_to(vec[KBR : KBR + 1, 0:LANES], (16, LANES))
    kb = nt(jnp.where(used_taps((16, LANES)), kb, 0.0).astype(bf16), perm)
    lane = iota((1, LANES), 1)
    flat[at : at + 1, :] = jnp.where(lane < KB, kb[0:1], flat[at : at + 1, :])


class Place:
    def __init__(self, outer, inner):
        self.outer, self.inner, self.count = outer, inner, outer * inner
        self.lines = inner // 2
        dp, fs = lax.axis_index("dp"), lax.axis_index("fsdp")
        self.y, self.x, self.z, self.c = dp // 2, lax.rem(dp, 2), fs // 2, lax.rem(fs, 2)
        self.me = dp * inner + fs

    def coords(self, dy=0, dx=0, z=None, dc=0):
        def flip(v, d):
            return 1 - v if d else v

        z = self.z if z is None else z
        return flip(self.y, dy) * 2 + flip(self.x, dx), z * 2 + flip(self.c, dc)

    def index(self, **d):
        o, i = self.coords(**d)
        return o * self.inner + i

    def device(self, n):
        return n // self.inner, lax.rem(n, self.inner)

    def item(self, t):
        s = (t + 1) // 2
        z = self.z - s if t % 2 else self.z + s
        return z, (z >= 0) & (z < self.lines), s, t % 2 == 1

    def call(self):
        barrier = pltpu.get_barrier_semaphore()
        for n in range(1, self.count):
            peer = self.device(lax.rem(self.me + n, self.count))
            pl.semaphore_signal(barrier, inc=1, device_id=peer, device_id_type=pl.DeviceIdType.MESH)

    def all_here(self):
        pl.semaphore_wait(pltpu.get_barrier_semaphore(), self.count - 1)


class Copies:
    def __init__(self, send, recv):
        self.send, self.recv, self.used, self.made = send, recv, 0, []

    def start(self, src, dst, peer, slot, ok=None, group=None):
        number = self.used if group is None else group
        if group is None:
            self.used += 1
        assert number < self.send.shape[0]

        def make():
            return pltpu.make_async_remote_copy(
                src_ref=src(),
                dst_ref=dst(),
                send_sem=self.send.at[number],
                recv_sem=self.recv.at[slot() if callable(slot) else slot],
                device_id=peer(),
                device_id_type=pl.DeviceIdType.MESH,
            )

        if group is None:
            self.made.append((make, ok))
        guarded(ok, lambda: make().start())

    def sent(self, ref, group):
        pltpu.make_async_copy(ref, ref, self.send.at[group]).wait()

    def arrived(self, dst, slot, ok=None):
        def wait():
            ref = dst()
            pltpu.make_async_copy(ref, ref, self.recv.at[slot]).wait()

        guarded(ok, wait)

    def finish(self):
        for make, ok in self.made:
            guarded(ok, lambda make=make: make().wait_send())


def guarded(ok, action):
    if ok is None:
        action()
    else:
        pl.when(ok())(action)


def half_of(chunk):
    return -(-chunk // 32) * 16


class Gather:
    @staticmethod
    def scratch(sect, inner):
        lines = inner // 2
        items = 2 * lines - 1
        return [
            VM((sect.count, sect.chunk, LANES), bf16),
            VM((sect.slots, sect.chunk, LANES), bf16),
            VM((sect.sources, sect.chunk, LANES), bf16),
            VM((sect.chunk, LANES), f32),
            pltpu.SemaphoreType.DMA((sect.slots + items + 3,)),
            pltpu.SemaphoreType.DMA((sect.sources + 9 * items,)),
        ]

    def __init__(self, sect, place, ownf, lead, scratch):
        self.sect, self.place, self.ownf, self.lead = sect, place, ownf, lead
        self.buf, self.win, self.land, self.frame, send, recv = scratch
        self.copies = Copies(send, recv)
        n = 2 * place.lines - 1
        self.items = n
        self.group = sect.slots + n + 2
        self.Z, self.X, self.Y, self.A, self.B, self.CZ, self.CX, self.CY, self.CD = (sect.sources + n * k for k in range(9))
        cut = half_of(sect.chunk)
        self.half = {"a": pl.ds(0, cut), "b": pl.ds(cut, sect.chunk - cut)}

    def offer(self):
        for k in range(self.sect.slots):
            self.give(k)

    def give(self, k):
        sect, place, me = self.sect, self.place, self.place.me
        v, ok = sect.of_owner(me, k)

        @pl.when(ok)
        def _():
            at = self.lead + sect.start(v) - sect.rows * me
            self.win[k] = self.ownf[pl.ds(at, sect.chunk), :].astype(bf16)

        @pl.when(ok & (sect.seat(v) == me))
        def _():
            self.land[sect.source_of(v, me)] = self.win[k]

        def chunk():
            return sect.of_owner(me, k)[0]

        def away():
            v, ok = sect.of_owner(me, k)
            return ok & (sect.seat(v) != me)

        def source():
            return jnp.clip(sect.source_of(chunk(), me), 0, sect.sources - 1)

        def seat():
            return jnp.clip(sect.seat(chunk()), 0, sect.count - 1)

        self.copies.start(lambda: self.win.at[k], lambda: self.land.at[source()], lambda: place.device(seat()), source, away)

    def form(self):
        sect, me = self.sect, self.place.me
        v = sect.chunk_at(me)
        row = iota((sect.chunk, LANES), 0) + sect.start(v)
        x = None
        for s in range(sect.sources):
            i, ok = sect.of_chunk(v, s)
            self.copies.arrived(lambda: self.land.at[s], s, lambda: ok & (i != me))
            here = self.land[s].astype(f32)
            x = here if x is None else jnp.where(row >= sect.rows * i, here, x)
        self.frame[...] = x

        def settle(per):
            tall = sect.chunk // per
            for c in range(per):
                self.buf[me, c * tall : (c + 1) * tall, :] = self.frame[pl.ds(c, tall, stride=per), :].astype(bf16)

        sect.by_kind(v, settle)

        @pl.when(v >= sect.used)
        def _():
            self.buf[me] = jnp.zeros((sect.chunk, LANES), bf16)

        self.pass_on(0)

    def ref(self, t, which=None, **way):
        def make():
            at = self.place.index(z=self.place.item(t)[0], **way)
            return self.buf.at[at] if which is None else self.buf.at[at, self.half[which]]

        return make

    def ok(self, t):
        return None if t == 0 else lambda: self.place.item(t)[1]

    def same(self, ref, peer, slot, ok, group=True):
        self.copies.start(ref, ref, peer, slot, ok, self.group if group else None)

    def finish(self):
        self.copies.sent(self.buf.at[pl.ds(0, 7 * self.place.lines)], self.group)
        self.copies.finish()

    def beside(self, **way):
        return lambda: self.place.coords(**way)

    def pass_on(self, t):
        place = self.place
        _, _, s, below = place.item(t)
        for way in (1, -1) if t == 0 else ((1,) if below else (-1,)):
            slot = 2 * s + 1 if way > 0 else 2 * s + 2

            def inside(way=way):
                there = place.z + way
                good = (there >= 0) & (there < place.lines)
                return good if t == 0 else good & place.item(t)[1]

            if slot < self.items:
                self.same(self.ref(t), lambda way=way: place.coords(z=place.z + way), self.Z + slot, inside, False)
        ok = self.ok(t)
        self.same(self.ref(t), self.beside(dx=1), self.X + t, ok)
        self.same(self.ref(t), self.beside(dy=1), self.Y + t, ok)
        self.same(self.ref(t), self.beside(dc=1), self.CZ + t, ok)

    def at_distance(self, s):
        return [0] if s == 0 else [2 * s - 1, 2 * s]

    def along(self, s):
        for t in self.at_distance(s):
            self.copies.arrived(self.ref(t), self.Z + t, self.ok(t))
            self.pass_on(t)

    def across(self, s):
        for t in self.at_distance(s):
            ok = self.ok(t)
            self.copies.arrived(self.ref(t, dx=1), self.X + t, ok)
            self.same(self.ref(t, "a", dx=1), self.beside(dy=1), self.A + t, ok)
            self.same(self.ref(t, dx=1), self.beside(dc=1), self.CX + t, ok)
            self.copies.arrived(self.ref(t, dy=1), self.Y + t, ok)
            self.same(self.ref(t, "b", dy=1), self.beside(dx=1), self.B + t, ok)
            self.same(self.ref(t, dy=1), self.beside(dc=1), self.CY + t, ok)

    def diagonal(self):
        for t in range(self.items):
            ok = self.ok(t)
            self.copies.arrived(self.ref(t, "a", dy=1, dx=1), self.A + t, ok)
            self.copies.arrived(self.ref(t, "b", dy=1, dx=1), self.B + t, ok)
            self.same(self.ref(t, dy=1, dx=1), self.beside(dc=1), self.CD + t, ok)

    def rest(self):
        for t in range(self.items):
            for k, way in ((self.CZ, {}), (self.CX, {"dx": 1}), (self.CY, {"dy": 1}), (self.CD, {"dy": 1, "dx": 1})):
                self.copies.arrived(self.ref(t, dc=1, **way), k + t, self.ok(t))


class Scatter:
    @staticmethod
    def scratch(sect, inner):
        lines = inner // 2
        cut = half_of(sect.chunk)
        return [
            VM((4 * lines, sect.chunk, LANES), bf16),
            VM((4 * lines, sect.chunk, LANES), bf16),
            VM((2 * lines, cut, LANES), bf16),
            VM((2 * lines, sect.chunk - cut, LANES), bf16),
            VM((lines, sect.chunk - cut, LANES), bf16),
            VM((lines, cut, LANES), bf16),
            VM((lines, sect.chunk, LANES), bf16),
            VM((sect.chunk, LANES), f32),
            VM((sect.chunk, LANES), f32),
            VM((sect.chunk, LANES), bf16),
            VM((sect.slots, sect.chunk, LANES), bf16),
            pltpu.SemaphoreType.DMA((sect.sources + 6,)),
            pltpu.SemaphoreType.DMA((11 * lines + sect.slots,)),
            pltpu.SemaphoreType.DMA((4 * lines,)),
        ]

    def __init__(self, sect, place, part, out, lead, scratch, close):
        self.close = close
        self.sect, self.place, self.part, self.out, self.lead = sect, place, part, out, lead
        (self.work, self.rc, self.ry, self.rx, self.ry2, self.rx2, self.rz, self.frame, self.flat, self.low, self.land,
         send, recv, self.near) = scratch
        self.copies = Copies(send, recv)
        lines = place.lines
        self.lines = lines
        cut = half_of(sect.chunk)
        self.a, self.b = pl.ds(0, cut), pl.ds(cut, sect.chunk - cut)
        self.C, self.YA, self.XB, self.XA, self.YB, self.Z, self.O = (lines * k for k in (0, 4, 6, 8, 9, 10, 11))
        self.far = list(range(1, lines)) + [0]
        self.group = sect.sources

    def sums(self):
        out = []
        for n in range(self.lines + 2):
            for lag, step in ((0, self.first), (1, self.second), (2, self.third)):
                if 0 <= n - lag < self.lines:
                    out.append(lambda step=step, d=self.far[n - lag]: step(d))
        return out

    def z(self, d):
        return lax.rem(self.place.z + d, self.lines) if d else self.place.z

    def at(self, dy, dx, d):
        return (dy * 2 + dx) * self.lines + d

    def own(self, dy, dx, d):
        k = self.at(dy, dx, d)
        there = self.place.index(dy=dy, dx=dx, z=self.z(d))
        return pltpu.make_async_copy(self.part(there), self.work.at[k], self.near.at[k])

    def core(self, *places):
        place = self.place

        def give(dy, dx, d):
            k = self.at(dy, dx, d)
            self.copies.start(
                lambda: self.part(place.index(dy=dy, dx=dx, z=self.z(d), dc=1)),
                lambda: self.rc.at[k],
                lambda: place.coords(dc=1),
                self.C + k,
                group=self.group,
            )
            if not self.close:
                self.own(dy, dx, d).start()

        for d in places or self.far:
            for dy, dx in ((1, 1), (1, 0), (0, 1), (0, 0)):
                give(dy, dx, d)

    def send(self, k, rows, buf, n, way, slot, group):
        self.copies.start(
            lambda: self.work.at[k, rows],
            lambda: buf.at[n],
            lambda: self.place.coords(**way),
            slot,
            group=self.group + group,
        )

    def finish(self):
        for k, ref in enumerate((self.rc, self.ry, self.rx, self.rx2, self.ry2, self.rz.at[pl.ds(1, self.lines - 1)])):
            self.copies.sent(ref, self.group + k)
        self.copies.finish()

    def got(self, buf, n, slot):
        self.copies.arrived(lambda: buf.at[n], slot)

    def plus(self, k, rows, other):
        self.work[k, rows] = (self.work[k, rows].astype(f32) + other.astype(f32)).astype(bf16)

    def first(self, d):
        lines = self.lines
        for dy, dx in ((1, 1), (1, 0), (0, 1), (0, 0)):
            k = self.at(dy, dx, d)
            if self.close:
                self.got(self.rc, k, self.C + k)
                mine = self.part(self.place.index(dy=dy, dx=dx, z=self.z(d)))[...]
                self.work[k] = (mine.astype(f32) + self.rc[k].astype(f32)).astype(bf16)
            else:
                self.own(dy, dx, d).wait()
                self.got(self.rc, k, self.C + k)
                self.plus(k, pl.ds(0, self.sect.chunk), self.rc[k])
            if dy:
                self.send(k, self.a, self.ry, dx * lines + d, {"dy": 1}, self.YA + dx * lines + d, 1)
            if dx:
                self.send(k, self.b, self.rx, dy * lines + d, {"dx": 1}, self.XB + dy * lines + d, 2)

    def second(self, d):
        n = self.lines + d
        self.got(self.ry, n, self.YA + n)
        self.plus(self.at(0, 1, d), self.a, self.ry[n])
        self.send(self.at(0, 1, d), self.a, self.rx2, d, {"dx": 1}, self.XA + d, 3)
        self.got(self.rx, n, self.XB + n)
        self.plus(self.at(1, 0, d), self.b, self.rx[n])
        self.send(self.at(1, 0, d), self.b, self.ry2, d, {"dy": 1}, self.YB + d, 4)

    def third(self, d):
        k = self.at(0, 0, d)
        self.got(self.ry, d, self.YA + d)
        self.got(self.rx, d, self.XB + d)
        self.got(self.rx2, d, self.XA + d)
        self.got(self.ry2, d, self.YB + d)
        self.plus(k, self.a, self.ry[d].astype(f32) + self.rx2[d].astype(f32))
        self.plus(k, self.b, self.rx[d].astype(f32) + self.ry2[d].astype(f32))
        if d:
            self.copies.start(
                lambda: self.work.at[k],
                lambda: self.rz.at[d],
                lambda: self.place.coords(z=self.z(d)),
                self.Z + d,
                group=self.group + 5,
            )

    def settle(self):
        sect, me = self.sect, self.place.me
        total = self.work[self.at(0, 0, 0)].astype(f32)
        for d in range(1, self.lines):
            self.got(self.rz, d, self.Z + d)
            total = total + self.rz[d].astype(f32)
        self.frame[...] = total

        def spread(per):
            tall = sect.chunk // per
            for c in range(per):
                self.flat[pl.ds(c, tall, stride=per), :] = self.frame[c * tall : (c + 1) * tall, :]

        self.flat[...] = total
        sect.by_kind(sect.chunk_at(me), spread)
        self.low[...] = self.flat[...].astype(bf16)
        for s in range(sect.sources):
            self.give(s)

    def give(self, s):
        sect, me = self.sect, self.place.me
        i, ok = sect.of_chunk(sect.chunk_at(me), s)

        @pl.when(ok & (i == me))
        def _():
            self.land[sect.slot_of(sect.chunk_at(me), i)] = self.low[...]

        def owner():
            return jnp.minimum(sect.of_chunk(sect.chunk_at(me), s)[0], sect.count - 1)

        def slot():
            return jnp.clip(sect.slot_of(sect.chunk_at(me), owner()), 0, sect.slots - 1)

        def away():
            i, ok = sect.of_chunk(sect.chunk_at(me), s)
            return ok & (i != me)

        self.copies.start(
            lambda: self.low, lambda: self.land.at[slot()], lambda: self.place.device(owner()), lambda: self.O + slot(), away
        )

    def take(self):
        sect, me = self.sect, self.place.me
        for k in range(sect.slots):
            v, ok = sect.of_owner(me, k)
            self.copies.arrived(lambda: self.land.at[k], self.O + k, lambda: ok & (sect.seat(v) != me))

            @pl.when(ok)
            def _():
                at = self.lead + sect.start(v) - sect.rows * me
                self.out[pl.ds(at, sect.chunk), :] = self.land[k].astype(f32)


def pumped(due):
    row = pl.program_id(0)

    def pump(point):
        for r, p, step in due:
            if p == point:
                pl.when(row == r)(step)

    return pump


def spread_over(steps, rows, points, spots):
    end = rows * points - 1
    return [(min(n, end) // points, min(n, end) % points, step) for step, n in zip(steps, spots)]


def doc_marks(r, length, len_ref, dcol, tm, mb):
    t = iota((length, LANES), 0)
    u = iota((8, length), 1)
    ends = jnp.int32(0)
    d = jnp.zeros((length, LANES), i32)
    e = jnp.zeros((8, length), i32)
    for j in range(SLOTS):
        ends = ends + len_ref[r, j]
        d = d + (t >= ends).astype(i32)
        e = e + (u >= ends).astype(i32)
    dcol[0:8, :] = jnp.full((8, LANES), -1, i32)
    dcol[8 : 8 + length, :] = d
    dcol[8 + length : 16 + length, :] = jnp.full((8, LANES), -1, i32)
    for j in range(KS):
        at = 8 + j - HALF
        tm[j] = (dcol[at : at + length, :] == d).astype(f32)
    for c in range(length // LANES):
        mb[:, c * LANES : (c + 1) * LANES] = jnp.where(d == e[0:1, c * LANES : (c + 1) * LANES], BIG, NEG)


def tap_lanes(tm, length):
    tap = iota((length, LANES), 1) >> 3
    out = jnp.zeros((length, LANES), f32)
    for j in range(KS):
        out = jnp.where(tap == j, tm[j], out)
    return jnp.where(used_taps((length, LANES)), out, 0.0)


def over_taps(x, op):
    for s in (8, 16, 32, 64):
        x = op(x, pltpu.roll(x, s, 1))
    return x


def fill_emat(emat):
    k, c = iota((2 * LANES, ATT), 0) & (LANES - 1), iota((2 * LANES, ATT), 1)
    for j in range(KS):
        emat[:, j * ATT : (j + 1) * ATT] = jnp.where(k == j * 8 + (c >> 6), 1.0, 0.0).astype(bf16)


def two_parts(x):
    high = x.astype(bf16)
    return jnp.concatenate([high, (x - high.astype(f32)).astype(bf16)], axis=1)


def zero_pads(ref, length):
    for c in range(ref.shape[0]):
        ref[c, 0:8, :] = jnp.zeros((8, LANES), f32)
        ref[c, 8 + length : 16 + length, :] = jnp.zeros((8, LANES), f32)


def fwd_kernel(length, pump, len_ref, tok_ref, wp_ref, pw_ref, kw_ref, vec_ref,
               qkvc_ref, kc_ref, dep_ref, ca_ref, tap_ref, join_ref, lse_ref,
               xs, cs, dcol, tm, mb, emat, acc):
    row = pl.program_id(0)
    pump(0)
    pl.when(row > 0)(lambda: doc_marks(row, length, len_ref, dcol, tm, mb))
    pump(1)
    tok = tok_ref[...]
    zero_pads(xs, length)
    zero_pads(cs, length)
    for c in range(6):
        xs[c, 8 : 8 + length, :] = tok[:, c * LANES : (c + 1) * LANES].astype(f32)
    for m, bias in ((0, QB), (1, None), (2, VB), (3, CB)):
        x = nn(tok, wp_ref[:, m * ATT : (m + 1) * ATT])
        if bias is not None:
            x = x + vec_ref[bias : bias + 1, 0:ATT]
        x = x.astype(bf16)
        qkvc_ref[:, m * ATT : (m + 1) * ATT] = x
        if m == 3:
            for c in range(3):
                cs[c, 8 : 8 + length, :] = x[:, c * LANES : (c + 1) * LANES].astype(f32)

    pump(2)
    step = 64

    for c in range(6):
        w = [vec_ref[DW + j : DW + j + 1, c * LANES : (c + 1) * LANES] for j in range(KS)]
        for r in range(0, length, step):
            total = w[HALF] * xs[c, 8 + r : 8 + r + step, :]
            for j in range(KS):
                if j != HALF:
                    at = 8 + r + j - HALF
                    total = total + w[j] * (xs[c, at : at + step, :] * tm[j, r : r + step, :])
            dep_ref[r : r + step, c * LANES : (c + 1) * LANES] = total.astype(bf16)

    pump(3)
    keyconv = nn(dep_ref[...], pw_ref[...]) + vec_ref[PB : PB + 1, 0:ATT]
    kc_ref[...] = keyconv.astype(bf16)
    ca = (keyconv * qkvc_ref[:, 0:ATT].astype(f32)).astype(bf16)
    ca_ref[...] = ca
    logits = nn(ca, kw_ref[...]) + vec_ref[KBR : KBR + 1, 0:LANES]
    e = jnp.exp(logits - over_taps(logits, jnp.maximum))
    taps = e / over_taps(e, jnp.add)
    tap_ref[...] = taps
    spread = two_parts(taps * tap_lanes(tm, length))
    for j in range(KS):
        if j in (0, 4, 8):
            pump(4 + j // 4)
        if j % 2 == 0:
            t = nn(spread, emat[:, j * ATT : min(j + 2, KS) * ATT])
        for c in range(3):
            at, k = 8 + j - HALF, (j % 2 * 3 + c) * LANES
            part = t[:, k : k + LANES] * cs[c, at : at + length, :]
            if j:
                part = part + acc[:, c * LANES : (c + 1) * LANES]
            if j < KS - 1:
                acc[:, c * LANES : (c + 1) * LANES] = part
            else:
                join_ref[:, ATT + c * LANES : ATT + (c + 1) * LANES] = part.astype(bf16)

    for p in range(3):
        pump(7 + p)
        cols = slice(p * LANES, (p + 1) * LANES)
        q, k, v = (qkvc_ref[:, m * ATT + p * LANES : m * ATT + (p + 1) * LANES] for m in range(3))
        qs = q.astype(f32) * SCALE
        vt = v.astype(f32).T
        lane, sub = iota((length, LANES), 1), iota((LANES, length), 0)
        halves = []
        for h in range(2):
            qh = jnp.where((lane >= HEAD_DIM) == bool(h), qs, 0.0).astype(bf16)
            vh = jnp.where((sub >= HEAD_DIM) == bool(h), vt, 1.0).astype(bf16)
            z = jnp.minimum(nt(k, qh), mb[...])
            top = jnp.max(z, axis=0, keepdims=True)
            o = nn(vh, jnp.exp(z - top).astype(bf16))
            s = o[(1 - h) * HEAD_DIM : (1 - h) * HEAD_DIM + 1, :]
            lse_ref[0, 2 * p + h : 2 * p + h + 1, :] = top + jnp.log(s)
            halves.append(o[h * HEAD_DIM : (h + 1) * HEAD_DIM, :] / s)
        join_ref[:, cols] = jnp.concatenate(halves, axis=0).T.astype(bf16)
    pump(10)


def blocked(rows, cols):
    return pl.BlockSpec((rows, cols), lambda r: (r, 0))


def row_scratch(length):
    return [
        VM((6, length + 16, LANES), f32),
        VM((3, length + 16, LANES), f32),
        VM((length + 16, LANES), i32),
        VM((KS, length, LANES), f32),
        VM((length, length), f32),
        VM((2 * LANES, KS * ATT), bf16),
    ]


FWD_POINTS = 11
FWD_SPOTS = (2, 4, 8, 10, 14, 16, 20, 25, 99)


def run_front(first, second, own, tokens, lengths):
    outer, inner = lax.axis_size("dp"), lax.axis_size("fsdp")
    rows, count = lengths.shape[0], tokens.shape[0]
    length = count // rows
    scratch = row_scratch(length) + [VM((length, ATT), f32)]
    n = len(scratch)
    lead = max(first.chunk, second.chunk)
    more = [
        VM((first.rows + 2 * lead + 16, LANES), f32),
        VM((first.small * first.chunk, LANES), f32),
        VM((512, LANES), f32),
    ]
    m = len(Gather.scratch(first, inner))

    def body(own_ref, len_ref, tok_ref, *refs):
        outs, (dw_ref, fi_ref, fo_ref, wp_ref, pw_ref, kw_ref, vec_ref), refs = refs[:7], refs[7:14], refs[14:]
        rows_refs, (ownf, flat, kwt), refs = refs[:n], refs[n : n + 3], refs[n + 3 :]
        place = Place(outer, inner)
        a = Gather(first, place, ownf, lead, refs[:m])
        b = Gather(second, place, ownf, lead, refs[m:])

        def begin():
            place.call()
            ownf[...] = jnp.zeros_like(ownf)
            ownf[lead : lead + first.rows, :] = own_ref[...].astype(f32)
            _, _, dcol, tm, mb, emat, _ = rows_refs
            fill_emat(emat)
            place.all_here()
            a.offer()
            b.offer()
            doc_marks(0, length, len_ref, dcol, tm, mb)
            a.form()
            for s in range(1, place.lines):
                a.along(s)
                a.across(s - 1)
            a.across(place.lines - 1)
            b.form()
            a.diagonal()
            a.rest()
            from_frames(first, a.buf, [(wp_ref, D, ATT, k * ATT) for k in range(4)] + [(pw_ref, D, ATT, 0)], flat)
            unpack_small(flat, kw_ref, vec_ref, kwt)

        def end():
            a.finish()
            b.rest()
            b.finish()
            from_frames(second, b.buf, ((dw_ref, D, D, 0), (fi_ref, D, FF // GROUPS, 0), (fo_ref, FF, D // GROUPS, 0)))

        steps = []
        for s in range(1, place.lines):
            steps.append(lambda s=s: b.along(s))
            steps.append(lambda s=s: b.across(s - 1))
        steps += [lambda: b.across(place.lines - 1), b.diagonal, end]
        spots = FWD_SPOTS if len(steps) == len(FWD_SPOTS) else [99] * len(steps)
        pump = pumped([(0, 0, begin)] + spread_over(steps, rows, FWD_POINTS, spots))
        fwd_kernel(length, pump, len_ref, tok_ref, wp_ref, pw_ref, kw_ref, vec_ref, *outs, *rows_refs)

    full = pl.BlockSpec(memory_space=VM)
    return pl.pallas_call(
        body,
        grid=(rows,),
        out_shape=[
            jax.ShapeDtypeStruct((count, 4 * ATT), bf16),
            jax.ShapeDtypeStruct((count, ATT), bf16),
            jax.ShapeDtypeStruct((count, D), bf16),
            jax.ShapeDtypeStruct((count, ATT), bf16),
            jax.ShapeDtypeStruct((count, LANES), f32),
            jax.ShapeDtypeStruct((count, D), bf16),
            jax.ShapeDtypeStruct((rows, 8, length), f32),
            jax.ShapeDtypeStruct((D, D), bf16),
            jax.ShapeDtypeStruct((D, FF // GROUPS), bf16),
            jax.ShapeDtypeStruct((FF, D // GROUPS), bf16),
            jax.ShapeDtypeStruct((D, 4 * ATT), bf16),
            jax.ShapeDtypeStruct((D, ATT), bf16),
            jax.ShapeDtypeStruct((ATT, LANES), bf16),
            jax.ShapeDtypeStruct((VROWS, FF), f32),
        ],
        in_specs=[full, pl.BlockSpec(memory_space=pltpu.SMEM), blocked(length, D)],
        out_specs=[
            blocked(length, 4 * ATT),
            blocked(length, ATT),
            blocked(length, D),
            blocked(length, ATT),
            blocked(length, LANES),
            blocked(length, D),
            pl.BlockSpec((1, 8, length), lambda r: (r, 0, 0)),
        ]
        + [full] * 7,
        scratch_shapes=scratch + more + Gather.scratch(first, inner) + Gather.scratch(second, inner),
        compiler_params=pltpu.CompilerParams(vmem_limit_bytes=VMEM_LIMIT, collective_id=0, has_side_effects=True),
        name="front",
    )(own, lengths, tokens)


def mid_kernel(sect, length, len_ref, tok_ref, join_ref, cot_ref, dw_ref, fi_ref, fo_ref, vec_ref,
               out_ref, gf_ref, gj_ref, part_ref, gv_ref,
               gdw_ref, gfi_ref, gfo_ref, xh1, rs1, nl, act, slope, gsec, gsl, wide):
    row = pl.program_id(0)
    fg, dg = FF // GROUPS, D // GROUPS

    @pl.when(row == 0)
    def _():
        for ref in (gdw_ref, gfi_ref, gfo_ref, gv_ref):
            ref[...] = jnp.zeros_like(ref)

    used = jnp.int32(0)
    for j in range(SLOTS):
        used = used + len_ref[row, j]

    def vec(r, n=D):
        return vec_ref[r : r + 1, 0:n]

    step = 128
    halves = [slice(k * (length // 2), (k + 1) * (length // 2)) for k in range(2)]
    for rows in halves:
        gsec[rows, :] = nn(join_ref[rows, :], dw_ref[...])

    def norm1(i):
        at = slice(i * step, (i + 1) * step)
        z = gsec[at, :] + vec(DB) + tok_ref[at, :].astype(f32)
        z = z - jnp.mean(z, axis=1, keepdims=True)
        r = lax.rsqrt(jnp.mean(z * z, axis=1, keepdims=True) + EPS)
        x = z * r
        xh1[at, :] = x
        rs1[at, :] = jnp.broadcast_to(r, (step, LANES))
        nl[at, :] = (x * vec(N1G) + vec(N1S)).astype(bf16)

    for k in range(length // step):
        norm1(k)

    tile = 768
    per = fg // tile

    tiles = [(g, i) for g in range(GROUPS) for i in range(per)]

    def inner(n):
        g, i = tiles[n]
        for rows in halves if n == 0 else [slice(0, length)]:
            wide[n % 2, rows, :] = nn(nl[rows, g * dg : (g + 1) * dg], fi_ref[g * dg : (g + 1) * dg, i * tile : (i + 1) * tile])

    inner(0)
    for n, (g, i) in enumerate(tiles):
        if n + 1 < len(tiles):
            inner(n + 1)
        col = slice(g * fg + i * tile, g * fg + (i + 1) * tile)
        for r in range(0, length, 64):
            x = wide[n % 2, r : r + 64, :] + vec_ref[FIB : FIB + 1, col]
            phi = 0.5 * lax.erf(x * math.sqrt(0.5)) + 0.5
            e = jnp.exp2(x * x * (-0.5 / math.log(2.0)))
            act[r : r + 64, col] = (x * phi).astype(bf16)
            slope[r : r + 64, col] = (phi + x * (1.0 / math.sqrt(2.0 * math.pi)) * e).astype(bf16)

    for rows in halves:
        for g in range(GROUPS):
            gsec[rows, g * dg : (g + 1) * dg] = nn(act[rows, g * fg : (g + 1) * fg], fo_ref[g * fg : (g + 1) * fg, :])

    def rows8(x):
        total = x[0:8]
        for k in range(8, x.shape[0], 8):
            total = total + x[k : k + 8]
        return total

    def norm2(i, carry):
        at = slice(i * step, (i + 1) * step)
        norm = xh1[at, :] * vec(N1G) + vec(N1S)
        z = gsec[at, :] + vec(FOB) + norm
        z = z - jnp.mean(z, axis=1, keepdims=True)
        r = lax.rsqrt(jnp.mean(z * z, axis=1, keepdims=True) + EPS)
        x = z * r
        keep = ((iota((step, 1), 0) + i * step) < used).astype(f32)
        out_ref[at, :] = ((x * vec(N2G) + vec(N2S)) * keep).astype(bf16)
        gf = cot_ref[at, :].astype(f32) * keep
        gx = gf * x
        e = gf * vec(N2G)
        gz = r * (e - jnp.mean(e, axis=1, keepdims=True) - x * jnp.mean(e * x, axis=1, keepdims=True))
        gsec[at, :] = gz
        gsl[at, :] = gz.astype(bf16)
        return (carry[0] + rows8(gx), carry[1] + rows8(gf), carry[2] + rows8(gz))

    none = jnp.zeros((8, D), f32)
    sums = (none, none, none)
    for k in range(length // step):
        sums = norm2(k, sums)

    def add(r, value):
        gv_ref[r : r + 1, 0 : value.shape[1]] += jnp.sum(value, axis=0, keepdims=True)

    for r, value in zip((N2G, N2S, FOB), sums):
        add(r, value)

    def slopes(n):
        g, i = tiles[n]
        at = slice(g * fg + i * tile, g * fg + (i + 1) * tile)
        for rows in halves if n == 0 else [slice(0, length)]:
            wide[n % 2, rows, :] = nt(gsl[rows, g * dg : (g + 1) * dg], fo_ref[at, :])

    slopes(0)
    for n, (g, i) in enumerate(tiles):
        if n + 1 < len(tiles):
            slopes(n + 1)
        at = slice(g * fg + i * tile, g * fg + (i + 1) * tile)
        total = jnp.zeros((8, tile), f32)
        for r in range(0, length, 64):
            x = wide[n % 2, r : r + 64, :] * slope[r : r + 64, at].astype(f32)
            slope[r : r + 64, at] = x.astype(bf16)
            total = total + rows8(x)
        gv_ref[FIB : FIB + 1, at] += jnp.sum(total, axis=0, keepdims=True)
    for rows in halves:
        for g in range(GROUPS):
            gsec[rows, g * dg : (g + 1) * dg] += nt(slope[rows, g * fg : (g + 1) * fg], fi_ref[g * dg : (g + 1) * dg, :])

    def norm1_back(i, carry):
        at = slice(i * step, (i + 1) * step)
        gn = gsec[at, :]
        x = xh1[at, :]
        e = gn * vec(N1G)
        r = rs1[at, :]
        r = jnp.concatenate([r] * (D // LANES), axis=1)
        gz = r * (e - jnp.mean(e, axis=1, keepdims=True) - x * jnp.mean(e * x, axis=1, keepdims=True))
        gf_ref[at, :] = gz.astype(bf16)
        return (carry[0] + rows8(gn * x), carry[1] + rows8(gn), carry[2] + rows8(gz))

    sums = (none, none, none)
    todo = list(enumerate(tiles))
    for k in range(length // step):
        sums = norm1_back(k, sums)
        if k % 2:
            rows = slice((k - 1) * step, (k + 1) * step)
            gj_ref[rows, :] = nt(gf_ref[rows, :], dw_ref[...]).astype(bf16)
        for n, (g, i) in todo[k * len(todo) // (length // step) : (k + 1) * len(todo) // (length // step)]:
            at = slice(g * fg + i * tile, g * fg + (i + 1) * tile)
            gfo_ref[at, :] += tn(act[:, at], gsl[:, g * dg : (g + 1) * dg])
            gfi_ref[g * dg : (g + 1) * dg, i * tile : (i + 1) * tile] += tn(nl[:, g * dg : (g + 1) * dg], slope[:, at])
    for r, value in zip((N1G, N1S, DB), sums):
        add(r, value)
    gdw_ref[...] += tn(join_ref[...], gf_ref[...])

    @pl.when(row == pl.num_programs(0) - 1)
    def _():
        to_frames(sect, part_ref, ((gdw_ref, D, D, 0), (gfi_ref, D, FF // GROUPS, 0), (gfo_ref, FF, D // GROUPS, 0)))


def run_mid(sect, tokens, lengths, joined, cotangent, dw, fi, fo, vec):
    rows, count = lengths.shape[0], tokens.shape[0]
    length = count // rows

    def body(*refs):
        mid_kernel(sect, length, *refs)

    full = pl.BlockSpec(memory_space=VM)
    return pl.pallas_call(
        body,
        grid=(rows,),
        out_shape=[
            jax.ShapeDtypeStruct((count, D), bf16),
            jax.ShapeDtypeStruct((count, D), bf16),
            jax.ShapeDtypeStruct((count, D), bf16),
            jax.ShapeDtypeStruct((sect.count, sect.chunk, LANES), bf16),
            jax.ShapeDtypeStruct((VROWS, FF), f32),
        ],
        in_specs=[pl.BlockSpec(memory_space=pltpu.SMEM)] + [blocked(length, D)] * 3 + [full] * 4,
        out_specs=[blocked(length, D)] * 3 + [full] * 2,
        scratch_shapes=[
            VM((D, D), f32),
            VM((D, FF // GROUPS), f32),
            VM((FF, D // GROUPS), f32),
            VM((length, D), f32),
            VM((length, LANES), f32),
            VM((length, D), bf16),
            VM((length, FF), bf16),
            VM((length, FF), bf16),
            VM((length, D), f32),
            VM((length, D), bf16),
            VM((2, length, 768), f32),
        ],
        compiler_params=pltpu.CompilerParams(vmem_limit_bytes=VMEM_LIMIT),
        name="mid",
    )(lengths, tokens, joined, cotangent, dw, fi, fo, vec)


def bwd_kernel(length, pump, len_ref, tok_ref, qkvc_ref, kc_ref, dep_ref, ca_ref, tap_ref, join_ref, lse_ref, gf_ref, gj_ref,
               wp_ref, pw_ref, kw_ref, vec_ref,
               gt_ref, gp_ref, gpw_ref, gkw_ref, gv_ref,
               ds, cs, dcol, tm, mb, emat, gs, tp, prod, gq, gfour, acc):
    row = pl.program_id(0)

    @pl.when(row == 0)
    def _():
        fill_emat(emat)
        for ref in (gp_ref, gpw_ref, gkw_ref, gv_ref):
            ref[...] = jnp.zeros_like(ref)

    doc_marks(row, length, len_ref, dcol, tm, mb)
    pump(0)
    for ref in (ds, cs, gs, tp):
        zero_pads(ref, length)

    def add(r, value):
        gv_ref[r : r + 1, 0 : value.shape[1]] += jnp.sum(value, axis=0, keepdims=True)

    for p in range(3):
        pump(1 + p)
        cols = slice(p * LANES, (p + 1) * LANES)
        q, k, v = (qkvc_ref[:, m * ATT + p * LANES : m * ATT + (p + 1) * LANES] for m in range(3))
        g = gj_ref[:, cols]
        lane, sub = iota((length, LANES), 1), iota((16, LANES), 1)
        which = iota((16, LANES), 0)
        marks = jnp.where((sub >= HEAD_DIM) == (which >= 8), 1.0, 0.0).astype(bf16)
        dots = g.astype(f32) * join_ref[:, cols].astype(f32)
        high = dots.astype(bf16)
        dots = nt(marks, high) + nt(marks, (dots - high.astype(f32)).astype(bf16))
        qs = q.astype(f32) * SCALE
        kt = k.astype(f32).T.astype(bf16)
        gk, gv, gqt = None, None, []
        for h in range(2):
            own = (lane >= HEAD_DIM) == bool(h)
            qh = jnp.where(own, qs, 0.0).astype(bf16)
            gh = jnp.where(own, g.astype(f32), 0.0).astype(bf16)
            prob = jnp.exp(jnp.minimum(nt(k, qh), mb[...]) - lse_ref[0, 2 * p + h : 2 * p + h + 1, :])
            dsc = (prob * (nt(v, gh) - dots[8 * h : 8 * h + 1, :])).astype(bf16)
            a, b = nn(prob.astype(bf16), gh), nn(dsc, qh)
            gv, gk = (a, b) if h == 0 else (gv + a, gk + b)
            gqt.append(nn(kt, dsc)[h * HEAD_DIM : (h + 1) * HEAD_DIM, :])
        gq[:, cols] = jnp.concatenate(gqt, axis=0).T * SCALE
        gfour[:, ATT + p * LANES : ATT + (p + 1) * LANES] = gk.astype(bf16)
        gfour[:, 2 * ATT + p * LANES : 2 * ATT + (p + 1) * LANES] = gv.astype(bf16)
        gv_ref[VB : VB + 1, cols] += jnp.sum(gv, axis=0, keepdims=True)

    pump(4)
    for c in range(3):
        cs[c, 8 : 8 + length, :] = qkvc_ref[:, 3 * ATT + c * LANES : 3 * ATT + (c + 1) * LANES].astype(f32)
        gs[c, 8 : 8 + length, :] = gj_ref[:, ATT + c * LANES : ATT + (c + 1) * LANES].astype(f32)
    gtaps = None
    for j in range(0, KS, 3):
        for k in range(3):
            for c in range(3):
                at, spot = 8 + j + k - HALF, ((j + k) * 3 + c) * length
                prod[spot : spot + length, :] = (gs[c, 8 : 8 + length, :] * cs[c, at : at + length, :]).astype(bf16)
        blocks = [prod[n * length : (n + 1) * length, :] for n in range(j * 3, j * 3 + 9)]
        x = nt(jnp.concatenate(blocks, axis=1), emat[0:LANES, j * ATT : (j + 3) * ATT])
        gtaps = x if gtaps is None else gtaps + x
    marks = tap_lanes(tm, length)
    gtaps = gtaps * marks
    pump(5)
    taps = jnp.where(used_taps((length, LANES)), tap_ref[...], 0.0)
    glog = taps * (gtaps - over_taps(taps * gtaps, jnp.add))
    add(KBR, glog)
    glog = glog.astype(bf16)
    gkw_ref[...] += tn(ca_ref[...], glog)
    gca = nt(glog, kw_ref[...])

    tp[0, 8 : 8 + length, :] = taps * marks
    tap = iota((length, LANES), 1) >> 3
    moved = jnp.zeros((length, LANES), f32)
    for j in range(KS):
        at = 8 + HALF - j
        moved = jnp.where(tap == j, tp[0, at : at + length, :], moved)
    spread = two_parts(moved)
    for j in range(KS):
        if j % 2 == 0:
            t = nn(spread, emat[:, j * ATT : min(j + 2, KS) * ATT])
        for c in range(3):
            at, k = 8 + HALF - j, (j % 2 * 3 + c) * LANES
            part = t[:, k : k + LANES] * gs[c, at : at + length, :]
            if j:
                part = part + acc[:, c * LANES : (c + 1) * LANES]
            if j < KS - 1:
                acc[:, c * LANES : (c + 1) * LANES] = part
            else:
                gfour[:, 3 * ATT + c * LANES : 3 * ATT + (c + 1) * LANES] = part.astype(bf16)
                gv_ref[CB : CB + 1, c * LANES : (c + 1) * LANES] += jnp.sum(part, axis=0, keepdims=True)

    pump(6)
    gkc = gca * qkvc_ref[:, 0:ATT].astype(f32)
    gquery = gq[...] + gca * kc_ref[...].astype(f32)
    add(QB, gquery)
    gfour[:, 0:ATT] = gquery.astype(bf16)
    add(PB, gkc)
    gkc = gkc.astype(bf16)
    gpw_ref[...] += tn(dep_ref[...], gkc)
    for c in range(3):
        x = nt(gkc, pw_ref[c * 256 : (c + 1) * 256, :])
        ds[2 * c, 8 : 8 + length, :] = x[:, 0:LANES]
        ds[2 * c + 1, 8 : 8 + length, :] = x[:, LANES:]
    pump(7)
    for m in range(2):
        cols = slice(2 * m * ATT, 2 * (m + 1) * ATT)
        gp_ref[:, cols] += tn(tok_ref[...], gfour[:, cols])

    pump(8)
    step = 64
    for c in range(6):
        cols = slice(c * LANES, (c + 1) * LANES)
        w = [vec_ref[DW + j : DW + j + 1, cols] for j in range(KS)]
        sums = [None] * KS
        if c % 2 == 0:
            direct = nt(gfour[...], wp_ref[c * LANES : (c + 2) * LANES, :])
        for r in range(0, length, step):
            tok = tok_ref[r : r + step, cols].astype(f32)
            total = gf_ref[r : r + step, cols].astype(f32) + direct[r : r + step, (c % 2) * LANES : (c % 2 + 1) * LANES]
            for j in range(KS):
                at = 8 + r + j - HALF
                u = ds[c, at : at + step, :]
                if j != HALF:
                    u = u * tm[j, r : r + step, :]
                total = total + w[KS - 1 - j] * u
                u = tok * u
                part = u[0:8]
                for s in range(8, step, 8):
                    part = part + u[s : s + 8]
                sums[j] = part if r == 0 else sums[j] + part
            gt_ref[r : r + step, cols] = total.astype(bf16)
        for j in range(KS):
            gv_ref[DW + KS - 1 - j : DW + KS - j, cols] += jnp.sum(sums[j], axis=0, keepdims=True)
    pump(9)


BWD_POINTS = 10
FIRST_AT, SECOND_AT, THIRD_AT = (2, 3, 6, 10), (5, 9, 13, 15), (9, 13, 16, 17)
SETTLE_AT, TAKE_AT = 21, 26


def run_back(first, second, part, va, tokens, lengths, saved, gf, gj, wp, pw, kw, vec):
    outer, inner = lax.axis_size("dp"), lax.axis_size("fsdp")
    qkvc, kc, dep, ca, taps, joined, lse = saved
    rows, count = lengths.shape[0], tokens.shape[0]
    length = count // rows
    lead = max(first.chunk, second.chunk)
    tall = -(-max(3 * KS * length, first.count * first.chunk) // 16) * 16
    scratch = row_scratch(length) + [
        VM((3, length + 16, LANES), f32),
        VM((1, length + 16, LANES), f32),
        VM((tall, LANES), bf16),
        VM((length, ATT), f32),
        VM((length, 4 * ATT), bf16),
        VM((length, ATT), f32),
    ]
    grads = [VM((D, 4 * ATT), f32), VM((D, ATT), f32), VM((ATT, LANES), f32), VM((VROWS, FF), f32)]
    more = [
        VM((first.rows + 2 * lead + 16, LANES), f32),
        VM((max(first.small * first.chunk, 384), LANES), f32),
        VM((512, LANES), f32),
    ]
    n, m = len(scratch), len(Scatter.scratch(first, inner))

    def body(part_ref, va_ref, *refs):
        ours, (gt_ref, own_ref), refs = refs[:15], refs[15:17], refs[17:]
        rows_refs, sums, refs = refs[:n], refs[n : n + 4], refs[n + 4 :]
        (out, flat, kwt), refs = refs[:3], refs[3:]
        gp_ref, gpw_ref, gkw_ref, gv_ref = sums
        stage = rows_refs[8]
        place = Place(outer, inner)
        a = Scatter(first, place, lambda v: stage.at[pl.ds(v * first.chunk, first.chunk)], out, lead, refs[:m], True)
        b = Scatter(second, place, lambda v: part_ref.at[v], out, lead, refs[m:], False)

        def begin():
            out[...] = jnp.zeros_like(out)
            place.all_here()
            b.core()

        def end():
            gv_ref[...] += va_ref[...]
            pack_small(flat, gkw_ref, gv_ref, kwt)
            to_frames(
                first,
                Rows(stage, first.chunk),
                [(gp_ref, D, ATT, k * ATT) for k in range(4)] + [(gpw_ref, D, ATT, 0)],
                flat,
            )
            steps = a.sums()
            a.core(*a.far[:2])
            for k, step in enumerate(steps):
                if k < len(a.far) - 2:
                    a.core(a.far[2 + k])
                step()
            b.finish()
            a.settle()
            a.take()
            a.finish()
            own_ref[...] = out[lead : lead + first.rows, :]

        due = [(0, 0, begin)]
        for step, spots in ((b.first, FIRST_AT), (b.second, SECOND_AT), (b.third, THIRD_AT)):
            steps = [lambda step=step, d=d: step(d) for d in b.far]
            due += spread_over(steps, rows, BWD_POINTS, list(spots) + [spots[-1]] * (len(steps) - len(spots)))
        due += spread_over([b.settle, b.take], rows, BWD_POINTS, (SETTLE_AT, TAKE_AT))
        pump = pumped(due + [(rows - 1, BWD_POINTS - 1, end)])
        pl.when(pl.program_id(0) == 0)(place.call)
        bwd_kernel(length, pump, *ours, gt_ref, *sums, *rows_refs)

    full = pl.BlockSpec(memory_space=VM)
    return pl.pallas_call(
        body,
        grid=(rows,),
        out_shape=[jax.ShapeDtypeStruct((count, D), bf16), jax.ShapeDtypeStruct((first.rows, LANES), f32)],
        in_specs=[
            pl.BlockSpec(memory_space=pl.ANY),
            full,
            pl.BlockSpec(memory_space=pltpu.SMEM),
            blocked(length, D),
            blocked(length, 4 * ATT),
            blocked(length, ATT),
            blocked(length, D),
            blocked(length, ATT),
            blocked(length, LANES),
            blocked(length, D),
            pl.BlockSpec((1, 8, length), lambda r: (r, 0, 0)),
            blocked(length, D),
            blocked(length, D),
            full,
            full,
            full,
            full,
        ],
        out_specs=[blocked(length, D), full],
        scratch_shapes=scratch + grads + more + Scatter.scratch(first, inner) + Scatter.scratch(second, inner),
        compiler_params=pltpu.CompilerParams(vmem_limit_bytes=VMEM_LIMIT, collective_id=1, has_side_effects=True),
        name="back",
    )(part, va, lengths, tokens, qkvc, kc, dep, ca, taps, joined, lse, gf, gj, wp, pw, kw, vec)


def hand_over(x, steps):
    def body(x_ref, out_ref):
        out_ref[...] = x_ref[...]

    block = blocked(x.shape[0] // steps, x.shape[1])
    return pl.pallas_call(
        body,
        grid=(steps,),
        out_shape=jax.ShapeDtypeStruct(x.shape, x.dtype),
        in_specs=[block],
        out_specs=block,
        compiler_params=pltpu.CompilerParams(vmem_limit_bytes=VMEM_LIMIT),
        name="hand_over",
    )(x)


def shards(tokens, doc_lengths, params, cotangent):
    rows = params.shape[0] // LANES
    outer, inner = lax.axis_size("dp"), lax.axis_size("fsdp")
    first, second = sections(outer * inner, rows, inner)
    *saved, dw, fi, fo, wp, pw, kw, vec = run_front(first, second, params.reshape(rows, LANES), tokens, doc_lengths)
    output, gf, gj, part, va = run_mid(second, tokens, doc_lengths, saved[5], cotangent, dw, fi, fo, vec)
    gt, own_grad = run_back(first, second, part, va, tokens, doc_lengths, saved, gf, gj, wp, pw, kw, vec)
    return output, hand_over(gt, 2 * doc_lengths.shape[0]), own_grad.reshape(rows * LANES)


def solution(mesh):
    axes = ("dp", "fsdp")
    placed = (P(axes, None), P(axes, None), P(axes), P(axes, None))
    return jax.shard_map(
        shards,
        mesh=mesh,
        in_specs=placed,
        out_specs=(P(axes, None), P(axes, None), P(axes)),
        check_vma=False,
    )
```
